32 devices in a mesh: dp: 32 (over z, y, x, core).
Axes of the slice: x: 2, y: 2, z: 4, core: 2. Of those that a mesh axis runs over, the one named last changes fastest.
Arguments:
- frames: bfloat16 [65536, 256], P('dp'), may hold values from -16 to 16
- dw_first: bfloat16 [5, 25, 256], P(None, None, 'dp'), may hold values from -1.25 to 1.25
- dw_second: bfloat16 [5, 27, 256], P(None, None, 'dp'), may hold values from -1.25 to 1.25
- point: bfloat16 [2, 6, 256, 256], P(None, None, 'dp'), may hold values from -0.375 to 0.375
- gains: bfloat16 [2, 6, 256], P(None, None, 'dp'), may hold values from 0.099609375 to 1.8984375
- shifts: bfloat16 [2, 6, 256], P(None, None, 'dp'), may hold values from -1.5 to 1.5
- se_down: bfloat16 [2, 256, 32], P(None, 'dp'), may hold values from -0.375 to 0.375
- se_up: bfloat16 [2, 32, 256], P(None, None, 'dp'), may hold values from -1 to 1
- cotangent: float32 [32768, 256], P('dp'), may hold values from -6 to 6
- lengths: int32 [64], P('dp'), may hold values from 130 to 1150, as said below
Outputs:
- output: float32 [32768, 256], P('dp')
- frames_grad: float32 [65536, 256], P('dp')
- dw_first_grad: float32 [5, 25, 256], P(None, None, 'dp')
- dw_second_grad: float32 [5, 27, 256], P(None, None, 'dp')
- point_grad: float32 [2, 6, 256, 256], P(None, None, 'dp')
- gains_grad: float32 [2, 6, 256], P(None, None, 'dp')
- shifts_grad: float32 [2, 6, 256], P(None, None, 'dp')
- se_down_grad: float32 [2, 256, 32], P(None, 'dp')
- se_up_grad: float32 [2, 32, 256], P(None, None, 'dp')
The draws below stay inside these ranges and needn't reach their ends.
Inputs may be any that keep to these rules, and one draw needn't show every extreme that they name: Entries 2 * j to 2 * j + 1 are device j's utterances; every length is even and positive; one device's lengths sum to at most 2048, and to exactly 2048 on some device.
All inputs are finite; a program needn't handle non-finite values.
Results may differ from the reference program's by a relative error of at most 0.025.
Values may be sent and summed in bfloat16 or wider, within the bound.
A program may use at most 320 MiB of HBM per device.

```python
import math
from functools import partial
import jax
import jax.numpy as jnp
from jax import lax

C = 256
SE = 32
R = 5
K1 = 25
K2 = 27
FR_DEV = 2048
UTT_DEV = 2
FRAMES = 65536
OUT_FRAMES = 32768
UTTERANCES = 64
N_DP = 32


def draw_lengths(key, part):
    key = jax.random.fold_in(key, 11)
    pick_key, full_key, jitter_key = jax.random.split(key, 3)
    device_total = UTTERANCES // UTT_DEV
    bucket = jax.random.randint(pick_key, (device_total,), 0, 4)
    chosen = jax.random.randint(full_key, (), 0, device_total)
    device_rows = jnp.arange(device_total)
    bucket = jnp.where(device_rows == chosen, 0, bucket)
    quarter = FR_DEV // (8 * UTT_DEV)
    spread = max(quarter // 2, 1)
    jitter = jax.random.randint(jitter_key, (device_total, UTT_DEV), 0, spread)
    leading = (jnp.arange(UTT_DEV) == 0).astype(jnp.int32)
    jitter = jnp.where((device_rows == chosen)[:, None], leading[None, :] * (spread - 1), jitter)
    halves = (quarter * (4 - bucket))[:, None] + jitter - jnp.roll(jitter, 1, axis=1)
    return (2 * halves).reshape(-1).astype(jnp.int32)


def device_position(devices_total):
    return jnp.arange(devices_total, dtype=jnp.float32) / float(max(devices_total - 1, 1))


def draw_frames(key, part):
    key = jax.random.fold_in(key, 5)
    noise_key = jax.random.fold_in(key, 0)
    wobble_key = jax.random.fold_in(key, 3)
    devices_total = FRAMES // FR_DEV
    position = device_position(devices_total)
    wobble = jax.random.uniform(wobble_key, (devices_total,), jnp.float32, -0.25, 0.25)
    device_scale = jnp.exp(math.log(0.35) + (math.log(2.0) - math.log(0.35)) * position + wobble)[:, None, None]
    device_shift = (2.0 * position - 1.0)[:, None, None]
    values = jax.random.normal(noise_key, (devices_total, FR_DEV, C), jnp.float32)
    values = device_scale * values + device_shift
    values = jnp.clip(values, -16.0, 16.0)
    return values.reshape(FRAMES, C).astype(jnp.bfloat16)


def draw_cotangent(key, part):
    key = jax.random.fold_in(key, 7)
    noise_key, wobble_key = jax.random.split(key, 2)
    frame_rows = FR_DEV // 2
    devices_total = OUT_FRAMES // frame_rows
    position = device_position(devices_total)
    wobble = jax.random.uniform(wobble_key, (devices_total,), jnp.float32, -0.3, 0.3)
    device_shift = (3.0 * position - 1.5 + wobble)[:, None, None]
    values = jax.random.normal(noise_key, (devices_total, frame_rows, C), jnp.float32)
    values = jnp.clip(values + device_shift, -6.0, 6.0)
    return values.reshape(OUT_FRAMES, C).astype(jnp.float32)


def block_scale(stream_key, extent, pieces, smallest, top_value):
    level, own = 1.0, jax.random.fold_in(stream_key, 6)
    for dim, shards_of in pieces:
        heights = jnp.exp(jax.random.uniform(jax.random.fold_in(own, dim), (shards_of,), jnp.float32, smallest / len(pieces), top_value / len(pieces)))
        level = level * jnp.repeat(heights, extent[dim] // shards_of).reshape([-1 if axis == dim else 1 for axis in range(len(extent))])
    return level


def noise(key, dims, scale, bound, cuts=(), kind=jnp.bfloat16):
    gain = block_scale(key, dims, cuts, -0.22, 0.18) if cuts else 1.0
    values = jax.random.normal(key, dims, jnp.float32) * scale * gain
    return jnp.minimum(jnp.maximum(values, -bound), bound).astype(kind)


def setup_inputs(seed: int = 0) -> dict:
    splits = jax.random.split(jax.random.key(seed), 11)
    return {
        "frames": draw_frames(jax.random.fold_in(splits[10], 71), 0),
        "dw_first": noise(splits[1], (R, K1, C), K1 ** -0.5, 1.25, ((2, 32),)),
        "dw_second": noise(splits[2], (R, K2, C), K2 ** -0.5, 1.25, ((2, 32),)),
        "point": noise(splits[3], (2, R + 1, C, C), C ** -0.5, 0.375, ((2, 32),)),
        "gains": jnp.clip(1.0 + 0.18 * jax.random.normal(splits[4], (2, R + 1, C), jnp.float32), 0.099609375, 1.8984375).astype(jnp.bfloat16),
        "shifts": noise(splits[5], (2, R + 1, C), 0.3, 1.5, ((2, 32),)),
        "se_down": noise(splits[6], (2, C, SE), C ** -0.5, 0.375, ((1, 32),)),
        "se_up": noise(splits[7], (2, SE, C), SE ** -0.5, 1.0, ((2, 32),)),
        "cotangent": draw_cotangent(jax.random.fold_in(splits[10], 71), 0),
        "lengths": draw_lengths(jax.random.fold_in(splits[10], 71), 0),
    }


EPSILON = 1e-05
HIGHEST = lax.Precision.HIGHEST

@jax.custom_vjp
def low(v):
    return lax.optimization_barrier(v.astype(jnp.bfloat16)).astype(jnp.float32)

@jax.custom_vjp
def low_back(v):
    return v

def low_keep(v):
    return (low(v), None)

def low_pass(kept, grad):
    return (grad,)

def back_keep(v):
    return (v, None)

def back_low(kept, grad):
    return (low(grad),)
low.defvjp(low_keep, low_pass)
low_back.defvjp(back_keep, back_low)

def depthwise(signal, kernel, source_ids, target_ids, stride):
    tap_count = kernel.shape[0]
    margin = (tap_count - 1) // 2
    outputs = target_ids.shape[0]
    channels = signal.shape[1]
    padded = jnp.pad(signal, ((margin, margin), (0, 0)))
    padded_ids = jnp.pad(source_ids, (margin, margin), constant_values=-1)
    result = jnp.zeros((outputs, channels), jnp.float32)
    for k in range(tap_count):
        slice_end = k + stride * (outputs - 1) + 1
        window = lax.slice(padded, (k, 0), (slice_end, channels), (stride, 1))
        window_ids = lax.slice(padded_ids, (k,), (slice_end,), (stride,))
        same_utterance = (window_ids == target_ids).astype(jnp.float32)[:, None]
        result = result + window * same_utterance * kernel[k]
    return result

def reference(frames, dw_first, dw_second, point, gains, shifts, se_down, se_up, cotangent, lengths):
    per_device = lengths.reshape(-1, UTT_DEV)
    utterance_ends = jnp.cumsum(per_device, axis=1, dtype=jnp.int32)
    positions = jnp.arange(FR_DEV, dtype=jnp.int32)
    segment_local = lax.optimization_barrier(jnp.sum((positions[None, :, None] >= utterance_ends[:, None, :]).astype(jnp.int32), axis=2, dtype=jnp.int32))
    device_rows = jnp.arange(N_DP, dtype=jnp.int32)[:, None]
    segment_in = (device_rows * (UTT_DEV + 1) + segment_local).reshape(-1).astype(jnp.int32)
    valid_in = (segment_local < UTT_DEV).astype(jnp.float32).reshape(-1, 1)
    utterance_ids = (device_rows * UTT_DEV + jnp.minimum(segment_local, UTT_DEV - 1)).reshape(-1)[::2].astype(jnp.int32)
    segment_out = segment_in[::2]
    valid_out = valid_in[::2]
    half_lengths = lengths.astype(jnp.float32) / 2.0
    frame_total = jnp.sum(lengths, dtype=jnp.int32).astype(jnp.float32) / 2.0

    def normalize(product, gain_row, shift_row):
        center = lax.optimization_barrier(jnp.sum(product * valid_out, axis=0)) / frame_total
        centered = (product - center) * valid_out
        variance = lax.optimization_barrier(jnp.sum(centered * centered, axis=0)) / frame_total
        return (product - center) * lax.rsqrt(variance + EPSILON) * gain_row + shift_row

    def sub_block(hidden, kernel, matrix, gain_row, shift_row, source_ids, step_size, is_last):
        filtered = depthwise(hidden, kernel, source_ids, segment_out, step_size)
        product = low_back(jnp.dot(low(filtered), matrix, precision=HIGHEST))
        normed = normalize(product, gain_row, shift_row)
        if is_last:
            return normed
        return jax.nn.silu(normed) * valid_out

    def block(signal, source_ids, stride, kernels, matrices, gain_table, shift_table, squeeze, expand):
        hidden = signal
        for r in range(R):
            step_size = stride if r == 0 else 1
            segment_ids = source_ids if r == 0 else segment_out
            checked = jax.checkpoint(partial(sub_block, source_ids=segment_ids, step_size=step_size, is_last=r == R - 1))
            hidden = checked(hidden, kernels[r], matrices[r], gain_table[r], shift_table[r])

        def tail(last_z, signal_in, matrix, gain_row, shift_row, squeeze_in, expand_in):
            strided = signal_in[::stride]
            residual = low_back(jnp.dot(low(strided), matrix, precision=HIGHEST))
            residual_z = normalize(residual, gain_row, shift_row)
            means = jax.ops.segment_sum(last_z * valid_out, utterance_ids, num_segments=UTTERANCES) / half_lengths[:, None]
            excited = jax.nn.silu(jnp.dot(means, squeeze_in, precision=HIGHEST))
            scale = jax.nn.sigmoid(jnp.dot(excited, expand_in, precision=HIGHEST))
            mixed = last_z * scale[utterance_ids]
            return jax.nn.silu(mixed + residual_z) * valid_out
        return jax.checkpoint(tail)(hidden, signal, matrices[R], gain_table[R], shift_table[R], squeeze, expand)

    def forward(frames_in, first_kernels, second_kernels, matrices, gain_table, shift_table, squeeze, expand):
        signal = frames_in * valid_in
        first_out = block(signal, segment_in, 2, first_kernels, matrices[0], gain_table[0], shift_table[0], squeeze[0], expand[0])
        return block(first_out, segment_out, 1, second_kernels, matrices[1], gain_table[1], shift_table[1], squeeze[1], expand[1])
    primals = tuple((value.astype(jnp.float32) for value in (frames, dw_first, dw_second, point, gains, shifts, se_down, se_up)))
    output, pullback = jax.vjp(forward, *primals)
    grads = pullback(cotangent)
    return (output, grads[0], grads[1], grads[2], grads[3], grads[4], grads[5], grads[6], grads[7])
```

```python
import functools

import jax
import jax.numpy as jnp
from jax import lax
from jax.experimental import pallas as pl
from jax.experimental.pallas import tpu as pltpu
from jax.sharding import PartitionSpec as P

EPSILON = 1e-05
HIGHEST = lax.Precision.HIGHEST
F32 = jnp.float32
BF16 = jnp.bfloat16
MESH = pl.DeviceIdType.MESH

GAP = 16
HALO = 13
LANES = 128


def sigmoid(v):
    return 0.5 * jnp.tanh(0.5 * v) + 0.5


class Plan:
    def __init__(self, slots, channels, taps_first, taps_second, sub_blocks, hidden, devices):
        self.slots = slots
        self.steps = (slots + GAP) // 8
        self.rows = 8 * self.steps
        self.channels = channels
        self.halves = channels // LANES
        self.taps = (taps_first, taps_second)
        self.max_taps = max(self.taps)
        self.sub = sub_blocks
        self.hidden = hidden
        self.devices = devices
        self.block = next(r for r in (26, 10, 2) if self.steps % r == 0)
        self.fine = next(r for r in (10, 26, 2) if self.steps % r == 0)
        self.pad = self.steps + 2 * HALO


def peers_of(me, n):
    if n != 32:
        return [lax.rem(me + k, n) for k in range(1, n)]
    core = lax.rem(me, 2)
    x = lax.rem(me // 2, 2)
    y = lax.rem(me // 4, 2)
    z = me // 8
    found = []
    for order, other in enumerate((3 - z, lax.rem(z + 2, 4), z + 1 - 2 * lax.rem(z, 2), z)):
        for dy in (1, 0):
            for dx in (1, 0):
                for dc in (0, 1):
                    if order == 3 and dy == 0 and dx == 0 and dc == 0:
                        continue
                    oy = lax.rem(y + dy, 2)
                    ox = lax.rem(x + dx, 2)
                    oc = lax.rem(core + dc, 2)
                    found.append((dy + dx + (3, 2, 1, 0)[order], other * 8 + oy * 4 + ox * 2 + oc))
    found.sort(key=lambda item: -item[0])
    return [item[1] for item in found]


def kernel(plan, lens, frames, cot, dw, point, gains, shifts, squeeze_t, expand,
           out, frames_grad, dw_grad, point_grad, gains_grad, shifts_grad, squeeze_grad, expand_grad,
           hid, acts, prods, gd, gz, gpb, gqb, pre, flat, wide, first_mask, second_mask, valid,
           stats, send4, recv4, counts, csend, send_sem, recv_sem, count_sems):
    N = plan.devices
    Q, R, RF = plan.steps, plan.block, plan.fine
    HV = range(plan.halves)
    SUB = plan.sub
    me = lax.axis_index("dp")
    peers = peers_of(me, N)

    barrier = pltpu.get_barrier_semaphore()
    for peer in peers:
        pl.semaphore_signal(barrier, inc=1, device_id=(peer,), device_id_type=MESH)

    len0 = lens[0]
    len1 = lens[1]
    half0 = len0 // 2
    half1 = len1 // 2
    count = (half0 + half1).astype(F32)
    inv_half = (1.0 / jnp.full((1, LANES), half0, jnp.int32).astype(F32),
                1.0 / jnp.full((1, LANES), half1, jnp.int32).astype(F32))

    def steps_loop(width, body, init=0):
        return lax.fori_loop(0, Q // width, lambda i, c: body(i * width, c), init)

    def mask_body(t0, c):
        step = t0 + lax.broadcasted_iota(jnp.int32, (RF, 8, LANES), 0)
        slot = step + Q * lax.broadcasted_iota(jnp.int32, (RF, 8, LANES), 1)
        a = (slot < half0).astype(F32)
        b = jnp.logical_and(slot >= half0 + GAP, slot < half0 + GAP + half1).astype(F32)
        first_mask[pl.ds(t0, RF)] = a
        second_mask[pl.ds(t0, RF)] = b
        valid[pl.ds(t0, RF)] = a + b
        return c

    steps_loop(RF, mask_body)

    top = 2 * GAP + 2 * plan.slots
    for h in HV:
        wide[h, 0:2 * GAP] = jnp.zeros((2 * GAP, LANES), F32)
        wide[h, top:] = jnp.zeros((wide.shape[1] - top, LANES), F32)

    def widen(i, c):
        rows = pl.ds(pl.multiple_of(i * 128, 128), 128)
        for h in HV:
            values = frames[rows, h * LANES:(h + 1) * LANES].astype(F32)
            wide[h, pl.ds(pl.multiple_of(i * 128 + 2 * GAP, 32), 128)] = values
        return c

    lax.fori_loop(0, 2 * plan.slots // 128, widen, 0)

    def set_halo(ref, half):
        sub = lax.broadcasted_iota(jnp.int32, (HALO, 8, LANES), 1)
        low = pltpu.roll(ref[half, pl.ds(Q, HALO)], 1, 1)
        ref[half, pl.ds(0, HALO)] = jnp.where(sub == 0, 0.0, low)
        high = pltpu.roll(ref[half, pl.ds(HALO, HALO)], 7, 1)
        ref[half, pl.ds(HALO + Q, HALO)] = jnp.where(sub == 7, 0.0, high)

    for phase in range(2):
        def deinterleave(t0, c):
            for j in range(RF):
                a_mask = first_mask[t0 + j]
                b_mask = second_mask[t0 + j]
                for h in HV:
                    a = wide[h, pl.ds(2 * (t0 + j) + 2 * GAP + phase, 8, stride=2 * Q)]
                    b = wide[h, pl.ds(2 * (t0 + j) + phase, 8, stride=2 * Q)]
                    hid[phase, h, HALO + t0 + j] = a * a_mask + b * b_mask
            return c
        steps_loop(RF, deinterleave)
        for h in HV:
            set_halo(hid.at[phase], h)

    csend[...] = jnp.full((4, LANES), count, F32)
    pl.semaphore_wait(barrier, N - 1)

    def send_to_all(src, dst, ssem, rsem):
        for peer in peers:
            pltpu.make_async_remote_copy(src_ref=src, dst_ref=dst, send_sem=ssem, recv_sem=rsem,
                                         device_id=(peer,), device_id_type=MESH).start()

    def wait_all(ref, sem):
        view = ref.at[pl.ds(0, N - 1)]
        pltpu.make_async_copy(view, view, sem).wait()

    send_to_all(csend, counts.at[me], count_sems.at[0], count_sems.at[1])
    counts[me] = csend[...]

    def exchange(slot, place, rows):
        send4[slot] = rows
        recv4[place, me] = rows
        send_to_all(send4.at[slot], recv4.at[place, me], send_sem.at[slot], recv_sem.at[slot])

    def received(slot, place):
        wait_all(recv4.at[place], recv_sem.at[slot])
        return recv4[place]

    def back_place(index):
        return lax.rem(index + SUB, 2 * SUB)

    def row(values):
        return values.reshape(1, 1, LANES)

    def accumulate(rows3):
        return jnp.sum(rows3, axis=0)

    def local_stats(index):
        def total(t0, c):
            v = valid[pl.ds(t0, R)]
            return tuple(c[h] + accumulate(prods[index, h, pl.ds(t0, R)] * v) for h in HV)
        zeros = tuple(jnp.zeros((8, LANES), F32) for h in HV)
        sums = steps_loop(R, total, zeros)
        means = [jnp.sum(sums[h], axis=0, keepdims=True) / jnp.full((1, LANES), count, F32) for h in HV]

        def squares(t0, c):
            v = valid[pl.ds(t0, R)]
            res = []
            for h in HV:
                d = (prods[index, h, pl.ds(t0, R)] - row(means[h])) * v
                res.append(c[h] + accumulate(d * d))
            return tuple(res)
        sq = steps_loop(R, squares, zeros)
        return jnp.concatenate(means + [jnp.sum(sq[h], axis=0, keepdims=True) for h in HV], axis=0)

    def merge_stats(slot, index):
        got = received(slot, slot)
        weight = counts[...]
        total = jnp.sum(weight, axis=0)
        mean = jnp.sum(weight * got, axis=0) / total
        mean4 = jnp.concatenate([mean[0:2], mean[0:2]], axis=0)
        diff = got - mean4
        between = jnp.sum(weight * diff * diff, axis=0)
        within = jnp.sum(got, axis=0)
        var = (within[2:4] + between[0:2]) / total[0:2]
        inv = lax.rsqrt(var + EPSILON)
        scale = inv * gains[index]
        offset = shifts[index] - mean[0:2] * scale
        stats[index] = jnp.concatenate([mean[0:2], inv, scale, offset], axis=0)

    def stat_row(index, kind, h):
        return row(stats[index, pl.ds(2 * kind + h, 1)])

    def layer_conv(index, pieces):
        def body(t0, c):
            for h in HV:
                acc = None
                for source, taps in pieces:
                    low = min(s for _, s in taps)
                    high = max(s for _, s in taps)
                    win = hid[source, h, pl.ds(t0 + HALO + low, R + high - low)]
                    for tap, shift in taps:
                        term = win[shift - low:shift - low + R] * dw[index, h, pl.ds(tap, 1)].reshape(1, 1, LANES)
                        acc = term if acc is None else acc + term
                rows = pl.ds(pl.multiple_of(8 * t0, 16), 8 * R)
                acts[index, rows, h * LANES:(h + 1) * LANES] = acc.reshape(8 * R, LANES).astype(BF16)
            return c
        steps_loop(R, body)

    def pointwise(act, index):
        def body(t0, c):
            rows = pl.ds(pl.multiple_of(8 * t0, 16), 8 * R)
            res = jnp.dot(acts[act, rows], point[index], preferred_element_type=F32)
            for h in HV:
                prods[index, h, pl.ds(t0, R)] = res[:, h * LANES:(h + 1) * LANES].reshape(R, 8, LANES)
            return c
        steps_loop(R, body)

    def activate(index, target):
        scales = [stat_row(index, 2, h) for h in HV]
        offsets = [stat_row(index, 3, h) for h in HV]

        def body(t0, c):
            v = valid[pl.ds(t0, RF)]
            for h in HV:
                z = prods[index, h, pl.ds(t0, RF)] * scales[h] + offsets[h]
                hid[target, h, pl.ds(HALO + t0, RF)] = z * sigmoid(z) * v
            return c
        steps_loop(RF, body)
        for h in HV:
            set_halo(hid.at[target], h)

    def block_pieces(b, r):
        taps = plan.taps[b]
        margin = (taps - 1) // 2
        if b == 0 and r == 0:
            even = [(k, (k - margin) // 2) for k in range(taps) if (k - margin) % 2 == 0]
            odd = [(k, (k - margin - 1) // 2) for k in range(taps) if (k - margin) % 2 == 1]
            return [(0, even), (1, odd)]
        return [(b * SUB + r + 1, [(k, k - margin) for k in range(taps)])]

    def residual_input(b):
        source = 0 if b == 0 else SUB + 1

        def body(t0, c):
            rows = pl.ds(pl.multiple_of(8 * t0, 16), 8 * R)
            for h in HV:
                values = hid[source, h, pl.ds(HALO + t0, R)].reshape(8 * R, LANES)
                acts[2 * SUB + b, rows, h * LANES:(h + 1) * LANES] = values.astype(BF16)
            return c
        steps_loop(R, body)

    def pair_rows(values):
        return jnp.concatenate([values, jnp.zeros((6, plan.channels), F32)], axis=0)

    def small(a, b, dims):
        return lax.dot_general(a, b, (dims, ((), ())), precision=HIGHEST, preferred_element_type=F32)

    def excite(b):
        last = b * SUB + SUB - 1
        scales = [stat_row(last, 2, h) for h in HV]
        offsets = [stat_row(last, 3, h) for h in HV]

        def sums(t0, c):
            a, s = first_mask[pl.ds(t0, RF)], second_mask[pl.ds(t0, RF)]
            res = []
            for h in HV:
                z = prods[last, h, pl.ds(t0, RF)] * scales[h] + offsets[h]
                res.append(c[2 * h] + accumulate(z * a))
                res.append(c[2 * h + 1] + accumulate(z * s))
            return tuple(res)
        tot = steps_loop(RF, sums, tuple(jnp.zeros((8, LANES), F32) for _ in range(2 * plan.halves)))
        means = jnp.concatenate(
            [jnp.concatenate([jnp.sum(tot[2 * h + u], axis=0, keepdims=True) * inv_half[u] for h in HV], axis=1)
             for u in range(2)], axis=0)
        means = pair_rows(means)
        inner = small(means, squeeze_t[b], ((1,), (1,)))
        excited = inner * sigmoid(inner)
        gate = sigmoid(small(excited, expand[b], ((1,), (0,))))
        return means, inner, excited, gate

    def gate_rows(gate):
        return [[row(gate[u:u + 1, h * LANES:(h + 1) * LANES]) for h in HV] for u in range(2)]

    def tail(b, gate, store):
        last, res = b * SUB + SUB - 1, 2 * SUB + b
        gates = gate_rows(gate)
        consts = [(stat_row(last, 2, h), stat_row(last, 3, h), stat_row(res, 2, h), stat_row(res, 3, h)) for h in HV]

        def body(t0, c):
            v = valid[pl.ds(t0, RF)]
            a = first_mask[pl.ds(t0, RF)]
            for h in HV:
                s1, o1, s2, o2 = consts[h]
                z = prods[last, h, pl.ds(t0, RF)] * s1 + o1
                y = prods[res, h, pl.ds(t0, RF)] * s2 + o2
                g = jnp.where(a > 0.5, gates[0][h], gates[1][h])
                s = z * g + y
                pre[b, h, pl.ds(t0, RF)] = s
                store(t0, h, s * sigmoid(s) * v)
            return c
        steps_loop(RF, body)

    def forward_block(b):
        def layer(r, pieces):
            index = b * SUB + r
            layer_conv(index, pieces)
            pointwise(index, index)
            exchange(index, index, local_stats(index))
        layer(0, block_pieces(b, 0))
        residual_input(b)
        pointwise(2 * SUB + b, 2 * SUB + b)
        exchange(2 * SUB + b, 2 * SUB + b, local_stats(2 * SUB + b))
        merge_stats(b * SUB, b * SUB)
        activate(b * SUB, b * SUB + 2)

        def rest(r, c):
            taps = plan.taps[b]
            margin = (taps - 1) // 2
            index = b * SUB + r
            layer(r, [(index + 1, [(k, k - margin) for k in range(taps)])])
            merge_stats(index, index)

            @pl.when(r < SUB - 1)
            def _():
                activate(index, index + 2)
            return c
        lax.fori_loop(1, SUB, rest, 0)
        merge_stats(2 * SUB + b, 2 * SUB + b)
        return excite(b)

    back_slot = 2 * SUB + 2

    def sum_rows(parts):
        return jnp.concatenate([jnp.sum(part, axis=0, keepdims=True) for part in parts], axis=0)

    def tail_back(b, kept, load):
        means, inner, excited, gate = kept
        last, res = b * SUB + SUB - 1, 2 * SUB + b
        gates = gate_rows(gate)
        consts = [(stat_row(last, 2, h), stat_row(last, 3, h)) for h in HV]

        def first(t0, c):
            v = valid[pl.ds(t0, RF)]
            a, q = first_mask[pl.ds(t0, RF)], second_mask[pl.ds(t0, RF)]
            out_c = []
            for h in HV:
                s = pre[b, h, pl.ds(t0, RF)]
                sg = sigmoid(s)
                gs = load(t0, h) * (sg * (1.0 + s * (1.0 - sg))) * v
                pre[b, h, pl.ds(t0, RF)] = gs
                z = prods[last, h, pl.ds(t0, RF)] * consts[h][0] + consts[h][1]
                gsz = gs * z
                out_c.append(c[2 * h] + accumulate(gsz * a))
                out_c.append(c[2 * h + 1] + accumulate(gsz * q))
            return tuple(out_c)
        zero4 = tuple(jnp.zeros((8, LANES), F32) for _ in range(2 * plan.halves))
        tot = steps_loop(RF, first, zero4)
        grad_gate = pair_rows(jnp.concatenate(
            [jnp.concatenate([jnp.sum(tot[2 * h + u], axis=0, keepdims=True) for h in HV], axis=1)
             for u in range(2)], axis=0))
        grad_up = grad_gate * gate * (1.0 - gate)
        expand_grad[b] = small(excited, grad_up, ((0,), (0,)))
        grad_excited = small(grad_up, expand[b], ((1,), (1,)))
        sg = sigmoid(inner)
        grad_inner = grad_excited * (sg * (1.0 + inner * (1.0 - sg)))
        squeeze_grad[b] = small(grad_inner, means, ((0,), (0,)))
        grad_means = small(grad_inner, squeeze_t[b], ((1,), (0,)))
        mean_rows = [[row(grad_means[u:u + 1, h * LANES:(h + 1) * LANES] * inv_half[u]) for h in HV]
                     for u in range(2)]
        norm1 = [(stat_row(last, 0, h), stat_row(last, 1, h)) for h in HV]
        norm2 = [(stat_row(res, 0, h), stat_row(res, 1, h)) for h in HV]

        def second(t0, c):
            a = first_mask[pl.ds(t0, RF)]
            v = valid[pl.ds(t0, RF)]
            out_c = []
            for h in HV:
                gs = pre[b, h, pl.ds(t0, RF)]
                g = jnp.where(a > 0.5, gates[0][h], gates[1][h])
                m = jnp.where(a > 0.5, mean_rows[0][h], mean_rows[1][h])
                grad = gs * g + m * v
                gz[h, pl.ds(t0, RF)] = grad
                x1 = (prods[last, h, pl.ds(t0, RF)] - norm1[h][0]) * norm1[h][1]
                x2 = (prods[res, h, pl.ds(t0, RF)] - norm2[h][0]) * norm2[h][1]
                out_c += [c[4 * h] + accumulate(grad), c[4 * h + 1] + accumulate(grad * x1),
                          c[4 * h + 2] + accumulate(gs), c[4 * h + 3] + accumulate(gs * x2)]
            return tuple(out_c)
        tot = steps_loop(RF, second, zero4 + zero4)
        exchange(back_slot + last, back_place(last), sum_rows([tot[0], tot[4], tot[1], tot[5]]))
        exchange(back_slot + res, 2 * SUB + 1 - b, sum_rows([tot[2], tot[6], tot[3], tot[7]]))

    def norm_back(index, place, load, target):
        sums = jnp.sum(received(back_slot + index, place), axis=0)
        shifts_grad[index] = sums[0:2]
        gains_grad[index] = sums[2:4]
        total = jnp.sum(counts[...], axis=0)[0:2]
        st = stats[index]
        mean, inv, scale = st[0:2], st[2:4], st[4:6]
        k1 = scale * sums[0:2] / total
        k2 = scale * sums[2:4] / total * inv
        rows3 = [[row(value[h:h + 1]) for value in (mean, scale, k1, k2)] for h in HV]

        def body(t0, c):
            v = valid[pl.ds(t0, R)]
            rows = pl.ds(pl.multiple_of(8 * t0, 16), 8 * R)
            for h in HV:
                mean_h, scale_h, k1_h, k2_h = rows3[h]
                grad = (scale_h * load(t0, h) - k1_h - k2_h * (prods[index, h, pl.ds(t0, R)] - mean_h)) * v
                target[rows, h * LANES:(h + 1) * LANES] = grad.reshape(8 * R, LANES).astype(BF16)
            return c
        steps_loop(R, body)

    def pointwise_back(index, source, store):
        def body(t0, c):
            rows = pl.ds(pl.multiple_of(8 * t0, 16), 8 * R)
            res = lax.dot_general(source[rows], point[index], (((1,), (1,)), ((), ())), preferred_element_type=F32)
            for h in HV:
                store(t0, h, res[:, h * LANES:(h + 1) * LANES].reshape(R, 8, LANES))
            return c
        steps_loop(R, body)

    def point_back(index, act, source):
        point_grad[index] = lax.dot_general(acts[act], source[...], (((0,), (0,)), ((), ())),
                                            preferred_element_type=F32)

    def store_gd(t0, h, values):
        gd[h, pl.ds(HALO + t0, R)] = values

    def conv_back_block(t0, h, index, taps):
        low = min(-s for _, s in taps)
        high = max(-s for _, s in taps)
        win = gd[h, pl.ds(t0 + HALO + low, R + high - low)]
        acc = None
        for tap, shift in taps:
            term = win[-shift - low:-shift - low + R] * dw[index, h, pl.ds(tap, 1)].reshape(1, 1, LANES)
            acc = term if acc is None else acc + term
        return acc

    def kernel_back(index, pieces):
        for source, taps in pieces:
            for h in HV:
                low = min(s for _, s in taps)
                high = max(s for _, s in taps)

                def body(t0, c):
                    g = gd[h, pl.ds(HALO + t0, RF)]
                    win = hid[source, h, pl.ds(t0 + HALO + low, RF + high - low)]
                    return tuple(acc + accumulate(g * win[s - low:s - low + RF]) for acc, (_, s) in zip(c, taps))
                accs = steps_loop(RF, body, tuple(jnp.zeros((8, LANES), F32) for _ in taps))
                for acc, (tap, _) in zip(accs, taps):
                    dw_grad[index, h, pl.ds(tap, 1)] = jnp.sum(acc, axis=0, keepdims=True)

    def hidden_back(index, taps):
        before = index - 1
        consts = [[stat_row(before, kind, h) for kind in range(4)] for h in HV]

        def body(t0, c):
            v = valid[pl.ds(t0, R)]
            res = []
            for h in HV:
                mean, inv, scale, offset = consts[h]
                p = prods[before, h, pl.ds(t0, R)]
                z = p * scale + offset
                sg = sigmoid(z)
                grad = conv_back_block(t0, h, index, taps) * (sg * (1.0 + z * (1.0 - sg))) * v
                gz[h, pl.ds(t0, R)] = grad
                xhat = (p - mean) * inv
                res += [c[2 * h] + accumulate(grad), c[2 * h + 1] + accumulate(grad * xhat)]
            return tuple(res)
        tot = steps_loop(R, body, tuple(jnp.zeros((8, LANES), F32) for _ in range(2 * plan.halves)))
        exchange(back_slot + before, back_place(before), sum_rows([tot[0], tot[2], tot[1], tot[3]]))

    def load_gz(t0, h):
        return gz[h, pl.ds(t0, R)]

    def backward_block(b):
        taps = plan.taps[b]
        margin = (taps - 1) // 2
        regular = [(k, k - margin) for k in range(taps)]
        res = 2 * SUB + b

        def step(j, c):
            r = SUB - 1 - j
            index = b * SUB + r
            norm_back(index, back_place(index), load_gz, gpb)
            pointwise_back(index, gpb, store_gd)
            for h in HV:
                set_halo(gd, h)
            hidden_back(index, regular)
            point_back(index, index, gpb)
            kernel_back(index, [(index + 1, regular)])
            return c
        lax.fori_loop(0, SUB - 1, step, 0)
        norm_back(res, 2 * SUB + 1 - b, lambda t0, h: pre[b, h, pl.ds(t0, R)], gqb)
        point_back(res, res, gqb)
        index = b * SUB
        norm_back(index, back_place(index), load_gz, gpb)
        pointwise_back(index, gpb, store_gd)
        for h in HV:
            set_halo(gd, h)

    wait_all(counts, count_sems.at[1])
    kept_first = forward_block(0)

    def store_middle(t0, h, values):
        hid[SUB + 1, h, pl.ds(HALO + t0, RF)] = values
    tail(0, kept_first[3], store_middle)
    for h in HV:
        set_halo(hid.at[SUB + 1], h)
    kept_second = forward_block(1)

    def store_out(t0, h, values):
        for j in range(RF):
            flat[h, pl.ds(t0 + j, 8, stride=Q)] = values[j]
    tail(1, kept_second[3], store_out)

    def ungap(i, c):
        rows = pl.ds(pl.multiple_of(i * 128, 128), 128)
        slot = i * 128 + lax.broadcasted_iota(jnp.int32, (128, LANES), 0)
        for h in HV:
            moved = flat[h, pl.ds(pl.multiple_of(i * 128 + GAP, 16), 128)]
            out[rows, h * LANES:(h + 1) * LANES] = jnp.where(slot < half0, flat[h, rows], moved)
        return c
    lax.fori_loop(0, plan.slots // 128, ungap, 0)

    for h in HV:
        flat[h, 0:GAP] = jnp.zeros((GAP, LANES), F32)
        flat[h, GAP + plan.slots:] = jnp.zeros((flat.shape[1] - GAP - plan.slots, LANES), F32)

    def place(i, c):
        rows = pl.ds(pl.multiple_of(i * 128, 128), 128)
        for h in HV:
            flat[h, pl.ds(pl.multiple_of(i * 128 + GAP, 16), 128)] = cot[rows, h * LANES:(h + 1) * LANES]
        return c
    lax.fori_loop(0, plan.slots // 128, place, 0)

    def load_cot(t0, h):
        parts = []
        for j in range(RF):
            a = flat[h, pl.ds(t0 + j + GAP, 8, stride=Q)]
            b = flat[h, pl.ds(t0 + j, 8, stride=Q)]
            parts.append(jnp.where(first_mask[t0 + j] > 0.5, a, b))
        return jnp.stack(parts, axis=0)

    tail_back(1, kept_second, load_cot)
    backward_block(1)
    margin = (plan.taps[1] - 1) // 2
    regular = [(k, k - margin) for k in range(plan.taps[1])]

    def store_gz(t0, h, values):
        gz[h, pl.ds(t0, R)] = values
    pointwise_back(2 * SUB + 1, gqb, store_gz)

    def middle(t0, c):
        for h in HV:
            gz[h, pl.ds(t0, R)] = gz[h, pl.ds(t0, R)] + conv_back_block(t0, h, SUB, regular)
        return c
    steps_loop(R, middle)
    tail_back(0, kept_first, lambda t0, h: gz[h, pl.ds(t0, RF)])
    point_back(SUB, SUB, gpb)
    kernel_back(SUB, [(SUB + 1, regular)])
    backward_block(0)
    pieces = block_pieces(0, 0)
    pointwise_back(2 * SUB, gqb, store_gz)

    def spread(t0, c):
        v = valid[pl.ds(t0, R)]
        for h in HV:
            even = (conv_back_block(t0, h, 0, pieces[0][1]) + gz[h, pl.ds(t0, R)]) * v
            odd = conv_back_block(t0, h, 0, pieces[1][1]) * v
            for j in range(R):
                wide[h, pl.ds(2 * (t0 + j), 8, stride=2 * Q)] = even[j]
                wide[h, pl.ds(2 * (t0 + j) + 1, 8, stride=2 * Q)] = odd[j]
        return c
    steps_loop(R, spread)

    def ungap_wide(i, c):
        rows = pl.ds(pl.multiple_of(i * 128, 128), 128)
        slot = i * 128 + lax.broadcasted_iota(jnp.int32, (128, LANES), 0)
        for h in HV:
            moved = wide[h, pl.ds(pl.multiple_of(i * 128 + 2 * GAP, 32), 128)]
            frames_grad[rows, h * LANES:(h + 1) * LANES] = jnp.where(slot < len0, wide[h, rows], moved)
        return c
    lax.fori_loop(0, 2 * plan.slots // 128, ungap_wide, 0)
    point_back(0, 0, gpb)
    kernel_back(0, pieces)

    wait_all(counts, count_sems.at[0])

    def drain(slot, c):
        wait_all(recv4.at[0], send_sem.at[slot])
        return c
    lax.fori_loop(0, send4.shape[0], drain, 0)


def body(frames, dw_first, dw_second, point, gains, shifts, se_down, se_up, cotangent, lengths, *, devices):
    sub, taps_first, shard = dw_first.shape
    taps_second = dw_second.shape[1]
    hidden = se_down.shape[2]
    channels = point.shape[3]
    plan = Plan(cotangent.shape[0], channels, taps_first, taps_second, sub, hidden, devices)
    halves, Q = plan.halves, plan.steps

    def gather(v, axis):
        return lax.all_gather(v, "dp", axis=axis, tiled=True)

    small = jnp.concatenate([
        dw_first.reshape(-1, shard), dw_second.reshape(-1, shard), gains.reshape(-1, shard),
        shifts.reshape(-1, shard), se_up.reshape(-1, shard),
        jnp.swapaxes(se_down, 1, 2).reshape(-1, shard)], axis=0)
    small = gather(small, 1)
    n1, n2, ng, ns = sub * taps_first, sub * taps_second, 2 * (sub + 1), 2 * hidden
    cuts = [0, n1, n1 + n2, n1 + n2 + ng, n1 + n2 + 2 * ng, n1 + n2 + 2 * ng + ns, n1 + n2 + 2 * ng + 2 * ns]
    part = [small[cuts[i]:cuts[i + 1]] for i in range(6)]
    K = 32

    def dw_layout(v, taps):
        v = v.astype(F32).reshape(sub, taps, halves, LANES).transpose(0, 2, 1, 3)
        return jnp.pad(v, ((0, 0), (0, 0), (0, K - taps), (0, 0)))
    dw = jnp.concatenate([dw_layout(part[0], taps_first), dw_layout(part[1], taps_second)], axis=0)

    def norm_layout(v):
        v = v.astype(F32).reshape(2, sub + 1, halves, LANES)
        return jnp.concatenate([v[:, :sub].reshape(2 * sub, halves, LANES), v[:, sub]], axis=0)
    matrices = gather(point, 2)
    matrices = jnp.concatenate([matrices[:, :sub].reshape(2 * sub, channels, channels), matrices[:, sub]], axis=0)
    expand = part[4].astype(F32).reshape(2, hidden, channels)
    squeeze_t = part[5].astype(F32).reshape(2, hidden, channels)

    layers = 2 * sub + 2
    slots = 2 * layers
    shapes = (
        jax.ShapeDtypeStruct((plan.slots, channels), F32),
        jax.ShapeDtypeStruct((2 * plan.slots, channels), F32),
        jax.ShapeDtypeStruct((2 * sub, halves, K, LANES), F32),
        jax.ShapeDtypeStruct((layers, channels, channels), F32),
        jax.ShapeDtypeStruct((layers, halves, LANES), F32),
        jax.ShapeDtypeStruct((layers, halves, LANES), F32),
        jax.ShapeDtypeStruct((2, hidden, channels), F32),
        jax.ShapeDtypeStruct((2, hidden, channels), F32),
    )
    vmem = pl.BlockSpec(memory_space=pltpu.VMEM)
    results = pl.pallas_call(
        functools.partial(kernel, plan),
        out_shape=shapes,
        in_specs=[pl.BlockSpec(memory_space=pltpu.SMEM)] + [vmem] * 8,
        out_specs=[vmem] * len(shapes),
        scratch_shapes=[
            pltpu.VMEM((2 * sub + 1, halves, plan.pad, 8, LANES), F32),
            pltpu.VMEM((layers, plan.rows, channels), BF16),
            pltpu.VMEM((layers, halves, Q, 8, LANES), F32),
            pltpu.VMEM((halves, plan.pad, 8, LANES), F32),
            pltpu.VMEM((halves, Q, 8, LANES), F32),
            pltpu.VMEM((plan.rows, channels), BF16),
            pltpu.VMEM((plan.rows, channels), BF16),
            pltpu.VMEM((2, halves, Q, 8, LANES), F32),
            pltpu.VMEM((halves, plan.slots + 2 * GAP, LANES), F32),
            pltpu.VMEM((halves, 2 * plan.slots + 4 * GAP, LANES), F32),
            pltpu.VMEM((Q, 8, LANES), F32),
            pltpu.VMEM((Q, 8, LANES), F32),
            pltpu.VMEM((Q, 8, LANES), F32),
            pltpu.VMEM((layers, 8, LANES), F32),
            pltpu.VMEM((slots, 4, LANES), F32),
            pltpu.VMEM((layers, devices, 4, LANES), F32),
            pltpu.VMEM((devices, 4, LANES), F32),
            pltpu.VMEM((4, LANES), F32),
            pltpu.SemaphoreType.DMA((slots,)),
            pltpu.SemaphoreType.DMA((slots,)),
            pltpu.SemaphoreType.DMA((2,)),
        ],
        compiler_params=pltpu.CompilerParams(
            collective_id=0, has_side_effects=True, vmem_limit_bytes=62 * 1024 * 1024),
    )(lengths, frames, cotangent, dw, matrices, norm_layout(gains_full(part[2], sub, channels)),
      norm_layout(gains_full(part[3], sub, channels)), squeeze_t, expand)
    output, frames_grad, dwg, pg, gg, sg, sqg, exg = results

    def scatter(v, axis):
        return lax.psum_scatter(v, "dp", scatter_dimension=axis, tiled=True)

    def dw_out(v, taps):
        return v[:, :, :taps].transpose(0, 2, 1, 3).reshape(sub * taps, channels)
    packed = jnp.concatenate([dw_out(dwg[:sub], taps_first), dw_out(dwg[sub:], taps_second),
                              sqg.reshape(-1, channels), exg.reshape(-1, channels)], axis=0)
    packed = scatter(packed, 1)
    g1 = packed[:n1].reshape(sub, taps_first, shard)
    g2 = packed[n1:n1 + n2].reshape(sub, taps_second, shard)
    gsq = jnp.swapaxes(packed[n1 + n2:n1 + n2 + ns].reshape(2, hidden, shard), 1, 2)
    gex = packed[n1 + n2 + ns:].reshape(2, hidden, shard)
    pg = jnp.concatenate([pg[:2 * sub].reshape(2, sub, channels, channels), pg[2 * sub:][:, None]], axis=1)
    pg = scatter(pg, 2)

    def norm_out(v):
        v = v.reshape(layers, channels)
        v = jnp.concatenate([v[:2 * sub].reshape(2, sub, channels), v[2 * sub:][:, None]], axis=1)
        return lax.dynamic_slice_in_dim(v, lax.axis_index("dp") * shard, shard, 2)
    return (output, frames_grad, g1, g2, pg, norm_out(gg), norm_out(sg), gsq, gex)


def gains_full(v, sub, channels):
    return v.reshape(2, sub + 1, channels)


def solution(mesh):
    return jax.shard_map(
        functools.partial(body, devices=mesh.shape["dp"]),
        mesh=mesh,
        in_specs=(
            P("dp", None),
            P(None, None, "dp"),
            P(None, None, "dp"),
            P(None, None, "dp", None),
            P(None, None, "dp"),
            P(None, None, "dp"),
            P(None, "dp", None),
            P(None, None, "dp"),
            P("dp", None),
            P("dp"),
        ),
        out_specs=(
            P("dp", None),
            P("dp", None),
            P(None, None, "dp"),
            P(None, None, "dp"),
            P(None, None, "dp", None),
            P(None, None, "dp"),
            P(None, None, "dp"),
            P(None, "dp", None),
            P(None, None, "dp"),
        ),
        check_vma=False,
    )
```

```python
import functools

import jax
import jax.numpy as jnp
from jax import lax
from jax.experimental import pallas as pl
from jax.experimental.pallas import tpu as pltpu
from jax.sharding import PartitionSpec as P

EPSILON = 1e-05
HIGHEST = lax.Precision.HIGHEST
F32 = jnp.float32
BF16 = jnp.bfloat16
MESH = pl.DeviceIdType.MESH

GAP = 16
HALO = 13
LANES = 128


def sigmoid(v):
    return 0.5 * jnp.tanh(0.5 * v) + 0.5


class Plan:
    def __init__(self, slots, channels, taps_first, taps_second, sub_blocks, hidden, devices):
        self.slots = slots
        self.steps = (slots + GAP) // 8
        self.rows = 8 * self.steps
        self.channels = channels
        self.halves = channels // LANES
        self.taps = (taps_first, taps_second)
        self.max_taps = max(self.taps)
        self.sub = sub_blocks
        self.hidden = hidden
        self.devices = devices
        self.block = next(r for r in (26, 10, 2) if self.steps % r == 0)
        self.fine = next(r for r in (10, 26, 2) if self.steps % r == 0)
        self.pad = self.steps + 2 * HALO
        self.per = sub_blocks + 1
        self.layers = 2 * self.per
        self.tap_rows = 32
        self.values = 2 * LANES
        self.shard = channels // devices
        self.fused = self.shard == 8 and devices % 2 == 0 and sub_blocks == 5 and hidden == 32 and self.max_taps <= 32

    def tap_row(self, r):
        return r * self.tap_rows + self.tap_rows * (r // 4)


SQUEEZE_ROW, EXPAND_ROW, GAIN_ROW, SHIFT_ROW = 128, 192, 224, 232


class Refs:
    def __init__(self, names, refs):
        for name, ref in zip(names, refs, strict=True):
            setattr(self, name, ref)


def peers_of(me, n):
    if n != 32:
        return [lax.rem(me + k, n) for k in range(1, n)]
    core = lax.rem(me, 2)
    x = lax.rem(me // 2, 2)
    y = lax.rem(me // 4, 2)
    z = me // 8
    found = []
    for order, other in enumerate((3 - z, lax.rem(z + 2, 4), z + 1 - 2 * lax.rem(z, 2), z)):
        for dy in (1, 0):
            for dx in (1, 0):
                for dc in (0, 1):
                    if order == 3 and dy == 0 and dx == 0 and dc == 0:
                        continue
                    oy = lax.rem(y + dy, 2)
                    ox = lax.rem(x + dx, 2)
                    oc = lax.rem(core + dc, 2)
                    found.append((dy + dx + (3, 2, 1, 0)[order], other * 8 + oy * 4 + ox * 2 + oc))
    found.sort(key=lambda item: -item[0])
    return [item[1] for item in found]


def same_core_peers(me, n):
    if n != 32:
        return [lax.rem(me + 2 * k, n) for k in range(1, n // 2)]
    core = lax.rem(me, 2)
    x = lax.rem(me // 2, 2)
    y = lax.rem(me // 4, 2)
    z = me // 8
    found = []
    for order, other in enumerate((3 - z, lax.rem(z + 2, 4), z + 1 - 2 * lax.rem(z, 2), z)):
        for dy in (1, 0):
            for dx in (1, 0):
                if order == 3 and dy == 0 and dx == 0:
                    continue
                oy = lax.rem(y + dy, 2)
                ox = lax.rem(x + dx, 2)
                found.append((dy + dx + (3, 2, 1, 0)[order], other * 8 + oy * 4 + ox * 2 + core))
    found.sort(key=lambda item: -item[0])
    return [item[1] for item in found]


def kernel(plan, names, *refs):
    k = Refs(names, refs)
    lens, frames, cot, dw, point, gains, shifts = k.lens, k.frames, k.cot, k.dw, k.point, k.gains, k.shifts
    squeeze_t, expand = k.squeeze_t, k.expand
    out, frames_grad = k.out, k.frames_grad
    hid, acts, prods, gd, gz, gpb, gqb, pre = k.hid, k.acts, k.prods, k.gd, k.gz, k.gpb, k.gqb, k.pre
    flat, wide, first_mask, second_mask, valid, stats = k.flat, k.wide, k.first_mask, k.second_mask, k.valid, k.stats
    send4, recv4, counts, csend = k.send4, k.recv4, k.counts, k.csend
    send_sem, recv_sem, count_sems = k.send_sem, k.recv_sem, k.count_sems
    N = plan.devices
    Q, R, RF = plan.steps, plan.block, plan.fine
    HV = range(plan.halves)
    SUB = plan.sub
    PER = plan.per
    me = lax.axis_index("dp")
    peers = peers_of(me, N)
    chips = N // 2
    chip, core = me // 2, lax.rem(me, 2)
    partner = me + 1 - 2 * core
    same_core = same_core_peers(me, N)

    barrier = pltpu.get_barrier_semaphore()
    for peer in peers:
        pl.semaphore_signal(barrier, inc=1, device_id=(peer,), device_id_type=MESH)

    len0 = lens[0]
    len1 = lens[1]
    half0 = len0 // 2
    half1 = len1 // 2
    count = (half0 + half1).astype(F32)
    inv_half = (1.0 / jnp.full((1, LANES), half0, jnp.int32).astype(F32),
                1.0 / jnp.full((1, LANES), half1, jnp.int32).astype(F32))

    def steps_loop(width, body, init=0):
        return lax.fori_loop(0, Q // width, lambda i, c: body(i * width, c), init)

    def mask_body(t0, c):
        step = t0 + lax.broadcasted_iota(jnp.int32, (RF, 8, LANES), 0)
        slot = step + Q * lax.broadcasted_iota(jnp.int32, (RF, 8, LANES), 1)
        a = (slot < half0).astype(F32)
        b = jnp.logical_and(slot >= half0 + GAP, slot < half0 + GAP + half1).astype(F32)
        first_mask[pl.ds(t0, RF)] = a
        second_mask[pl.ds(t0, RF)] = b
        valid[pl.ds(t0, RF)] = a + b
        return c

    steps_loop(RF, mask_body)

    top = 2 * GAP + 2 * plan.slots
    for h in HV:
        wide[h, 0:2 * GAP] = jnp.zeros((2 * GAP, LANES), F32)
        wide[h, top:] = jnp.zeros((wide.shape[1] - top, LANES), F32)

    def widen(i, c):
        rows = pl.ds(pl.multiple_of(i * 128, 128), 128)
        for h in HV:
            values = frames[rows, h * LANES:(h + 1) * LANES].astype(F32)
            wide[h, pl.ds(pl.multiple_of(i * 128 + 2 * GAP, 32), 128)] = values
        return c

    lax.fori_loop(0, 2 * plan.slots // 128, widen, 0)

    def set_halo(ref, half):
        sub = lax.broadcasted_iota(jnp.int32, (HALO, 8, LANES), 1)
        low = pltpu.roll(ref[half, pl.ds(Q, HALO)], 1, 1)
        ref[half, pl.ds(0, HALO)] = jnp.where(sub == 0, 0.0, low)
        high = pltpu.roll(ref[half, pl.ds(HALO, HALO)], 7, 1)
        ref[half, pl.ds(HALO + Q, HALO)] = jnp.where(sub == 7, 0.0, high)

    for phase in range(2):
        def deinterleave(t0, c):
            for j in range(RF):
                a_mask = first_mask[t0 + j]
                b_mask = second_mask[t0 + j]
                for h in HV:
                    a = wide[h, pl.ds(2 * (t0 + j) + 2 * GAP + phase, 8, stride=2 * Q)]
                    b = wide[h, pl.ds(2 * (t0 + j) + phase, 8, stride=2 * Q)]
                    hid[phase, h, HALO + t0 + j] = a * a_mask + b * b_mask
            return c
        steps_loop(RF, deinterleave)
        for h in HV:
            set_halo(hid.at[phase], h)

    def load_shard():
        for b in range(2):
            source = (k.dw_first, k.dw_second)[b]
            k.packed[...] = jnp.zeros((plan.values, LANES), F32)
            for r in range(SUB):
                k.packed[pl.ds(plan.tap_row(r), plan.taps[b]), 0:plan.shard] = source[r].astype(F32)
            k.packed[EXPAND_ROW:EXPAND_ROW + plan.hidden, 0:plan.shard] = k.se_up[b].astype(F32)
            k.packed[GAIN_ROW:GAIN_ROW + PER, 0:plan.shard] = k.gains_in[b].astype(F32)
            k.packed[SHIFT_ROW:SHIFT_ROW + PER, 0:plan.shard] = k.shifts_in[b].astype(F32)
            for tile in range(2):
                k.packed_t[8 * b:8 * b + 8, tile * LANES:(tile + 1) * LANES] = jnp.transpose(
                    k.packed[tile * LANES:(tile + 1) * LANES])[0:8]
            k.packed_t[8 * b:8 * b + 8, SQUEEZE_ROW:SQUEEZE_ROW + plan.hidden] = k.se_down[b].astype(F32)
        k.gath[0, chip, core] = k.packed_t[...].astype(BF16)
        for pair in range(PER):
            rows = [k.point_in[i // PER, i % PER].astype(F32) for i in (2 * pair, 2 * pair + 1)]
            k.gath[1 + pair, chip, core] = jnp.concatenate(rows, axis=0).astype(BF16)

    def gather_send(unit):
        view = k.gath.at[unit, chip, core]
        for peer in same_core:
            pltpu.make_async_remote_copy(src_ref=view, dst_ref=view, send_sem=k.unit_sems.at[0, unit],
                                         recv_sem=k.unit_sems.at[1, unit], device_id=(peer,),
                                         device_id_type=MESH).start()

    def gather_forward(unit):
        view = k.gath.at[unit, pl.ds(0, chips - 1), 0]
        pltpu.make_async_copy(view, view, k.unit_sems.at[1, unit]).wait()
        view = k.gath.at[unit, :, core]
        pltpu.make_async_remote_copy(src_ref=view, dst_ref=view, send_sem=k.unit_sems.at[2, unit],
                                     recv_sem=k.unit_sems.at[3, unit], device_id=(partner,),
                                     device_id_type=MESH).start()

    def gather_wait(unit):
        view = k.gath.at[unit, :, 0]
        pltpu.make_async_copy(view, view, k.unit_sems.at[3, unit]).wait()

    def unpack_values():
        got = k.gath[0].astype(F32).reshape(N, 16, plan.values)
        for b in range(2):
            block = got[:, 8 * b:8 * b + 8].reshape(plan.channels, plan.values)
            for h in HV:
                for tile in range(2):
                    part = block[h * LANES:(h + 1) * LANES, tile * LANES:(tile + 1) * LANES]
                    k.unpacked[tile * LANES:(tile + 1) * LANES] = jnp.transpose(part)
                for r in range(SUB):
                    dw[b * PER + r, h] = k.unpacked[plan.tap_row(r):plan.tap_row(r) + plan.tap_rows]
                for r in range(PER):
                    gains[b * PER + r, h:h + 1] = k.unpacked[GAIN_ROW + r:GAIN_ROW + r + 1]
                    shifts[b * PER + r, h:h + 1] = k.unpacked[SHIFT_ROW + r:SHIFT_ROW + r + 1]
                lanes = slice(h * LANES, (h + 1) * LANES)
                expand[b, :, lanes] = k.unpacked[EXPAND_ROW:EXPAND_ROW + plan.hidden]
                squeeze_t[b, :, lanes] = k.unpacked[SQUEEZE_ROW:SQUEEZE_ROW + plan.hidden]

    def unpack_pair(pair):
        got = k.gath[1 + pair].astype(F32).reshape(N, 16, plan.channels)
        for side in range(2):
            block = got[:, 8 * side:8 * side + 8].reshape(plan.channels, plan.channels)
            point[2 * pair + side] = block.astype(BF16)

    if plan.fused:
        load_shard()

    csend[...] = jnp.full((4, LANES), count, F32)
    pl.semaphore_wait(barrier, N - 1)

    def send_to_all(src, dst, ssem, rsem):
        for peer in peers:
            pltpu.make_async_remote_copy(src_ref=src, dst_ref=dst, send_sem=ssem, recv_sem=rsem,
                                         device_id=(peer,), device_id_type=MESH).start()

    def wait_all(ref, sem):
        view = ref.at[pl.ds(0, N - 1)]
        pltpu.make_async_copy(view, view, sem).wait()

    if plan.fused:
        gather_send(0)
        gather_send(1)
    send_to_all(csend, counts.at[me], count_sems.at[0], count_sems.at[1])
    if plan.fused:
        gather_send(2)
    counts[me] = csend[...]

    def exchange(slot, place, rows):
        send4[slot] = rows
        recv4[place, me] = rows
        send_to_all(send4.at[slot], recv4.at[place, me], send_sem.at[slot], recv_sem.at[slot])

    def received(slot, place):
        wait_all(recv4.at[place], recv_sem.at[slot])
        return recv4[place]

    def back_place(index):
        return lax.rem(index + PER, 2 * PER)

    def row(values):
        return values.reshape(1, 1, LANES)

    def accumulate(rows3):
        return jnp.sum(rows3, axis=0)

    def local_stats(index):
        def total(t0, c):
            v = valid[pl.ds(t0, R)]
            return tuple(c[h] + accumulate(prods[index, h, pl.ds(t0, R)] * v) for h in HV)
        zeros = tuple(jnp.zeros((8, LANES), F32) for h in HV)
        sums = steps_loop(R, total, zeros)
        means = [jnp.sum(sums[h], axis=0, keepdims=True) / jnp.full((1, LANES), count, F32) for h in HV]

        def squares(t0, c):
            v = valid[pl.ds(t0, R)]
            res = []
            for h in HV:
                d = (prods[index, h, pl.ds(t0, R)] - row(means[h])) * v
                res.append(c[h] + accumulate(d * d))
            return tuple(res)
        sq = steps_loop(R, squares, zeros)
        return jnp.concatenate(means + [jnp.sum(sq[h], axis=0, keepdims=True) for h in HV], axis=0)

    def merge_stats(slot, index):
        got = received(slot, slot)
        weight = counts[...]
        total = jnp.sum(weight, axis=0)
        mean = jnp.sum(weight * got, axis=0) / total
        mean4 = jnp.concatenate([mean[0:2], mean[0:2]], axis=0)
        diff = got - mean4
        between = jnp.sum(weight * diff * diff, axis=0)
        within = jnp.sum(got, axis=0)
        var = (within[2:4] + between[0:2]) / total[0:2]
        inv = lax.rsqrt(var + EPSILON)
        scale = inv * gains[index]
        offset = shifts[index] - mean[0:2] * scale
        stats[index] = jnp.concatenate([mean[0:2], inv, scale, offset], axis=0)

    def stat_row(index, kind, h):
        return row(stats[index, pl.ds(2 * kind + h, 1)])

    def layer_conv(index, pieces):
        def body(t0, c):
            for h in HV:
                acc = None
                for source, taps in pieces:
                    low = min(s for _, s in taps)
                    high = max(s for _, s in taps)
                    win = hid[source, h, pl.ds(t0 + HALO + low, R + high - low)]
                    for tap, shift in taps:
                        term = win[shift - low:shift - low + R] * dw[index, h, pl.ds(tap, 1)].reshape(1, 1, LANES)
                        acc = term if acc is None else acc + term
                rows = pl.ds(pl.multiple_of(8 * t0, 16), 8 * R)
                acts[index, rows, h * LANES:(h + 1) * LANES] = acc.reshape(8 * R, LANES).astype(BF16)
            return c
        steps_loop(R, body)

    def pointwise(act, index):
        def body(t0, c):
            rows = pl.ds(pl.multiple_of(8 * t0, 16), 8 * R)
            res = jnp.dot(acts[act, rows], point[index], preferred_element_type=F32)
            for h in HV:
                prods[index, h, pl.ds(t0, R)] = res[:, h * LANES:(h + 1) * LANES].reshape(R, 8, LANES)
            return c
        steps_loop(R, body)

    def activate(index, target):
        scales = [stat_row(index, 2, h) for h in HV]
        offsets = [stat_row(index, 3, h) for h in HV]

        def body(t0, c):
            v = valid[pl.ds(t0, RF)]
            for h in HV:
                z = prods[index, h, pl.ds(t0, RF)] * scales[h] + offsets[h]
                hid[target, h, pl.ds(HALO + t0, RF)] = z * sigmoid(z) * v
            return c
        steps_loop(RF, body)
        for h in HV:
            set_halo(hid.at[target], h)

    def hid_of(b, r):
        return b * SUB + r + 1

    def regular_taps(b):
        margin = (plan.taps[b] - 1) // 2
        return [(t, t - margin) for t in range(plan.taps[b])]

    def block_pieces(b):
        if b == 0:
            taps = regular_taps(0)
            even = [(t, s // 2) for t, s in taps if s % 2 == 0]
            odd = [(t, (s - 1) // 2) for t, s in taps if s % 2 == 1]
            return [(0, even), (1, odd)]
        return [(hid_of(1, 0), regular_taps(1))]

    def residual_forward(b):
        source = 0 if b == 0 else hid_of(1, 0)
        res = b * PER + SUB

        def body(t0, c):
            rows = pl.ds(pl.multiple_of(8 * t0, 16), 8 * R)
            for h in HV:
                values = hid[source, h, pl.ds(HALO + t0, R)].reshape(8 * R, LANES)
                acts[res, rows, h * LANES:(h + 1) * LANES] = values.astype(BF16)
            return c
        steps_loop(R, body)
        pointwise(res, res)
        exchange(res, res, local_stats(res))

    def pair_rows(values):
        return jnp.concatenate([values, jnp.zeros((6, plan.channels), F32)], axis=0)

    def small(a, b, dims):
        return lax.dot_general(a, b, (dims, ((), ())), precision=HIGHEST, preferred_element_type=F32)

    def excite(b):
        last = b * PER + SUB - 1
        scales = [stat_row(last, 2, h) for h in HV]
        offsets = [stat_row(last, 3, h) for h in HV]

        def sums(t0, c):
            a, s = first_mask[pl.ds(t0, RF)], second_mask[pl.ds(t0, RF)]
            res = []
            for h in HV:
                z = prods[last, h, pl.ds(t0, RF)] * scales[h] + offsets[h]
                res.append(c[2 * h] + accumulate(z * a))
                res.append(c[2 * h + 1] + accumulate(z * s))
            return tuple(res)
        tot = steps_loop(RF, sums, tuple(jnp.zeros((8, LANES), F32) for _ in range(2 * plan.halves)))
        means = jnp.concatenate(
            [jnp.concatenate([jnp.sum(tot[2 * h + u], axis=0, keepdims=True) * inv_half[u] for h in HV], axis=1)
             for u in range(2)], axis=0)
        means = pair_rows(means)
        inner = small(means, squeeze_t[b], ((1,), (1,)))
        excited = inner * sigmoid(inner)
        gate = sigmoid(small(excited, expand[b], ((1,), (0,))))
        return means, inner, excited, gate

    def gate_rows(gate):
        return [[row(gate[u:u + 1, h * LANES:(h + 1) * LANES]) for h in HV] for u in range(2)]

    def tail(b, gate, store):
        last, res = b * PER + SUB - 1, b * PER + SUB
        gates = gate_rows(gate)
        consts = [(stat_row(last, 2, h), stat_row(last, 3, h), stat_row(res, 2, h), stat_row(res, 3, h)) for h in HV]

        def body(t0, c):
            v = valid[pl.ds(t0, RF)]
            a = first_mask[pl.ds(t0, RF)]
            for h in HV:
                s1, o1, s2, o2 = consts[h]
                z = prods[last, h, pl.ds(t0, RF)] * s1 + o1
                y = prods[res, h, pl.ds(t0, RF)] * s2 + o2
                g = jnp.where(a > 0.5, gates[0][h], gates[1][h])
                s = z * g + y
                pre[b, h, pl.ds(t0, RF)] = s
                store(t0, h, s * sigmoid(s) * v)
            return c
        steps_loop(RF, body)

    def forward_aside(b, r):
        if plan.fused:
            step = b * SUB + r

            @pl.when(jnp.logical_and(step >= 1, step < PER))
            def _():
                gather_wait(1 + step)
                unpack_pair(step)

            @pl.when(step < PER - 1)
            def _():
                gather_forward(2 + step)

            @pl.when(step < PER - 2)
            def _():
                gather_send(3 + step)

        @pl.when(r == SUB - 2)
        def _():
            residual_forward(b)

    def forward_block(b):
        def layer(r, pieces, before=None):
            index = b * PER + r
            layer_conv(index, pieces)
            if before is not None:
                before()
            pointwise(index, index)
            exchange(index, index, local_stats(index))
            forward_aside(b, r)
            merge_stats(index, index)

        def first_matrices():
            gather_wait(1)
            unpack_pair(0)
        layer(0, block_pieces(b), first_matrices if plan.fused and b == 0 else None)
        activate(b * PER, hid_of(b, 1))

        def rest(r, c):
            layer(r, [(hid_of(b, r), regular_taps(b))])

            @pl.when(r < SUB - 1)
            def _():
                activate(b * PER + r, hid_of(b, r + 1))
            return c
        lax.fori_loop(1, SUB, rest, 0)
        merge_stats(b * PER + SUB, b * PER + SUB)
        return excite(b)

    back_slot = 2 * PER

    def sum_rows(parts):
        return jnp.concatenate([jnp.sum(part, axis=0, keepdims=True) for part in parts], axis=0)

    def tail_back(b, kept, load):
        means, inner, excited, gate = kept
        last, res = b * PER + SUB - 1, b * PER + SUB
        gates = gate_rows(gate)
        consts = [(stat_row(last, 2, h), stat_row(last, 3, h)) for h in HV]

        def first(t0, c):
            v = valid[pl.ds(t0, RF)]
            a, q = first_mask[pl.ds(t0, RF)], second_mask[pl.ds(t0, RF)]
            out_c = []
            for h in HV:
                s = pre[b, h, pl.ds(t0, RF)]
                sg = sigmoid(s)
                gs = load(t0, h) * (sg * (1.0 + s * (1.0 - sg))) * v
                pre[b, h, pl.ds(t0, RF)] = gs
                z = prods[last, h, pl.ds(t0, RF)] * consts[h][0] + consts[h][1]
                gsz = gs * z
                out_c.append(c[2 * h] + accumulate(gsz * a))
                out_c.append(c[2 * h + 1] + accumulate(gsz * q))
            return tuple(out_c)
        zero4 = tuple(jnp.zeros((8, LANES), F32) for _ in range(2 * plan.halves))
        tot = steps_loop(RF, first, zero4)
        grad_gate = pair_rows(jnp.concatenate(
            [jnp.concatenate([jnp.sum(tot[2 * h + u], axis=0, keepdims=True) for h in HV], axis=1)
             for u in range(2)], axis=0))
        grad_up = grad_gate * gate * (1.0 - gate)
        k.expand_grad[b] = small(excited, grad_up, ((0,), (0,)))
        grad_excited = small(grad_up, expand[b], ((1,), (1,)))
        sg = sigmoid(inner)
        grad_inner = grad_excited * (sg * (1.0 + inner * (1.0 - sg)))
        k.squeeze_grad[b] = small(grad_inner, means, ((0,), (0,)))
        grad_means = small(grad_inner, squeeze_t[b], ((1,), (0,)))
        mean_rows = [[row(grad_means[u:u + 1, h * LANES:(h + 1) * LANES] * inv_half[u]) for h in HV]
                     for u in range(2)]
        norm1 = [(stat_row(last, 0, h), stat_row(last, 1, h)) for h in HV]
        norm2 = [(stat_row(res, 0, h), stat_row(res, 1, h)) for h in HV]

        def second(t0, c):
            a = first_mask[pl.ds(t0, RF)]
            v = valid[pl.ds(t0, RF)]
            out_c = []
            for h in HV:
                gs = pre[b, h, pl.ds(t0, RF)]
                g = jnp.where(a > 0.5, gates[0][h], gates[1][h])
                m = jnp.where(a > 0.5, mean_rows[0][h], mean_rows[1][h])
                grad = gs * g + m * v
                gz[h, pl.ds(t0, RF)] = grad
                x1 = (prods[last, h, pl.ds(t0, RF)] - norm1[h][0]) * norm1[h][1]
                x2 = (prods[res, h, pl.ds(t0, RF)] - norm2[h][0]) * norm2[h][1]
                out_c += [c[4 * h] + accumulate(grad), c[4 * h + 1] + accumulate(grad * x1),
                          c[4 * h + 2] + accumulate(gs), c[4 * h + 3] + accumulate(gs * x2)]
            return tuple(out_c)
        tot = steps_loop(RF, second, zero4 + zero4)
        exchange(back_slot + last, back_place(last), sum_rows([tot[0], tot[4], tot[1], tot[5]]))
        exchange(back_slot + res, back_place(res), sum_rows([tot[2], tot[6], tot[3], tot[7]]))

    def norm_back(index, load, target):
        sums = jnp.sum(received(back_slot + index, back_place(index)), axis=0)
        k.shifts_grad[index] = sums[0:2]
        k.gains_grad[index] = sums[2:4]
        total = jnp.sum(counts[...], axis=0)[0:2]
        st = stats[index]
        mean, inv, scale = st[0:2], st[2:4], st[4:6]
        k1 = scale * sums[0:2] / total
        k2 = scale * sums[2:4] / total * inv
        rows3 = [[row(value[h:h + 1]) for value in (mean, scale, k1, k2)] for h in HV]

        def body(t0, c):
            v = valid[pl.ds(t0, R)]
            rows = pl.ds(pl.multiple_of(8 * t0, 16), 8 * R)
            for h in HV:
                mean_h, scale_h, k1_h, k2_h = rows3[h]
                grad = (scale_h * load(t0, h) - k1_h - k2_h * (prods[index, h, pl.ds(t0, R)] - mean_h)) * v
                target[rows, h * LANES:(h + 1) * LANES] = grad.reshape(8 * R, LANES).astype(BF16)
            return c
        steps_loop(R, body)

    def pointwise_back(index, source, store):
        def body(t0, c):
            rows = pl.ds(pl.multiple_of(8 * t0, 16), 8 * R)
            res = lax.dot_general(source[rows], point[index], (((1,), (1,)), ((), ())), preferred_element_type=F32)
            for h in HV:
                store(t0, h, res[:, h * LANES:(h + 1) * LANES].reshape(R, 8, LANES))
            return c
        steps_loop(R, body)

    def point_back(index, source):
        place = lax.rem(index, 2) if plan.fused else index
        k.point_grad[place] = lax.dot_general(acts[index], source[...], (((0,), (0,)), ((), ())),
                                              preferred_element_type=F32)

    def store_gd(t0, h, values):
        gd[h, pl.ds(HALO + t0, R)] = values

    def conv_back_block(t0, h, index, taps):
        low = min(-s for _, s in taps)
        high = max(-s for _, s in taps)
        win = gd[h, pl.ds(t0 + HALO + low, R + high - low)]
        acc = None
        for tap, shift in taps:
            term = win[-shift - low:-shift - low + R] * dw[index, h, pl.ds(tap, 1)].reshape(1, 1, LANES)
            acc = term if acc is None else acc + term
        return acc

    def kernel_back(index, pieces):
        for source, taps in pieces:
            for h in HV:
                low = min(s for _, s in taps)
                high = max(s for _, s in taps)

                def body(t0, c):
                    g = gd[h, pl.ds(HALO + t0, RF)]
                    win = hid[source, h, pl.ds(t0 + HALO + low, RF + high - low)]
                    return tuple(acc + accumulate(g * win[s - low:s - low + RF]) for acc, (_, s) in zip(c, taps))
                accs = steps_loop(RF, body, tuple(jnp.zeros((8, LANES), F32) for _ in taps))
                for acc, (tap, _) in zip(accs, taps):
                    k.dw_grad[index, h, pl.ds(tap, 1)] = jnp.sum(acc, axis=0, keepdims=True)

    def hidden_back(index, taps):
        before = index - 1
        consts = [[stat_row(before, kind, h) for kind in range(4)] for h in HV]

        def body(t0, c):
            v = valid[pl.ds(t0, R)]
            res = []
            for h in HV:
                mean, inv, scale, offset = consts[h]
                p = prods[before, h, pl.ds(t0, R)]
                z = p * scale + offset
                sg = sigmoid(z)
                grad = conv_back_block(t0, h, index, taps) * (sg * (1.0 + z * (1.0 - sg))) * v
                gz[h, pl.ds(t0, R)] = grad
                xhat = (p - mean) * inv
                res += [c[2 * h] + accumulate(grad), c[2 * h + 1] + accumulate(grad * xhat)]
            return tuple(res)
        tot = steps_loop(R, body, tuple(jnp.zeros((8, LANES), F32) for _ in range(2 * plan.halves)))
        exchange(back_slot + before, back_place(before), sum_rows([tot[0], tot[2], tot[1], tot[3]]))

    def load_gz(t0, h):
        return gz[h, pl.ds(t0, R)]

    def scatter_start(unit, place):
        pltpu.make_async_remote_copy(src_ref=k.shares.at[place, :, 1 - core], dst_ref=k.inbox.at[unit],
                                     send_sem=k.unit_sems.at[4, unit], recv_sem=k.unit_sems.at[5, unit],
                                     device_id=(partner,), device_id_type=MESH).start()

    def scatter_send(unit, place):
        view = k.inbox.at[unit]
        pltpu.make_async_copy(view, view, k.unit_sems.at[5, unit]).wait()
        pltpu.make_async_copy(view, view, k.unit_sems.at[4, unit]).wait()
        k.sums[unit] = (k.shares[place, :, core].astype(F32) + k.inbox[unit].astype(F32)).astype(BF16)
        k.gained[unit, chip] = k.sums[unit, chip]
        for peer in same_core:
            pltpu.make_async_remote_copy(src_ref=k.sums.at[unit, peer // 2], dst_ref=k.gained.at[unit, chip],
                                         send_sem=k.unit_sems.at[6, unit], recv_sem=k.unit_sems.at[7, unit],
                                         device_id=(peer,), device_id_type=MESH).start()

    def scatter_finish(unit):
        view = k.gained.at[unit, pl.ds(0, chips - 1)]
        pltpu.make_async_copy(view, view, k.unit_sems.at[7, unit]).wait()
        return jnp.sum(k.gained[unit].astype(F32), axis=0)

    def pair_start(pair):
        both = [k.point_grad[side].reshape(N, 8, plan.channels) for side in range(2)]
        k.shares[0] = jnp.concatenate(both, axis=1).astype(BF16).reshape(chips, 2, 16, plan.channels)
        scatter_start(1 + pair, 0)

    def pair_finish(pair):
        total = scatter_finish(1 + pair)
        b = pair // (PER // 2)
        r = 2 * lax.rem(pair, PER // 2)
        k.point_out[b, r] = total[0:8]
        k.point_out[b, r + 1] = total[8:16]

    def values_start():
        k.packed[...] = jnp.zeros((plan.values, LANES), F32)
        blocks = []
        for b in range(2):
            columns = []
            for h in HV:
                for r in range(SUB):
                    k.packed[plan.tap_row(r):plan.tap_row(r) + plan.tap_rows] = k.dw_grad[b * PER + r, h]
                lanes = slice(h * LANES, (h + 1) * LANES)
                k.packed[EXPAND_ROW:EXPAND_ROW + plan.hidden] = k.expand_grad[b, :, lanes]
                k.packed[SQUEEZE_ROW:SQUEEZE_ROW + plan.hidden] = k.squeeze_grad[b, :, lanes]
                for r in range(PER):
                    k.packed[GAIN_ROW + r:GAIN_ROW + r + 1] = k.gains_grad[b * PER + r, h:h + 1]
                    k.packed[SHIFT_ROW + r:SHIFT_ROW + r + 1] = k.shifts_grad[b * PER + r, h:h + 1]
                columns.append(jnp.concatenate(
                    [jnp.transpose(k.packed[t * LANES:(t + 1) * LANES]) for t in range(2)], axis=1))
            whole = jnp.concatenate(columns, axis=0)
            k.own_norm[b] = whole[:, LANES:]
            blocks.append(whole.reshape(N, 8, plan.values))
        k.shares[1] = jnp.concatenate(blocks, axis=1).astype(BF16).reshape(chips, 2, 16, plan.values)
        scatter_start(0, 1)

    def values_finish():
        total = scatter_finish(0)
        mine = pl.ds(pl.multiple_of(me * 8, 8), 8)
        for b in range(2):
            rows = total[8 * b:8 * b + 8]
            k.squeeze_out[b] = rows[:, SQUEEZE_ROW:SQUEEZE_ROW + plan.hidden]
            fill = jnp.zeros((LANES - 8, LANES), F32)
            for t in range(2):
                k.packed[t * LANES:(t + 1) * LANES] = jnp.transpose(
                    jnp.concatenate([rows[:, t * LANES:(t + 1) * LANES], fill], axis=0))
            dw_out = (k.dw_first_out, k.dw_second_out)[b]
            for r in range(SUB):
                dw_out[r] = k.packed[plan.tap_row(r):plan.tap_row(r) + plan.taps[b], 0:plan.shard]
            k.expand_out[b] = k.packed[EXPAND_ROW:EXPAND_ROW + plan.hidden, 0:plan.shard]
            k.packed[LANES:] = jnp.transpose(jnp.concatenate([k.own_norm[b, mine], fill], axis=0))
            k.gains_out[b] = k.packed[GAIN_ROW:GAIN_ROW + PER, 0:plan.shard]
            k.shifts_out[b] = k.packed[SHIFT_ROW:SHIFT_ROW + PER, 0:plan.shard]

    HALF = PER // 2

    def backward_aside(b, r):
        index = b * PER + r
        if plan.fused:
            if b == 0:
                @pl.when(r == SUB - 1)
                def _():
                    scatter_send(1 + HALF, 0)

                @pl.when(r == SUB - 2)
                def _():
                    pair_finish(HALF)

            @pl.when(lax.rem(r, 2) == 1)
            def _():
                scatter_send(1 + HALF * b + (r + 1) // 2, 0)

            @pl.when(jnp.logical_and(lax.rem(r, 2) == 0, r < SUB - 1))
            def _():
                pair_finish(HALF * b + r // 2 + 1)
        point_back(index, gpb)

        @pl.when(r == SUB - 1)
        def _():
            res = b * PER + SUB
            norm_back(res, lambda t0, h: pre[b, h, pl.ds(t0, R)], gqb)
            point_back(res, gqb)
        if plan.fused:
            @pl.when(lax.rem(r, 2) == 0)
            def _():
                pair_start(HALF * b + r // 2)

    def backward_block(b):
        def filtered(index):
            norm_back(index, load_gz, gpb)
            pointwise_back(index, gpb, store_gd)
            for h in HV:
                set_halo(gd, h)

        def step(j, c):
            r = SUB - 1 - j
            index = b * PER + r
            filtered(index)
            hidden_back(index, regular_taps(b))
            backward_aside(b, r)
            kernel_back(index, [(hid_of(b, r), regular_taps(b))])
            return c
        lax.fori_loop(0, SUB - 1, step, 0)
        filtered(b * PER)

    if plan.fused:
        for unit in range(2):
            gather_forward(unit)
        gather_wait(0)
        unpack_values()
    wait_all(counts, count_sems.at[1])
    kept_first = forward_block(0)

    def store_middle(t0, h, values):
        hid[hid_of(1, 0), h, pl.ds(HALO + t0, RF)] = values
    tail(0, kept_first[3], store_middle)
    for h in HV:
        set_halo(hid.at[hid_of(1, 0)], h)
    kept_second = forward_block(1)

    def store_out(t0, h, values):
        for j in range(RF):
            flat[h, pl.ds(t0 + j, 8, stride=Q)] = values[j]
    tail(1, kept_second[3], store_out)

    def ungap(i, c):
        rows = pl.ds(pl.multiple_of(i * 128, 128), 128)
        slot = i * 128 + lax.broadcasted_iota(jnp.int32, (128, LANES), 0)
        for h in HV:
            moved = flat[h, pl.ds(pl.multiple_of(i * 128 + GAP, 16), 128)]
            out[rows, h * LANES:(h + 1) * LANES] = jnp.where(slot < half0, flat[h, rows], moved)
        return c
    lax.fori_loop(0, plan.slots // 128, ungap, 0)

    for h in HV:
        flat[h, 0:GAP] = jnp.zeros((GAP, LANES), F32)
        flat[h, GAP + plan.slots:] = jnp.zeros((flat.shape[1] - GAP - plan.slots, LANES), F32)

    def place(i, c):
        rows = pl.ds(pl.multiple_of(i * 128, 128), 128)
        for h in HV:
            flat[h, pl.ds(pl.multiple_of(i * 128 + GAP, 16), 128)] = cot[rows, h * LANES:(h + 1) * LANES]
        return c
    lax.fori_loop(0, plan.slots // 128, place, 0)

    def load_cot(t0, h):
        parts = []
        for j in range(RF):
            a = flat[h, pl.ds(t0 + j + GAP, 8, stride=Q)]
            b = flat[h, pl.ds(t0 + j, 8, stride=Q)]
            parts.append(jnp.where(first_mask[t0 + j] > 0.5, a, b))
        return jnp.stack(parts, axis=0)

    tail_back(1, kept_second, load_cot)
    backward_block(1)

    def store_gz(t0, h, values):
        gz[h, pl.ds(t0, R)] = values
    pointwise_back(PER + SUB, gqb, store_gz)

    def middle(t0, c):
        for h in HV:
            gz[h, pl.ds(t0, R)] = gz[h, pl.ds(t0, R)] + conv_back_block(t0, h, PER, regular_taps(1))
        return c
    steps_loop(R, middle)
    tail_back(0, kept_first, lambda t0, h: gz[h, pl.ds(t0, RF)])
    backward_aside(1, 0)
    kernel_back(PER, [(hid_of(1, 0), regular_taps(1))])
    backward_block(0)
    pieces = block_pieces(0)
    backward_aside(0, 0)
    kernel_back(0, pieces)
    if plan.fused:
        values_start()
        scatter_send(1, 0)
        scatter_send(0, 1)
    pointwise_back(SUB, gqb, store_gz)

    def spread(t0, c):
        v = valid[pl.ds(t0, R)]
        for h in HV:
            even = (conv_back_block(t0, h, 0, pieces[0][1]) + gz[h, pl.ds(t0, R)]) * v
            odd = conv_back_block(t0, h, 0, pieces[1][1]) * v
            for j in range(R):
                wide[h, pl.ds(2 * (t0 + j), 8, stride=2 * Q)] = even[j]
                wide[h, pl.ds(2 * (t0 + j) + 1, 8, stride=2 * Q)] = odd[j]
        return c
    steps_loop(R, spread)

    def ungap_wide(i, c):
        rows = pl.ds(pl.multiple_of(i * 128, 128), 128)
        slot = i * 128 + lax.broadcasted_iota(jnp.int32, (128, LANES), 0)
        for h in HV:
            moved = wide[h, pl.ds(pl.multiple_of(i * 128 + 2 * GAP, 32), 128)]
            frames_grad[rows, h * LANES:(h + 1) * LANES] = jnp.where(slot < len0, wide[h, rows], moved)
        return c
    lax.fori_loop(0, 2 * plan.slots // 128, ungap_wide, 0)
    if plan.fused:
        pair_finish(0)
        values_finish()

    wait_all(counts, count_sems.at[0])

    def drain(slot, c):
        wait_all(recv4.at[0], send_sem.at[slot])
        return c
    lax.fori_loop(0, send4.shape[0], drain, 0)
    if plan.fused:
        def drain_units(unit, c):
            view = k.gath.at[0, pl.ds(0, chips - 1), 0]
            pltpu.make_async_copy(view, view, k.unit_sems.at[0, unit]).wait()
            view = k.gath.at[0, :, 0]
            pltpu.make_async_copy(view, view, k.unit_sems.at[2, unit]).wait()
            view = k.gained.at[0, pl.ds(0, chips - 1)]
            pltpu.make_async_copy(view, view, k.unit_sems.at[6, unit]).wait()
            return c
        lax.fori_loop(0, 1 + PER, drain_units, 0)


def call_kernel(plan, inputs):
    layers, halves, Q, channels = plan.layers, plan.halves, plan.steps, plan.channels
    vals, shard, hidden, devices = plan.values, plan.shard, plan.hidden, plan.devices
    slots = 2 * layers

    def shape(*dims, dtype=F32):
        return jax.ShapeDtypeStruct(dims, dtype)
    outs = {
        "out": shape(plan.slots, channels),
        "frames_grad": shape(2 * plan.slots, channels),
    }
    params = {
        "dw": shape(layers, halves, plan.tap_rows, LANES),
        "point": shape(layers, channels, channels, dtype=BF16),
        "gains": shape(layers, halves, LANES),
        "shifts": shape(layers, halves, LANES),
        "squeeze_t": shape(2, hidden, channels),
        "expand": shape(2, hidden, channels),
    }
    grads = {
        "dw_grad": shape(layers, halves, plan.tap_rows, LANES),
        "point_grad": shape(2 if plan.fused else layers, channels, channels),
        "gains_grad": shape(layers, halves, LANES),
        "shifts_grad": shape(layers, halves, LANES),
        "squeeze_grad": shape(2, hidden, channels),
        "expand_grad": shape(2, hidden, channels),
    }
    scratch = {
        "hid": shape(2 * plan.sub + 1, halves, plan.pad, 8, LANES),
        "acts": shape(layers, plan.rows, channels, dtype=BF16),
        "prods": shape(layers, halves, Q, 8, LANES),
        "gd": shape(halves, plan.pad, 8, LANES),
        "gz": shape(halves, Q, 8, LANES),
        "gpb": shape(plan.rows, channels, dtype=BF16),
        "gqb": shape(plan.rows, channels, dtype=BF16),
        "pre": shape(2, halves, Q, 8, LANES),
        "flat": shape(halves, plan.slots + 2 * GAP, LANES),
        "wide": shape(halves, 2 * plan.slots + 4 * GAP, LANES),
        "first_mask": shape(Q, 8, LANES),
        "second_mask": shape(Q, 8, LANES),
        "valid": shape(Q, 8, LANES),
        "stats": shape(layers, 8, LANES),
        "send4": shape(slots, 4, LANES),
        "recv4": shape(layers, devices, 4, LANES),
        "counts": shape(devices, 4, LANES),
        "csend": shape(4, LANES),
    }
    sems = {"send_sem": (slots,), "recv_sem": (slots,), "count_sems": (2,)}
    if plan.fused:
        units, chips = 1 + plan.per, devices // 2
        outs.update({
            "dw_first_out": shape(plan.sub, plan.taps[0], shard),
            "dw_second_out": shape(plan.sub, plan.taps[1], shard),
            "point_out": shape(2, plan.per, shard, channels),
            "gains_out": shape(2, plan.per, shard),
            "shifts_out": shape(2, plan.per, shard),
            "squeeze_out": shape(2, shard, hidden),
            "expand_out": shape(2, hidden, shard),
        })
        scratch.update(params)
        scratch.update(grads)
        scratch.update({
            "packed": shape(vals, LANES),
            "packed_t": shape(16, vals),
            "unpacked": shape(vals, LANES),
            "gath": shape(units, chips, 2, 16, channels, dtype=BF16),
            "shares": shape(2, chips, 2, 16, channels, dtype=BF16),
            "inbox": shape(units, chips, 16, channels, dtype=BF16),
            "sums": shape(units, chips, 16, channels, dtype=BF16),
            "gained": shape(units, chips, 16, channels, dtype=BF16),
            "own_norm": shape(2, channels, LANES),
        })
        sems["unit_sems"] = (8, units)
    else:
        outs.update(grads)
    vmem = pl.BlockSpec(memory_space=pltpu.VMEM)
    names = list(inputs) + list(outs) + list(scratch) + list(sems)
    results = pl.pallas_call(
        functools.partial(kernel, plan, names),
        out_shape=list(outs.values()),
        in_specs=[pl.BlockSpec(memory_space=pltpu.SMEM) if name == "lens" else vmem for name in inputs],
        out_specs=[vmem] * len(outs),
        scratch_shapes=[pltpu.VMEM(v.shape, v.dtype) for v in scratch.values()]
        + [pltpu.SemaphoreType.DMA(v) for v in sems.values()],
        compiler_params=pltpu.CompilerParams(
            collective_id=0, has_side_effects=True, vmem_limit_bytes=62 * 1024 * 1024),
    )(*inputs.values())
    return dict(zip(outs, results, strict=True))


def body(frames, dw_first, dw_second, point, gains, shifts, se_down, se_up, cotangent, lengths, *, devices):
    sub, taps_first, shard = dw_first.shape
    taps_second = dw_second.shape[1]
    hidden = se_down.shape[2]
    channels = point.shape[3]
    plan = Plan(cotangent.shape[0], channels, taps_first, taps_second, sub, hidden, devices)
    if plan.fused:
        res = call_kernel(plan, {
            "lens": lengths, "frames": frames, "cot": cotangent, "dw_first": dw_first, "dw_second": dw_second,
            "point_in": point, "gains_in": gains, "shifts_in": shifts, "se_down": se_down, "se_up": se_up})
        return tuple(res[name] for name in (
            "out", "frames_grad", "dw_first_out", "dw_second_out", "point_out", "gains_out", "shifts_out",
            "squeeze_out", "expand_out"))

    per, layers, halves = plan.per, plan.layers, plan.halves

    def gather(v, axis):
        return lax.all_gather(v, "dp", axis=axis, tiled=True)
    small = jnp.concatenate([
        dw_first.reshape(-1, shard), dw_second.reshape(-1, shard), gains.reshape(-1, shard),
        shifts.reshape(-1, shard), se_up.reshape(-1, shard),
        jnp.swapaxes(se_down, 1, 2).reshape(-1, shard)], axis=0)
    small = gather(small, 1).astype(F32)
    sizes = [sub * taps_first, sub * taps_second, layers, layers, 2 * hidden, 2 * hidden]
    part = jnp.split(small, [sum(sizes[:i]) for i in range(1, 6)], axis=0)

    def dw_layout(v, taps):
        v = v.reshape(sub, taps, halves, LANES).transpose(0, 2, 1, 3)
        return jnp.pad(v, ((0, 1), (0, 0), (0, plan.tap_rows - taps), (0, 0)))
    res = call_kernel(plan, {
        "lens": lengths, "frames": frames, "cot": cotangent,
        "dw": jnp.concatenate([dw_layout(part[0], taps_first), dw_layout(part[1], taps_second)], axis=0),
        "point": gather(point, 2).reshape(layers, channels, channels),
        "gains": part[2].reshape(layers, halves, LANES),
        "shifts": part[3].reshape(layers, halves, LANES),
        "squeeze_t": part[5].reshape(2, hidden, channels),
        "expand": part[4].reshape(2, hidden, channels)})

    def scatter(v, axis):
        return lax.psum_scatter(v, "dp", scatter_dimension=axis, tiled=True)

    def dw_out(v, taps):
        return v[:sub, :, :taps].transpose(0, 2, 1, 3).reshape(sub * taps, channels)
    grads = res["dw_grad"]
    packed = scatter(jnp.concatenate(
        [dw_out(grads[:per], taps_first), dw_out(grads[per:], taps_second),
         res["squeeze_grad"].reshape(-1, channels), res["expand_grad"].reshape(-1, channels)], axis=0), 1)
    g1, g2, gsq, gex = jnp.split(packed, [sizes[0], sizes[0] + sizes[1], sizes[0] + sizes[1] + sizes[5]], axis=0)

    def norm_out(v):
        return lax.dynamic_slice_in_dim(v.reshape(2, per, channels), lax.axis_index("dp") * shard, shard, 2)
    return (
        res["out"], res["frames_grad"], g1.reshape(sub, taps_first, shard), g2.reshape(sub, taps_second, shard),
        scatter(res["point_grad"].reshape(2, per, channels, channels), 2),
        norm_out(res["gains_grad"]), norm_out(res["shifts_grad"]),
        jnp.swapaxes(gsq.reshape(2, hidden, shard), 1, 2), gex.reshape(2, hidden, shard))


def solution(mesh):
    return jax.shard_map(
        functools.partial(body, devices=mesh.shape["dp"]),
        mesh=mesh,
        in_specs=(
            P("dp", None),
            P(None, None, "dp"),
            P(None, None, "dp"),
            P(None, None, "dp", None),
            P(None, None, "dp"),
            P(None, None, "dp"),
            P(None, "dp", None),
            P(None, None, "dp"),
            P("dp", None),
            P("dp"),
        ),
        out_specs=(
            P("dp", None),
            P("dp", None),
            P(None, None, "dp"),
            P(None, None, "dp"),
            P(None, None, "dp", None),
            P(None, None, "dp"),
            P(None, None, "dp"),
            P(None, "dp", None),
            P(None, None, "dp"),
        ),
        check_vma=False,
    )
```

```python
import functools

import jax
import jax.numpy as jnp
from jax import lax
from jax.experimental import pallas as pl
from jax.experimental.pallas import tpu as pltpu
from jax.sharding import PartitionSpec as P

EPSILON = 1e-05
HIGHEST = lax.Precision.HIGHEST
F32 = jnp.float32
BF16 = jnp.bfloat16
MESH = pl.DeviceIdType.MESH

GAP = 16
HALO = 13
LANES = 128


def sigmoid(v):
    return 0.5 * jnp.tanh(0.5 * v) + 0.5


class Plan:
    def __init__(self, slots, channels, taps_first, taps_second, sub_blocks, hidden, devices):
        self.slots = slots
        self.steps = (slots + GAP) // 8
        self.rows = 8 * self.steps
        self.channels = channels
        self.halves = channels // LANES
        self.taps = (taps_first, taps_second)
        self.max_taps = max(self.taps)
        self.sub = sub_blocks
        self.hidden = hidden
        self.devices = devices
        self.block = next(r for r in (26, 10, 2) if self.steps % r == 0)
        self.fine = next(r for r in (10, 26, 2) if self.steps % r == 0)
        self.pad = self.steps + 2 * HALO
        self.per = sub_blocks + 1
        self.layers = 2 * self.per
        self.tap_rows = 32
        self.tap_sets = (32, 48, 64, 80)
        self.dw_rows = 96
        self.values = 2 * LANES
        self.shard = channels // devices
        self.fused = self.shard == 8 and devices % 2 == 0 and sub_blocks == 5 and hidden == 32 and self.max_taps <= 32

    def tap_row(self, r):
        return r * self.tap_rows + self.tap_rows * (r // 4)


SQUEEZE_ROW, EXPAND_ROW, GAIN_ROW, SHIFT_ROW = 128, 192, 224, 232


class Refs:
    def __init__(self, names, refs):
        for name, ref in zip(names, refs, strict=True):
            setattr(self, name, ref)


def peers_of(me, n):
    if n != 32:
        return [lax.rem(me + k, n) for k in range(1, n)]
    core = lax.rem(me, 2)
    x = lax.rem(me // 2, 2)
    y = lax.rem(me // 4, 2)
    z = me // 8
    found = []
    for order, other in enumerate((3 - z, lax.rem(z + 2, 4), z + 1 - 2 * lax.rem(z, 2), z)):
        for dy in (1, 0):
            for dx in (1, 0):
                for dc in (0, 1):
                    if order == 3 and dy == 0 and dx == 0 and dc == 0:
                        continue
                    oy = lax.rem(y + dy, 2)
                    ox = lax.rem(x + dx, 2)
                    oc = lax.rem(core + dc, 2)
                    found.append((dy + dx + (3, 2, 1, 0)[order], other * 8 + oy * 4 + ox * 2 + oc))
    found.sort(key=lambda item: -item[0])
    return [item[1] for item in found]


def same_core_peers(me, n):
    if n != 32:
        return [lax.rem(me + 2 * k, n) for k in range(1, n // 2)]
    core = lax.rem(me, 2)
    x = lax.rem(me // 2, 2)
    y = lax.rem(me // 4, 2)
    z = me // 8
    found = []
    for order, other in enumerate((3 - z, lax.rem(z + 2, 4), z + 1 - 2 * lax.rem(z, 2), z)):
        for dy in (1, 0):
            for dx in (1, 0):
                if order == 3 and dy == 0 and dx == 0:
                    continue
                oy = lax.rem(y + dy, 2)
                ox = lax.rem(x + dx, 2)
                found.append((dy + dx + (3, 2, 1, 0)[order], other * 8 + oy * 4 + ox * 2 + core))
    found.sort(key=lambda item: -item[0])
    return [item[1] for item in found]


def kernel(plan, names, *refs):
    k = Refs(names, refs)
    lens, frames, cot, dw, point, gains, shifts = k.lens, k.frames, k.cot, k.dw, k.point, k.gains, k.shifts
    squeeze_t, expand = k.squeeze_t, k.expand
    out, frames_grad = k.out, k.frames_grad
    hid, acts, prods, gd, gz, gpb, gqb, pre = k.hid, k.acts, k.prods, k.gd, k.gz, k.gpb, k.gqb, k.pre
    wide, first_mask, valid, stats = k.wide, k.first_mask, k.valid, k.stats
    flat = wide.at[:, pl.ds(0, plan.slots + 2 * GAP)]
    send4, recv4, counts, csend = k.send4, k.recv4, k.counts, k.csend
    send_sem, recv_sem, count_sems = k.send_sem, k.recv_sem, k.count_sems
    N = plan.devices
    Q, R, RF = plan.steps, plan.block, plan.fine
    HV = range(plan.halves)
    SUB = plan.sub
    PER = plan.per
    me = lax.axis_index("dp")
    peers = peers_of(me, N)
    chips = N // 2
    chip, core = me // 2, lax.rem(me, 2)
    partner = me + 1 - 2 * core
    same_core = same_core_peers(me, N)

    barrier = pltpu.get_barrier_semaphore()
    for peer in peers:
        pl.semaphore_signal(barrier, inc=1, device_id=(peer,), device_id_type=MESH)

    len0 = lens[0]
    len1 = lens[1]
    half0 = len0 // 2
    half1 = len1 // 2
    count = (half0 + half1).astype(F32)
    def steps_loop(width, body, init=0):
        return lax.fori_loop(0, Q // width, lambda i, c: body(i * width, c), init)

    def mask_body(t0, c):
        step = t0 + lax.broadcasted_iota(jnp.int32, (RF, 8, LANES), 0)
        slot = step + Q * lax.broadcasted_iota(jnp.int32, (RF, 8, LANES), 1)
        a = (slot < half0).astype(F32)
        b = jnp.logical_and(slot >= half0 + GAP, slot < half0 + GAP + half1).astype(F32)
        first_mask[pl.ds(t0, RF)] = a
        valid[pl.ds(t0, RF)] = a + b
        return c

    steps_loop(RF, mask_body)

    top = 2 * GAP + 2 * plan.slots
    for h in HV:
        wide[h, 0:2 * GAP] = jnp.zeros((2 * GAP, LANES), F32)
        wide[h, top:] = jnp.zeros((wide.shape[1] - top, LANES), F32)

    def widen(i, c):
        rows = pl.ds(pl.multiple_of(i * 128, 128), 128)
        for h in HV:
            values = frames[rows, h * LANES:(h + 1) * LANES].astype(F32)
            wide[h, pl.ds(pl.multiple_of(i * 128 + 2 * GAP, 32), 128)] = values
        return c

    lax.fori_loop(0, 2 * plan.slots // 128, widen, 0)

    def set_halo(ref, half):
        sub = lax.broadcasted_iota(jnp.int32, (HALO, 8, LANES), 1)
        low = pltpu.roll(ref[half, pl.ds(Q, HALO)], 1, 1)
        ref[half, pl.ds(0, HALO)] = jnp.where(sub == 0, 0.0, low)
        high = pltpu.roll(ref[half, pl.ds(HALO, HALO)], 7, 1)
        ref[half, pl.ds(HALO + Q, HALO)] = jnp.where(sub == 7, 0.0, high)

    for phase in range(2):
        def deinterleave(t0, c):
            for j in range(RF):
                a_mask = first_mask[t0 + j]
                b_mask = valid[t0 + j] - a_mask
                for h in HV:
                    a = wide[h, pl.ds(2 * (t0 + j) + 2 * GAP + phase, 8, stride=2 * Q)]
                    b = wide[h, pl.ds(2 * (t0 + j) + phase, 8, stride=2 * Q)]
                    hid[phase, h, HALO + t0 + j] = a * a_mask + b * b_mask
            return c
        steps_loop(RF, deinterleave)
        for h in HV:
            set_halo(hid.at[phase], h)

    def spread_lanes(values, lane):
        k.tile[...] = jnp.zeros((8, LANES), F32)
        k.tile[:, 0:values.shape[1]] = values
        return pltpu.roll(k.tile[...], lane, 1) if lane else k.tile[...]

    def load_shard():
        for b in range(2):
            source = (k.dw_first, k.dw_second)[b]
            tiles = [jnp.zeros((8, LANES), F32) for _ in range(2)]
            for r in range(SUB):
                tile, lane = divmod(plan.tap_row(r), LANES)
                tiles[tile] = tiles[tile] + spread_lanes(source[r].astype(F32), lane)
            tiles[1] = tiles[1] + spread_lanes(k.se_up[b].astype(F32), EXPAND_ROW - LANES)
            tiles[1] = tiles[1] + spread_lanes(k.se_down[b].astype(F32), SQUEEZE_ROW - LANES)
            k.packed[0:LANES] = jnp.zeros((LANES, LANES), F32)
            for r in range(PER):
                k.packed[GAIN_ROW - LANES + r:GAIN_ROW - LANES + r + 1, 0:8] = k.gains_in[r, b:b + 1].astype(F32)
                k.packed[SHIFT_ROW - LANES + r:SHIFT_ROW - LANES + r + 1, 0:8] = k.shifts_in[r, b:b + 1].astype(F32)
            tiles[1] = tiles[1] + jnp.transpose(k.packed[0:LANES])[0:8]
            for tile in range(2):
                k.packed_t[8 * b:8 * b + 8, tile * LANES:(tile + 1) * LANES] = tiles[tile]
        k.gath[0, chip, core] = k.packed_t[...].astype(BF16)
        for pair in range(PER):
            rows = [k.point_in[i // PER, i % PER].astype(F32) for i in (2 * pair, 2 * pair + 1)]
            k.gath[1 + pair, chip, core] = jnp.concatenate(rows, axis=0).astype(BF16)

    def gather_send(unit):
        view = k.gath.at[unit, chip, core]
        for peer in same_core:
            pltpu.make_async_remote_copy(src_ref=view, dst_ref=view, send_sem=k.unit_sems.at[0, unit],
                                         recv_sem=k.unit_sems.at[1, unit], device_id=(peer,),
                                         device_id_type=MESH).start()

    def gather_forward(unit):
        view = k.gath.at[unit, pl.ds(0, chips - 1), 0]
        pltpu.make_async_copy(view, view, k.unit_sems.at[1, unit]).wait()
        view = k.gath.at[unit, :, core]
        pltpu.make_async_remote_copy(src_ref=view, dst_ref=view, send_sem=k.unit_sems.at[2, unit],
                                     recv_sem=k.unit_sems.at[3, unit], device_id=(partner,),
                                     device_id_type=MESH).start()

    def gather_wait(unit):
        view = k.gath.at[unit, :, 0]
        pltpu.make_async_copy(view, view, k.unit_sems.at[3, unit]).wait()

    def split_taps(b, r, h):
        taps = plan.taps[b]
        row0, row1, row2, row3 = plan.tap_sets
        low, high = (taps + 1) // 2, taps // 2
        rows = [dw[b * PER + r, h, t:t + 1] for t in range(taps)] + [jnp.zeros((1, LANES), F32)]
        dw[b * PER + r, h, row0:row0 + low] = jnp.concatenate(rows[0:taps:2], axis=0)
        dw[b * PER + r, h, row1:row1 + high] = jnp.concatenate(rows[1:taps:2], axis=0)
        dw[b * PER + r, h, row2:row2 + low] = jnp.concatenate(
            [rows[2 * j + 1] - rows[2 * j] for j in range(low)], axis=0)
        back = rows[taps - 1::-1] + [rows[taps]]
        dw[b * PER + r, h, row3:row3 + low] = jnp.concatenate(
            [back[2 * j + 1] - back[2 * j] for j in range(low)], axis=0)

    def unpack_values():
        got = k.gath[0].astype(F32).reshape(N, 16, plan.values)
        for b in range(2):
            block = got[:, 8 * b:8 * b + 8].reshape(plan.channels, plan.values)
            for h in HV:
                for tile in range(2):
                    part = block[h * LANES:(h + 1) * LANES, tile * LANES:(tile + 1) * LANES]
                    k.unpacked[tile * LANES:(tile + 1) * LANES] = jnp.transpose(part)
                for r in range(SUB):
                    dw[b * PER + r, h, 0:plan.tap_rows] = k.unpacked[plan.tap_row(r):plan.tap_row(r) + plan.tap_rows]
                    split_taps(b, r, h)
                for r in range(PER):
                    gains[b * PER + r, h:h + 1] = k.unpacked[GAIN_ROW + r:GAIN_ROW + r + 1]
                    shifts[b * PER + r, h:h + 1] = k.unpacked[SHIFT_ROW + r:SHIFT_ROW + r + 1]
                lanes = slice(h * LANES, (h + 1) * LANES)
                expand[b, :, lanes] = k.unpacked[EXPAND_ROW:EXPAND_ROW + plan.hidden]
                squeeze_t[b, :, lanes] = k.unpacked[SQUEEZE_ROW:SQUEEZE_ROW + plan.hidden]

    def unpack_pair(pair):
        got = k.gath[1 + pair].astype(F32).reshape(N, 16, plan.channels)
        for side in range(2):
            block = got[:, 8 * side:8 * side + 8].reshape(plan.channels, plan.channels)
            point[2 * pair + side] = block.astype(BF16)
            k.point_t[2 * pair + side] = jnp.transpose(block).astype(BF16)

    if plan.fused:
        load_shard()

    csend[...] = jnp.full((4, LANES), count, F32)
    pl.semaphore_wait(barrier, N - 1)

    def send_to_all(src, dst, ssem, rsem):
        for peer in peers:
            pltpu.make_async_remote_copy(src_ref=src, dst_ref=dst, send_sem=ssem, recv_sem=rsem,
                                         device_id=(peer,), device_id_type=MESH).start()

    def wait_all(ref, sem):
        view = ref.at[pl.ds(0, N - 1)]
        pltpu.make_async_copy(view, view, sem).wait()

    if plan.fused:
        gather_send(0)
        gather_send(1)
    send_to_all(csend, counts.at[me], count_sems.at[0], count_sems.at[1])
    if plan.fused:
        gather_send(2)
    counts[me] = csend[...]

    def exchange(slot, place, rows):
        send4[slot] = rows
        recv4[place, me] = rows
        send_to_all(send4.at[slot], recv4.at[place, me], send_sem.at[slot], recv_sem.at[slot])

    def received(slot, place):
        wait_all(recv4.at[place], recv_sem.at[slot])
        return recv4[place]

    def back_place(index):
        return lax.rem(index + PER, 2 * PER)

    def row(values):
        return values.reshape(1, 1, LANES)

    def accumulate(rows3):
        return jnp.sum(rows3, axis=0)

    def merge_stats(slot, index):
        got = received(slot, slot)
        weight = counts[...]
        total = jnp.sum(weight, axis=0)
        mean = jnp.sum(weight * got, axis=0) / total
        mean4 = jnp.concatenate([mean[0:2], mean[0:2]], axis=0)
        diff = got - mean4
        between = jnp.sum(weight * diff * diff, axis=0)
        within = jnp.sum(got, axis=0)
        var = (within[2:4] + between[0:2]) / total[0:2]
        inv = lax.rsqrt(var + EPSILON)
        scale = inv * gains[index]
        offset = shifts[index] - mean[0:2] * scale
        stats[index] = jnp.concatenate([mean[0:2], inv, scale, offset], axis=0)

    def stat_row(index, kind, h):
        return row(stats[index, pl.ds(2 * kind + h, 1)])

    def tap(index, h, t):
        return dw[index, h, pl.ds(t, 1)].reshape(1, 1, LANES)

    def direct(win, low, index, h, taps):
        acc = None
        for t, shift in taps:
            term = win[shift - low:shift - low + R] * tap(index, h, t)
            acc = term if acc is None else acc + term
        return acc

    def paired(win, index, h, taps, back):
        low, high = (taps + 1) // 2, taps // 2
        row0, row1, row2, row3 = plan.tap_sets
        m = R // 2
        split = win.reshape(-1, 2, 8, LANES)
        x0, x1 = split[:, 0], split[:, 1]
        both = x0[:m + low - 1] + x1[:m + low - 1]
        late = x0[1:m + high] + x1[:m + high - 1]

        def run(x, count, row):
            acc = None
            for j in range(count):
                term = x[j:j + m] * tap(index, h, row(j))
                acc = term if acc is None else acc + term
            return acc
        shared = run(x1, low, lambda j: (row3 if back else row2) + j)
        first = run(both, low, lambda j: row0 + (low - 1 - j if back else j)) + shared
        second = run(late, high, lambda j: row1 + (high - 1 - j if back else j)) - shared
        return jnp.stack([first, second], axis=1).reshape(R, 8, LANES)

    def layer_conv(index, pieces):
        def body(t0, c):
            for h in HV:
                acc = None
                if len(pieces) == 1:
                    source, taps = pieces[0]
                    low = taps[0][1]
                    acc = paired(hid[source, h, pl.ds(t0 + HALO + low, R + len(taps) - 1)], index, h, len(taps), False)
                else:
                    for source, taps in pieces:
                        low, high = taps[0][1], taps[-1][1]
                        part = direct(hid[source, h, pl.ds(t0 + HALO + low, R + high - low)], low, index, h, taps)
                        acc = part if acc is None else acc + part
                rows = pl.ds(pl.multiple_of(8 * t0, 16), 8 * R)
                acts[index, rows, h * LANES:(h + 1) * LANES] = acc.reshape(8 * R, LANES).astype(BF16)
            return c
        steps_loop(R, body)

    def half_lanes(values, h):
        return values[:, h * LANES:(h + 1) * LANES]

    def pointwise(index):
        pivot = [None] * plan.halves
        sums = [jnp.zeros((8, LANES), F32) for _ in HV]
        squares = [jnp.zeros((8, LANES), F32) for _ in HV]
        for t0 in range(0, Q, R):
            res = jnp.dot(acts[index, 8 * t0:8 * (t0 + R)], point[index], preferred_element_type=F32)
            v = valid[t0:t0 + R]
            for h in HV:
                p = half_lanes(res, h).reshape(R, 8, LANES)
                prods[index, h, t0:t0 + R] = p
                if t0 == 0:
                    pivot[h] = p[0, 0:1]
                d = p - row(pivot[h])
                dv = d * v
                sums[h] = sums[h] + accumulate(dv)
                squares[h] = squares[h] + accumulate(dv * d)
        n = jnp.full((1, LANES), count, F32)
        shift = [jnp.sum(sums[h], axis=0, keepdims=True) / n for h in HV]
        spread = [jnp.sum(squares[h], axis=0, keepdims=True) - n * shift[h] * shift[h] for h in HV]
        return jnp.concatenate([pivot[h] + shift[h] for h in HV] + spread, axis=0)

    def activate(index, target):
        scales = [0.5 * stat_row(index, 2, h) for h in HV]
        offsets = [0.5 * stat_row(index, 3, h) for h in HV]

        def body(t0, c):
            v = valid[pl.ds(t0, RF)]
            for h in HV:
                u = prods[index, h, pl.ds(t0, RF)] * scales[h] + offsets[h]
                hid[target, h, pl.ds(HALO + t0, RF)] = (u + u * jnp.tanh(u)) * v
            return c
        steps_loop(RF, body)
        for h in HV:
            set_halo(hid.at[target], h)

    def hid_of(b, r):
        return b * SUB + r + 1

    def regular_taps(b):
        margin = (plan.taps[b] - 1) // 2
        return [(t, t - margin) for t in range(plan.taps[b])]

    def block_pieces(b):
        if b == 0:
            taps = regular_taps(0)
            even = [(t, s // 2) for t, s in taps if s % 2 == 0]
            odd = [(t, (s - 1) // 2) for t, s in taps if s % 2 == 1]
            return [(0, even), (1, odd)]
        return [(hid_of(1, 0), regular_taps(1))]

    def residual_forward(b):
        source = 0 if b == 0 else hid_of(1, 0)
        res = b * PER + SUB

        def body(t0, c):
            rows = pl.ds(pl.multiple_of(8 * t0, 16), 8 * R)
            for h in HV:
                values = hid[source, h, pl.ds(HALO + t0, R)].reshape(8 * R, LANES)
                acts[res, rows, h * LANES:(h + 1) * LANES] = values.astype(BF16)
            return c
        steps_loop(R, body)
        exchange(res, res, pointwise(res))

    def small(a, b, dims):
        return lax.dot_general(a, b, (dims, ((), ())), precision=HIGHEST, preferred_element_type=F32)

    def thin(a, matrix, dim):
        hi = a.astype(BF16).astype(F32)
        mid = (a - hi).astype(BF16).astype(F32)
        low = a - hi - mid
        rows = jnp.concatenate([hi, mid, low, jnp.zeros_like(a)], axis=0).astype(BF16)
        res = lax.dot_general(rows, matrix.astype(BF16), (((1,), (dim,)), ((), ())), preferred_element_type=F32)
        return res[0:2] + res[2:4] + res[4:6]

    def eight(values):
        return jnp.concatenate([values, jnp.zeros((6, values.shape[1]), F32)], axis=0)

    def whole_row(index, kind):
        return jnp.concatenate([stats[index, pl.ds(2 * kind + h, 1)] for h in HV], axis=1)

    def join(parts):
        return jnp.concatenate([jnp.sum(part, axis=0, keepdims=True) for part in parts], axis=1)

    half_count = [jnp.full((1, plan.channels), n, jnp.int32).astype(F32) for n in (half0, half1)]

    def utterance_sums(b):
        last = b * PER + SUB - 1

        def sums(t0, c):
            a = first_mask[pl.ds(t0, RF)]
            s = valid[pl.ds(t0, RF)] - a
            res = []
            for h in HV:
                p = prods[last, h, pl.ds(t0, RF)]
                res += [c[2 * h] + accumulate(p * a), c[2 * h + 1] + accumulate(p * s)]
            return tuple(res)
        tot = steps_loop(RF, sums, tuple(jnp.zeros((8, LANES), F32) for _ in range(2 * plan.halves)))
        for u in range(2):
            k.psum[b, u:u + 1] = join([tot[2 * h + u] for h in HV])

    def excite(b):
        last = b * PER + SUB - 1
        scale, offset = whole_row(last, 2), whole_row(last, 3)
        means = jnp.concatenate([scale * (k.psum[b, u:u + 1] / half_count[u]) + offset for u in range(2)], axis=0)
        inner = thin(means, squeeze_t[b], 1)
        excited = inner * sigmoid(inner)
        gate = sigmoid(thin(excited, expand[b], 0))
        return means, inner, excited, gate

    def tail_half(b, gate):
        last, res = b * PER + SUB - 1, b * PER + SUB
        consts = []
        for h in HV:
            g = [half_lanes(gate[u:u + 1], h) for u in range(2)]
            s1, o1, s2, o2 = [0.5 * stats[i, pl.ds(2 * kind + h, 1)] for i, kind in
                              ((last, 2), (last, 3), (res, 2), (res, 3))]
            consts.append([row(v) for v in (s1 * g[0], s1 * g[1], s2, o1 * g[0] + o2, o1 * g[1] + o2)])

        def get(t0, h):
            a0, a1, s2, b0, b1 = consts[h]
            a = first_mask[pl.ds(t0, RF)] > 0.5
            return (prods[last, h, pl.ds(t0, RF)] * jnp.where(a, a0, a1)
                    + prods[res, h, pl.ds(t0, RF)] * s2 + jnp.where(a, b0, b1))
        return get

    def tail(b, gate, store):
        get = tail_half(b, gate)

        def body(t0, c):
            v = valid[pl.ds(t0, RF)]
            for h in HV:
                u = get(t0, h)
                store(t0, h, (u + u * jnp.tanh(u)) * v)
            return c
        steps_loop(RF, body)

    def slope_of(u):
        t = jnp.tanh(u)
        return (0.5 * t + 0.5) * (1.0 + u - u * t)

    def tail_slope(b, gate):
        get = tail_half(b, gate)

        def body(t0, c):
            v = valid[pl.ds(t0, RF)]
            for h in HV:
                pre[b, h, pl.ds(t0, RF)] = slope_of(get(t0, h)) * v
            return c
        steps_loop(RF, body)

    def forward_aside(b, r, extras):
        if plan.fused:
            step = b * SUB + r

            @pl.when(jnp.logical_and(step >= 1, step < PER))
            def _():
                gather_wait(1 + step)
                unpack_pair(step)

            @pl.when(step < PER - 1)
            def _():
                gather_forward(2 + step)

            @pl.when(step < PER - 2)
            def _():
                gather_send(3 + step)

        @pl.when(r == SUB - 2)
        def _():
            residual_forward(b)

        @pl.when(r == SUB - 1)
        def _():
            utterance_sums(b)
        for when, extra in extras:
            pl.when(r == when)(extra)

    def forward_block(b, extras=()):
        def layer(r, pieces, before=None):
            index = b * PER + r
            layer_conv(index, pieces)
            if before is not None:
                before()
            exchange(index, index, pointwise(index))
            forward_aside(b, r, extras)
            merge_stats(index, index)

        def first_matrices():
            gather_wait(1)
            unpack_pair(0)
        layer(0, block_pieces(b), first_matrices if plan.fused and b == 0 else None)
        activate(b * PER, hid_of(b, 1))

        def rest(r, c):
            layer(r, [(hid_of(b, r), regular_taps(b))])

            @pl.when(r < SUB - 1)
            def _():
                activate(b * PER + r, hid_of(b, r + 1))
            return c
        lax.fori_loop(1, SUB, rest, 0)
        merge_stats(b * PER + SUB, b * PER + SUB)
        return excite(b)

    back_slot = 2 * PER

    def sum_rows(parts):
        return jnp.concatenate([jnp.sum(part, axis=0, keepdims=True) for part in parts], axis=0)

    def tail_back(b, kept, load):
        means, inner, excited, gate = kept
        last = b * PER + SUB - 1
        mean = [stat_row(last, 0, h) for h in HV]

        def first(t0, c):
            a = first_mask[pl.ds(t0, RF)]
            res = []
            for h in HV:
                gs = load(t0, h)
                pre[b, h, pl.ds(t0, RF)] = gs
                gx = gs * (prods[last, h, pl.ds(t0, RF)] - mean[h])
                res += [c[4 * h] + accumulate(gs * a), c[4 * h + 1] + accumulate(gs),
                        c[4 * h + 2] + accumulate(gx * a), c[4 * h + 3] + accumulate(gx)]
            return tuple(res)
        tot = steps_loop(RF, first, tuple(jnp.zeros((8, LANES), F32) for _ in range(4 * plan.halves)))
        s0, s_all, x0, x_all = [join([tot[4 * h + i] for h in HV]) for i in range(4)]
        gs_sum = (s0, s_all - s0)
        gx_sum = (x0, x_all - x0)
        mean_row, inv_row, scale_row = [whole_row(last, kind) for kind in range(3)]
        shift_row = jnp.concatenate([shifts[last, h:h + 1] for h in HV], axis=1)
        grad_gate = jnp.concatenate([scale_row * gx_sum[u] + shift_row * gs_sum[u] for u in range(2)], axis=0)
        grad_up = grad_gate * gate * (1.0 - gate)
        sg = sigmoid(inner)
        grad_inner = thin(grad_up, expand[b], 1) * (sg * (1.0 + inner * (1.0 - sg)))
        grad_means = thin(grad_inner, squeeze_t[b], 0)
        per_slot = [grad_means[u:u + 1] / half_count[u] for u in range(2)]
        sum1, sum2 = 0.0, 0.0
        for u in range(2):
            g = gate[u:u + 1]
            sum1 = sum1 + g * gs_sum[u] + grad_means[u:u + 1]
            sum2 = sum2 + g * gx_sum[u] + per_slot[u] * (k.psum[b, u:u + 1] - half_count[u] * mean_row)
        sum2 = sum2 * inv_row
        exchange(back_slot + last, back_place(last),
                 jnp.concatenate([half_lanes(v, h) for v in (sum1, sum2) for h in HV], axis=0))
        return grad_up, grad_inner, per_slot

    def tail_back_aside(b, kept, found):
        means, inner, excited, gate = kept
        grad_up, grad_inner, per_slot = found
        res = b * PER + SUB
        gates = [[row(half_lanes(gate[u:u + 1], h)) for h in HV] for u in range(2)]
        slots = [[row(half_lanes(per_slot[u], h)) for h in HV] for u in range(2)]
        norm = [(stat_row(res, 0, h), stats[res, pl.ds(2 + h, 1)]) for h in HV]

        def second(t0, c):
            a = first_mask[pl.ds(t0, RF)] > 0.5
            v = valid[pl.ds(t0, RF)]
            out_c = []
            for h in HV:
                gs = pre[b, h, pl.ds(t0, RF)]
                gz[h, pl.ds(t0, RF)] = (gs * jnp.where(a, gates[0][h], gates[1][h])
                                        + jnp.where(a, slots[0][h], slots[1][h]) * v)
                x = prods[res, h, pl.ds(t0, RF)] - norm[h][0]
                out_c += [c[2 * h] + accumulate(gs), c[2 * h + 1] + accumulate(gs * x)]
            return tuple(out_c)
        tot = steps_loop(RF, second, tuple(jnp.zeros((8, LANES), F32) for _ in range(2 * plan.halves)))
        sums = [jnp.sum(part, axis=0, keepdims=True) for part in tot]
        exchange(back_slot + res, back_place(res), jnp.concatenate(
            [sums[2 * h] for h in HV] + [sums[2 * h + 1] * norm[h][1] for h in HV], axis=0))
        k.expand_grad[b] = small(eight(excited), eight(grad_up), ((0,), (0,)))
        k.squeeze_grad[b] = small(eight(grad_inner), eight(means), ((0,), (0,)))

    def norm_back(index, load, target, store):
        sums = jnp.sum(received(back_slot + index, back_place(index)), axis=0)
        k.shifts_grad[index] = sums[0:2]
        k.gains_grad[index] = sums[2:4]
        total = jnp.sum(counts[...], axis=0)[0:2]
        st = stats[index]
        mean, inv, scale = st[0:2], st[2:4], st[4:6]
        k1 = scale * sums[0:2] / total
        k2 = scale * sums[2:4] / total * inv
        rows3 = [[row(value[h:h + 1]) for value in (mean, scale, k1, k2)] for h in HV]
        for t0 in range(0, Q, R):
            v = valid[t0:t0 + R]
            parts = []
            for h in HV:
                mean_h, scale_h, k1_h, k2_h = rows3[h]
                grad = scale_h * load(t0, h) - (k1_h + k2_h * (prods[index, h, t0:t0 + R] - mean_h)) * v
                parts.append(grad.reshape(8 * R, LANES).astype(BF16))
            both = jnp.concatenate(parts, axis=1)
            target[8 * t0:8 * (t0 + R)] = both
            if plan.fused:
                res = jnp.dot(both, k.point_t[index], preferred_element_type=F32)
            else:
                res = lax.dot_general(both, point[index], (((1,), (1,)), ((), ())), preferred_element_type=F32)
            for h in HV:
                store(t0, h, half_lanes(res, h).reshape(R, 8, LANES))

    def point_back(index, source):
        place = lax.rem(index, 2) if plan.fused else index
        k.point_grad[place] = lax.dot_general(acts[index], source[...], (((0,), (0,)), ((), ())),
                                              preferred_element_type=F32)

    def store_gd(t0, h, values):
        gd[h, HALO + t0:HALO + t0 + R] = values

    def store_skip(t0, h, values):
        k.skip[h, t0:t0 + R] = values

    def conv_back_block(t0, h, index, taps):
        low, high = -taps[-1][1], -taps[0][1]
        win = gd[h, pl.ds(t0 + HALO + low, R + high - low)]
        if len(taps) >= plan.taps[0]:
            return paired(win, index, h, len(taps), True)
        return direct(win, low, index, h, [(t, -shift) for t, shift in taps])

    def kernel_back(index, pieces):
        for source, taps in pieces:
            for h in HV:
                low = min(s for _, s in taps)
                high = max(s for _, s in taps)

                def body(t0, c):
                    g = gd[h, pl.ds(HALO + t0, RF)]
                    win = hid[source, h, pl.ds(t0 + HALO + low, RF + high - low)]
                    return tuple(acc + accumulate(g * win[s - low:s - low + RF]) for acc, (_, s) in zip(c, taps))
                accs = steps_loop(RF, body, tuple(jnp.zeros((8, LANES), F32) for _ in taps))
                for acc, (tap, _) in zip(accs, taps):
                    k.dw_grad[index, h, pl.ds(tap, 1)] = jnp.sum(acc, axis=0, keepdims=True)

    def slopes(index):
        scales = [0.5 * stat_row(index, 2, h) for h in HV]
        offsets = [0.5 * stat_row(index, 3, h) for h in HV]

        def body(t0, c):
            v = valid[pl.ds(t0, RF)]
            for h in HV:
                k.slope[h, pl.ds(t0, RF)] = slope_of(prods[index, h, pl.ds(t0, RF)] * scales[h] + offsets[h]) * v
            return c
        steps_loop(RF, body)

    def hidden_back(index, taps):
        before = index - 1
        mean = [stat_row(before, 0, h) for h in HV]

        def body(t0, c):
            res = []
            for h in HV:
                grad = conv_back_block(t0, h, index, taps) * k.slope[h, pl.ds(t0, R)]
                gz[h, pl.ds(t0, R)] = grad
                gx = grad * (prods[before, h, pl.ds(t0, R)] - mean[h])
                res += [c[2 * h] + accumulate(grad), c[2 * h + 1] + accumulate(gx)]
            return tuple(res)
        tot = steps_loop(R, body, tuple(jnp.zeros((8, LANES), F32) for _ in range(2 * plan.halves)))
        sums = [jnp.sum(part, axis=0, keepdims=True) for part in tot]
        exchange(back_slot + before, back_place(before), jnp.concatenate(
            [sums[2 * h] for h in HV] + [sums[2 * h + 1] * stats[before, pl.ds(2 + h, 1)] for h in HV], axis=0))

    def load_gz(t0, h):
        return gz[h, t0:t0 + R]

    def scatter_start(unit, place):
        pltpu.make_async_remote_copy(src_ref=k.shares.at[place, :, 1 - core], dst_ref=k.inbox.at[unit],
                                     send_sem=k.unit_sems.at[4, unit], recv_sem=k.unit_sems.at[5, unit],
                                     device_id=(partner,), device_id_type=MESH).start()

    def scatter_send(unit, place):
        view = k.inbox.at[unit]
        pltpu.make_async_copy(view, view, k.unit_sems.at[5, unit]).wait()
        pltpu.make_async_copy(view, view, k.unit_sems.at[4, unit]).wait()
        k.sums[unit] = (k.shares[place, :, core].astype(F32) + k.inbox[unit].astype(F32)).astype(BF16)
        k.gained[unit, chip] = k.sums[unit, chip]
        for peer in same_core:
            pltpu.make_async_remote_copy(src_ref=k.sums.at[unit, peer // 2], dst_ref=k.gained.at[unit, chip],
                                         send_sem=k.unit_sems.at[6, unit], recv_sem=k.unit_sems.at[7, unit],
                                         device_id=(peer,), device_id_type=MESH).start()

    def scatter_finish(unit):
        view = k.gained.at[unit, pl.ds(0, chips - 1)]
        pltpu.make_async_copy(view, view, k.unit_sems.at[7, unit]).wait()
        return jnp.sum(k.gained[unit].astype(F32), axis=0)

    def pair_start(pair):
        both = [k.point_grad[side].reshape(N, 8, plan.channels) for side in range(2)]
        k.shares[0] = jnp.concatenate(both, axis=1).astype(BF16).reshape(chips, 2, 16, plan.channels)
        scatter_start(1 + pair, 0)

    def pair_finish(pair):
        total = scatter_finish(1 + pair)
        b = pair // (PER // 2)
        r = 2 * lax.rem(pair, PER // 2)
        k.point_out[b, r] = total[0:8]
        k.point_out[b, r + 1] = total[8:16]

    def values_start():
        k.packed[...] = jnp.zeros((plan.values, LANES), F32)
        blocks = []
        for b in range(2):
            columns = []
            for h in HV:
                for r in range(SUB):
                    k.packed[plan.tap_row(r):plan.tap_row(r) + plan.tap_rows] = k.dw_grad[b * PER + r, h]
                lanes = slice(h * LANES, (h + 1) * LANES)
                k.packed[EXPAND_ROW:EXPAND_ROW + plan.hidden] = k.expand_grad[b, :, lanes]
                k.packed[SQUEEZE_ROW:SQUEEZE_ROW + plan.hidden] = k.squeeze_grad[b, :, lanes]
                for r in range(PER):
                    k.packed[GAIN_ROW + r:GAIN_ROW + r + 1] = k.gains_grad[b * PER + r, h:h + 1]
                    k.packed[SHIFT_ROW + r:SHIFT_ROW + r + 1] = k.shifts_grad[b * PER + r, h:h + 1]
                columns.append(jnp.concatenate(
                    [jnp.transpose(k.packed[t * LANES:(t + 1) * LANES]) for t in range(2)], axis=1))
            whole = jnp.concatenate(columns, axis=0)
            k.own_norm[b] = whole[:, LANES:]
            blocks.append(whole.reshape(N, 8, plan.values))
        k.shares[1] = jnp.concatenate(blocks, axis=1).astype(BF16).reshape(chips, 2, 16, plan.values)
        scatter_start(0, 1)

    def values_finish():
        total = scatter_finish(0)
        mine = pl.ds(pl.multiple_of(me * 8, 8), 8)
        for b in range(2):
            rows = total[8 * b:8 * b + 8]

            def lanes(start, size):
                tile, lane = divmod(start, LANES)
                part = rows[:, tile * LANES:(tile + 1) * LANES]
                return (pltpu.roll(part, LANES - lane, 1) if lane else part)[:, 0:size]
            dw_out = (k.dw_first_out, k.dw_second_out)[b]
            for r in range(SUB):
                dw_out[r] = lanes(plan.tap_row(r), plan.taps[b])
            k.squeeze_out[b] = lanes(SQUEEZE_ROW, plan.hidden)
            k.expand_out[b] = lanes(EXPAND_ROW, plan.hidden)
            k.packed[0:LANES] = jnp.transpose(
                jnp.concatenate([k.own_norm[b, mine], jnp.zeros((LANES - 8, LANES), F32)], axis=0))
            for r in range(PER):
                k.gains_out[r, b:b + 1] = k.packed[GAIN_ROW - LANES + r:GAIN_ROW - LANES + r + 1, 0:8]
                k.shifts_out[r, b:b + 1] = k.packed[SHIFT_ROW - LANES + r:SHIFT_ROW - LANES + r + 1, 0:8]

    HALF = PER // 2

    def backward_aside(b, r):
        index = b * PER + r
        if plan.fused:
            if b == 0:
                @pl.when(r == SUB - 1)
                def _():
                    scatter_send(1 + HALF, 0)

                @pl.when(r == SUB - 2)
                def _():
                    pair_finish(HALF)

            @pl.when(lax.rem(r, 2) == 1)
            def _():
                scatter_send(1 + HALF * b + (r + 1) // 2, 0)

            @pl.when(jnp.logical_and(lax.rem(r, 2) == 0, r < SUB - 1))
            def _():
                pair_finish(HALF * b + r // 2 + 1)
        point_back(index, gpb)

        @pl.when(r == SUB - 1)
        def _():
            res = b * PER + SUB
            norm_back(res, lambda t0, h: pre[b, h, t0:t0 + R], gqb, store_skip)
            point_back(res, gqb)
        if plan.fused:
            @pl.when(lax.rem(r, 2) == 0)
            def _():
                pair_start(HALF * b + r // 2)

    def backward_block(b):
        def filtered(index):
            norm_back(index, load_gz, gpb, store_gd)
            for h in HV:
                set_halo(gd, h)

        def step(j, c):
            r = SUB - 1 - j
            index = b * PER + r
            filtered(index)
            hidden_back(index, regular_taps(b))
            backward_aside(b, r)
            kernel_back(index, [(hid_of(b, r), regular_taps(b))])

            @pl.when(r >= 2)
            def _():
                slopes(index - 2)
            return c
        lax.fori_loop(0, SUB - 1, step, 0)
        filtered(b * PER)

    if plan.fused:
        for unit in range(2):
            gather_forward(unit)
        gather_wait(0)
        unpack_values()
    else:
        dw[...] = k.dw_in[...]
        for b in range(2):
            for r in range(SUB):
                for h in HV:
                    split_taps(b, r, h)
    wait_all(counts, count_sems.at[1])
    kept_first = forward_block(0)

    def store_middle(t0, h, values):
        hid[hid_of(1, 0), h, pl.ds(HALO + t0, RF)] = values
    tail(0, kept_first[3], store_middle)
    for h in HV:
        set_halo(hid.at[hid_of(1, 0)], h)

    def place_cot():
        for h in HV:
            flat[h, 0:GAP] = jnp.zeros((GAP, LANES), F32)
            flat[h, GAP + plan.slots:] = jnp.zeros((flat.shape[1] - GAP - plan.slots, LANES), F32)

        def place(i, c):
            rows = pl.ds(pl.multiple_of(i * 128, 128), 128)
            for h in HV:
                flat[h, pl.ds(pl.multiple_of(i * 128 + GAP, 16), 128)] = cot[rows, h * LANES:(h + 1) * LANES]
            return c
        lax.fori_loop(0, plan.slots // 128, place, 0)

        def pick(t0, c):
            for h in HV:
                for j in range(RF):
                    here = flat[h, pl.ds(t0 + j + GAP, 8, stride=Q)]
                    moved = flat[h, pl.ds(t0 + j, 8, stride=Q)]
                    gz[h, t0 + j] = jnp.where(first_mask[t0 + j] > 0.5, here, moved)
            return c
        steps_loop(RF, pick)
    kept_second = forward_block(1, ((0, lambda: tail_slope(0, kept_first[3])), (1, place_cot)))

    last_half = tail_half(1, kept_second[3])

    def load_last(t0, h):
        return gz[h, pl.ds(t0, RF)] * (slope_of(last_half(t0, h)) * valid[pl.ds(t0, RF)])
    found = tail_back(1, kept_second, load_last)

    def store_out(t0, h, values):
        for j in range(RF):
            flat[h, pl.ds(t0 + j, 8, stride=Q)] = values[j]

    def ungap(i, c):
        rows = pl.ds(pl.multiple_of(i * 128, 128), 128)
        slot = i * 128 + lax.broadcasted_iota(jnp.int32, (128, LANES), 0)
        for h in HV:
            moved = flat[h, pl.ds(pl.multiple_of(i * 128 + GAP, 16), 128)]
            out[rows, h * LANES:(h + 1) * LANES] = jnp.where(slot < half0, flat[h, rows], moved)
        return c
    tail_back_aside(1, kept_second, found)
    slopes(PER + SUB - 2)
    tail(1, kept_second[3], store_out)
    lax.fori_loop(0, plan.slots // 128, ungap, 0)
    backward_block(1)

    def sum_back(t0, c):
        for h in HV:
            gz[h, pl.ds(t0, R)] = conv_back_block(t0, h, PER, regular_taps(1)) + k.skip[h, pl.ds(t0, R)]
        return c
    steps_loop(R, sum_back)
    found = tail_back(0, kept_first, lambda t0, h: gz[h, pl.ds(t0, RF)] * pre[0, h, pl.ds(t0, RF)])
    tail_back_aside(0, kept_first, found)
    slopes(SUB - 2)
    backward_aside(1, 0)
    kernel_back(PER, [(hid_of(1, 0), regular_taps(1))])
    backward_block(0)
    pieces = block_pieces(0)
    backward_aside(0, 0)
    kernel_back(0, pieces)
    if plan.fused:
        scatter_send(1, 0)
        values_start()
        scatter_send(0, 1)

    def spread(t0, c):
        v = valid[pl.ds(t0, R)]
        for h in HV:
            even = (conv_back_block(t0, h, 0, pieces[0][1]) + k.skip[h, pl.ds(t0, R)]) * v
            odd = conv_back_block(t0, h, 0, pieces[1][1]) * v
            for j in range(R):
                wide[h, pl.ds(2 * (t0 + j), 8, stride=2 * Q)] = even[j]
                wide[h, pl.ds(2 * (t0 + j) + 1, 8, stride=2 * Q)] = odd[j]
        return c
    steps_loop(R, spread)

    def ungap_wide(i, c):
        rows = pl.ds(pl.multiple_of(i * 128, 128), 128)
        slot = i * 128 + lax.broadcasted_iota(jnp.int32, (128, LANES), 0)
        for h in HV:
            moved = wide[h, pl.ds(pl.multiple_of(i * 128 + 2 * GAP, 32), 128)]
            frames_grad[rows, h * LANES:(h + 1) * LANES] = jnp.where(slot < len0, wide[h, rows], moved)
        return c
    lax.fori_loop(0, 2 * plan.slots // 128, ungap_wide, 0)
    if plan.fused:
        pair_finish(0)
        values_finish()

    wait_all(counts, count_sems.at[0])

    def drain(slot, c):
        wait_all(recv4.at[0], send_sem.at[slot])
        return c
    lax.fori_loop(0, send4.shape[0], drain, 0)
    if plan.fused:
        def drain_units(unit, c):
            view = k.gath.at[0, pl.ds(0, chips - 1), 0]
            pltpu.make_async_copy(view, view, k.unit_sems.at[0, unit]).wait()
            view = k.gath.at[0, :, 0]
            pltpu.make_async_copy(view, view, k.unit_sems.at[2, unit]).wait()
            view = k.gained.at[0, pl.ds(0, chips - 1)]
            pltpu.make_async_copy(view, view, k.unit_sems.at[6, unit]).wait()
            return c
        lax.fori_loop(0, 1 + PER, drain_units, 0)


def call_kernel(plan, inputs):
    layers, halves, Q, channels = plan.layers, plan.halves, plan.steps, plan.channels
    vals, shard, hidden, devices = plan.values, plan.shard, plan.hidden, plan.devices
    slots = 2 * layers

    def shape(*dims, dtype=F32):
        return jax.ShapeDtypeStruct(dims, dtype)
    outs = {
        "out": shape(plan.slots, channels),
        "frames_grad": shape(2 * plan.slots, channels),
    }
    params = {
        "dw": shape(layers, halves, plan.dw_rows, LANES),
        "point": shape(layers, channels, channels, dtype=BF16),
        "gains": shape(layers, halves, LANES),
        "shifts": shape(layers, halves, LANES),
        "squeeze_t": shape(2, hidden, channels),
        "expand": shape(2, hidden, channels),
    }
    grads = {
        "dw_grad": shape(layers, halves, plan.tap_rows, LANES),
        "point_grad": shape(2 if plan.fused else layers, channels, channels),
        "gains_grad": shape(layers, halves, LANES),
        "shifts_grad": shape(layers, halves, LANES),
        "squeeze_grad": shape(2, hidden, channels),
        "expand_grad": shape(2, hidden, channels),
    }
    scratch = {
        "hid": shape(2 * plan.sub + 1, halves, plan.pad, 8, LANES),
        "acts": shape(layers, plan.rows, channels, dtype=BF16),
        "prods": shape(layers, halves, Q, 8, LANES),
        "gd": shape(halves, plan.pad, 8, LANES),
        "gz": shape(halves, Q, 8, LANES),
        "gpb": shape(plan.rows, channels, dtype=BF16),
        "gqb": shape(plan.rows, channels, dtype=BF16),
        "pre": shape(2, halves, Q, 8, LANES),
        "wide": shape(halves, 2 * plan.slots + 4 * GAP, LANES),
        "first_mask": shape(Q, 8, LANES),
        "valid": shape(Q, 8, LANES),
        "slope": shape(halves, Q, 8, LANES),
        "skip": shape(halves, Q, 8, LANES),
        "psum": shape(2, 8, channels),
        "stats": shape(layers, 8, LANES),
        "send4": shape(slots, 4, LANES),
        "recv4": shape(layers, devices, 4, LANES),
        "counts": shape(devices, 4, LANES),
        "csend": shape(4, LANES),
    }
    sems = {"send_sem": (slots,), "recv_sem": (slots,), "count_sems": (2,)}
    if plan.fused:
        units, chips = 1 + plan.per, devices // 2
        outs.update({
            "dw_first_out": shape(plan.sub, shard, plan.taps[0]),
            "dw_second_out": shape(plan.sub, shard, plan.taps[1]),
            "point_out": shape(2, plan.per, shard, channels),
            "gains_out": shape(plan.per, 2, shard),
            "shifts_out": shape(plan.per, 2, shard),
            "squeeze_out": shape(2, shard, hidden),
            "expand_out": shape(2, shard, hidden),
        })
        scratch.update(params)
        scratch.update(grads)
        scratch.update({
            "tile": shape(8, LANES),
            "point_t": shape(layers, channels, channels, dtype=BF16),
            "packed": shape(vals, LANES),
            "packed_t": shape(16, vals),
            "unpacked": shape(vals, LANES),
            "gath": shape(units, chips, 2, 16, channels, dtype=BF16),
            "shares": shape(2, chips, 2, 16, channels, dtype=BF16),
            "inbox": shape(units, chips, 16, channels, dtype=BF16),
            "sums": shape(units, chips, 16, channels, dtype=BF16),
            "gained": shape(units, chips, 16, channels, dtype=BF16),
            "own_norm": shape(2, channels, LANES),
        })
        sems["unit_sems"] = (8, units)
    else:
        outs.update(grads)
        scratch["dw"] = params["dw"]
    vmem = pl.BlockSpec(memory_space=pltpu.VMEM)
    names = list(inputs) + list(outs) + list(scratch) + list(sems)
    results = pl.pallas_call(
        functools.partial(kernel, plan, names),
        out_shape=list(outs.values()),
        in_specs=[pl.BlockSpec(memory_space=pltpu.SMEM) if name == "lens" else vmem for name in inputs],
        out_specs=[vmem] * len(outs),
        scratch_shapes=[pltpu.VMEM(v.shape, v.dtype) for v in scratch.values()]
        + [pltpu.SemaphoreType.DMA(v) for v in sems.values()],
        compiler_params=pltpu.CompilerParams(
            collective_id=0, has_side_effects=True, vmem_limit_bytes=63 * 1024 * 1024),
    )(*inputs.values())
    return dict(zip(outs, results, strict=True))


def body(frames, dw_first, dw_second, point, gains, shifts, se_down, se_up, cotangent, lengths, *, devices):
    sub, taps_first, shard = dw_first.shape
    taps_second = dw_second.shape[1]
    hidden = se_down.shape[2]
    channels = point.shape[3]
    plan = Plan(cotangent.shape[0], channels, taps_first, taps_second, sub, hidden, devices)
    if plan.fused:
        res = call_kernel(plan, {
            "lens": lengths, "frames": frames, "cot": cotangent,
            "dw_first": jnp.swapaxes(dw_first, 1, 2), "dw_second": jnp.swapaxes(dw_second, 1, 2),
            "point_in": point, "gains_in": jnp.swapaxes(gains, 0, 1), "shifts_in": jnp.swapaxes(shifts, 0, 1),
            "se_down": se_down, "se_up": jnp.swapaxes(se_up, 1, 2)})
        return (
            res["out"], res["frames_grad"], jnp.swapaxes(res["dw_first_out"], 1, 2),
            jnp.swapaxes(res["dw_second_out"], 1, 2), res["point_out"], jnp.swapaxes(res["gains_out"], 0, 1),
            jnp.swapaxes(res["shifts_out"], 0, 1), res["squeeze_out"], jnp.swapaxes(res["expand_out"], 1, 2))

    per, layers, halves = plan.per, plan.layers, plan.halves

    def gather(v, axis):
        return lax.all_gather(v, "dp", axis=axis, tiled=True)
    small = jnp.concatenate([
        dw_first.reshape(-1, shard), dw_second.reshape(-1, shard), gains.reshape(-1, shard),
        shifts.reshape(-1, shard), se_up.reshape(-1, shard),
        jnp.swapaxes(se_down, 1, 2).reshape(-1, shard)], axis=0)
    small = gather(small, 1).astype(F32)
    sizes = [sub * taps_first, sub * taps_second, layers, layers, 2 * hidden, 2 * hidden]
    part = jnp.split(small, [sum(sizes[:i]) for i in range(1, 6)], axis=0)

    def dw_layout(v, taps):
        v = v.reshape(sub, taps, halves, LANES).transpose(0, 2, 1, 3)
        return jnp.pad(v, ((0, 1), (0, 0), (0, plan.dw_rows - taps), (0, 0)))
    res = call_kernel(plan, {
        "lens": lengths, "frames": frames, "cot": cotangent,
        "dw_in": jnp.concatenate([dw_layout(part[0], taps_first), dw_layout(part[1], taps_second)], axis=0),
        "point": gather(point, 2).reshape(layers, channels, channels),
        "gains": part[2].reshape(layers, halves, LANES),
        "shifts": part[3].reshape(layers, halves, LANES),
        "squeeze_t": part[5].reshape(2, hidden, channels),
        "expand": part[4].reshape(2, hidden, channels)})

    def scatter(v, axis):
        return lax.psum_scatter(v, "dp", scatter_dimension=axis, tiled=True)

    def dw_out(v, taps):
        return v[:sub, :, :taps].transpose(0, 2, 1, 3).reshape(sub * taps, channels)
    grads = res["dw_grad"]
    packed = scatter(jnp.concatenate(
        [dw_out(grads[:per], taps_first), dw_out(grads[per:], taps_second),
         res["squeeze_grad"].reshape(-1, channels), res["expand_grad"].reshape(-1, channels)], axis=0), 1)
    g1, g2, gsq, gex = jnp.split(packed, [sizes[0], sizes[0] + sizes[1], sizes[0] + sizes[1] + sizes[5]], axis=0)

    def norm_out(v):
        return lax.dynamic_slice_in_dim(v.reshape(2, per, channels), lax.axis_index("dp") * shard, shard, 2)
    return (
        res["out"], res["frames_grad"], g1.reshape(sub, taps_first, shard), g2.reshape(sub, taps_second, shard),
        scatter(res["point_grad"].reshape(2, per, channels, channels), 2),
        norm_out(res["gains_grad"]), norm_out(res["shifts_grad"]),
        jnp.swapaxes(gsq.reshape(2, hidden, shard), 1, 2), gex.reshape(2, hidden, shard))


def solution(mesh):
    return jax.shard_map(
        functools.partial(body, devices=mesh.shape["dp"]),
        mesh=mesh,
        in_specs=(
            P("dp", None),
            P(None, None, "dp"),
            P(None, None, "dp"),
            P(None, None, "dp", None),
            P(None, None, "dp"),
            P(None, None, "dp"),
            P(None, "dp", None),
            P(None, None, "dp"),
            P("dp", None),
            P("dp"),
        ),
        out_specs=(
            P("dp", None),
            P("dp", None),
            P(None, None, "dp"),
            P(None, None, "dp"),
            P(None, None, "dp", None),
            P(None, None, "dp"),
            P(None, None, "dp"),
            P(None, "dp", None),
            P(None, None, "dp"),
        ),
        check_vma=False,
    )
```

```python
import functools

import jax
import jax.numpy as jnp
from jax import lax
from jax.experimental import pallas as pl
from jax.experimental.pallas import tpu as pltpu
from jax.sharding import PartitionSpec as P

EPSILON = 1e-05
HIGHEST = lax.Precision.HIGHEST
F32 = jnp.float32
BF16 = jnp.bfloat16
MESH = pl.DeviceIdType.MESH

GAP = 16
HALO = 13
LANES = 128


def sigmoid(v):
    return 0.5 * jnp.tanh(0.5 * v) + 0.5


class Plan:
    def __init__(self, slots, channels, taps_first, taps_second, sub_blocks, hidden, devices):
        self.slots = slots
        self.steps = (slots + GAP) // 8
        self.rows = 8 * self.steps
        self.channels = channels
        self.halves = channels // LANES
        self.taps = (taps_first, taps_second)
        self.max_taps = max(self.taps)
        self.sub = sub_blocks
        self.hidden = hidden
        self.devices = devices
        self.block = next(r for r in (26, 10, 2) if self.steps % r == 0)
        self.fine = next(r for r in (10, 26, 2) if self.steps % r == 0)
        self.pad = self.steps + 2 * HALO
        self.per = sub_blocks + 1
        self.layers = 2 * self.per
        self.tap_rows = 32
        self.tap_sets = (32, 48, 64, 80)
        self.dw_rows = 96
        self.values = 2 * LANES
        self.shard = channels // devices
        self.fused = self.shard == 8 and devices == 32 and sub_blocks == 5 and hidden == 32 and self.max_taps <= 32

    def tap_row(self, r):
        return r * self.tap_rows + self.tap_rows * (r // 4)


SQUEEZE_ROW, EXPAND_ROW, GAIN_ROW, SHIFT_ROW = 128, 192, 224, 232


PARAMS = ("dw_first", "dw_second", "point_in", "gains_in", "shifts_in", "se_down", "se_up")


class Refs:
    def __init__(self, names, refs):
        for name, ref in zip(names, refs, strict=True):
            setattr(self, name, ref)


def peers_of(me, n):
    if n != 32:
        return [lax.rem(me + k, n) for k in range(1, n)]
    core = lax.rem(me, 2)
    x = lax.rem(me // 2, 2)
    y = lax.rem(me // 4, 2)
    z = me // 8
    found = []
    for order, other in enumerate((3 - z, lax.rem(z + 2, 4), z + 1 - 2 * lax.rem(z, 2), z)):
        for dy in (1, 0):
            for dx in (1, 0):
                for dc in (0, 1):
                    if order == 3 and dy == 0 and dx == 0 and dc == 0:
                        continue
                    oy = lax.rem(y + dy, 2)
                    ox = lax.rem(x + dx, 2)
                    oc = lax.rem(core + dc, 2)
                    found.append((dy + dx + (3, 2, 1, 0)[order], other * 8 + oy * 4 + ox * 2 + oc))
    found.sort(key=lambda item: -item[0])
    return [item[1] for item in found]


def same_core_peers(me, n):
    if n != 32:
        return [lax.rem(me + 2 * k, n) for k in range(1, n // 2)]
    core = lax.rem(me, 2)
    x = lax.rem(me // 2, 2)
    y = lax.rem(me // 4, 2)
    z = me // 8
    found = []
    for order, other in enumerate((3 - z, lax.rem(z + 2, 4), z + 1 - 2 * lax.rem(z, 2), z)):
        for dy in (1, 0):
            for dx in (1, 0):
                if order == 3 and dy == 0 and dx == 0:
                    continue
                oy = lax.rem(y + dy, 2)
                ox = lax.rem(x + dx, 2)
                found.append((dy + dx + (3, 2, 1, 0)[order], other * 8 + oy * 4 + ox * 2 + core))
    found.sort(key=lambda item: -item[0])
    return [item[1] for item in found]


def kernel(plan, names, *refs):
    k = Refs(names, refs)
    lens, dw, point, gains, shifts = k.lens, k.dw, k.point, k.gains, k.shifts
    squeeze_t, expand = k.squeeze_t, k.expand
    hid, acts, prods, gd, gz, gpb, gqb, pre = k.hid, k.acts, k.prods, k.gd, k.gz, k.gpb, k.gqb, k.pre
    wide, first_mask, valid, stats = k.wide, k.first_mask, k.valid, k.stats
    flat = wide.at[:, pl.ds(0, plan.slots + 2 * GAP)]
    send4, recv4, counts, csend = k.send4, k.recv4, k.counts, k.csend
    send_sem, recv_sem, count_sems = k.send_sem, k.recv_sem, k.count_sems
    N = plan.devices
    Q, R, RF = plan.steps, plan.block, plan.fine
    HV = range(plan.halves)
    SUB = plan.sub
    PER = plan.per
    me = lax.axis_index("dp")
    peers = peers_of(me, N)
    chips = N // 2
    chip, core = me // 2, lax.rem(me, 2)
    partner = me + 1 - 2 * core
    depth, plane = me // 8, lax.rem(me // 2, 4)

    def at_depth(d):
        return lax.rem(depth + d, 4) * 8 + 2 * plane + core

    def in_plane(d):
        return depth * 8 + 2 * lax.rem(plane + d, 4) + core

    same_core = same_core_peers(me, N)

    barrier = pltpu.get_barrier_semaphore()
    for peer in peers:
        pl.semaphore_signal(barrier, inc=1, device_id=(peer,), device_id_type=MESH)

    load_frames = pltpu.make_async_copy(k.frames, k.frames_v, k.io_sems.at[0])
    load_params = []
    if plan.fused:
        for i, name in enumerate(PARAMS):
            load_params.append(pltpu.make_async_copy(getattr(k, name), getattr(k, name + "_v"), k.param_sems.at[i]))
            load_params[-1].start()
    load_cot = pltpu.make_async_copy(k.cot, k.cot_v, k.io_sems.at[1])
    save_out = pltpu.make_async_copy(k.cot_v, k.out, k.io_sems.at[2])
    load_frames.start()
    load_cot.start()
    len0 = lens[0]
    len1 = lens[1]
    half0 = len0 // 2
    half1 = len1 // 2
    count = (half0 + half1).astype(F32)
    def steps_loop(width, body, init=0):
        return lax.fori_loop(0, Q // width, lambda i, c: body(i * width, c), init)

    def mask_body(t0, c):
        step = t0 + lax.broadcasted_iota(jnp.int32, (RF, 8, LANES), 0)
        slot = step + Q * lax.broadcasted_iota(jnp.int32, (RF, 8, LANES), 1)
        a = (slot < half0).astype(F32)
        b = jnp.logical_and(slot >= half0 + GAP, slot < half0 + GAP + half1).astype(F32)
        first_mask[pl.ds(t0, RF)] = a
        valid[pl.ds(t0, RF)] = a + b
        return c

    steps_loop(RF, mask_body)

    top = 2 * GAP + 2 * plan.slots
    for h in HV:
        wide[h, 0:2 * GAP] = jnp.zeros((2 * GAP, LANES), F32)
        wide[h, top:] = jnp.zeros((wide.shape[1] - top, LANES), F32)

    load_frames.wait()

    def widen(i, c):
        rows = pl.ds(pl.multiple_of(i * 128, 128), 128)
        for h in HV:
            values = k.frames_v[rows, h * LANES:(h + 1) * LANES].astype(F32)
            wide[h, pl.ds(pl.multiple_of(i * 128 + 2 * GAP, 32), 128)] = values
        return c

    lax.fori_loop(0, 2 * plan.slots // 128, widen, 0)

    def set_halo(ref, half):
        sub = lax.broadcasted_iota(jnp.int32, (HALO, 8, LANES), 1)
        low = pltpu.roll(ref[half, pl.ds(Q, HALO)], 1, 1)
        ref[half, pl.ds(0, HALO)] = jnp.where(sub == 0, 0.0, low)
        high = pltpu.roll(ref[half, pl.ds(HALO, HALO)], 7, 1)
        ref[half, pl.ds(HALO + Q, HALO)] = jnp.where(sub == 7, 0.0, high)

    for phase in range(2):
        def deinterleave(t0, c):
            for j in range(RF):
                a_mask = first_mask[t0 + j]
                b_mask = valid[t0 + j] - a_mask
                for h in HV:
                    a = wide[h, pl.ds(2 * (t0 + j) + 2 * GAP + phase, 8, stride=2 * Q)]
                    b = wide[h, pl.ds(2 * (t0 + j) + phase, 8, stride=2 * Q)]
                    hid[phase, h, HALO + t0 + j] = a * a_mask + b * b_mask
            return c
        steps_loop(RF, deinterleave)
        for h in HV:
            set_halo(hid.at[phase], h)

    def spread_lanes(values, lane):
        k.tile[...] = jnp.zeros((8, LANES), F32)
        k.tile[:, 0:values.shape[1]] = values
        return pltpu.roll(k.tile[...], lane, 1) if lane else k.tile[...]

    def load_shard():
        for b in range(2):
            source = (k.dw_first_v, k.dw_second_v)[b]
            tiles = [jnp.zeros((8, LANES), F32) for _ in range(2)]
            for r in range(SUB):
                tile, lane = divmod(plan.tap_row(r), LANES)
                tiles[tile] = tiles[tile] + spread_lanes(source[r].astype(F32), lane)
            tiles[1] = tiles[1] + spread_lanes(k.se_up_v[b].astype(F32), EXPAND_ROW - LANES)
            tiles[1] = tiles[1] + spread_lanes(k.se_down_v[b].astype(F32), SQUEEZE_ROW - LANES)
            k.packed[0:LANES] = jnp.zeros((LANES, LANES), F32)
            for r in range(PER):
                k.packed[GAIN_ROW - LANES + r:GAIN_ROW - LANES + r + 1, 0:8] = k.gains_in_v[r, b:b + 1].astype(F32)
                k.packed[SHIFT_ROW - LANES + r:SHIFT_ROW - LANES + r + 1, 0:8] = k.shifts_in_v[r, b:b + 1].astype(F32)
            tiles[1] = tiles[1] + jnp.transpose(k.packed[0:LANES])[0:8]
            for tile in range(2):
                k.packed_t[8 * b:8 * b + 8, tile * LANES:(tile + 1) * LANES] = tiles[tile]
            if b == 0:
                lane = lax.broadcasted_iota(jnp.int32, (8, LANES), 1)
                k.first[me] = jnp.where(lane == plan.tap_rows - 1, count, tiles[0])
        k.gath[0, depth, plane, core] = k.packed_t[...].astype(BF16)
        for pair in range(PER):
            rows = [k.point_in_v[i // PER, i % PER].astype(F32) for i in (2 * pair, 2 * pair + 1)]
            k.gath[1 + pair, depth, plane, core] = jnp.concatenate(rows, axis=0).astype(BF16)

    def remote(src, dst, sems, unit, to):
        pltpu.make_async_remote_copy(src_ref=src, dst_ref=dst, send_sem=k.unit_sems.at[sems, unit],
                                     recv_sem=k.unit_sems.at[sems + 1, unit], device_id=(to,),
                                     device_id_type=MESH).start()

    def blocks_wait(count, sem, unit):
        view = k.gained.at[0, pl.ds(0, count)]
        pltpu.make_async_copy(view, view, k.unit_sems.at[sem, unit]).wait()

    def gather_send(unit):
        view = k.gath.at[unit, depth, plane, core]
        for peer in same_core:
            remote(view, view, 0, unit, peer)

    def gather_z(unit):
        view = k.gath.at[unit, depth, plane, core]
        for d in (2, 1, 3):
            remote(view, view, 0, unit, at_depth(d))

    def gather_plane(unit):
        blocks_wait(3, 1, unit)
        view = k.gath.at[unit, :, plane, core]
        for d in (3, 2, 1):
            remote(view, view, 2, unit, in_plane(d))

    def gather_core(unit, straight):
        blocks_wait(chips - 1 if straight else 12, 1 if straight else 3, unit)
        view = k.gath.at[unit, :, :, core]
        remote(view, view, 4, unit, partner)

    def gather_wait(unit):
        blocks_wait(chips, 5, unit)

    def split_taps(b, r, h):
        taps = plan.taps[b]
        row0, row1, row2, row3 = plan.tap_sets
        low, high = (taps + 1) // 2, taps // 2
        rows = [dw[b * PER + r, h, t:t + 1] for t in range(taps)] + [jnp.zeros((1, LANES), F32)]
        dw[b * PER + r, h, row0:row0 + low] = jnp.concatenate(rows[0:taps:2], axis=0)
        dw[b * PER + r, h, row1:row1 + high] = jnp.concatenate(rows[1:taps:2], axis=0)
        dw[b * PER + r, h, row2:row2 + low] = jnp.concatenate(
            [rows[2 * j + 1] - rows[2 * j] for j in range(low)], axis=0)
        back = rows[taps - 1::-1] + [rows[taps]]
        dw[b * PER + r, h, row3:row3 + low] = jnp.concatenate(
            [back[2 * j + 1] - back[2 * j] for j in range(low)], axis=0)

    def unpack_first():
        got = k.first[...]
        counts[...] = jnp.broadcast_to(got[:, 0:4, plan.tap_rows - 1:plan.tap_rows], counts.shape)
        block = got.reshape(plan.channels, LANES)
        for h in HV:
            k.unpacked[0:LANES] = jnp.transpose(block[h * LANES:(h + 1) * LANES])
            dw[0, h, 0:plan.tap_rows] = k.unpacked[0:plan.tap_rows]

    def unpack_values():
        got = k.gath[0].astype(F32).reshape(N, 16, plan.values)
        for b in range(2):
            block = got[:, 8 * b:8 * b + 8].reshape(plan.channels, plan.values)
            for h in HV:
                for tile in range(2):
                    part = block[h * LANES:(h + 1) * LANES, tile * LANES:(tile + 1) * LANES]
                    k.unpacked[tile * LANES:(tile + 1) * LANES] = jnp.transpose(part)
                for r in range(SUB):
                    dw[b * PER + r, h, 0:plan.tap_rows] = k.unpacked[plan.tap_row(r):plan.tap_row(r) + plan.tap_rows]
                    split_taps(b, r, h)
                for r in range(PER):
                    gains[b * PER + r, h:h + 1] = k.unpacked[GAIN_ROW + r:GAIN_ROW + r + 1]
                    shifts[b * PER + r, h:h + 1] = k.unpacked[SHIFT_ROW + r:SHIFT_ROW + r + 1]
                lanes = slice(h * LANES, (h + 1) * LANES)
                expand[b, :, lanes] = k.unpacked[EXPAND_ROW:EXPAND_ROW + plan.hidden]
                squeeze_t[b, :, lanes] = k.unpacked[SQUEEZE_ROW:SQUEEZE_ROW + plan.hidden]

    def unpack_pair(pair):
        got = k.gath[1 + pair].astype(F32).reshape(N, 16, plan.channels)
        for side in range(2):
            block = got[:, 8 * side:8 * side + 8].reshape(plan.channels, plan.channels)
            point[2 * pair + side] = block.astype(BF16)
            k.point_t[2 * pair + side] = jnp.transpose(block).astype(BF16)

    if plan.fused:
        for copy in load_params:
            copy.wait()
        load_shard()

    if not plan.fused:
        csend[...] = jnp.full((4, LANES), count, F32)
    pl.semaphore_wait(barrier, N - 1)

    def send_to_all(src, dst, ssem, rsem):
        for peer in peers:
            pltpu.make_async_remote_copy(src_ref=src, dst_ref=dst, send_sem=ssem, recv_sem=rsem,
                                         device_id=(peer,), device_id_type=MESH).start()

    def wait_all(ref, sem):
        view = ref.at[pl.ds(0, N - 1)]
        pltpu.make_async_copy(view, view, sem).wait()

    if plan.fused:
        send_to_all(k.first.at[me], k.first.at[me], count_sems.at[0], count_sems.at[1])
        gather_send(1)
        gather_send(0)
        gather_z(2)
    else:
        send_to_all(csend, counts.at[me], count_sems.at[0], count_sems.at[1])
        counts[me] = csend[...]

    def exchange(slot, place, rows):
        send4[slot] = rows
        recv4[place, me] = rows
        send_to_all(send4.at[slot], recv4.at[place, me], send_sem.at[slot], recv_sem.at[slot])

    def received(slot, place):
        wait_all(recv4.at[place], recv_sem.at[slot])
        return recv4[place]

    def back_place(index):
        return lax.rem(index + PER, 2 * PER)

    def row(values):
        return values.reshape(1, 1, LANES)

    def accumulate(rows3):
        return jnp.sum(rows3, axis=0)

    def merge_stats(slot, index):
        got = received(slot, slot)
        weight = counts[...]
        total = jnp.sum(weight, axis=0)
        mean = jnp.sum(weight * got, axis=0) / total
        mean4 = jnp.concatenate([mean[0:2], mean[0:2]], axis=0)
        diff = got - mean4
        between = jnp.sum(weight * diff * diff, axis=0)
        within = jnp.sum(got, axis=0)
        var = (within[2:4] + between[0:2]) / total[0:2]
        inv = lax.rsqrt(var + EPSILON)
        scale = inv * gains[index]
        offset = shifts[index] - mean[0:2] * scale
        stats[index] = jnp.concatenate([mean[0:2], inv, scale, offset], axis=0)

    def stat_row(index, kind, h):
        return row(stats[index, pl.ds(2 * kind + h, 1)])

    def tap(index, h, t):
        return dw[index, h, pl.ds(t, 1)].reshape(1, 1, LANES)

    def direct(win, low, index, h, taps):
        acc = None
        for t, shift in taps:
            term = win[shift - low:shift - low + R] * tap(index, h, t)
            acc = term if acc is None else acc + term
        return acc

    def paired(win, index, h, taps, back):
        low, high = (taps + 1) // 2, taps // 2
        row0, row1, row2, row3 = plan.tap_sets
        m = R // 2
        split = win.reshape(-1, 2, 8, LANES)
        x0, x1 = split[:, 0], split[:, 1]
        both = x0[:m + low - 1] + x1[:m + low - 1]
        late = x0[1:m + high] + x1[:m + high - 1]

        def run(x, count, row):
            acc = None
            for j in range(count):
                term = x[j:j + m] * tap(index, h, row(j))
                acc = term if acc is None else acc + term
            return acc
        shared = run(x1, low, lambda j: (row3 if back else row2) + j)
        first = run(both, low, lambda j: row0 + (low - 1 - j if back else j)) + shared
        second = run(late, high, lambda j: row1 + (high - 1 - j if back else j)) - shared
        return jnp.stack([first, second], axis=1).reshape(R, 8, LANES)

    def layer_conv(index, pieces, between=None):
        def body(t0, c):
            for h in HV:
                acc = None
                if len(pieces) == 1:
                    source, taps = pieces[0]
                    low = taps[0][1]
                    acc = paired(hid[source, h, pl.ds(t0 + HALO + low, R + len(taps) - 1)], index, h, len(taps), False)
                else:
                    for source, taps in pieces:
                        low, high = taps[0][1], taps[-1][1]
                        part = direct(hid[source, h, pl.ds(t0 + HALO + low, R + high - low)], low, index, h, taps)
                        acc = part if acc is None else acc + part
                rows = pl.ds(pl.multiple_of(8 * t0, 16), 8 * R)
                acts[index, rows, h * LANES:(h + 1) * LANES] = acc.reshape(8 * R, LANES).astype(BF16)
            return c
        if between is None:
            steps_loop(R, body)
        else:
            cut = Q // R - 2
            lax.fori_loop(0, cut, lambda i, c: body(i * R, c), 0)
            between()
            lax.fori_loop(cut, Q // R, lambda i, c: body(i * R, c), 0)

    def half_lanes(values, h):
        return values[:, h * LANES:(h + 1) * LANES]

    def pointwise(index):
        pivot = [None] * plan.halves
        sums = [jnp.zeros((8, LANES), F32) for _ in HV]
        squares = [jnp.zeros((8, LANES), F32) for _ in HV]
        for t0 in range(0, Q, R):
            res = jnp.dot(acts[index, 8 * t0:8 * (t0 + R)], point[index], preferred_element_type=F32)
            v = valid[t0:t0 + R]
            for h in HV:
                p = half_lanes(res, h).reshape(R, 8, LANES)
                prods[index, h, t0:t0 + R] = p
                if t0 == 0:
                    pivot[h] = p[0, 0:1]
                d = p - row(pivot[h])
                dv = d * v
                sums[h] = sums[h] + accumulate(dv)
                squares[h] = squares[h] + accumulate(dv * d)
        n = jnp.full((1, LANES), count, F32)
        shift = [jnp.sum(sums[h], axis=0, keepdims=True) / n for h in HV]
        spread = [jnp.sum(squares[h], axis=0, keepdims=True) - n * shift[h] * shift[h] for h in HV]
        return jnp.concatenate([pivot[h] + shift[h] for h in HV] + spread, axis=0)

    def activate(index, target):
        scales = [0.5 * stat_row(index, 2, h) for h in HV]
        offsets = [0.5 * stat_row(index, 3, h) for h in HV]

        def body(t0, c):
            v = valid[pl.ds(t0, RF)]
            for h in HV:
                u = prods[index, h, pl.ds(t0, RF)] * scales[h] + offsets[h]
                hid[target, h, pl.ds(HALO + t0, RF)] = (u + u * jnp.tanh(u)) * v
            return c
        steps_loop(RF, body)
        for h in HV:
            set_halo(hid.at[target], h)

    def hid_of(b, r):
        return b * SUB + r + 1

    def regular_taps(b):
        margin = (plan.taps[b] - 1) // 2
        return [(t, t - margin) for t in range(plan.taps[b])]

    def block_pieces(b):
        if b == 0:
            taps = regular_taps(0)
            even = [(t, s // 2) for t, s in taps if s % 2 == 0]
            odd = [(t, (s - 1) // 2) for t, s in taps if s % 2 == 1]
            return [(0, even), (1, odd)]
        return [(hid_of(1, 0), regular_taps(1))]

    def residual_forward(b):
        source = 0 if b == 0 else hid_of(1, 0)
        res = b * PER + SUB

        def body(t0, c):
            rows = pl.ds(pl.multiple_of(8 * t0, 16), 8 * R)
            for h in HV:
                values = hid[source, h, pl.ds(HALO + t0, R)].reshape(8 * R, LANES)
                acts[res, rows, h * LANES:(h + 1) * LANES] = values.astype(BF16)
            return c
        steps_loop(R, body)
        exchange(res, res, pointwise(res))

    def small(a, b, dims):
        return lax.dot_general(a, b, (dims, ((), ())), precision=HIGHEST, preferred_element_type=F32)

    def thin(a, matrix, dim):
        hi = a.astype(BF16).astype(F32)
        mid = (a - hi).astype(BF16).astype(F32)
        low = a - hi - mid
        rows = jnp.concatenate([hi, mid, low, jnp.zeros_like(a)], axis=0).astype(BF16)
        res = lax.dot_general(rows, matrix.astype(BF16), (((1,), (dim,)), ((), ())), preferred_element_type=F32)
        return res[0:2] + res[2:4] + res[4:6]

    def eight(values):
        return jnp.concatenate([values, jnp.zeros((6, values.shape[1]), F32)], axis=0)

    def whole_row(index, kind):
        return jnp.concatenate([stats[index, pl.ds(2 * kind + h, 1)] for h in HV], axis=1)

    def join(parts):
        return jnp.concatenate([jnp.sum(part, axis=0, keepdims=True) for part in parts], axis=1)

    half_count = [jnp.full((1, plan.channels), n, jnp.int32).astype(F32) for n in (half0, half1)]

    def utterance_sums(b):
        last = b * PER + SUB - 1

        def sums(t0, c):
            a = first_mask[pl.ds(t0, RF)]
            s = valid[pl.ds(t0, RF)] - a
            res = []
            for h in HV:
                p = prods[last, h, pl.ds(t0, RF)]
                res += [c[2 * h] + accumulate(p * a), c[2 * h + 1] + accumulate(p * s)]
            return tuple(res)
        tot = steps_loop(RF, sums, tuple(jnp.zeros((8, LANES), F32) for _ in range(2 * plan.halves)))
        for u in range(2):
            k.psum[b, u:u + 1] = join([tot[2 * h + u] for h in HV])

    def excite(b):
        last = b * PER + SUB - 1
        scale, offset = whole_row(last, 2), whole_row(last, 3)
        means = jnp.concatenate([scale * (k.psum[b, u:u + 1] / half_count[u]) + offset for u in range(2)], axis=0)
        inner = thin(means, squeeze_t[b], 1)
        excited = inner * sigmoid(inner)
        gate = sigmoid(thin(excited, expand[b], 0))
        return means, inner, excited, gate

    def tail_half(b, gate):
        last, res = b * PER + SUB - 1, b * PER + SUB
        consts = []
        for h in HV:
            g = [half_lanes(gate[u:u + 1], h) for u in range(2)]
            s1, o1, s2, o2 = [0.5 * stats[i, pl.ds(2 * kind + h, 1)] for i, kind in
                              ((last, 2), (last, 3), (res, 2), (res, 3))]
            consts.append([row(v) for v in (s1 * g[0], s1 * g[1], s2, o1 * g[0] + o2, o1 * g[1] + o2)])

        def get(t0, h):
            a0, a1, s2, b0, b1 = consts[h]
            a = first_mask[pl.ds(t0, RF)] > 0.5
            return (prods[last, h, pl.ds(t0, RF)] * jnp.where(a, a0, a1)
                    + prods[res, h, pl.ds(t0, RF)] * s2 + jnp.where(a, b0, b1))
        return get

    def tail(b, gate, store):
        get = tail_half(b, gate)

        def body(t0, c):
            v = valid[pl.ds(t0, RF)]
            for h in HV:
                u = get(t0, h)
                store(t0, h, (u + u * jnp.tanh(u)) * v)
            return c
        steps_loop(RF, body)

    def slope_of(u):
        t = jnp.tanh(u)
        return (0.5 * t + 0.5) * (1.0 + u - u * t)

    def tail_slope(b, gate):
        get = tail_half(b, gate)

        def body(t0, c):
            v = valid[pl.ds(t0, RF)]
            for h in HV:
                pre[b, h, pl.ds(t0, RF)] = slope_of(get(t0, h)) * v
            return c
        steps_loop(RF, body)

    def forward_aside(b, r, extras):
        if plan.fused:
            step = b * SUB + r

            @pl.when(step == 0)
            def _():
                gather_core(0, True)
                gather_wait(0)
                unpack_values()

            @pl.when(jnp.logical_and(step >= 1, step < PER))
            def _():
                gather_core(1 + step, False)
                gather_wait(1 + step)
                unpack_pair(step)

        @pl.when(r == SUB - 2)
        def _():
            residual_forward(b)

        @pl.when(r == SUB - 1)
        def _():
            utterance_sums(b)
        for when, extra in extras:
            pl.when(r == when)(extra)

    def forward_block(b, extras=()):
        def layer(r, pieces, before=None):
            index = b * PER + r
            first = before is not None
            layer_conv(index, pieces, (lambda: gather_core(1, True)) if first else None)
            if first:
                before()
            exchange(index, index, pointwise(index))
            forward_aside(b, r, extras)
            merge_stats(index, index)
            if plan.fused:
                step = b * SUB + r

                @pl.when(step < PER - 2)
                def _():
                    gather_z(3 + step)

                @pl.when(step < PER - 1)
                def _():
                    gather_plane(2 + step)

        def first_matrices():
            gather_wait(1)
            unpack_pair(0)
        layer(0, block_pieces(b), first_matrices if plan.fused and b == 0 else None)
        activate(b * PER, hid_of(b, 1))

        def rest(r, c):
            layer(r, [(hid_of(b, r), regular_taps(b))])

            @pl.when(r < SUB - 1)
            def _():
                activate(b * PER + r, hid_of(b, r + 1))
            return c
        lax.fori_loop(1, SUB, rest, 0)
        merge_stats(b * PER + SUB, b * PER + SUB)
        return excite(b)

    back_slot = 2 * PER

    def sum_rows(parts):
        return jnp.concatenate([jnp.sum(part, axis=0, keepdims=True) for part in parts], axis=0)

    def tail_back(b, kept, load):
        means, inner, excited, gate = kept
        last = b * PER + SUB - 1
        mean = [stat_row(last, 0, h) for h in HV]

        def first(t0, c):
            a = first_mask[pl.ds(t0, RF)]
            res = []
            for h in HV:
                gs = load(t0, h)
                pre[b, h, pl.ds(t0, RF)] = gs
                gx = gs * (prods[last, h, pl.ds(t0, RF)] - mean[h])
                res += [c[4 * h] + accumulate(gs * a), c[4 * h + 1] + accumulate(gs),
                        c[4 * h + 2] + accumulate(gx * a), c[4 * h + 3] + accumulate(gx)]
            return tuple(res)
        tot = steps_loop(RF, first, tuple(jnp.zeros((8, LANES), F32) for _ in range(4 * plan.halves)))
        s0, s_all, x0, x_all = [join([tot[4 * h + i] for h in HV]) for i in range(4)]
        gs_sum = (s0, s_all - s0)
        gx_sum = (x0, x_all - x0)
        mean_row, inv_row, scale_row = [whole_row(last, kind) for kind in range(3)]
        shift_row = jnp.concatenate([shifts[last, h:h + 1] for h in HV], axis=1)
        grad_gate = jnp.concatenate([scale_row * gx_sum[u] + shift_row * gs_sum[u] for u in range(2)], axis=0)
        grad_up = grad_gate * gate * (1.0 - gate)
        sg = sigmoid(inner)
        grad_inner = thin(grad_up, expand[b], 1) * (sg * (1.0 + inner * (1.0 - sg)))
        grad_means = thin(grad_inner, squeeze_t[b], 0)
        per_slot = [grad_means[u:u + 1] / half_count[u] for u in range(2)]
        sum1, sum2 = 0.0, 0.0
        for u in range(2):
            g = gate[u:u + 1]
            sum1 = sum1 + g * gs_sum[u] + grad_means[u:u + 1]
            sum2 = sum2 + g * gx_sum[u] + per_slot[u] * (k.psum[b, u:u + 1] - half_count[u] * mean_row)
        sum2 = sum2 * inv_row
        exchange(back_slot + last, back_place(last),
                 jnp.concatenate([half_lanes(v, h) for v in (sum1, sum2) for h in HV], axis=0))
        return grad_up, grad_inner, per_slot

    def tail_back_aside(b, kept, found):
        means, inner, excited, gate = kept
        grad_up, grad_inner, per_slot = found
        res = b * PER + SUB
        gates = [[row(half_lanes(gate[u:u + 1], h)) for h in HV] for u in range(2)]
        slots = [[row(half_lanes(per_slot[u], h)) for h in HV] for u in range(2)]
        norm = [(stat_row(res, 0, h), stats[res, pl.ds(2 + h, 1)]) for h in HV]

        def second(t0, c):
            a = first_mask[pl.ds(t0, RF)] > 0.5
            v = valid[pl.ds(t0, RF)]
            out_c = []
            for h in HV:
                gs = pre[b, h, pl.ds(t0, RF)]
                gz[h, pl.ds(t0, RF)] = (gs * jnp.where(a, gates[0][h], gates[1][h])
                                        + jnp.where(a, slots[0][h], slots[1][h]) * v)
                x = prods[res, h, pl.ds(t0, RF)] - norm[h][0]
                out_c += [c[2 * h] + accumulate(gs), c[2 * h + 1] + accumulate(gs * x)]
            return tuple(out_c)
        tot = steps_loop(RF, second, tuple(jnp.zeros((8, LANES), F32) for _ in range(2 * plan.halves)))
        sums = [jnp.sum(part, axis=0, keepdims=True) for part in tot]
        exchange(back_slot + res, back_place(res), jnp.concatenate(
            [sums[2 * h] for h in HV] + [sums[2 * h + 1] * norm[h][1] for h in HV], axis=0))
        k.expand_grad[b] = small(eight(excited), eight(grad_up), ((0,), (0,)))
        k.squeeze_grad[b] = small(eight(grad_inner), eight(means), ((0,), (0,)))

    def norm_back(index, load, target, store, then=None):
        sums = jnp.sum(received(back_slot + index, back_place(index)), axis=0)
        if then is not None:
            then()
        k.shifts_grad[index] = sums[0:2]
        k.gains_grad[index] = sums[2:4]
        total = jnp.sum(counts[...], axis=0)[0:2]
        st = stats[index]
        mean, inv, scale = st[0:2], st[2:4], st[4:6]
        k1 = scale * sums[0:2] / total
        k2 = scale * sums[2:4] / total * inv
        rows3 = [[row(value[h:h + 1]) for value in (mean, scale, k1, k2)] for h in HV]
        for t0 in range(0, Q, R):
            v = valid[t0:t0 + R]
            parts = []
            for h in HV:
                mean_h, scale_h, k1_h, k2_h = rows3[h]
                grad = scale_h * load(t0, h) - (k1_h + k2_h * (prods[index, h, t0:t0 + R] - mean_h)) * v
                parts.append(grad.reshape(8 * R, LANES).astype(BF16))
            both = jnp.concatenate(parts, axis=1)
            target[8 * t0:8 * (t0 + R)] = both
            if plan.fused:
                res = jnp.dot(both, k.point_t[index], preferred_element_type=F32)
            else:
                res = lax.dot_general(both, point[index], (((1,), (1,)), ((), ())), preferred_element_type=F32)
            for h in HV:
                store(t0, h, half_lanes(res, h).reshape(R, 8, LANES))

    def point_back(index, source):
        place = lax.rem(index, 2) if plan.fused else index
        k.point_grad[place] = lax.dot_general(acts[index], source[...], (((0,), (0,)), ((), ())),
                                              preferred_element_type=F32)

    def store_gd(t0, h, values):
        gd[h, HALO + t0:HALO + t0 + R] = values

    def store_skip(t0, h, values):
        k.skip[h, t0:t0 + R] = values

    def conv_back_block(t0, h, index, taps):
        low, high = -taps[-1][1], -taps[0][1]
        win = gd[h, pl.ds(t0 + HALO + low, R + high - low)]
        if len(taps) >= plan.taps[0]:
            return paired(win, index, h, len(taps), True)
        return direct(win, low, index, h, [(t, -shift) for t, shift in taps])

    def kernel_back(index, pieces):
        for source, taps in pieces:
            for h in HV:
                low = min(s for _, s in taps)
                high = max(s for _, s in taps)

                def body(t0, c):
                    g = gd[h, pl.ds(HALO + t0, RF)]
                    win = hid[source, h, pl.ds(t0 + HALO + low, RF + high - low)]
                    return tuple(acc + accumulate(g * win[s - low:s - low + RF]) for acc, (_, s) in zip(c, taps))
                accs = steps_loop(RF, body, tuple(jnp.zeros((8, LANES), F32) for _ in taps))
                for acc, (tap, _) in zip(accs, taps):
                    k.dw_grad[index, h, pl.ds(tap, 1)] = jnp.sum(acc, axis=0, keepdims=True)

    def slopes(index):
        scales = [0.5 * stat_row(index, 2, h) for h in HV]
        offsets = [0.5 * stat_row(index, 3, h) for h in HV]

        def body(t0, c):
            v = valid[pl.ds(t0, RF)]
            for h in HV:
                k.slope[h, pl.ds(t0, RF)] = slope_of(prods[index, h, pl.ds(t0, RF)] * scales[h] + offsets[h]) * v
            return c
        steps_loop(RF, body)

    def hidden_back(index, taps):
        before = index - 1
        mean = [stat_row(before, 0, h) for h in HV]

        def body(t0, c):
            res = []
            for h in HV:
                grad = conv_back_block(t0, h, index, taps) * k.slope[h, pl.ds(t0, R)]
                gz[h, pl.ds(t0, R)] = grad
                gx = grad * (prods[before, h, pl.ds(t0, R)] - mean[h])
                res += [c[2 * h] + accumulate(grad), c[2 * h + 1] + accumulate(gx)]
            return tuple(res)
        tot = steps_loop(R, body, tuple(jnp.zeros((8, LANES), F32) for _ in range(2 * plan.halves)))
        sums = [jnp.sum(part, axis=0, keepdims=True) for part in tot]
        exchange(back_slot + before, back_place(before), jnp.concatenate(
            [sums[2 * h] for h in HV] + [sums[2 * h + 1] * stats[before, pl.ds(2 + h, 1)] for h in HV], axis=0))

    def load_gz(t0, h):
        return gz[h, t0:t0 + R]

    def scatter_start(unit, place):
        remote(k.shares.at[place, :, :, 1 - core], k.inbox.at[unit], 6, unit, partner)

    def scatter_sum(unit, place):
        blocks_wait(chips, 7, unit)
        blocks_wait(chips, 6, unit)
        slot = lax.rem(unit, 3)
        k.sums[slot] = (k.shares[place, :, :, core].astype(F32) + k.inbox[unit].astype(F32)).astype(BF16)

    def scatter_send(unit):
        slot = lax.rem(unit, 3)
        k.gained[unit, chip] = k.sums[slot, depth, plane]
        for peer in same_core:
            remote(k.sums.at[slot, peer // 8, lax.rem(peer // 2, 4)], k.gained.at[unit, chip], 8, unit, peer)

    def scatter_finish(unit):
        blocks_wait(chips - 1, 9, unit)
        return jnp.sum(k.gained[unit].astype(F32), axis=0)

    def scatter_plane(unit):
        slot = lax.rem(unit, 3)
        k.by_plane[unit, plane] = k.sums[slot, :, plane]
        for d in (3, 2, 1):
            there = lax.rem(plane + d, 4)
            remote(k.sums.at[slot, :, there], k.by_plane.at[unit, plane], 8, unit, in_plane(d))

    def scatter_mid(unit):
        blocks_wait(12, 9, unit)
        blocks_wait(12, 8, unit)
        k.line[unit] = jnp.sum(k.by_plane[unit].astype(F32), axis=0).astype(BF16)
        k.by_depth[unit, depth] = k.line[unit, depth]

    def scatter_z(unit):
        for d in (2, 1, 3):
            there = lax.rem(depth + d, 4)
            remote(k.line.at[unit, there], k.by_depth.at[unit, depth], 10, unit, at_depth(d))

    def scatter_end(unit):
        blocks_wait(3, 11, unit)
        return jnp.sum(k.by_depth[unit].astype(F32), axis=0)

    def pair_start(pair):
        both = [k.point_grad[side].reshape(N, 8, plan.channels) for side in range(2)]
        k.shares[0] = jnp.concatenate(both, axis=1).astype(BF16).reshape(4, 4, 2, 16, plan.channels)
        scatter_start(1 + pair, 0)

    def pair_finish(pair, straight=False):
        total = scatter_finish(1 + pair) if straight else scatter_end(1 + pair)
        b = pair // (PER // 2)
        r = 2 * lax.rem(pair, PER // 2)
        k.point_out[b, r] = total[0:8]
        k.point_out[b, r + 1] = total[8:16]

    def last_start():
        k.packed[0:LANES] = jnp.zeros((LANES, LANES), F32)
        columns = []
        for h in HV:
            k.packed[0:plan.tap_rows] = k.dw_grad[0, h]
            columns.append(jnp.transpose(k.packed[0:LANES]))
        k.last_mine[...] = jnp.concatenate(columns, axis=0).reshape(N, 8, LANES)
        k.last[me] = k.last_mine[me]
        for peer in peers:
            pltpu.make_async_remote_copy(src_ref=k.last_mine.at[peer], dst_ref=k.last.at[me],
                                         send_sem=k.last_sems.at[0], recv_sem=k.last_sems.at[1],
                                         device_id=(peer,), device_id_type=MESH).start()

    def last_finish():
        wait_all(k.last, k.last_sems.at[1])
        k.dw_first_out[0] = jnp.sum(k.last[...], axis=0)[:, 0:plan.taps[0]]

    def values_start():
        k.packed[...] = jnp.zeros((plan.values, LANES), F32)
        blocks = []
        for b in range(2):
            columns = []
            for h in HV:
                for r in range(1 - b, SUB):
                    k.packed[plan.tap_row(r):plan.tap_row(r) + plan.tap_rows] = k.dw_grad[b * PER + r, h]
                lanes = slice(h * LANES, (h + 1) * LANES)
                k.packed[EXPAND_ROW:EXPAND_ROW + plan.hidden] = k.expand_grad[b, :, lanes]
                k.packed[SQUEEZE_ROW:SQUEEZE_ROW + plan.hidden] = k.squeeze_grad[b, :, lanes]
                columns.append(jnp.concatenate(
                    [jnp.transpose(k.packed[t * LANES:(t + 1) * LANES]) for t in range(2)], axis=1))
            blocks.append(jnp.concatenate(columns, axis=0).reshape(N, 8, plan.values))
        k.shares[1] = jnp.concatenate(blocks, axis=1).astype(BF16).reshape(4, 4, 2, 16, plan.values)
        scatter_start(0, 1)

    def values_finish():
        total = scatter_finish(0)
        for b in range(2):
            rows = total[8 * b:8 * b + 8]

            def lanes(start, size):
                tile, lane = divmod(start, LANES)
                part = rows[:, tile * LANES:(tile + 1) * LANES]
                return (pltpu.roll(part, LANES - lane, 1) if lane else part)[:, 0:size]
            dw_out = (k.dw_first_out, k.dw_second_out)[b]
            for r in range(1 - b, SUB):
                dw_out[r] = lanes(plan.tap_row(r), plan.taps[b])
            k.squeeze_out[b] = lanes(SQUEEZE_ROW, plan.hidden)
            k.expand_out[b] = lanes(EXPAND_ROW, plan.hidden)

    def own_norms():
        mine = pl.ds(pl.multiple_of(me * 8, 8), 8)
        k.packed[0:LANES] = jnp.zeros((LANES, LANES), F32)
        for h in HV:
            for b in range(2):
                for r in range(PER):
                    k.packed[16 * b + r:16 * b + r + 1] = k.gains_grad[b * PER + r, h:h + 1]
                    k.packed[16 * b + 8 + r:16 * b + 9 + r] = k.shifts_grad[b * PER + r, h:h + 1]
            k.own_norm[h * LANES:(h + 1) * LANES] = jnp.transpose(k.packed[0:LANES])
        k.packed[0:LANES] = jnp.transpose(
            jnp.concatenate([k.own_norm[mine], jnp.zeros((LANES - 8, LANES), F32)], axis=0))
        for b in range(2):
            for r in range(PER):
                k.gains_out[r, b:b + 1] = k.packed[16 * b + r:16 * b + r + 1, 0:8]
                k.shifts_out[r, b:b + 1] = k.packed[16 * b + 8 + r:16 * b + 9 + r, 0:8]

    HALF = PER // 2

    def backward_aside(b, r):
        index = b * PER + r
        if plan.fused:
            if b == 0:
                @pl.when(r == SUB - 1)
                def _():
                    scatter_sum(1 + HALF, 0)

            @pl.when(lax.rem(r, 2) == 1)
            def _():
                scatter_sum(1 + HALF * b + (r + 1) // 2, 0)
        point_back(index, gpb)

        @pl.when(r == SUB - 1)
        def _():
            res = b * PER + SUB
            norm_back(res, lambda t0, h: pre[b, h, t0:t0 + R], gqb, store_skip)
            point_back(res, gqb)
        if plan.fused:
            @pl.when(lax.rem(r, 2) == 0)
            def _():
                pair_start(HALF * b + r // 2)

    def backward_late(b, r):
        if not plan.fused:
            return
        if b == 0:
            @pl.when(r == SUB - 1)
            def _():
                pair_finish(HALF + 1)

            @pl.when(r == SUB - 2)
            def _():
                scatter_mid(1 + HALF)

            @pl.when(r == SUB - 3)
            def _():
                pair_finish(HALF)

        @pl.when(jnp.logical_or(r == 2, r == 0))
        def _():
            scatter_mid(1 + HALF * b + r // 2 + 1)

        @pl.when(r == 1)
        def _():
            pair_finish(HALF * b + 2)

    def backward_block(b):
        def go(r):
            if plan.fused:
                @pl.when(jnp.logical_or(r == 2, r == 0))
                def _():
                    scatter_plane(1 + HALF * b + r // 2 + 1)

                @pl.when(r == 1)
                def _():
                    scatter_z(1 + HALF * b + 2)
                if b == 0:
                    @pl.when(r == SUB - 1)
                    def _():
                        scatter_z(1 + HALF + 1)

                    @pl.when(r == SUB - 2)
                    def _():
                        scatter_plane(1 + HALF)

                    @pl.when(r == SUB - 3)
                    def _():
                        scatter_z(1 + HALF)

        def filtered(r):
            norm_back(b * PER + r, load_gz, gpb, store_gd, lambda: go(r))
            for h in HV:
                set_halo(gd, h)

        def step(j, c):
            r = SUB - 1 - j
            index = b * PER + r
            filtered(r)
            hidden_back(index, regular_taps(b))
            backward_aside(b, r)
            kernel_back(index, [(hid_of(b, r), regular_taps(b))])

            @pl.when(r >= 2)
            def _():
                slopes(index - 2)
            backward_late(b, r)
            return c
        lax.fori_loop(0, SUB - 1, step, 0)
        if plan.fused and b == 0:
            values_start()
        filtered(0)

    if plan.fused:
        wait_all(k.first, count_sems.at[1])
        unpack_first()
    else:
        wait_all(counts, count_sems.at[1])
        dw[...] = k.dw_in[...]
        for b in range(2):
            for r in range(SUB):
                for h in HV:
                    split_taps(b, r, h)
    kept_first = forward_block(0)

    def store_middle(t0, h, values):
        hid[hid_of(1, 0), h, pl.ds(HALO + t0, RF)] = values
    tail(0, kept_first[3], store_middle)
    for h in HV:
        set_halo(hid.at[hid_of(1, 0)], h)

    def place_cot():
        load_cot.wait()
        for h in HV:
            flat[h, 0:GAP] = jnp.zeros((GAP, LANES), F32)
            flat[h, GAP + plan.slots:] = jnp.zeros((flat.shape[1] - GAP - plan.slots, LANES), F32)

        def place(i, c):
            rows = pl.ds(pl.multiple_of(i * 128, 128), 128)
            for h in HV:
                flat[h, pl.ds(pl.multiple_of(i * 128 + GAP, 16), 128)] = k.cot_v[rows, h * LANES:(h + 1) * LANES]
            return c
        lax.fori_loop(0, plan.slots // 128, place, 0)

        def pick(t0, c):
            for h in HV:
                for j in range(RF):
                    here = flat[h, pl.ds(t0 + j + GAP, 8, stride=Q)]
                    moved = flat[h, pl.ds(t0 + j, 8, stride=Q)]
                    gz[h, t0 + j] = jnp.where(first_mask[t0 + j] > 0.5, here, moved)
            return c
        steps_loop(RF, pick)
    kept_second = forward_block(1, ((0, lambda: tail_slope(0, kept_first[3])), (1, place_cot)))

    last_half = tail_half(1, kept_second[3])

    def load_last(t0, h):
        return gz[h, pl.ds(t0, RF)] * (slope_of(last_half(t0, h)) * valid[pl.ds(t0, RF)])
    found = tail_back(1, kept_second, load_last)

    def store_out(t0, h, values):
        for j in range(RF):
            flat[h, pl.ds(t0 + j, 8, stride=Q)] = values[j]

    def ungap(i, c):
        rows = pl.ds(pl.multiple_of(i * 128, 128), 128)
        slot = i * 128 + lax.broadcasted_iota(jnp.int32, (128, LANES), 0)
        for h in HV:
            moved = flat[h, pl.ds(pl.multiple_of(i * 128 + GAP, 16), 128)]
            k.cot_v[rows, h * LANES:(h + 1) * LANES] = jnp.where(slot < half0, flat[h, rows], moved)
        return c
    tail_back_aside(1, kept_second, found)
    slopes(PER + SUB - 2)
    tail(1, kept_second[3], store_out)
    lax.fori_loop(0, plan.slots // 128, ungap, 0)
    save_out.start()
    backward_block(1)

    def sum_back(t0, c):
        for h in HV:
            gz[h, pl.ds(t0, R)] = conv_back_block(t0, h, PER, regular_taps(1)) + k.skip[h, pl.ds(t0, R)]
        return c
    steps_loop(R, sum_back)
    found = tail_back(0, kept_first, lambda t0, h: gz[h, pl.ds(t0, RF)] * pre[0, h, pl.ds(t0, RF)])
    tail_back_aside(0, kept_first, found)
    slopes(SUB - 2)
    backward_aside(1, 0)
    kernel_back(PER, [(hid_of(1, 0), regular_taps(1))])
    backward_late(1, 0)
    backward_block(0)
    pieces = block_pieces(0)
    backward_aside(0, 0)
    if plan.fused:
        scatter_sum(0, 1)
        scatter_send(0)
    kernel_back(0, pieces)
    if plan.fused:
        last_start()
        scatter_sum(1, 0)
        scatter_send(1)
        backward_late(0, 0)
        scatter_z(2)
        own_norms()

    def spread(t0, c):
        v = valid[pl.ds(t0, R)]
        for h in HV:
            even = (conv_back_block(t0, h, 0, pieces[0][1]) + k.skip[h, pl.ds(t0, R)]) * v
            odd = conv_back_block(t0, h, 0, pieces[1][1]) * v
            for j in range(R):
                wide[h, pl.ds(2 * (t0 + j), 8, stride=2 * Q)] = even[j]
                wide[h, pl.ds(2 * (t0 + j) + 1, 8, stride=2 * Q)] = odd[j]
        return c
    steps_loop(R, spread)

    def ungap_wide(i, c):
        rows = pl.ds(pl.multiple_of(i * 128, 128), 128)
        slot = i * 128 + lax.broadcasted_iota(jnp.int32, (128, LANES), 0)
        for h in HV:
            moved = wide[h, pl.ds(pl.multiple_of(i * 128 + 2 * GAP, 32), 128)]
            k.frames_grad_v[rows, h * LANES:(h + 1) * LANES] = jnp.where(slot < len0, wide[h, rows], moved)
        return c
    save_frames = []
    pieces_out = 4
    for piece in range(pieces_out):
        size = 2 * plan.slots // pieces_out
        lax.fori_loop(piece * size // 128, (piece + 1) * size // 128, ungap_wide, 0)
        rows = pl.ds(piece * size, size)
        save_frames.append(pltpu.make_async_copy(k.frames_grad_v.at[rows], k.frames_grad.at[rows],
                                                 k.io_sems.at[3 + piece]))
        save_frames[-1].start()
    if plan.fused:
        pair_finish(1)
        values_finish()
        pair_finish(0, True)
        last_finish()

    save_out.wait()
    for copy in save_frames:
        copy.wait()
    wait_all(k.first if plan.fused else counts, count_sems.at[0])

    def drain(slot, c):
        wait_all(recv4.at[0], send_sem.at[slot])
        return c
    lax.fori_loop(0, send4.shape[0], drain, 0)
    if plan.fused:
        for unit in range(1 + PER):
            blocks_wait(chips - 1 if unit < 2 else 3, 0, unit)
            if unit >= 2:
                blocks_wait(12, 2, unit)
                blocks_wait(3, 10, unit)
            else:
                blocks_wait(chips - 1, 8, unit)
            blocks_wait(chips, 4, unit)
        wait_all(k.last, k.last_sems.at[0])


def call_kernel(plan, inputs):
    layers, halves, Q, channels = plan.layers, plan.halves, plan.steps, plan.channels
    vals, shard, hidden, devices = plan.values, plan.shard, plan.hidden, plan.devices
    vmem = pl.BlockSpec(memory_space=pltpu.VMEM)
    anywhere = pl.BlockSpec(memory_space=pl.ANY)
    places = {"lens": pl.BlockSpec(memory_space=pltpu.SMEM), "frames": anywhere, "cot": anywhere,
              "out": anywhere, "frames_grad": anywhere}
    slots = 2 * layers

    def shape(*dims, dtype=F32):
        return jax.ShapeDtypeStruct(dims, dtype)
    outs = {
        "out": shape(plan.slots, channels),
        "frames_grad": shape(2 * plan.slots, channels),
    }
    params = {
        "dw": shape(layers, halves, plan.dw_rows, LANES),
        "point": shape(layers, channels, channels, dtype=BF16),
        "gains": shape(layers, halves, LANES),
        "shifts": shape(layers, halves, LANES),
        "squeeze_t": shape(2, hidden, channels),
        "expand": shape(2, hidden, channels),
    }
    grads = {
        "dw_grad": shape(layers, halves, plan.tap_rows, LANES),
        "point_grad": shape(2 if plan.fused else layers, channels, channels),
        "gains_grad": shape(layers, halves, LANES),
        "shifts_grad": shape(layers, halves, LANES),
        "squeeze_grad": shape(2, hidden, channels),
        "expand_grad": shape(2, hidden, channels),
    }
    scratch = {
        "hid": shape(2 * plan.sub + 1, halves, plan.pad, 8, LANES),
        "acts": shape(layers, plan.rows, channels, dtype=BF16),
        "prods": shape(layers, halves, Q, 8, LANES),
        "gd": shape(halves, plan.pad, 8, LANES),
        "gz": shape(halves, Q, 8, LANES),
        "gpb": shape(plan.rows, channels, dtype=BF16),
        "gqb": shape(plan.rows, channels, dtype=BF16),
        "pre": shape(2, halves, Q, 8, LANES),
        "wide": shape(halves, 2 * plan.slots + 4 * GAP, LANES),
        "frames_v": shape(2 * plan.slots, channels, dtype=BF16),
        "cot_v": shape(plan.slots, channels),
        "frames_grad_v": shape(2 * plan.slots, channels),
        "first_mask": shape(Q, 8, LANES),
        "valid": shape(Q, 8, LANES),
        "slope": shape(halves, Q, 8, LANES),
        "skip": shape(halves, Q, 8, LANES),
        "psum": shape(2, 8, channels),
        "stats": shape(layers, 8, LANES),
        "send4": shape(slots, 4, LANES),
        "recv4": shape(layers, devices, 4, LANES),
        "counts": shape(devices, 4, LANES),
        "csend": shape(4, LANES),
    }
    sems = {"send_sem": (slots,), "recv_sem": (slots,), "count_sems": (2,), "io_sems": (7,)}
    if plan.fused:
        units, chips = 1 + plan.per, devices // 2
        outs.update({
            "dw_first_out": shape(plan.sub, shard, plan.taps[0]),
            "dw_second_out": shape(plan.sub, shard, plan.taps[1]),
            "point_out": shape(2, plan.per, shard, channels),
            "gains_out": shape(plan.per, 2, shard),
            "shifts_out": shape(plan.per, 2, shard),
            "squeeze_out": shape(2, shard, hidden),
            "expand_out": shape(2, shard, hidden),
        })
        scratch.update(params)
        scratch.update(grads)
        scratch.update({
            "tile": shape(8, LANES),
            "point_t": shape(layers, channels, channels, dtype=BF16),
            "packed": shape(vals, LANES),
            "packed_t": shape(16, vals),
            "first": shape(devices, 8, LANES),
            "last_mine": shape(devices, 8, LANES),
            "last": shape(devices, 8, LANES),
            "unpacked": shape(vals, LANES),
            "gath": shape(units, 4, 4, 2, 16, channels, dtype=BF16),
            "shares": shape(2, 4, 4, 2, 16, channels, dtype=BF16),
            "inbox": shape(units, 4, 4, 16, channels, dtype=BF16),
            "sums": shape(3, 4, 4, 16, channels, dtype=BF16),
            "gained": shape(2, chips, 16, channels, dtype=BF16),
            "by_plane": shape(units, 4, 4, 16, channels, dtype=BF16),
            "line": shape(units, 4, 16, channels, dtype=BF16),
            "by_depth": shape(units, 4, 16, channels, dtype=BF16),
            "own_norm": shape(channels, LANES),
        })
        sems["unit_sems"] = (12, units)
        sems["last_sems"] = (2,)
        sems["param_sems"] = (len(PARAMS),)
        for name in PARAMS:
            scratch[name + "_v"] = inputs[name]
            places[name] = anywhere
    else:
        outs.update(grads)
        scratch["dw"] = params["dw"]
    names = list(inputs) + list(outs) + list(scratch) + list(sems)
    results = pl.pallas_call(
        functools.partial(kernel, plan, names),
        out_shape=list(outs.values()),
        in_specs=[places.get(name, vmem) for name in inputs],
        out_specs=[places.get(name, vmem) for name in outs],
        scratch_shapes=[pltpu.VMEM(v.shape, v.dtype) for v in scratch.values()]
        + [pltpu.SemaphoreType.DMA(v) for v in sems.values()],
        compiler_params=pltpu.CompilerParams(
            collective_id=0, has_side_effects=True, vmem_limit_bytes=63 * 1024 * 1024),
    )(*inputs.values())
    if plan.fused:
        results = hand_on(results)
    return dict(zip(outs, results, strict=True))


def hand_on(arrays):
    n = len(arrays)
    whole = 1024
    parts = [(i, start, min(whole, v.shape[0] - start)) for i, v in enumerate(arrays)
             for start in range(0, v.shape[0], whole)]

    def move(*refs):
        here, there, held, sems = refs[:n], refs[n:2 * n], refs[2 * n:3 * n], refs[3 * n]
        into, out = [], []
        for p, (i, start, size) in enumerate(parts):
            rows = pl.ds(start, size)
            into.append(pltpu.make_async_copy(here[i].at[rows], held[i].at[rows], sems.at[0, p]))
            out.append(pltpu.make_async_copy(held[i].at[rows], there[i].at[rows], sems.at[1, p]))
        for copy in into:
            copy.start()
        for p in range(len(parts)):
            into[p].wait()
            out[p].start()
        for copy in out:
            copy.wait()
    anywhere = pl.BlockSpec(memory_space=pl.ANY)
    return pl.pallas_call(
        move,
        out_shape=[jax.ShapeDtypeStruct(v.shape, v.dtype) for v in arrays],
        in_specs=[anywhere] * n,
        out_specs=[anywhere] * n,
        scratch_shapes=[pltpu.VMEM(v.shape, v.dtype) for v in arrays] + [pltpu.SemaphoreType.DMA((2, len(parts)))],
    )(*arrays)


def body(frames, dw_first, dw_second, point, gains, shifts, se_down, se_up, cotangent, lengths, *, devices):
    sub, taps_first, shard = dw_first.shape
    taps_second = dw_second.shape[1]
    hidden = se_down.shape[2]
    channels = point.shape[3]
    plan = Plan(cotangent.shape[0], channels, taps_first, taps_second, sub, hidden, devices)
    if plan.fused:
        res = call_kernel(plan, {
            "lens": lengths, "frames": frames, "cot": cotangent,
            "dw_first": jnp.swapaxes(dw_first, 1, 2), "dw_second": jnp.swapaxes(dw_second, 1, 2),
            "point_in": point, "gains_in": jnp.swapaxes(gains, 0, 1), "shifts_in": jnp.swapaxes(shifts, 0, 1),
            "se_down": se_down, "se_up": jnp.swapaxes(se_up, 1, 2)})
        return (
            res["out"], res["frames_grad"], jnp.swapaxes(res["dw_first_out"], 1, 2),
            jnp.swapaxes(res["dw_second_out"], 1, 2), res["point_out"], jnp.swapaxes(res["gains_out"], 0, 1),
            jnp.swapaxes(res["shifts_out"], 0, 1), res["squeeze_out"], jnp.swapaxes(res["expand_out"], 1, 2))

    per, layers, halves = plan.per, plan.layers, plan.halves

    def gather(v, axis):
        return lax.all_gather(v, "dp", axis=axis, tiled=True)
    small = jnp.concatenate([
        dw_first.reshape(-1, shard), dw_second.reshape(-1, shard), gains.reshape(-1, shard),
        shifts.reshape(-1, shard), se_up.reshape(-1, shard),
        jnp.swapaxes(se_down, 1, 2).reshape(-1, shard)], axis=0)
    small = gather(small, 1).astype(F32)
    sizes = [sub * taps_first, sub * taps_second, layers, layers, 2 * hidden, 2 * hidden]
    part = jnp.split(small, [sum(sizes[:i]) for i in range(1, 6)], axis=0)

    def dw_layout(v, taps):
        v = v.reshape(sub, taps, halves, LANES).transpose(0, 2, 1, 3)
        return jnp.pad(v, ((0, 1), (0, 0), (0, plan.dw_rows - taps), (0, 0)))
    res = call_kernel(plan, {
        "lens": lengths, "frames": frames, "cot": cotangent,
        "dw_in": jnp.concatenate([dw_layout(part[0], taps_first), dw_layout(part[1], taps_second)], axis=0),
        "point": gather(point, 2).reshape(layers, channels, channels),
        "gains": part[2].reshape(layers, halves, LANES),
        "shifts": part[3].reshape(layers, halves, LANES),
        "squeeze_t": part[5].reshape(2, hidden, channels),
        "expand": part[4].reshape(2, hidden, channels)})

    def scatter(v, axis):
        return lax.psum_scatter(v, "dp", scatter_dimension=axis, tiled=True)

    def dw_out(v, taps):
        return v[:sub, :, :taps].transpose(0, 2, 1, 3).reshape(sub * taps, channels)
    grads = res["dw_grad"]
    packed = scatter(jnp.concatenate(
        [dw_out(grads[:per], taps_first), dw_out(grads[per:], taps_second),
         res["squeeze_grad"].reshape(-1, channels), res["expand_grad"].reshape(-1, channels)], axis=0), 1)
    g1, g2, gsq, gex = jnp.split(packed, [sizes[0], sizes[0] + sizes[1], sizes[0] + sizes[1] + sizes[5]], axis=0)

    def norm_out(v):
        return lax.dynamic_slice_in_dim(v.reshape(2, per, channels), lax.axis_index("dp") * shard, shard, 2)
    return (
        res["out"], res["frames_grad"], g1.reshape(sub, taps_first, shard), g2.reshape(sub, taps_second, shard),
        scatter(res["point_grad"].reshape(2, per, channels, channels), 2),
        norm_out(res["gains_grad"]), norm_out(res["shifts_grad"]),
        jnp.swapaxes(gsq.reshape(2, hidden, shard), 1, 2), gex.reshape(2, hidden, shard))


def solution(mesh):
    return jax.shard_map(
        functools.partial(body, devices=mesh.shape["dp"]),
        mesh=mesh,
        in_specs=(
            P("dp", None),
            P(None, None, "dp"),
            P(None, None, "dp"),
            P(None, None, "dp", None),
            P(None, None, "dp"),
            P(None, None, "dp"),
            P(None, "dp", None),
            P(None, None, "dp"),
            P("dp", None),
            P("dp"),
        ),
        out_specs=(
            P("dp", None),
            P("dp", None),
            P(None, None, "dp"),
            P(None, None, "dp"),
            P(None, None, "dp", None),
            P(None, None, "dp"),
            P(None, None, "dp"),
            P(None, "dp", None),
            P(None, None, "dp"),
        ),
        check_vma=False,
    )
```

```python
import functools

import jax
import jax.numpy as jnp
from jax import lax
from jax.experimental import pallas as pl
from jax.experimental.pallas import tpu as pltpu
from jax.sharding import PartitionSpec as P

EPSILON = 1e-05
HIGHEST = lax.Precision.HIGHEST
F32 = jnp.float32
BF16 = jnp.bfloat16
MESH = pl.DeviceIdType.MESH

GAP = 32
HALO = 13
LANES = 128


def sigmoid(v):
    return 0.5 * jnp.tanh(0.5 * v) + 0.5


class Plan:
    def __init__(self, slots, channels, taps_first, taps_second, sub_blocks, hidden, devices):
        self.slots = slots
        self.steps = (slots + GAP) // 8
        self.rows = 8 * self.steps
        self.channels = channels
        self.halves = channels // LANES
        self.taps = (taps_first, taps_second)
        self.max_taps = max(self.taps)
        self.sub = sub_blocks
        self.hidden = hidden
        self.devices = devices
        self.block = next(r for r in (44, 12, 4) if self.steps % r == 0)
        self.fine = next(r for r in (22, 12, 4) if self.steps % r == 0)
        self.pad = self.steps + 2 * HALO
        self.per = sub_blocks + 1
        self.layers = 2 * self.per
        self.tap_rows = 32
        self.tap_sets = (32, 104)
        self.dw_rows = 176
        self.values = 2 * LANES
        self.shard = channels // devices
        self.fused = self.shard == 8 and devices == 32 and sub_blocks == 5 and hidden == 32 and self.max_taps <= 32

    def tap_row(self, r):
        return r * self.tap_rows + self.tap_rows * (r // 4)


SQUEEZE_ROW, EXPAND_ROW, GAIN_ROW, SHIFT_ROW = 128, 192, 224, 232


PARAMS = ("dw_first", "dw_second", "point_in", "gains_in", "shifts_in", "se_down", "se_up")


class Refs:
    def __init__(self, names, refs):
        for name, ref in zip(names, refs, strict=True):
            setattr(self, name, ref)


def peers_of(me, n):
    if n != 32:
        return [lax.rem(me + k, n) for k in range(1, n)]
    core = lax.rem(me, 2)
    x = lax.rem(me // 2, 2)
    y = lax.rem(me // 4, 2)
    z = me // 8
    found = []
    for order, other in enumerate((3 - z, lax.rem(z + 2, 4), z + 1 - 2 * lax.rem(z, 2), z)):
        for dy in (1, 0):
            for dx in (1, 0):
                for dc in (0, 1):
                    if order == 3 and dy == 0 and dx == 0 and dc == 0:
                        continue
                    oy = lax.rem(y + dy, 2)
                    ox = lax.rem(x + dx, 2)
                    oc = lax.rem(core + dc, 2)
                    found.append((dy + dx + (3, 2, 1, 0)[order], other * 8 + oy * 4 + ox * 2 + oc))
    found.sort(key=lambda item: -item[0])
    return [item[1] for item in found]


def same_core_peers(me, n):
    if n != 32:
        return [lax.rem(me + 2 * k, n) for k in range(1, n // 2)]
    core = lax.rem(me, 2)
    x = lax.rem(me // 2, 2)
    y = lax.rem(me // 4, 2)
    z = me // 8
    found = []
    for order, other in enumerate((3 - z, lax.rem(z + 2, 4), z + 1 - 2 * lax.rem(z, 2), z)):
        for dy in (1, 0):
            for dx in (1, 0):
                if order == 3 and dy == 0 and dx == 0:
                    continue
                oy = lax.rem(y + dy, 2)
                ox = lax.rem(x + dx, 2)
                found.append((dy + dx + (3, 2, 1, 0)[order], other * 8 + oy * 4 + ox * 2 + core))
    found.sort(key=lambda item: -item[0])
    return [item[1] for item in found]


def kernel(plan, names, *refs):
    k = Refs(names, refs)
    lens, dw, point, gains, shifts = k.lens, k.dw, k.point, k.gains, k.shifts
    squeeze_t, expand = k.squeeze_t, k.expand
    hid, acts, prods, gd, gz, gpb, gqb, pre = k.hid, k.acts, k.prods, k.gd, k.gz, k.gpb, k.gqb, k.pre
    wide, first_mask, valid, stats = k.wide, k.first_mask, k.valid, k.stats
    flat = wide.at[:, pl.ds(0, plan.slots + 2 * GAP)]
    send4, recv4, counts, csend = k.send4, k.recv4, k.counts, k.csend
    send_sem, recv_sem, count_sems = k.send_sem, k.recv_sem, k.count_sems
    N = plan.devices
    Q, R, RF = plan.steps, plan.block, plan.fine
    HV = range(plan.halves)
    SUB = plan.sub
    PER = plan.per
    me = lax.axis_index("dp")
    peers = peers_of(me, N)
    chips = N // 2
    chip, core = me // 2, lax.rem(me, 2)
    partner = me + 1 - 2 * core
    depth, plane = me // 8, lax.rem(me // 2, 4)

    def at_depth(d):
        return lax.rem(depth + d, 4) * 8 + 2 * plane + core

    def in_plane(d):
        return depth * 8 + 2 * lax.rem(plane + d, 4) + core

    same_core = same_core_peers(me, N)

    barrier = pltpu.get_barrier_semaphore()
    for peer in peers:
        pl.semaphore_signal(barrier, inc=1, device_id=(peer,), device_id_type=MESH)

    load_frames = pltpu.make_async_copy(k.frames, k.frames_v, k.io_sems.at[0])
    load_params = []
    if plan.fused:
        for i, name in enumerate(PARAMS):
            load_params.append(pltpu.make_async_copy(getattr(k, name), getattr(k, name + "_v"), k.param_sems.at[i]))
            load_params[-1].start()
    load_cot = pltpu.make_async_copy(k.cot, k.cot_v, k.io_sems.at[1])
    save_out = pltpu.make_async_copy(k.cot_v, k.out, k.io_sems.at[2])
    load_frames.start()
    load_cot.start()
    len0 = lens[0]
    len1 = lens[1]
    half0 = len0 // 2
    half1 = len1 // 2
    count = (half0 + half1).astype(F32)
    inv_count = 1.0 / jnp.full((1, LANES), half0 + half1, jnp.int32).astype(F32)

    def steps_loop(width, body, init=0):
        return lax.fori_loop(0, Q // width, lambda i, c: body(i * width, c), init)

    def mask_body(t0, c):
        step = t0 + lax.broadcasted_iota(jnp.int32, (RF, 8, LANES), 0)
        slot = step + Q * lax.broadcasted_iota(jnp.int32, (RF, 8, LANES), 1)
        a = (slot < half0).astype(F32)
        b = jnp.logical_and(slot >= half0 + GAP, slot < half0 + GAP + half1).astype(F32)
        first_mask[pl.ds(t0, RF)] = a
        valid[pl.ds(t0, RF)] = a + b
        return c

    def set_halo(ref, half):
        sub = lax.broadcasted_iota(jnp.int32, (HALO, 8, LANES), 1)
        low = pltpu.roll(ref[half, pl.ds(Q, HALO)], 1, 1)
        ref[half, pl.ds(0, HALO)] = jnp.where(sub == 0, 0.0, low)
        high = pltpu.roll(ref[half, pl.ds(HALO, HALO)], 7, 1)
        ref[half, pl.ds(HALO + Q, HALO)] = jnp.where(sub == 7, 0.0, high)

    def prepare_slots():
        steps_loop(RF, mask_body)

        top = 2 * GAP + 2 * plan.slots
        for h in HV:
            wide[h, 0:2 * GAP] = jnp.zeros((2 * GAP, LANES), F32)
            wide[h, top:] = jnp.zeros((wide.shape[1] - top, LANES), F32)

        load_frames.wait()

        def widen(i, c):
            rows = pl.ds(pl.multiple_of(i * 128, 128), 128)
            for h in HV:
                values = k.frames_v[rows, h * LANES:(h + 1) * LANES].astype(F32)
                wide[h, pl.ds(pl.multiple_of(i * 128 + 2 * GAP, 32), 128)] = values
            return c

        lax.fori_loop(0, 2 * plan.slots // 128, widen, 0)

        for phase in range(2):
            def deinterleave(t0, c):
                for j in range(RF):
                    a_mask = first_mask[t0 + j]
                    b_mask = valid[t0 + j] - a_mask
                    for h in HV:
                        a = wide[h, pl.ds(2 * (t0 + j) + 2 * GAP + phase, 8, stride=2 * Q)]
                        b = wide[h, pl.ds(2 * (t0 + j) + phase, 8, stride=2 * Q)]
                        hid[phase, h, HALO + t0 + j] = a * a_mask + b * b_mask
                return c
            steps_loop(RF, deinterleave)
            for h in HV:
                set_halo(hid.at[phase], h)

    def spread_lanes(values, lane):
        k.tile[...] = jnp.zeros((8, LANES), F32)
        k.tile[:, 0:values.shape[1]] = values
        return pltpu.roll(k.tile[...], lane, 1) if lane else k.tile[...]

    def load_first():
        taps = spread_lanes(k.dw_first_v[0].astype(F32), 0)
        lane = lax.broadcasted_iota(jnp.int32, (8, LANES), 1)
        taps = jnp.where(lane == plan.tap_rows - 1, count, taps)
        k.first[me] = taps[0:4] + pltpu.roll(taps, plan.tap_rows, 1)[4:8]

    def load_shard():
        for b in range(2):
            source = (k.dw_first_v, k.dw_second_v)[b]
            tiles = [jnp.zeros((8, LANES), F32) for _ in range(2)]
            for r in range(SUB):
                tile, lane = divmod(plan.tap_row(r), LANES)
                tiles[tile] = tiles[tile] + spread_lanes(source[r].astype(F32), lane)
            tiles[1] = tiles[1] + spread_lanes(k.se_up_v[b].astype(F32), EXPAND_ROW - LANES)
            tiles[1] = tiles[1] + spread_lanes(k.se_down_v[b].astype(F32), SQUEEZE_ROW - LANES)
            k.packed[0:LANES] = jnp.zeros((LANES, LANES), F32)
            for r in range(PER):
                k.packed[GAIN_ROW - LANES + r:GAIN_ROW - LANES + r + 1, 0:8] = k.gains_in_v[r, b:b + 1].astype(F32)
                k.packed[SHIFT_ROW - LANES + r:SHIFT_ROW - LANES + r + 1, 0:8] = k.shifts_in_v[r, b:b + 1].astype(F32)
            tiles[1] = tiles[1] + jnp.transpose(k.packed[0:LANES])[0:8]
            for tile in range(2):
                k.packed_t[8 * b:8 * b + 8, tile * LANES:(tile + 1) * LANES] = tiles[tile]
        k.gath[0, depth, plane, core] = k.packed_t[...].astype(BF16)

    def load_pairs(pairs):
        for pair in pairs:
            rows = [k.point_in_v[i // PER, i % PER].astype(F32) for i in (2 * pair, 2 * pair + 1)]
            k.gath[1 + pair, depth, plane, core] = jnp.concatenate(rows, axis=0).astype(BF16)

    def remote(src, dst, sems, unit, to):
        pltpu.make_async_remote_copy(src_ref=src, dst_ref=dst, send_sem=k.unit_sems.at[sems, unit],
                                     recv_sem=k.unit_sems.at[sems + 1, unit], device_id=(to,),
                                     device_id_type=MESH).start()

    def blocks_wait(count, sem, unit):
        view = k.gained.at[0, pl.ds(0, count)]
        pltpu.make_async_copy(view, view, k.unit_sems.at[sem, unit]).wait()

    def gather_send(unit):
        view = k.gath.at[unit, depth, plane, core]
        for peer in same_core:
            remote(view, view, 0, unit, peer)

    def gather_z(unit):
        view = k.gath.at[unit, depth, plane, core]
        for d in (2, 1, 3):
            remote(view, view, 0, unit, at_depth(d))

    def gather_plane(unit):
        blocks_wait(3, 1, unit)
        view = k.gath.at[unit, :, plane, core]
        for d in (3, 2, 1):
            remote(view, view, 2, unit, in_plane(d))

    def gather_core(unit, straight):
        blocks_wait(chips - 1 if straight else 12, 1 if straight else 3, unit)
        view = k.gath.at[unit, :, :, core]
        remote(view, view, 4, unit, partner)

    def gather_wait(unit):
        blocks_wait(chips, 5, unit)

    def split_filter(rows):
        even, odd = rows[0::2], rows[1::2]
        full = odd + [jnp.zeros((1, LANES), F32)] * (len(even) - len(odd))
        return even, odd, [o - e for e, o in zip(even, full)]

    def split_taps(b, r, h):
        taps = plan.taps[b]
        rows = [dw[b * PER + r, h, t:t + 1] for t in range(taps)]
        for base, ordered in zip(plan.tap_sets, (rows, rows[::-1])):
            for i, part in enumerate(split_filter(ordered)):
                for j, piece in enumerate(split_filter(part)):
                    start = base + 24 * i + 8 * j
                    dw[b * PER + r, h, start:start + len(piece)] = jnp.concatenate(piece, axis=0)

    def unpack_first():
        got = k.first[...].reshape(4 * N, LANES)
        lane = lax.broadcasted_iota(jnp.int32, (4 * N, LANES), 1)
        low = jnp.where(lane < plan.tap_rows, got, 0.0).reshape(N, 4, LANES)
        high = jnp.where(lane < plan.tap_rows, pltpu.roll(got, LANES - plan.tap_rows, 1), 0.0).reshape(N, 4, LANES)
        counts[...] = jnp.broadcast_to(low[:, :, plan.tap_rows - 1:plan.tap_rows], counts.shape)
        block = jnp.concatenate([low, high], axis=1).reshape(plan.channels, LANES)
        for h in HV:
            k.unpacked[0:LANES] = jnp.transpose(block[h * LANES:(h + 1) * LANES])
            dw[0, h, 0:plan.tap_rows] = k.unpacked[0:plan.tap_rows]

    def unpack_values(b):
        got = k.gath[0].astype(F32).reshape(N, 16, plan.values)
        block = got[:, 8 * b:8 * b + 8].reshape(plan.channels, plan.values)
        for h in HV:
            for tile in range(2):
                part = block[h * LANES:(h + 1) * LANES, tile * LANES:(tile + 1) * LANES]
                k.unpacked[tile * LANES:(tile + 1) * LANES] = jnp.transpose(part)
            for r in range(SUB):
                dw[b * PER + r, h, 0:plan.tap_rows] = k.unpacked[plan.tap_row(r):plan.tap_row(r) + plan.tap_rows]
                split_taps(b, r, h)
            for r in range(PER):
                gains[b * PER + r, h:h + 1] = k.unpacked[GAIN_ROW + r:GAIN_ROW + r + 1]
                shifts[b * PER + r, h:h + 1] = k.unpacked[SHIFT_ROW + r:SHIFT_ROW + r + 1]
            lanes = slice(h * LANES, (h + 1) * LANES)
            expand[b, :, lanes] = k.unpacked[EXPAND_ROW:EXPAND_ROW + plan.hidden]
            squeeze_t[b, :, lanes] = k.unpacked[SQUEEZE_ROW:SQUEEZE_ROW + plan.hidden]

    def unpack_pair(pair):
        got = k.gath[1 + pair].astype(F32).reshape(N, 16, plan.channels)
        for side in range(2):
            block = got[:, 8 * side:8 * side + 8].reshape(plan.channels, plan.channels)
            point[2 * pair + side] = block.astype(BF16)
            k.point_t[2 * pair + side] = jnp.transpose(block).astype(BF16)

    if plan.fused:
        for copy in load_params:
            copy.wait()
        load_first()

    if not plan.fused:
        csend[...] = jnp.full((4, LANES), count, F32)
    pl.semaphore_wait(barrier, N - 1)

    def send_to_all(src, dst, ssem, rsem):
        for peer in peers:
            pltpu.make_async_remote_copy(src_ref=src, dst_ref=dst, send_sem=ssem, recv_sem=rsem,
                                         device_id=(peer,), device_id_type=MESH).start()

    def wait_all(ref, sem):
        view = ref.at[pl.ds(0, N - 1)]
        pltpu.make_async_copy(view, view, sem).wait()

    if plan.fused:
        send_to_all(k.first.at[me], k.first.at[me], count_sems.at[0], count_sems.at[1])
        load_pairs(range(1))
        gather_send(1)
        load_shard()
        gather_send(0)
        load_pairs(range(1, PER))
        gather_z(2)
    else:
        send_to_all(csend, counts.at[me], count_sems.at[0], count_sems.at[1])
        counts[me] = csend[...]
    prepare_slots()

    def exchange(slot, place, rows):
        send4[slot] = rows
        recv4[place, me] = rows
        send_to_all(send4.at[slot], recv4.at[place, me], send_sem.at[slot], recv_sem.at[slot])

    def received(slot, place):
        wait_all(recv4.at[place], recv_sem.at[slot])
        return recv4[place]

    def back_place(index):
        return lax.rem(index + PER, 2 * PER)

    def row(values):
        return values.reshape(1, 1, LANES)

    def accumulate(rows3):
        return jnp.sum(rows3, axis=0)

    def count_slots():
        inv_total = 1.0 / jnp.sum(counts[...], axis=0)
        k.norm_count[...] = inv_total
        counts[...] = counts[...] * inv_total

    def shares():
        return counts[...]

    def merge_stats(slot, index):
        got = received(slot, slot)
        weight = shares()
        mean = jnp.sum(weight * got, axis=0)
        mean4 = jnp.concatenate([mean[0:2], mean[0:2]], axis=0)
        diff = got - mean4
        between = jnp.sum(weight * diff * diff, axis=0)
        within = jnp.sum(got, axis=0)
        var = within[2:4] * k.norm_count[0:2] + between[0:2]
        inv = lax.rsqrt(var + EPSILON)
        scale = inv * gains[index]
        offset = shifts[index] - mean[0:2] * scale
        stats[index] = jnp.concatenate([mean[0:2], inv, scale, offset], axis=0)

    def stat_row(index, kind, h):
        return row(stats[index, pl.ds(2 * kind + h, 1)])

    def tap(index, h, t):
        return dw[index, h, pl.ds(t, 1)].reshape(1, 1, LANES)

    def direct(win, low, index, h, taps):
        acc = None
        for t, shift in taps:
            term = win[shift - low:shift - low + R] * tap(index, h, t)
            acc = term if acc is None else acc + term
        return acc

    def paired(x, count, steps, levels, run, base):
        if levels == 0:
            return run(x, count, steps, base)
        low, high = (count + 1) // 2, count // 2
        m = steps // 2
        if x.shape[0] % 2:
            x = jnp.concatenate([x, x[-1:]], axis=0)
        split = x.reshape(-1, 2, 8, LANES)
        x0, x1 = split[:, 0], split[:, 1]
        gap = 24 if levels == 2 else 8

        def part(values, n, i):
            return paired(values, n, m, levels - 1, run, base + gap * i)
        shared = part(x1[:m + low - 1], low, 2)
        first = part(x0[:m + low - 1] + x1[:m + low - 1], low, 0) + shared
        second = part(x0[1:m + high] + x1[:m + high - 1], high, 1) - shared
        return jnp.stack([first, second], axis=1).reshape(steps, 8, LANES)

    def all_taps(win, index, h, taps, back):
        def run(x, count, steps, base):
            acc = None
            for j in range(count):
                term = x[j:j + steps] * tap(index, h, base + j)
                acc = term if acc is None else acc + term
            return acc
        return paired(win, taps, R, 2, run, plan.tap_sets[1 if back else 0])

    def layer_conv(index, pieces, between=None):
        def body(t0, c):
            for h in HV:
                acc = None
                if len(pieces) == 1:
                    source, taps = pieces[0]
                    low = taps[0][1]
                    acc = all_taps(hid[source, h, pl.ds(t0 + HALO + low, R + len(taps) - 1)], index, h, len(taps), False)
                else:
                    for source, taps in pieces:
                        low, high = taps[0][1], taps[-1][1]
                        part = direct(hid[source, h, pl.ds(t0 + HALO + low, R + high - low)], low, index, h, taps)
                        acc = part if acc is None else acc + part
                rows = pl.ds(pl.multiple_of(8 * t0, 16), 8 * R)
                acts[index, rows, h * LANES:(h + 1) * LANES] = acc.reshape(8 * R, LANES).astype(BF16)
            return c
        if between is None:
            steps_loop(R, body)
        else:
            cut = Q // R - 1
            lax.fori_loop(0, cut, lambda i, c: body(i * R, c), 0)
            between()
            lax.fori_loop(cut, Q // R, lambda i, c: body(i * R, c), 0)

    def half_lanes(values, h):
        return values[:, h * LANES:(h + 1) * LANES]

    def pointwise(index):
        pivot = [None] * plan.halves
        sums = [jnp.zeros((8, LANES), F32) for _ in HV]
        squares = [jnp.zeros((8, LANES), F32) for _ in HV]
        for t0 in range(0, Q, R):
            res = jnp.dot(acts[index, 8 * t0:8 * (t0 + R)], point[index], preferred_element_type=F32)
            v = valid[t0:t0 + R]
            for h in HV:
                p = half_lanes(res, h).reshape(R, 8, LANES)
                prods[index, h, t0:t0 + R] = p
                if t0 == 0:
                    pivot[h] = p[0, 0:1]
                d = p - row(pivot[h])
                dv = d * v
                sums[h] = sums[h] + accumulate(dv)
                squares[h] = squares[h] + accumulate(dv * d)
        n = jnp.full((1, LANES), count, F32)
        shift = [jnp.sum(sums[h], axis=0, keepdims=True) * inv_count for h in HV]
        spread = [jnp.sum(squares[h], axis=0, keepdims=True) - n * shift[h] * shift[h] for h in HV]
        return jnp.concatenate([pivot[h] + shift[h] for h in HV] + spread, axis=0)

    def activate(index, target):
        scales = [0.5 * stat_row(index, 2, h) for h in HV]
        offsets = [0.5 * stat_row(index, 3, h) for h in HV]

        def body(t0, c):
            v = valid[pl.ds(t0, RF)]
            for h in HV:
                u = prods[index, h, pl.ds(t0, RF)] * scales[h] + offsets[h]
                hid[target, h, pl.ds(HALO + t0, RF)] = (u + u * jnp.tanh(u)) * v
            return c
        steps_loop(RF, body)
        for h in HV:
            set_halo(hid.at[target], h)

    def hid_of(b, r):
        return b * SUB + r + 1

    def regular_taps(b):
        margin = (plan.taps[b] - 1) // 2
        return [(t, t - margin) for t in range(plan.taps[b])]

    def block_pieces(b):
        if b == 0:
            taps = regular_taps(0)
            even = [(t, s // 2) for t, s in taps if s % 2 == 0]
            odd = [(t, (s - 1) // 2) for t, s in taps if s % 2 == 1]
            return [(0, even), (1, odd)]
        return [(hid_of(1, 0), regular_taps(1))]

    def residual_forward(b):
        source = 0 if b == 0 else hid_of(1, 0)
        res = b * PER + SUB

        def body(t0, c):
            rows = pl.ds(pl.multiple_of(8 * t0, 16), 8 * R)
            for h in HV:
                values = hid[source, h, pl.ds(HALO + t0, R)].reshape(8 * R, LANES)
                acts[res, rows, h * LANES:(h + 1) * LANES] = values.astype(BF16)
            return c
        steps_loop(R, body)
        exchange(res, res, pointwise(res))

    def small(a, b, dims):
        return lax.dot_general(a, b, (dims, ((), ())), precision=HIGHEST, preferred_element_type=F32)

    def thin(a, matrix, dim):
        hi = a.astype(BF16).astype(F32)
        mid = (a - hi).astype(BF16).astype(F32)
        low = a - hi - mid
        rows = jnp.concatenate([hi, mid, low, jnp.zeros_like(a)], axis=0).astype(BF16)
        res = lax.dot_general(rows, matrix.astype(BF16), (((1,), (dim,)), ((), ())), preferred_element_type=F32)
        return res[0:2] + res[2:4] + res[4:6]

    def eight(values):
        return jnp.concatenate([values, jnp.zeros((6, values.shape[1]), F32)], axis=0)

    def whole_row(index, kind):
        return jnp.concatenate([stats[index, pl.ds(2 * kind + h, 1)] for h in HV], axis=1)

    def join(parts):
        return jnp.concatenate([jnp.sum(part, axis=0, keepdims=True) for part in parts], axis=1)

    half_count = [jnp.full((1, plan.channels), n, jnp.int32).astype(F32) for n in (half0, half1)]

    def utterance_sums(b):
        last = b * PER + SUB - 1

        def sums(t0, c):
            a = first_mask[pl.ds(t0, RF)]
            s = valid[pl.ds(t0, RF)] - a
            res = []
            for h in HV:
                p = prods[last, h, pl.ds(t0, RF)]
                res += [c[2 * h] + accumulate(p * a), c[2 * h + 1] + accumulate(p * s)]
            return tuple(res)
        tot = steps_loop(RF, sums, tuple(jnp.zeros((8, LANES), F32) for _ in range(2 * plan.halves)))
        for u in range(2):
            k.psum[b, u:u + 1] = join([tot[2 * h + u] for h in HV])

    def excite(b):
        last = b * PER + SUB - 1
        scale, offset = whole_row(last, 2), whole_row(last, 3)
        means = jnp.concatenate([scale * (k.psum[b, u:u + 1] / half_count[u]) + offset for u in range(2)], axis=0)
        inner = thin(means, squeeze_t[b], 1)
        excited = inner * sigmoid(inner)
        gate = sigmoid(thin(excited, expand[b], 0))
        return means, inner, excited, gate

    def tail_half(b, gate):
        last, res = b * PER + SUB - 1, b * PER + SUB
        consts = []
        for h in HV:
            g = [half_lanes(gate[u:u + 1], h) for u in range(2)]
            s1, o1, s2, o2 = [0.5 * stats[i, pl.ds(2 * kind + h, 1)] for i, kind in
                              ((last, 2), (last, 3), (res, 2), (res, 3))]
            consts.append([row(v) for v in (s1 * g[0], s1 * g[1], s2, o1 * g[0] + o2, o1 * g[1] + o2)])

        def get(t0, h):
            a0, a1, s2, b0, b1 = consts[h]
            a = first_mask[pl.ds(t0, RF)] > 0.5
            return (prods[last, h, pl.ds(t0, RF)] * jnp.where(a, a0, a1)
                    + prods[res, h, pl.ds(t0, RF)] * s2 + jnp.where(a, b0, b1))
        return get

    def tail(b, gate, store):
        get = tail_half(b, gate)

        def body(t0, c):
            v = valid[pl.ds(t0, RF)]
            for h in HV:
                u = get(t0, h)
                store(t0, h, (u + u * jnp.tanh(u)) * v)
            return c
        steps_loop(RF, body)

    def slope_of(u):
        t = jnp.tanh(u)
        return (0.5 * t + 0.5) * (1.0 + u - u * t)

    def tail_slope(b, gate):
        get = tail_half(b, gate)

        def body(t0, c):
            v = valid[pl.ds(t0, RF)]
            for h in HV:
                pre[b, h, pl.ds(t0, RF)] = slope_of(get(t0, h)) * v
            return c
        steps_loop(RF, body)

    def forward_aside(b, r, extras):
        if plan.fused:
            step = b * SUB + r

            @pl.when(step == 0)
            def _():
                gather_core(0, True)
                gather_wait(0)
                unpack_values(0)

            @pl.when(step == 1)
            def _():
                unpack_values(1)

            @pl.when(jnp.logical_and(step >= 1, step < PER))
            def _():
                gather_core(1 + step, False)
                gather_wait(1 + step)
                unpack_pair(step)

        @pl.when(r == SUB - 2)
        def _():
            residual_forward(b)

        @pl.when(r == SUB - 1)
        def _():
            utterance_sums(b)
        for when, extra in extras:
            pl.when(r == when)(extra)

    def forward_block(b, extras=()):
        def layer(r, pieces, before=None):
            index = b * PER + r
            first = before is not None
            layer_conv(index, pieces, (lambda: gather_core(1, True)) if first else None)
            if first:
                before()
            exchange(index, index, pointwise(index))
            forward_aside(b, r, extras)
            merge_stats(index, index)
            if plan.fused:
                step = b * SUB + r

                @pl.when(step < PER - 2)
                def _():
                    gather_z(3 + step)

                @pl.when(step < PER - 1)
                def _():
                    gather_plane(2 + step)

        def first_matrices():
            gather_wait(1)
            unpack_pair(0)
        layer(0, block_pieces(b), first_matrices if plan.fused and b == 0 else None)
        activate(b * PER, hid_of(b, 1))

        def rest(r, c):
            layer(r, [(hid_of(b, r), regular_taps(b))])

            @pl.when(r < SUB - 1)
            def _():
                activate(b * PER + r, hid_of(b, r + 1))
            return c
        lax.fori_loop(1, SUB, rest, 0)
        merge_stats(b * PER + SUB, b * PER + SUB)
        return excite(b)

    back_slot = 2 * PER

    def sum_rows(parts):
        return jnp.concatenate([jnp.sum(part, axis=0, keepdims=True) for part in parts], axis=0)

    def tail_back(b, kept, load):
        means, inner, excited, gate = kept
        last = b * PER + SUB - 1
        mean = [stat_row(last, 0, h) for h in HV]

        def first(t0, c):
            a = first_mask[pl.ds(t0, RF)]
            res = []
            for h in HV:
                gs = load(t0, h)
                pre[b, h, pl.ds(t0, RF)] = gs
                gx = gs * (prods[last, h, pl.ds(t0, RF)] - mean[h])
                res += [c[4 * h] + accumulate(gs * a), c[4 * h + 1] + accumulate(gs),
                        c[4 * h + 2] + accumulate(gx * a), c[4 * h + 3] + accumulate(gx)]
            return tuple(res)
        tot = steps_loop(RF, first, tuple(jnp.zeros((8, LANES), F32) for _ in range(4 * plan.halves)))
        s0, s_all, x0, x_all = [join([tot[4 * h + i] for h in HV]) for i in range(4)]
        gs_sum = (s0, s_all - s0)
        gx_sum = (x0, x_all - x0)
        mean_row, inv_row, scale_row = [whole_row(last, kind) for kind in range(3)]
        shift_row = jnp.concatenate([shifts[last, h:h + 1] for h in HV], axis=1)
        grad_gate = jnp.concatenate([scale_row * gx_sum[u] + shift_row * gs_sum[u] for u in range(2)], axis=0)
        grad_up = grad_gate * gate * (1.0 - gate)
        sg = sigmoid(inner)
        grad_inner = thin(grad_up, expand[b], 1) * (sg * (1.0 + inner * (1.0 - sg)))
        grad_means = thin(grad_inner, squeeze_t[b], 0)
        per_slot = [grad_means[u:u + 1] / half_count[u] for u in range(2)]
        sum1, sum2 = 0.0, 0.0
        for u in range(2):
            g = gate[u:u + 1]
            sum1 = sum1 + g * gs_sum[u] + grad_means[u:u + 1]
            sum2 = sum2 + g * gx_sum[u] + per_slot[u] * (k.psum[b, u:u + 1] - half_count[u] * mean_row)
        sum2 = sum2 * inv_row
        exchange(back_slot + last, back_place(last),
                 jnp.concatenate([half_lanes(v, h) for v in (sum1, sum2) for h in HV], axis=0))
        return grad_up, grad_inner, per_slot

    def tail_back_aside(b, kept, found):
        means, inner, excited, gate = kept
        grad_up, grad_inner, per_slot = found
        res = b * PER + SUB
        gates = [[row(half_lanes(gate[u:u + 1], h)) for h in HV] for u in range(2)]
        slots = [[row(half_lanes(per_slot[u], h)) for h in HV] for u in range(2)]
        norm = [(stat_row(res, 0, h), stats[res, pl.ds(2 + h, 1)]) for h in HV]

        def second(t0, c):
            a = first_mask[pl.ds(t0, RF)] > 0.5
            v = valid[pl.ds(t0, RF)]
            out_c = []
            for h in HV:
                gs = pre[b, h, pl.ds(t0, RF)]
                gz[h, pl.ds(t0, RF)] = (gs * jnp.where(a, gates[0][h], gates[1][h])
                                        + jnp.where(a, slots[0][h], slots[1][h]) * v)
                x = prods[res, h, pl.ds(t0, RF)] - norm[h][0]
                out_c += [c[2 * h] + accumulate(gs), c[2 * h + 1] + accumulate(gs * x)]
            return tuple(out_c)
        tot = steps_loop(RF, second, tuple(jnp.zeros((8, LANES), F32) for _ in range(2 * plan.halves)))
        sums = [jnp.sum(part, axis=0, keepdims=True) for part in tot]
        exchange(back_slot + res, back_place(res), jnp.concatenate(
            [sums[2 * h] for h in HV] + [sums[2 * h + 1] * norm[h][1] for h in HV], axis=0))
        k.expand_grad[b] = small(eight(excited), eight(grad_up), ((0,), (0,)))
        k.squeeze_grad[b] = small(eight(grad_inner), eight(means), ((0,), (0,)))

    def norm_back(index, load, target, store, then=None):
        sums = jnp.sum(received(back_slot + index, back_place(index)), axis=0)
        if then is not None:
            then()
        k.shifts_grad[index] = sums[0:2]
        k.gains_grad[index] = sums[2:4]
        inv_total = k.norm_count[0:2]
        st = stats[index]
        mean, inv, scale = st[0:2], st[2:4], st[4:6]
        k1 = scale * sums[0:2] * inv_total
        k2 = scale * sums[2:4] * inv_total * inv
        rows3 = [[row(value[h:h + 1]) for value in (mean, scale, k1, k2)] for h in HV]
        for t0 in range(0, Q, R):
            v = valid[t0:t0 + R]
            parts = []
            for h in HV:
                mean_h, scale_h, k1_h, k2_h = rows3[h]
                grad = scale_h * load(t0, h) - (k1_h + k2_h * (prods[index, h, t0:t0 + R] - mean_h)) * v
                parts.append(grad.reshape(8 * R, LANES).astype(BF16))
            both = jnp.concatenate(parts, axis=1)
            target[8 * t0:8 * (t0 + R)] = both
            if plan.fused:
                res = jnp.dot(both, k.point_t[index], preferred_element_type=F32)
            else:
                res = lax.dot_general(both, point[index], (((1,), (1,)), ((), ())), preferred_element_type=F32)
            for h in HV:
                store(t0, h, half_lanes(res, h).reshape(R, 8, LANES))

    def point_back(index, source):
        place = lax.rem(index, 2) if plan.fused else index
        k.point_grad[place] = lax.dot_general(acts[index], source[...], (((0,), (0,)), ((), ())),
                                              preferred_element_type=F32)

    def store_gd(t0, h, values):
        gd[h, HALO + t0:HALO + t0 + R] = values

    def store_skip(t0, h, values):
        k.skip[h, t0:t0 + R] = values

    def conv_back_block(t0, h, index, taps):
        low, high = -taps[-1][1], -taps[0][1]
        win = gd[h, pl.ds(t0 + HALO + low, R + high - low)]
        if len(taps) >= plan.taps[0]:
            return all_taps(win, index, h, len(taps), True)
        return direct(win, low, index, h, [(t, -shift) for t, shift in taps])

    def kernel_back(index, pieces):
        for source, taps in pieces:
            for h in HV:
                low = min(s for _, s in taps)
                high = max(s for _, s in taps)

                def body(t0, c):
                    g = gd[h, pl.ds(HALO + t0, RF)]
                    win = hid[source, h, pl.ds(t0 + HALO + low, RF + high - low)]
                    return tuple(acc + accumulate(g * win[s - low:s - low + RF]) for acc, (_, s) in zip(c, taps))
                accs = steps_loop(RF, body, tuple(jnp.zeros((8, LANES), F32) for _ in taps))
                for acc, (tap, _) in zip(accs, taps):
                    k.dw_grad[index, h, pl.ds(tap, 1)] = jnp.sum(acc, axis=0, keepdims=True)

    def slopes(index):
        scales = [0.5 * stat_row(index, 2, h) for h in HV]
        offsets = [0.5 * stat_row(index, 3, h) for h in HV]

        def body(t0, c):
            v = valid[pl.ds(t0, RF)]
            for h in HV:
                k.slope[h, pl.ds(t0, RF)] = slope_of(prods[index, h, pl.ds(t0, RF)] * scales[h] + offsets[h]) * v
            return c
        steps_loop(RF, body)

    def hidden_back(index, taps):
        before = index - 1
        mean = [stat_row(before, 0, h) for h in HV]

        def body(t0, c):
            res = []
            for h in HV:
                grad = conv_back_block(t0, h, index, taps) * k.slope[h, pl.ds(t0, R)]
                gz[h, pl.ds(t0, R)] = grad
                gx = grad * (prods[before, h, pl.ds(t0, R)] - mean[h])
                res += [c[2 * h] + accumulate(grad), c[2 * h + 1] + accumulate(gx)]
            return tuple(res)
        tot = steps_loop(R, body, tuple(jnp.zeros((8, LANES), F32) for _ in range(2 * plan.halves)))
        sums = [jnp.sum(part, axis=0, keepdims=True) for part in tot]
        exchange(back_slot + before, back_place(before), jnp.concatenate(
            [sums[2 * h] for h in HV] + [sums[2 * h + 1] * stats[before, pl.ds(2 + h, 1)] for h in HV], axis=0))

    def load_gz(t0, h):
        return gz[h, t0:t0 + R]

    def scatter_start(unit, place):
        remote(k.shares.at[place, :, :, 1 - core], k.inbox.at[unit], 6, unit, partner)

    def scatter_sum(unit, place):
        blocks_wait(chips, 7, unit)
        blocks_wait(chips, 6, unit)
        slot = lax.rem(unit, 3)
        k.sums[slot] = (k.shares[place, :, :, core].astype(F32) + k.inbox[unit].astype(F32)).astype(BF16)

    def scatter_send(unit):
        slot = lax.rem(unit, 3)
        k.gained[unit, chip] = k.sums[slot, depth, plane]
        for peer in same_core:
            remote(k.sums.at[slot, peer // 8, lax.rem(peer // 2, 4)], k.gained.at[unit, chip], 8, unit, peer)

    def scatter_finish(unit):
        blocks_wait(chips - 1, 9, unit)
        return jnp.sum(k.gained[unit].astype(F32), axis=0)

    def scatter_plane(unit):
        slot = lax.rem(unit, 3)
        k.by_plane[unit, plane] = k.sums[slot, :, plane]
        for d in (3, 2, 1):
            there = lax.rem(plane + d, 4)
            remote(k.sums.at[slot, :, there], k.by_plane.at[unit, plane], 8, unit, in_plane(d))

    def scatter_mid(unit):
        blocks_wait(12, 9, unit)
        blocks_wait(12, 8, unit)
        k.line[unit] = jnp.sum(k.by_plane[unit].astype(F32), axis=0).astype(BF16)
        k.by_depth[unit, depth] = k.line[unit, depth]

    def scatter_z(unit):
        for d in (2, 1, 3):
            there = lax.rem(depth + d, 4)
            remote(k.line.at[unit, there], k.by_depth.at[unit, depth], 10, unit, at_depth(d))

    def scatter_end(unit):
        blocks_wait(3, 11, unit)
        return jnp.sum(k.by_depth[unit].astype(F32), axis=0)

    def pair_start(pair):
        both = [k.point_grad[side].reshape(N, 8, plan.channels) for side in range(2)]
        k.shares[0] = jnp.concatenate(both, axis=1).astype(BF16).reshape(4, 4, 2, 16, plan.channels)
        scatter_start(1 + pair, 0)

    def pair_finish(pair, straight=False):
        total = scatter_finish(1 + pair) if straight else scatter_end(1 + pair)
        b = pair // (PER // 2)
        r = 2 * lax.rem(pair, PER // 2)
        k.point_out[b, r] = total[0:8]
        k.point_out[b, r + 1] = total[8:16]

    def last_start():
        k.packed[0:LANES] = jnp.zeros((LANES, LANES), F32)
        columns = []
        for h in HV:
            k.packed[0:plan.tap_rows] = k.dw_grad[0, h]
            columns.append(jnp.transpose(k.packed[0:LANES]))
        whole = jnp.concatenate(columns, axis=0)
        moved = pltpu.roll(whole, plan.tap_rows, 1).reshape(N, 8, LANES)
        k.last_mine[...] = whole.reshape(N, 8, LANES)[:, 0:4] + moved[:, 4:8]
        k.last[me] = k.last_mine[me]
        for peer in peers:
            pltpu.make_async_remote_copy(src_ref=k.last_mine.at[peer], dst_ref=k.last.at[me],
                                         send_sem=k.last_sems.at[0], recv_sem=k.last_sems.at[1],
                                         device_id=(peer,), device_id_type=MESH).start()

    def last_finish():
        wait_all(k.last, k.last_sems.at[1])
        total = jnp.sum(k.last[...], axis=0)
        both = jnp.concatenate([total, pltpu.roll(jnp.concatenate([total, total], axis=0),
                                                  LANES - plan.tap_rows, 1)[0:4]], axis=0)
        k.dw_first_out[0] = both[:, 0:plan.taps[0]]

    def values_start():
        k.packed[...] = jnp.zeros((plan.values, LANES), F32)
        blocks = []
        for b in range(2):
            columns = []
            for h in HV:
                for r in range(1 - b, SUB):
                    k.packed[plan.tap_row(r):plan.tap_row(r) + plan.tap_rows] = k.dw_grad[b * PER + r, h]
                lanes = slice(h * LANES, (h + 1) * LANES)
                k.packed[EXPAND_ROW:EXPAND_ROW + plan.hidden] = k.expand_grad[b, :, lanes]
                k.packed[SQUEEZE_ROW:SQUEEZE_ROW + plan.hidden] = k.squeeze_grad[b, :, lanes]
                columns.append(jnp.concatenate(
                    [jnp.transpose(k.packed[t * LANES:(t + 1) * LANES]) for t in range(2)], axis=1))
            blocks.append(jnp.concatenate(columns, axis=0).reshape(N, 8, plan.values))
        k.shares[1] = jnp.concatenate(blocks, axis=1).astype(BF16).reshape(4, 4, 2, 16, plan.values)
        scatter_start(0, 1)

    def values_finish():
        total = scatter_finish(0)
        for b in range(2):
            rows = total[8 * b:8 * b + 8]

            def lanes(start, size):
                tile, lane = divmod(start, LANES)
                part = rows[:, tile * LANES:(tile + 1) * LANES]
                return (pltpu.roll(part, LANES - lane, 1) if lane else part)[:, 0:size]
            dw_out = (k.dw_first_out, k.dw_second_out)[b]
            for r in range(1 - b, SUB):
                dw_out[r] = lanes(plan.tap_row(r), plan.taps[b])
            k.squeeze_out[b] = lanes(SQUEEZE_ROW, plan.hidden)
            k.expand_out[b] = lanes(EXPAND_ROW, plan.hidden)

    def own_norms():
        mine = pl.ds(pl.multiple_of(me * 8, 8), 8)
        k.packed[0:LANES] = jnp.zeros((LANES, LANES), F32)
        for h in HV:
            for b in range(2):
                for r in range(PER):
                    k.packed[16 * b + r:16 * b + r + 1] = k.gains_grad[b * PER + r, h:h + 1]
                    k.packed[16 * b + 8 + r:16 * b + 9 + r] = k.shifts_grad[b * PER + r, h:h + 1]
            k.own_norm[h * LANES:(h + 1) * LANES] = jnp.transpose(k.packed[0:LANES])
        k.packed[0:LANES] = jnp.transpose(
            jnp.concatenate([k.own_norm[mine], jnp.zeros((LANES - 8, LANES), F32)], axis=0))
        for b in range(2):
            for r in range(PER):
                k.gains_out[r, b:b + 1] = k.packed[16 * b + r:16 * b + r + 1, 0:8]
                k.shifts_out[r, b:b + 1] = k.packed[16 * b + 8 + r:16 * b + 9 + r, 0:8]

    HALF = PER // 2

    def backward_aside(b, r):
        index = b * PER + r
        if plan.fused:
            if b == 0:
                @pl.when(r == SUB - 1)
                def _():
                    scatter_sum(1 + HALF, 0)

            @pl.when(lax.rem(r, 2) == 1)
            def _():
                scatter_sum(1 + HALF * b + (r + 1) // 2, 0)
        point_back(index, gpb)

        @pl.when(r == SUB - 1)
        def _():
            res = b * PER + SUB
            norm_back(res, lambda t0, h: pre[b, h, t0:t0 + R], gqb, store_skip)
            point_back(res, gqb)
        if plan.fused:
            @pl.when(lax.rem(r, 2) == 0)
            def _():
                pair_start(HALF * b + r // 2)

    def backward_late(b, r):
        if not plan.fused:
            return
        if b == 0:
            @pl.when(r == SUB - 1)
            def _():
                pair_finish(HALF + 1)

            @pl.when(r == SUB - 2)
            def _():
                scatter_mid(1 + HALF)

            @pl.when(r == SUB - 3)
            def _():
                pair_finish(HALF)

        @pl.when(jnp.logical_or(r == 2, r == 0))
        def _():
            scatter_mid(1 + HALF * b + r // 2 + 1)

        @pl.when(r == 1)
        def _():
            pair_finish(HALF * b + 2)

    def backward_block(b):
        def go(r):
            if plan.fused:
                @pl.when(jnp.logical_or(r == 2, r == 0))
                def _():
                    scatter_plane(1 + HALF * b + r // 2 + 1)

                @pl.when(r == 1)
                def _():
                    scatter_z(1 + HALF * b + 2)
                if b == 0:
                    @pl.when(r == SUB - 1)
                    def _():
                        scatter_z(1 + HALF + 1)

                    @pl.when(r == SUB - 2)
                    def _():
                        scatter_plane(1 + HALF)

                    @pl.when(r == SUB - 3)
                    def _():
                        scatter_z(1 + HALF)

        def filtered(r):
            norm_back(b * PER + r, load_gz, gpb, store_gd, lambda: go(r))
            for h in HV:
                set_halo(gd, h)

        def step(j, c):
            r = SUB - 1 - j
            index = b * PER + r
            filtered(r)
            hidden_back(index, regular_taps(b))
            backward_aside(b, r)
            kernel_back(index, [(hid_of(b, r), regular_taps(b))])

            @pl.when(r >= 2)
            def _():
                slopes(index - 2)
            backward_late(b, r)
            return c
        lax.fori_loop(0, SUB - 1, step, 0)
        if plan.fused and b == 0:
            values_start()
        filtered(0)

    if plan.fused:
        wait_all(k.first, count_sems.at[1])
        unpack_first()
    else:
        wait_all(counts, count_sems.at[1])
        dw[...] = k.dw_in[...]
        for b in range(2):
            for r in range(SUB):
                for h in HV:
                    split_taps(b, r, h)
    count_slots()
    kept_first = forward_block(0)

    def store_middle(t0, h, values):
        hid[hid_of(1, 0), h, pl.ds(HALO + t0, RF)] = values
    tail(0, kept_first[3], store_middle)
    for h in HV:
        set_halo(hid.at[hid_of(1, 0)], h)

    def place_cot():
        load_cot.wait()
        for h in HV:
            flat[h, 0:GAP] = jnp.zeros((GAP, LANES), F32)
            flat[h, GAP + plan.slots:] = jnp.zeros((flat.shape[1] - GAP - plan.slots, LANES), F32)

        def place(i, c):
            rows = pl.ds(pl.multiple_of(i * 128, 128), 128)
            for h in HV:
                flat[h, pl.ds(pl.multiple_of(i * 128 + GAP, 16), 128)] = k.cot_v[rows, h * LANES:(h + 1) * LANES]
            return c
        lax.fori_loop(0, plan.slots // 128, place, 0)

        def pick(t0, c):
            for h in HV:
                for j in range(RF):
                    here = flat[h, pl.ds(t0 + j + GAP, 8, stride=Q)]
                    moved = flat[h, pl.ds(t0 + j, 8, stride=Q)]
                    gz[h, t0 + j] = jnp.where(first_mask[t0 + j] > 0.5, here, moved)
            return c
        steps_loop(RF, pick)
    kept_second = forward_block(1, ((0, lambda: tail_slope(0, kept_first[3])), (1, place_cot)))

    last_half = tail_half(1, kept_second[3])

    def load_last(t0, h):
        return gz[h, pl.ds(t0, RF)] * (slope_of(last_half(t0, h)) * valid[pl.ds(t0, RF)])
    found = tail_back(1, kept_second, load_last)

    def store_out(t0, h, values):
        for j in range(RF):
            flat[h, pl.ds(t0 + j, 8, stride=Q)] = values[j]

    def ungap(i, c):
        rows = pl.ds(pl.multiple_of(i * 128, 128), 128)
        slot = i * 128 + lax.broadcasted_iota(jnp.int32, (128, LANES), 0)
        for h in HV:
            moved = flat[h, pl.ds(pl.multiple_of(i * 128 + GAP, 16), 128)]
            k.cot_v[rows, h * LANES:(h + 1) * LANES] = jnp.where(slot < half0, flat[h, rows], moved)
        return c
    tail_back_aside(1, kept_second, found)
    slopes(PER + SUB - 2)
    tail(1, kept_second[3], store_out)
    lax.fori_loop(0, plan.slots // 128, ungap, 0)
    save_out.start()
    backward_block(1)

    def sum_back(t0, c):
        for h in HV:
            gz[h, pl.ds(t0, R)] = conv_back_block(t0, h, PER, regular_taps(1)) + k.skip[h, pl.ds(t0, R)]
        return c
    steps_loop(R, sum_back)
    found = tail_back(0, kept_first, lambda t0, h: gz[h, pl.ds(t0, RF)] * pre[0, h, pl.ds(t0, RF)])
    tail_back_aside(0, kept_first, found)
    slopes(SUB - 2)
    backward_aside(1, 0)
    kernel_back(PER, [(hid_of(1, 0), regular_taps(1))])
    backward_late(1, 0)
    backward_block(0)
    pieces = block_pieces(0)
    backward_aside(0, 0)
    if plan.fused:
        scatter_sum(0, 1)
        scatter_send(0)
    kernel_back(0, pieces)
    if plan.fused:
        last_start()
        scatter_sum(1, 0)
        scatter_send(1)
        backward_late(0, 0)
        scatter_z(2)
        own_norms()

    def spread(t0, c):
        v = valid[pl.ds(t0, R)]
        for h in HV:
            even = (conv_back_block(t0, h, 0, pieces[0][1]) + k.skip[h, pl.ds(t0, R)]) * v
            odd = conv_back_block(t0, h, 0, pieces[1][1]) * v
            for j in range(R):
                wide[h, pl.ds(2 * (t0 + j), 8, stride=2 * Q)] = even[j]
                wide[h, pl.ds(2 * (t0 + j) + 1, 8, stride=2 * Q)] = odd[j]
        return c
    steps_loop(R, spread)

    def ungap_wide(i, c):
        rows = pl.ds(pl.multiple_of(i * 128, 128), 128)
        slot = i * 128 + lax.broadcasted_iota(jnp.int32, (128, LANES), 0)
        for h in HV:
            moved = wide[h, pl.ds(pl.multiple_of(i * 128 + 2 * GAP, 32), 128)]
            k.frames_grad_v[lax.rem(i, 2 * per_piece), :, h * LANES:(h + 1) * LANES] = jnp.where(
                slot < len0, wide[h, rows], moved)
        return c
    pieces_out = 8
    per_piece = 2 * plan.slots // pieces_out // 128
    save_frames = []
    for piece in range(pieces_out):
        if piece >= 2:
            save_frames[piece - 2].wait()
        lax.fori_loop(piece * per_piece, (piece + 1) * per_piece, ungap_wide, 0)
        save_frames.append(pltpu.make_async_copy(
            k.frames_grad_v.at[pl.ds((piece % 2) * per_piece, per_piece)],
            k.frames_grad.at[pl.ds(piece * per_piece, per_piece)], k.io_sems.at[3 + piece]))
        save_frames[-1].start()
    if plan.fused:
        pair_finish(1)
        values_finish()
        pair_finish(0, True)
        last_finish()

    save_out.wait()
    for copy in save_frames[-2:]:
        copy.wait()
    wait_all(k.first if plan.fused else counts, count_sems.at[0])

    def drain(slot, c):
        wait_all(recv4.at[0], send_sem.at[slot])
        return c
    lax.fori_loop(0, send4.shape[0], drain, 0)
    if plan.fused:
        for unit in range(1 + PER):
            blocks_wait(chips - 1 if unit < 2 else 3, 0, unit)
            if unit >= 2:
                blocks_wait(12, 2, unit)
                blocks_wait(3, 10, unit)
            else:
                blocks_wait(chips - 1, 8, unit)
            blocks_wait(chips, 4, unit)
        wait_all(k.last, k.last_sems.at[0])


def call_kernel(plan, inputs):
    layers, halves, Q, channels = plan.layers, plan.halves, plan.steps, plan.channels
    vals, shard, hidden, devices = plan.values, plan.shard, plan.hidden, plan.devices
    vmem = pl.BlockSpec(memory_space=pltpu.VMEM)
    anywhere = pl.BlockSpec(memory_space=pl.ANY)
    places = {"lens": pl.BlockSpec(memory_space=pltpu.SMEM), "frames": anywhere, "cot": anywhere,
              "out": anywhere, "frames_grad": anywhere}
    slots = 2 * layers

    def shape(*dims, dtype=F32):
        return jax.ShapeDtypeStruct(dims, dtype)
    outs = {
        "out": shape(plan.slots, channels),
        "frames_grad": shape(2 * plan.slots // 128, 128, channels),
    }
    params = {
        "dw": shape(layers, halves, plan.dw_rows, LANES),
        "point": shape(layers, channels, channels, dtype=BF16),
        "gains": shape(layers, halves, LANES),
        "shifts": shape(layers, halves, LANES),
        "squeeze_t": shape(2, hidden, channels),
        "expand": shape(2, hidden, channels),
    }
    grads = {
        "dw_grad": shape(layers, halves, plan.tap_rows, LANES),
        "point_grad": shape(2 if plan.fused else layers, channels, channels),
        "gains_grad": shape(layers, halves, LANES),
        "shifts_grad": shape(layers, halves, LANES),
        "squeeze_grad": shape(2, hidden, channels),
        "expand_grad": shape(2, hidden, channels),
    }
    scratch = {
        "hid": shape(2 * plan.sub + 1, halves, plan.pad, 8, LANES),
        "acts": shape(layers, plan.rows, channels, dtype=BF16),
        "prods": shape(layers, halves, Q, 8, LANES),
        "gd": shape(halves, plan.pad, 8, LANES),
        "gz": shape(halves, Q, 8, LANES),
        "gpb": shape(plan.rows, channels, dtype=BF16),
        "gqb": shape(plan.rows, channels, dtype=BF16),
        "pre": shape(2, halves, Q, 8, LANES),
        "wide": shape(halves, 2 * plan.slots + 4 * GAP, LANES),
        "frames_v": shape(2 * plan.slots, channels, dtype=BF16),
        "cot_v": shape(plan.slots, channels),
        "frames_grad_v": shape(plan.slots // 256, 128, channels),
        "first_mask": shape(Q, 8, LANES),
        "valid": shape(Q, 8, LANES),
        "slope": shape(halves, Q, 8, LANES),
        "skip": shape(halves, Q, 8, LANES),
        "psum": shape(2, 8, channels),
        "stats": shape(layers, 8, LANES),
        "send4": shape(slots, 4, LANES),
        "recv4": shape(layers, devices, 4, LANES),
        "counts": shape(devices, 4, LANES),
        "csend": shape(4, LANES),
        "norm_count": shape(4, LANES),
    }
    sems = {"send_sem": (slots,), "recv_sem": (slots,), "count_sems": (2,), "io_sems": (11,)}
    if plan.fused:
        units, chips = 1 + plan.per, devices // 2
        outs.update({
            "dw_first_out": shape(plan.sub, shard, plan.taps[0]),
            "dw_second_out": shape(plan.sub, shard, plan.taps[1]),
            "point_out": shape(2, plan.per, shard, channels),
            "gains_out": shape(plan.per, 2, shard),
            "shifts_out": shape(plan.per, 2, shard),
            "squeeze_out": shape(2, shard, hidden),
            "expand_out": shape(2, shard, hidden),
        })
        scratch.update(params)
        scratch.update(grads)
        scratch.update({
            "tile": shape(8, LANES),
            "point_t": shape(layers, channels, channels, dtype=BF16),
            "packed": shape(vals, LANES),
            "packed_t": shape(16, vals),
            "first": shape(devices, 4, LANES),
            "last_mine": shape(devices, 4, LANES),
            "last": shape(devices, 4, LANES),
            "unpacked": shape(vals, LANES),
            "gath": shape(units, 4, 4, 2, 16, channels, dtype=BF16),
            "shares": shape(2, 4, 4, 2, 16, channels, dtype=BF16),
            "inbox": shape(units, 4, 4, 16, channels, dtype=BF16),
            "sums": shape(3, 4, 4, 16, channels, dtype=BF16),
            "gained": shape(2, chips, 16, channels, dtype=BF16),
            "by_plane": shape(units, 4, 4, 16, channels, dtype=BF16),
            "line": shape(units, 4, 16, channels, dtype=BF16),
            "by_depth": shape(units, 4, 16, channels, dtype=BF16),
            "own_norm": shape(channels, LANES),
        })
        sems["unit_sems"] = (12, units)
        sems["last_sems"] = (2,)
        sems["param_sems"] = (len(PARAMS),)
        for name in PARAMS:
            scratch[name + "_v"] = inputs[name]
            places[name] = anywhere
    else:
        outs.update(grads)
        scratch["dw"] = params["dw"]
    names = list(inputs) + list(outs) + list(scratch) + list(sems)
    results = pl.pallas_call(
        functools.partial(kernel, plan, names),
        out_shape=list(outs.values()),
        in_specs=[places.get(name, vmem) for name in inputs],
        out_specs=[places.get(name, vmem) for name in outs],
        scratch_shapes=[pltpu.VMEM(v.shape, v.dtype) for v in scratch.values()]
        + [pltpu.SemaphoreType.DMA(v) for v in sems.values()],
        compiler_params=pltpu.CompilerParams(
            collective_id=0, has_side_effects=True, vmem_limit_bytes=63 * 1024 * 1024),
    )(*inputs.values())
    if plan.fused:
        results = hand_on(results)
    return dict(zip(outs, results, strict=True))


def hand_on(arrays):
    n = len(arrays)
    parts = []
    for i, v in enumerate(arrays):
        rows = max(1, v.shape[0] * (1 << 20) // (4 * v.size))
        parts += [(i, start, min(rows, v.shape[0] - start)) for start in range(0, v.shape[0], rows)]

    def move(*refs):
        here, there, held, sems = refs[:n], refs[n:2 * n], refs[2 * n:3 * n], refs[3 * n]
        into, out = [], []
        for p, (i, start, size) in enumerate(parts):
            rows = pl.ds(start, size)
            into.append(pltpu.make_async_copy(here[i].at[rows], held[i].at[rows], sems.at[0, p]))
            out.append(pltpu.make_async_copy(held[i].at[rows], there[i].at[rows], sems.at[1, p]))
        for copy in into:
            copy.start()
        for p in range(len(parts)):
            into[p].wait()
            out[p].start()
        for copy in out:
            copy.wait()
    anywhere = pl.BlockSpec(memory_space=pl.ANY)
    return pl.pallas_call(
        move,
        out_shape=[jax.ShapeDtypeStruct(v.shape, v.dtype) for v in arrays],
        in_specs=[anywhere] * n,
        out_specs=[anywhere] * n,
        scratch_shapes=[pltpu.VMEM(v.shape, v.dtype) for v in arrays] + [pltpu.SemaphoreType.DMA((2, len(parts)))],
    )(*arrays)


def body(frames, dw_first, dw_second, point, gains, shifts, se_down, se_up, cotangent, lengths, *, devices):
    sub, taps_first, shard = dw_first.shape
    taps_second = dw_second.shape[1]
    hidden = se_down.shape[2]
    channels = point.shape[3]
    plan = Plan(cotangent.shape[0], channels, taps_first, taps_second, sub, hidden, devices)
    if plan.fused:
        res = call_kernel(plan, {
            "lens": lengths, "frames": frames, "cot": cotangent,
            "dw_first": jnp.swapaxes(dw_first, 1, 2), "dw_second": jnp.swapaxes(dw_second, 1, 2),
            "point_in": point, "gains_in": jnp.swapaxes(gains, 0, 1), "shifts_in": jnp.swapaxes(shifts, 0, 1),
            "se_down": se_down, "se_up": jnp.swapaxes(se_up, 1, 2)})
        return (
            res["out"], res["frames_grad"].reshape(2 * plan.slots, channels), jnp.swapaxes(res["dw_first_out"], 1, 2),
            jnp.swapaxes(res["dw_second_out"], 1, 2), res["point_out"], jnp.swapaxes(res["gains_out"], 0, 1),
            jnp.swapaxes(res["shifts_out"], 0, 1), res["squeeze_out"], jnp.swapaxes(res["expand_out"], 1, 2))

    per, layers, halves = plan.per, plan.layers, plan.halves

    def gather(v, axis):
        return lax.all_gather(v, "dp", axis=axis, tiled=True)
    small = jnp.concatenate([
        dw_first.reshape(-1, shard), dw_second.reshape(-1, shard), gains.reshape(-1, shard),
        shifts.reshape(-1, shard), se_up.reshape(-1, shard),
        jnp.swapaxes(se_down, 1, 2).reshape(-1, shard)], axis=0)
    small = gather(small, 1).astype(F32)
    sizes = [sub * taps_first, sub * taps_second, layers, layers, 2 * hidden, 2 * hidden]
    part = jnp.split(small, [sum(sizes[:i]) for i in range(1, 6)], axis=0)

    def dw_layout(v, taps):
        v = v.reshape(sub, taps, halves, LANES).transpose(0, 2, 1, 3)
        return jnp.pad(v, ((0, 1), (0, 0), (0, plan.dw_rows - taps), (0, 0)))
    res = call_kernel(plan, {
        "lens": lengths, "frames": frames, "cot": cotangent,
        "dw_in": jnp.concatenate([dw_layout(part[0], taps_first), dw_layout(part[1], taps_second)], axis=0),
        "point": gather(point, 2).reshape(layers, channels, channels),
        "gains": part[2].reshape(layers, halves, LANES),
        "shifts": part[3].reshape(layers, halves, LANES),
        "squeeze_t": part[5].reshape(2, hidden, channels),
        "expand": part[4].reshape(2, hidden, channels)})

    def scatter(v, axis):
        return lax.psum_scatter(v, "dp", scatter_dimension=axis, tiled=True)

    def dw_out(v, taps):
        return v[:sub, :, :taps].transpose(0, 2, 1, 3).reshape(sub * taps, channels)
    grads = res["dw_grad"]
    packed = scatter(jnp.concatenate(
        [dw_out(grads[:per], taps_first), dw_out(grads[per:], taps_second),
         res["squeeze_grad"].reshape(-1, channels), res["expand_grad"].reshape(-1, channels)], axis=0), 1)
    g1, g2, gsq, gex = jnp.split(packed, [sizes[0], sizes[0] + sizes[1], sizes[0] + sizes[1] + sizes[5]], axis=0)

    def norm_out(v):
        return lax.dynamic_slice_in_dim(v.reshape(2, per, channels), lax.axis_index("dp") * shard, shard, 2)
    return (
        res["out"], res["frames_grad"].reshape(2 * plan.slots, channels), g1.reshape(sub, taps_first, shard), g2.reshape(sub, taps_second, shard),
        scatter(res["point_grad"].reshape(2, per, channels, channels), 2),
        norm_out(res["gains_grad"]), norm_out(res["shifts_grad"]),
        jnp.swapaxes(gsq.reshape(2, hidden, shard), 1, 2), gex.reshape(2, hidden, shard))


def solution(mesh):
    return jax.shard_map(
        functools.partial(body, devices=mesh.shape["dp"]),
        mesh=mesh,
        in_specs=(
            P("dp", None),
            P(None, None, "dp"),
            P(None, None, "dp"),
            P(None, None, "dp", None),
            P(None, None, "dp"),
            P(None, None, "dp"),
            P(None, "dp", None),
            P(None, None, "dp"),
            P("dp", None),
            P("dp"),
        ),
        out_specs=(
            P("dp", None),
            P("dp", None),
            P(None, None, "dp"),
            P(None, None, "dp"),
            P(None, None, "dp", None),
            P(None, None, "dp"),
            P(None, None, "dp"),
            P(None, "dp", None),
            P(None, None, "dp"),
        ),
        check_vma=False,
    )
```

```python
import functools

import jax
import jax.numpy as jnp
from jax import lax
from jax.experimental import pallas as pl
from jax.experimental.pallas import tpu as pltpu
from jax.sharding import PartitionSpec as P

EPSILON = 1e-05
HIGHEST = lax.Precision.HIGHEST
F32 = jnp.float32
BF16 = jnp.bfloat16
MESH = pl.DeviceIdType.MESH

GAP = 32
HALO = 13
LANES = 128


def sigmoid(v):
    return 0.5 * jnp.tanh(0.5 * v) + 0.5


class Plan:
    def __init__(self, slots, channels, taps_first, taps_second, sub_blocks, hidden, devices):
        self.slots = slots
        self.steps = (slots + GAP) // 8
        self.rows = 8 * self.steps
        self.channels = channels
        self.halves = channels // LANES
        self.taps = (taps_first, taps_second)
        self.max_taps = max(self.taps)
        self.sub = sub_blocks
        self.hidden = hidden
        self.devices = devices
        self.block = next(r for r in (44, 12, 4) if self.steps % r == 0)
        self.fine = next(r for r in (22, 12, 4) if self.steps % r == 0)
        self.pad = self.steps + 2 * HALO
        self.per = sub_blocks + 1
        self.layers = 2 * self.per
        self.tap_rows = 32
        self.tap_sets = (32, 104)
        self.dw_rows = 176
        self.values = 2 * LANES
        self.shard = channels // devices
        self.fused = self.shard == 8 and devices == 32 and sub_blocks == 5 and hidden == 32 and self.max_taps <= 32

    def tap_row(self, r):
        return r * self.tap_rows + self.tap_rows * (r // 4)


SQUEEZE_ROW, EXPAND_ROW, GAIN_ROW, SHIFT_ROW = 128, 192, 224, 232


PARAMS = ("dw_first", "dw_second", "point_in", "gains_in", "shifts_in", "se_down", "se_up")


class Refs:
    def __init__(self, names, refs):
        for name, ref in zip(names, refs, strict=True):
            setattr(self, name, ref)


def peers_of(me, n):
    if n != 32:
        return [lax.rem(me + k, n) for k in range(1, n)]
    core = lax.rem(me, 2)
    x = lax.rem(me // 2, 2)
    y = lax.rem(me // 4, 2)
    z = me // 8
    found = []
    for order, other in enumerate((3 - z, lax.rem(z + 2, 4), z + 1 - 2 * lax.rem(z, 2), z)):
        for dy in (1, 0):
            for dx in (1, 0):
                for dc in (0, 1):
                    if order == 3 and dy == 0 and dx == 0 and dc == 0:
                        continue
                    oy = lax.rem(y + dy, 2)
                    ox = lax.rem(x + dx, 2)
                    oc = lax.rem(core + dc, 2)
                    found.append((dy + dx + (3, 2, 1, 0)[order], other * 8 + oy * 4 + ox * 2 + oc))
    found.sort(key=lambda item: -item[0])
    return [item[1] for item in found]


def same_core_peers(me, n):
    if n != 32:
        return [lax.rem(me + 2 * k, n) for k in range(1, n // 2)]
    core = lax.rem(me, 2)
    x = lax.rem(me // 2, 2)
    y = lax.rem(me // 4, 2)
    z = me // 8
    found = []
    for order, other in enumerate((3 - z, lax.rem(z + 2, 4), z + 1 - 2 * lax.rem(z, 2), z)):
        for dy in (1, 0):
            for dx in (1, 0):
                if order == 3 and dy == 0 and dx == 0:
                    continue
                oy = lax.rem(y + dy, 2)
                ox = lax.rem(x + dx, 2)
                found.append((dy + dx + (3, 2, 1, 0)[order], other * 8 + oy * 4 + ox * 2 + core))
    found.sort(key=lambda item: -item[0])
    return [item[1] for item in found]


def kernel(plan, names, *refs):
    k = Refs(names, refs)
    lens, dw, point, gains, shifts = k.lens, k.dw, k.point, k.gains, k.shifts
    squeeze_t, expand = k.squeeze_t, k.expand
    hid, acts, prods, gd, gz, gpb, gqb, pre = k.hid, k.acts, k.prods, k.gd, k.gz, k.gpb, k.gqb, k.pre
    wide, first_mask, valid, stats = k.wide, k.first_mask, k.valid, k.stats
    flat = wide.at[:, pl.ds(0, plan.slots + 2 * GAP)]
    send4, recv4, counts, csend = k.send4, k.recv4, k.counts, k.csend
    send_sem, recv_sem, count_sems = k.send_sem, k.recv_sem, k.count_sems
    N = plan.devices
    Q, R, RF = plan.steps, plan.block, plan.fine
    HV = range(plan.halves)
    SUB = plan.sub
    PER = plan.per
    me = lax.axis_index("dp")
    peers = peers_of(me, N)
    chips = N // 2
    chip, core = me // 2, lax.rem(me, 2)
    partner = me + 1 - 2 * core
    depth, plane = me // 8, lax.rem(me // 2, 4)

    def at_depth(d):
        return lax.rem(depth + d, 4) * 8 + 2 * plane + core

    def in_plane(d):
        return depth * 8 + 2 * lax.rem(plane + d, 4) + core

    same_core = same_core_peers(me, N)

    barrier = pltpu.get_barrier_semaphore()
    for peer in peers:
        pl.semaphore_signal(barrier, inc=1, device_id=(peer,), device_id_type=MESH)

    load_frames = pltpu.make_async_copy(k.frames, k.frames_v, k.io_sems.at[0])
    load_params = []
    if plan.fused:
        for i, name in enumerate(PARAMS):
            load_params.append(pltpu.make_async_copy(getattr(k, name), getattr(k, name + "_v"), k.param_sems.at[i]))
            load_params[-1].start()
    load_cot = pltpu.make_async_copy(k.cot, k.cot_v, k.io_sems.at[1])
    save_out = pltpu.make_async_copy(k.cot_v, k.out, k.io_sems.at[2])
    load_frames.start()
    load_cot.start()
    len0 = lens[0]
    len1 = lens[1]
    half0 = len0 // 2
    half1 = len1 // 2
    count = (half0 + half1).astype(F32)
    inv_count = 1.0 / jnp.full((1, LANES), half0 + half1, jnp.int32).astype(F32)

    def steps_loop(width, body, init=0):
        return lax.fori_loop(0, Q // width, lambda i, c: body(i * width, c), init)

    def mask_body(t0, c):
        step = t0 + lax.broadcasted_iota(jnp.int32, (RF, 8, LANES), 0)
        slot = step + Q * lax.broadcasted_iota(jnp.int32, (RF, 8, LANES), 1)
        a = (slot < half0).astype(F32)
        b = jnp.logical_and(slot >= half0 + GAP, slot < half0 + GAP + half1).astype(F32)
        first_mask[pl.ds(t0, RF)] = a
        valid[pl.ds(t0, RF)] = a + b
        return c

    def set_halo(ref, half):
        sub = lax.broadcasted_iota(jnp.int32, (HALO, 8, LANES), 1)
        low = pltpu.roll(ref[half, pl.ds(Q, HALO)], 1, 1)
        ref[half, pl.ds(0, HALO)] = jnp.where(sub == 0, 0.0, low)
        high = pltpu.roll(ref[half, pl.ds(HALO, HALO)], 7, 1)
        ref[half, pl.ds(HALO + Q, HALO)] = jnp.where(sub == 7, 0.0, high)

    def prepare_slots():
        steps_loop(RF, mask_body)

        top = 2 * GAP + 2 * plan.slots
        for h in HV:
            wide[h, 0:2 * GAP] = jnp.zeros((2 * GAP, LANES), F32)
            wide[h, top:] = jnp.zeros((wide.shape[1] - top, LANES), F32)

        load_frames.wait()

        def widen(i, c):
            rows = pl.ds(pl.multiple_of(i * 128, 128), 128)
            for h in HV:
                values = k.frames_v[rows, h * LANES:(h + 1) * LANES].astype(F32)
                wide[h, pl.ds(pl.multiple_of(i * 128 + 2 * GAP, 32), 128)] = values
            return c

        lax.fori_loop(0, 2 * plan.slots // 128, widen, 0)

        for phase in range(2):
            def deinterleave(t0, c):
                for j in range(RF):
                    a_mask = first_mask[t0 + j]
                    b_mask = valid[t0 + j] - a_mask
                    for h in HV:
                        a = wide[h, pl.ds(2 * (t0 + j) + 2 * GAP + phase, 8, stride=2 * Q)]
                        b = wide[h, pl.ds(2 * (t0 + j) + phase, 8, stride=2 * Q)]
                        hid[phase, h, HALO + t0 + j] = a * a_mask + b * b_mask
                return c
            steps_loop(RF, deinterleave)
            for h in HV:
                set_halo(hid.at[phase], h)

    def spread_lanes(values, lane):
        k.tile[...] = jnp.zeros((8, LANES), F32)
        k.tile[:, 0:values.shape[1]] = values
        return pltpu.roll(k.tile[...], lane, 1) if lane else k.tile[...]

    def load_first():
        taps = spread_lanes(k.dw_first_v[0].astype(F32), 0)
        lane = lax.broadcasted_iota(jnp.int32, (8, LANES), 1)
        taps = jnp.where(lane == plan.tap_rows - 1, count, taps)
        k.first[me] = taps[0:4] + pltpu.roll(taps, plan.tap_rows, 1)[4:8]

    def load_shard():
        for b in range(2):
            source = (k.dw_first_v, k.dw_second_v)[b]
            tiles = [jnp.zeros((8, LANES), F32) for _ in range(2)]
            for r in range(SUB):
                tile, lane = divmod(plan.tap_row(r), LANES)
                tiles[tile] = tiles[tile] + spread_lanes(source[r].astype(F32), lane)
            tiles[1] = tiles[1] + spread_lanes(k.se_up_v[b].astype(F32), EXPAND_ROW - LANES)
            tiles[1] = tiles[1] + spread_lanes(k.se_down_v[b].astype(F32), SQUEEZE_ROW - LANES)
            k.packed[0:LANES] = jnp.zeros((LANES, LANES), F32)
            for r in range(PER):
                k.packed[GAIN_ROW - LANES + r:GAIN_ROW - LANES + r + 1, 0:8] = k.gains_in_v[r, b:b + 1].astype(F32)
                k.packed[SHIFT_ROW - LANES + r:SHIFT_ROW - LANES + r + 1, 0:8] = k.shifts_in_v[r, b:b + 1].astype(F32)
            tiles[1] = tiles[1] + jnp.transpose(k.packed[0:LANES])[0:8]
            for tile in range(2):
                k.packed_t[8 * b:8 * b + 8, tile * LANES:(tile + 1) * LANES] = tiles[tile]
        k.gath[0, depth, plane, core] = k.packed_t[...].astype(BF16)

    def load_pairs(pairs):
        for pair in pairs:
            rows = [k.point_in_v[i // PER, i % PER].astype(F32) for i in (2 * pair, 2 * pair + 1)]
            k.gath[1 + pair, depth, plane, core] = jnp.concatenate(rows, axis=0).astype(BF16)

    def remote(src, dst, sems, unit, to):
        pltpu.make_async_remote_copy(src_ref=src, dst_ref=dst, send_sem=k.unit_sems.at[sems, unit],
                                     recv_sem=k.unit_sems.at[sems + 1, unit], device_id=(to,),
                                     device_id_type=MESH).start()

    def blocks_wait(count, sem, unit):
        view = k.gained.at[0, pl.ds(0, count)]
        pltpu.make_async_copy(view, view, k.unit_sems.at[sem, unit]).wait()

    def lead_wait(count, sem, side):
        view = k.gained.at[0, pl.ds(0, count), :, pl.ds(0, LANES)]
        pltpu.make_async_copy(view, view, k.lead_sems.at[sem, side]).wait()

    def lead_copy(src, dst, sem, side, to):
        pltpu.make_async_remote_copy(src_ref=src, dst_ref=dst, send_sem=k.lead_sems.at[sem, side],
                                     recv_sem=k.lead_sems.at[sem + 1, side], device_id=(to,),
                                     device_id_type=MESH).start()

    def lead_send(side):
        rows = k.point_in_v[0, side].astype(F32)
        k.lead[side, depth, plane, core] = jnp.concatenate(
            [rows[:, h * LANES:(h + 1) * LANES] for h in HV], axis=0).astype(BF16)
        view = k.lead.at[side, depth, plane, core]
        for peer in same_core:
            lead_copy(view, view, 0, side, peer)

    def lead_core(side):
        lead_wait(chips - 1, 1, side)
        view = k.lead.at[side, :, :, core]
        lead_copy(view, view, 2, side, partner)

    def lead_unpack(side):
        lead_wait(chips, 3, side)
        got = k.lead[side].astype(F32).reshape(N, 16, LANES)
        block = jnp.concatenate([got[:, 8 * h:8 * h + 8].reshape(plan.channels, LANES) for h in HV], axis=1)
        point[side] = block.astype(BF16)
        k.point_t[side] = jnp.transpose(block).astype(BF16)

    def gather_send(unit):
        view = k.gath.at[unit, depth, plane, core]
        for peer in same_core:
            remote(view, view, 0, unit, peer)

    def gather_z(unit):
        view = k.gath.at[unit, depth, plane, core]
        for d in (2, 1, 3):
            remote(view, view, 0, unit, at_depth(d))

    def gather_plane(unit):
        blocks_wait(3, 1, unit)
        view = k.gath.at[unit, :, plane, core]
        for d in (3, 2, 1):
            remote(view, view, 2, unit, in_plane(d))

    def gather_core(unit, straight):
        blocks_wait(chips - 1 if straight else 12, 1 if straight else 3, unit)
        view = k.gath.at[unit, :, :, core]
        remote(view, view, 4, unit, partner)

    def gather_wait(unit):
        blocks_wait(chips, 5, unit)

    def split_filter(rows):
        even, odd = rows[0::2], rows[1::2]
        full = odd + [jnp.zeros((1, LANES), F32)] * (len(even) - len(odd))
        return even, odd, [o - e for e, o in zip(even, full)]

    def split_taps(b, r, h):
        taps = plan.taps[b]
        rows = [dw[b * PER + r, h, t:t + 1] for t in range(taps)]
        both = (rows, rows[::-1])
        if b == 0 and r == 0:
            start = (taps - 1) // 2 % 2
            both = (rows[start::2], rows[1 - start::2])
        for base, ordered in zip(plan.tap_sets, both):
            for i, part in enumerate(split_filter(ordered)):
                for j, piece in enumerate(split_filter(part)):
                    start = base + 24 * i + 8 * j
                    dw[b * PER + r, h, start:start + len(piece)] = jnp.concatenate(piece, axis=0)

    def unpack_first():
        got = k.first[...].reshape(4 * N, LANES)
        lane = lax.broadcasted_iota(jnp.int32, (4 * N, LANES), 1)
        low = jnp.where(lane < plan.tap_rows, got, 0.0).reshape(N, 4, LANES)
        high = jnp.where(lane < plan.tap_rows, pltpu.roll(got, LANES - plan.tap_rows, 1), 0.0).reshape(N, 4, LANES)
        counts[...] = jnp.broadcast_to(low[:, :, plan.tap_rows - 1:plan.tap_rows], counts.shape)
        block = jnp.concatenate([low, high], axis=1).reshape(plan.channels, LANES)
        for h in HV:
            k.unpacked[0:LANES] = jnp.transpose(block[h * LANES:(h + 1) * LANES])
            dw[0, h, 0:plan.tap_rows] = k.unpacked[0:plan.tap_rows]
            split_taps(0, 0, h)

    def unpack_values(b):
        got = k.gath[0].astype(F32).reshape(N, 16, plan.values)
        block = got[:, 8 * b:8 * b + 8].reshape(plan.channels, plan.values)
        for h in HV:
            for tile in range(2):
                part = block[h * LANES:(h + 1) * LANES, tile * LANES:(tile + 1) * LANES]
                k.unpacked[tile * LANES:(tile + 1) * LANES] = jnp.transpose(part)
            for r in range(1 - b, SUB):
                dw[b * PER + r, h, 0:plan.tap_rows] = k.unpacked[plan.tap_row(r):plan.tap_row(r) + plan.tap_rows]
                split_taps(b, r, h)
            for r in range(PER):
                gains[b * PER + r, h:h + 1] = k.unpacked[GAIN_ROW + r:GAIN_ROW + r + 1]
                shifts[b * PER + r, h:h + 1] = k.unpacked[SHIFT_ROW + r:SHIFT_ROW + r + 1]
            lanes = slice(h * LANES, (h + 1) * LANES)
            expand[b, :, lanes] = k.unpacked[EXPAND_ROW:EXPAND_ROW + plan.hidden]
            squeeze_t[b, :, lanes] = k.unpacked[SQUEEZE_ROW:SQUEEZE_ROW + plan.hidden]

    def unpack_pair(pair):
        got = k.gath[1 + pair].astype(F32).reshape(N, 16, plan.channels)
        for side in range(2):
            block = got[:, 8 * side:8 * side + 8].reshape(plan.channels, plan.channels)
            point[2 * pair + side] = block.astype(BF16)
            k.point_t[2 * pair + side] = jnp.transpose(block).astype(BF16)

    if plan.fused:
        for copy in load_params:
            copy.wait()
        load_first()

    if not plan.fused:
        csend[...] = jnp.full((4, LANES), count, F32)
    pl.semaphore_wait(barrier, N - 1)

    def send_to_all(src, dst, ssem, rsem):
        for peer in peers:
            pltpu.make_async_remote_copy(src_ref=src, dst_ref=dst, send_sem=ssem, recv_sem=rsem,
                                         device_id=(peer,), device_id_type=MESH).start()

    def wait_all(ref, sem):
        view = ref.at[pl.ds(0, N - 1)]
        pltpu.make_async_copy(view, view, sem).wait()

    if plan.fused:
        send_to_all(k.first.at[me], k.first.at[me], count_sems.at[0], count_sems.at[1])
        lead_send(0)
        load_shard()
        gather_send(0)
        lead_send(1)
        load_pairs(range(1, PER))
        gather_z(2)
    else:
        send_to_all(csend, counts.at[me], count_sems.at[0], count_sems.at[1])
        counts[me] = csend[...]
    prepare_slots()

    def exchange(slot, place, rows):
        send4[slot] = rows
        send_to_all(send4.at[slot], recv4.at[place, me], send_sem.at[slot], recv_sem.at[slot])
        recv4[place, me] = rows

    def received(slot, place):
        wait_all(recv4.at[place], recv_sem.at[slot])
        return recv4[place]

    def back_place(index):
        return lax.rem(index + PER, 2 * PER)

    def row(values):
        return values.reshape(1, 1, LANES)

    def accumulate(rows3):
        return jnp.sum(rows3, axis=0)

    def count_slots():
        inv_total = 1.0 / jnp.sum(counts[...], axis=0)
        k.norm_count[...] = inv_total
        counts[...] = counts[...] * inv_total

    def shares():
        return counts[...]

    def merge_stats(slot, index):
        got = received(slot, slot)
        weight = shares()
        mean = jnp.sum(weight * got, axis=0)
        mean4 = jnp.concatenate([mean[0:2], mean[0:2]], axis=0)
        diff = got - mean4
        between = jnp.sum(weight * diff * diff, axis=0)
        within = jnp.sum(got, axis=0)
        var = within[2:4] * k.norm_count[0:2] + between[0:2]
        inv = lax.rsqrt(var + EPSILON)
        scale = inv * gains[index]
        offset = shifts[index] - mean[0:2] * scale
        stats[index] = jnp.concatenate([mean[0:2], inv, scale, offset], axis=0)

    def stat_row(index, kind, h):
        return row(stats[index, pl.ds(2 * kind + h, 1)])

    def tap(index, h, t):
        return dw[index, h, pl.ds(t, 1)].reshape(1, 1, LANES)

    def direct(win, low, index, h, taps):
        acc = None
        for t, shift in taps:
            term = win[shift - low:shift - low + R] * tap(index, h, t)
            acc = term if acc is None else acc + term
        return acc

    def paired(x, count, steps, levels, run, base):
        if levels == 0:
            return run(x, count, steps, base)
        low, high = (count + 1) // 2, count // 2
        m = steps // 2
        if x.shape[0] % 2:
            x = jnp.concatenate([x, x[-1:]], axis=0)
        split = x.reshape(-1, 2, 8, LANES)
        x0, x1 = split[:, 0], split[:, 1]
        gap = 24 if levels == 2 else 8

        def part(values, n, i):
            return paired(values, n, m, levels - 1, run, base + gap * i)
        shared = part(x1[:m + low - 1], low, 2)
        first = part(x0[:m + low - 1] + x1[:m + low - 1], low, 0) + shared
        second = part(x0[1:m + high] + x1[:m + high - 1], high, 1) - shared
        return jnp.stack([first, second], axis=1).reshape(steps, 8, LANES)

    def all_taps(win, index, h, taps, side):
        def run(x, count, steps, base):
            acc = None
            for j in range(count):
                term = x[j:j + steps] * tap(index, h, base + j)
                acc = term if acc is None else acc + term
            return acc
        return paired(win, taps, R, 2, run, plan.tap_sets[side])

    def layer_conv(index, pieces, between=None):
        def body(t0, c):
            for h in HV:
                acc = None
                if len(pieces) == 1:
                    source, taps = pieces[0]
                    low = taps[0][1]
                    acc = all_taps(hid[source, h, pl.ds(t0 + HALO + low, R + len(taps) - 1)], index, h, len(taps), 0)
                else:
                    for side, (source, taps) in enumerate(pieces):
                        low, high = taps[0][1], taps[-1][1]
                        win = hid[source, h, pl.ds(t0 + HALO + low, R + high - low)]
                        part = all_taps(win, index, h, len(taps), side)
                        acc = part if acc is None else acc + part
                rows = pl.ds(pl.multiple_of(8 * t0, 16), 8 * R)
                acts[index, rows, h * LANES:(h + 1) * LANES] = acc.reshape(8 * R, LANES).astype(BF16)
            return c
        if between is None:
            steps_loop(R, body)
        else:
            cut = Q // R - 1
            lax.fori_loop(0, cut, lambda i, c: body(i * R, c), 0)
            between()
            lax.fori_loop(cut, Q // R, lambda i, c: body(i * R, c), 0)

    def half_lanes(values, h):
        return values[:, h * LANES:(h + 1) * LANES]

    def pointwise(index):
        pivot = [None] * plan.halves
        sums = [jnp.zeros((8, LANES), F32) for _ in HV]
        squares = [jnp.zeros((8, LANES), F32) for _ in HV]
        for t0 in range(0, Q, R):
            res = jnp.dot(acts[index, 8 * t0:8 * (t0 + R)], point[index], preferred_element_type=F32)
            v = valid[t0:t0 + R]
            for h in HV:
                p = half_lanes(res, h).reshape(R, 8, LANES)
                prods[index, h, t0:t0 + R] = p
                if t0 == 0:
                    pivot[h] = p[0, 0:1]
                d = p - row(pivot[h])
                dv = d * v
                sums[h] = sums[h] + accumulate(dv)
                squares[h] = squares[h] + accumulate(dv * d)
        n = jnp.full((1, LANES), count, F32)
        shift = [jnp.sum(sums[h], axis=0, keepdims=True) * inv_count for h in HV]
        spread = [jnp.sum(squares[h], axis=0, keepdims=True) - n * shift[h] * shift[h] for h in HV]
        return jnp.concatenate([pivot[h] + shift[h] for h in HV] + spread, axis=0)

    def activate(index, target):
        scales = [0.5 * stat_row(index, 2, h) for h in HV]
        offsets = [0.5 * stat_row(index, 3, h) for h in HV]

        def body(t0, c):
            v = valid[pl.ds(t0, RF)]
            for h in HV:
                u = prods[index, h, pl.ds(t0, RF)] * scales[h] + offsets[h]
                hid[target, h, pl.ds(HALO + t0, RF)] = (u + u * jnp.tanh(u)) * v
            return c
        steps_loop(RF, body)
        for h in HV:
            set_halo(hid.at[target], h)

    def hid_of(b, r):
        return b * SUB + r + 1

    def regular_taps(b):
        margin = (plan.taps[b] - 1) // 2
        return [(t, t - margin) for t in range(plan.taps[b])]

    def block_pieces(b):
        if b == 0:
            taps = regular_taps(0)
            even = [(t, s // 2) for t, s in taps if s % 2 == 0]
            odd = [(t, (s - 1) // 2) for t, s in taps if s % 2 == 1]
            return [(0, even), (1, odd)]
        return [(hid_of(1, 0), regular_taps(1))]

    def residual_forward(b):
        source = 0 if b == 0 else hid_of(1, 0)
        res = b * PER + SUB

        def body(t0, c):
            rows = pl.ds(pl.multiple_of(8 * t0, 16), 8 * R)
            for h in HV:
                values = hid[source, h, pl.ds(HALO + t0, R)].reshape(8 * R, LANES)
                acts[res, rows, h * LANES:(h + 1) * LANES] = values.astype(BF16)
            return c
        steps_loop(R, body)
        exchange(res, res, pointwise(res))

    def small(a, b, dims):
        return lax.dot_general(a, b, (dims, ((), ())), precision=HIGHEST, preferred_element_type=F32)

    def thin(a, matrix, dim):
        hi = a.astype(BF16).astype(F32)
        mid = (a - hi).astype(BF16).astype(F32)
        low = a - hi - mid
        rows = jnp.concatenate([hi, mid, low, jnp.zeros_like(a)], axis=0).astype(BF16)
        res = lax.dot_general(rows, matrix.astype(BF16), (((1,), (dim,)), ((), ())), preferred_element_type=F32)
        return res[0:2] + res[2:4] + res[4:6]

    def eight(values):
        return jnp.concatenate([values, jnp.zeros((6, values.shape[1]), F32)], axis=0)

    def whole_row(index, kind):
        return jnp.concatenate([stats[index, pl.ds(2 * kind + h, 1)] for h in HV], axis=1)

    def join(parts):
        return jnp.concatenate([jnp.sum(part, axis=0, keepdims=True) for part in parts], axis=1)

    half_count = [jnp.full((1, plan.channels), n, jnp.int32).astype(F32) for n in (half0, half1)]

    def utterance_sums(b):
        last = b * PER + SUB - 1

        def sums(t0, c):
            a = first_mask[pl.ds(t0, RF)]
            s = valid[pl.ds(t0, RF)] - a
            res = []
            for h in HV:
                p = prods[last, h, pl.ds(t0, RF)]
                res += [c[2 * h] + accumulate(p * a), c[2 * h + 1] + accumulate(p * s)]
            return tuple(res)
        tot = steps_loop(RF, sums, tuple(jnp.zeros((8, LANES), F32) for _ in range(2 * plan.halves)))
        for u in range(2):
            k.psum[b, u:u + 1] = join([tot[2 * h + u] for h in HV])

    def excite(b):
        last = b * PER + SUB - 1
        scale, offset = whole_row(last, 2), whole_row(last, 3)
        means = jnp.concatenate([scale * (k.psum[b, u:u + 1] / half_count[u]) + offset for u in range(2)], axis=0)
        inner = thin(means, squeeze_t[b], 1)
        excited = inner * sigmoid(inner)
        gate = sigmoid(thin(excited, expand[b], 0))
        return means, inner, excited, gate

    def tail_half(b, gate):
        last, res = b * PER + SUB - 1, b * PER + SUB
        consts = []
        for h in HV:
            g = [half_lanes(gate[u:u + 1], h) for u in range(2)]
            s1, o1, s2, o2 = [0.5 * stats[i, pl.ds(2 * kind + h, 1)] for i, kind in
                              ((last, 2), (last, 3), (res, 2), (res, 3))]
            consts.append([row(v) for v in (s1 * g[0], s1 * g[1], s2, o1 * g[0] + o2, o1 * g[1] + o2)])

        def get(t0, h):
            a0, a1, s2, b0, b1 = consts[h]
            a = first_mask[pl.ds(t0, RF)] > 0.5
            return (prods[last, h, pl.ds(t0, RF)] * jnp.where(a, a0, a1)
                    + prods[res, h, pl.ds(t0, RF)] * s2 + jnp.where(a, b0, b1))
        return get

    def tail(b, gate, store):
        get = tail_half(b, gate)

        def body(t0, c):
            v = valid[pl.ds(t0, RF)]
            for h in HV:
                u = get(t0, h)
                store(t0, h, (u + u * jnp.tanh(u)) * v)
            return c
        steps_loop(RF, body)

    def slope_of(u):
        t = jnp.tanh(u)
        return (0.5 * t + 0.5) * (1.0 + u - u * t)

    def tail_slope(b, gate):
        get = tail_half(b, gate)

        def body(t0, c):
            v = valid[pl.ds(t0, RF)]
            for h in HV:
                pre[b, h, pl.ds(t0, RF)] = slope_of(get(t0, h)) * v
            return c
        steps_loop(RF, body)

    def forward_aside(b, r, extras):
        if plan.fused:
            step = b * SUB + r

            @pl.when(step == 0)
            def _():
                gather_core(0, True)
                lead_core(1)
                gather_wait(0)
                lead_unpack(1)
                unpack_values(0)

            @pl.when(step == 1)
            def _():
                unpack_values(1)

            @pl.when(jnp.logical_and(step >= 1, step < PER))
            def _():
                gather_core(1 + step, False)
                gather_wait(1 + step)
                unpack_pair(step)

        @pl.when(r == SUB - 2)
        def _():
            residual_forward(b)

        @pl.when(r == SUB - 1)
        def _():
            utterance_sums(b)
        for when, extra in extras:
            pl.when(r == when)(extra)

    def forward_block(b, extras=()):
        def layer(r, pieces, before=None):
            index = b * PER + r
            first = before is not None
            layer_conv(index, pieces, (lambda: lead_core(0)) if first else None)
            if first:
                before()
            exchange(index, index, pointwise(index))
            forward_aside(b, r, extras)
            merge_stats(index, index)
            if plan.fused:
                step = b * SUB + r

                @pl.when(step < PER - 2)
                def _():
                    gather_z(3 + step)

                @pl.when(step < PER - 1)
                def _():
                    gather_plane(2 + step)

        def first_matrices():
            lead_unpack(0)
        layer(0, block_pieces(b), first_matrices if plan.fused and b == 0 else None)
        activate(b * PER, hid_of(b, 1))

        def rest(r, c):
            layer(r, [(hid_of(b, r), regular_taps(b))])

            @pl.when(r < SUB - 1)
            def _():
                activate(b * PER + r, hid_of(b, r + 1))
            return c
        lax.fori_loop(1, SUB, rest, 0)
        merge_stats(b * PER + SUB, b * PER + SUB)
        return excite(b)

    back_slot = 2 * PER

    def sum_rows(parts):
        return jnp.concatenate([jnp.sum(part, axis=0, keepdims=True) for part in parts], axis=0)

    def tail_back(b, kept, load):
        means, inner, excited, gate = kept
        last = b * PER + SUB - 1
        mean = [stat_row(last, 0, h) for h in HV]

        def first(t0, c):
            a = first_mask[pl.ds(t0, RF)]
            res = []
            for h in HV:
                gs = load(t0, h)
                pre[b, h, pl.ds(t0, RF)] = gs
                gx = gs * (prods[last, h, pl.ds(t0, RF)] - mean[h])
                res += [c[4 * h] + accumulate(gs * a), c[4 * h + 1] + accumulate(gs),
                        c[4 * h + 2] + accumulate(gx * a), c[4 * h + 3] + accumulate(gx)]
            return tuple(res)
        tot = steps_loop(RF, first, tuple(jnp.zeros((8, LANES), F32) for _ in range(4 * plan.halves)))
        s0, s_all, x0, x_all = [join([tot[4 * h + i] for h in HV]) for i in range(4)]
        gs_sum = (s0, s_all - s0)
        gx_sum = (x0, x_all - x0)
        mean_row, inv_row, scale_row = [whole_row(last, kind) for kind in range(3)]
        shift_row = jnp.concatenate([shifts[last, h:h + 1] for h in HV], axis=1)
        grad_gate = jnp.concatenate([scale_row * gx_sum[u] + shift_row * gs_sum[u] for u in range(2)], axis=0)
        grad_up = grad_gate * gate * (1.0 - gate)
        sg = sigmoid(inner)
        grad_inner = thin(grad_up, expand[b], 1) * (sg * (1.0 + inner * (1.0 - sg)))
        grad_means = thin(grad_inner, squeeze_t[b], 0)
        per_slot = [grad_means[u:u + 1] / half_count[u] for u in range(2)]
        sum1, sum2 = 0.0, 0.0
        for u in range(2):
            g = gate[u:u + 1]
            sum1 = sum1 + g * gs_sum[u] + grad_means[u:u + 1]
            sum2 = sum2 + g * gx_sum[u] + per_slot[u] * (k.psum[b, u:u + 1] - half_count[u] * mean_row)
        sum2 = sum2 * inv_row
        exchange(back_slot + last, back_place(last),
                 jnp.concatenate([half_lanes(v, h) for v in (sum1, sum2) for h in HV], axis=0))
        return grad_up, grad_inner, per_slot

    def tail_back_aside(b, kept, found):
        means, inner, excited, gate = kept
        grad_up, grad_inner, per_slot = found
        res = b * PER + SUB
        gates = [[row(half_lanes(gate[u:u + 1], h)) for h in HV] for u in range(2)]
        slots = [[row(half_lanes(per_slot[u], h)) for h in HV] for u in range(2)]
        norm = [(stat_row(res, 0, h), stats[res, pl.ds(2 + h, 1)]) for h in HV]

        def second(t0, c):
            a = first_mask[pl.ds(t0, RF)] > 0.5
            v = valid[pl.ds(t0, RF)]
            out_c = []
            for h in HV:
                gs = pre[b, h, pl.ds(t0, RF)]
                gz[h, pl.ds(t0, RF)] = (gs * jnp.where(a, gates[0][h], gates[1][h])
                                        + jnp.where(a, slots[0][h], slots[1][h]) * v)
                x = prods[res, h, pl.ds(t0, RF)] - norm[h][0]
                out_c += [c[2 * h] + accumulate(gs), c[2 * h + 1] + accumulate(gs * x)]
            return tuple(out_c)
        tot = steps_loop(RF, second, tuple(jnp.zeros((8, LANES), F32) for _ in range(2 * plan.halves)))
        sums = [jnp.sum(part, axis=0, keepdims=True) for part in tot]
        exchange(back_slot + res, back_place(res), jnp.concatenate(
            [sums[2 * h] for h in HV] + [sums[2 * h + 1] * norm[h][1] for h in HV], axis=0))
        k.expand_grad[b] = small(eight(excited), eight(grad_up), ((0,), (0,)))
        k.squeeze_grad[b] = small(eight(grad_inner), eight(means), ((0,), (0,)))

    def norm_back(index, load, target, store, then=None):
        sums = jnp.sum(received(back_slot + index, back_place(index)), axis=0)
        if then is not None:
            then()
        k.shifts_grad[index] = sums[0:2]
        k.gains_grad[index] = sums[2:4]
        inv_total = k.norm_count[0:2]
        st = stats[index]
        mean, inv, scale = st[0:2], st[2:4], st[4:6]
        k1 = scale * sums[0:2] * inv_total
        k2 = scale * sums[2:4] * inv_total * inv
        rows3 = [[row(value[h:h + 1]) for value in (mean, scale, k1, k2)] for h in HV]
        for t0 in range(0, Q, R):
            v = valid[t0:t0 + R]
            parts = []
            for h in HV:
                mean_h, scale_h, k1_h, k2_h = rows3[h]
                grad = scale_h * load(t0, h) - (k1_h + k2_h * (prods[index, h, t0:t0 + R] - mean_h)) * v
                parts.append(grad.reshape(8 * R, LANES).astype(BF16))
            both = jnp.concatenate(parts, axis=1)
            target[8 * t0:8 * (t0 + R)] = both
            if plan.fused:
                res = jnp.dot(both, k.point_t[index], preferred_element_type=F32)
            else:
                res = lax.dot_general(both, point[index], (((1,), (1,)), ((), ())), preferred_element_type=F32)
            for h in HV:
                store(t0, h, half_lanes(res, h).reshape(R, 8, LANES))

    def point_back(index, source):
        place = lax.rem(index, 2) if plan.fused else index
        k.point_grad[place] = lax.dot_general(acts[index], source[...], (((0,), (0,)), ((), ())),
                                              preferred_element_type=F32)

    def store_gd(t0, h, values):
        gd[h, HALO + t0:HALO + t0 + R] = values

    def store_skip(t0, h, values):
        k.skip[h, t0:t0 + R] = values

    def conv_back_block(t0, h, index, taps):
        low, high = -taps[-1][1], -taps[0][1]
        win = gd[h, pl.ds(t0 + HALO + low, R + high - low)]
        if len(taps) >= plan.taps[0]:
            return all_taps(win, index, h, len(taps), 1)
        return direct(win, low, index, h, [(t, -shift) for t, shift in taps])

    def kernel_back(index, pieces):
        for source, taps in pieces:
            for h in HV:
                low = min(s for _, s in taps)
                high = max(s for _, s in taps)

                def body(t0, c):
                    g = gd[h, pl.ds(HALO + t0, RF)]
                    win = hid[source, h, pl.ds(t0 + HALO + low, RF + high - low)]
                    return tuple(acc + accumulate(g * win[s - low:s - low + RF]) for acc, (_, s) in zip(c, taps))
                def paired_body(t0, c):
                    g = gd[h, pl.ds(HALO + t0, RF)].reshape(RF // 2, 2, 8, LANES)
                    win = hid[source, h, pl.ds(t0 + HALO + low, RF + high - low)]
                    if win.shape[0] % 2:
                        win = jnp.concatenate([win, win[-1:]], axis=0)
                    x = win.reshape(-1, 2, 8, LANES)
                    g0, g1, x0, x1 = g[:, 0], g[:, 1], x[:, 0], x[:, 1]
                    n, even, odd = RF // 2, (len(taps) + 1) // 2, len(taps) // 2
                    both = x0[:n + even - 1] + x1[:n + even - 1]
                    late = x0[1:n + odd] + x1[:n + odd - 1]
                    gap = g0 - g1
                    new = ([accumulate(g0 * both[i:i + n]) for i in range(even)]
                           + [accumulate(gap * x1[i:i + n]) for i in range(even)]
                           + [accumulate(g1 * late[i:i + n]) for i in range(odd)])
                    return tuple(acc + value for acc, value in zip(c, new))
                if len(taps) < plan.taps[0]:
                    even, odd = (len(taps) + 1) // 2, len(taps) // 2
                    parts = steps_loop(RF, paired_body, tuple(
                        jnp.zeros((8, LANES), F32) for _ in range(2 * even + odd)))
                    accs = [parts[2 * even + i // 2] + parts[even + i // 2] if i % 2
                            else parts[i // 2] - parts[even + i // 2] for i in range(len(taps))]
                else:
                    accs = steps_loop(RF, body, tuple(jnp.zeros((8, LANES), F32) for _ in taps))
                for acc, (tap, _) in zip(accs, taps):
                    k.dw_grad[index, h, pl.ds(tap, 1)] = jnp.sum(acc, axis=0, keepdims=True)

    def slopes(index):
        scales = [0.5 * stat_row(index, 2, h) for h in HV]
        offsets = [0.5 * stat_row(index, 3, h) for h in HV]

        def body(t0, c):
            v = valid[pl.ds(t0, RF)]
            for h in HV:
                k.slope[h, pl.ds(t0, RF)] = slope_of(prods[index, h, pl.ds(t0, RF)] * scales[h] + offsets[h]) * v
            return c
        steps_loop(RF, body)

    def hidden_back(index, taps):
        before = index - 1
        mean = [stat_row(before, 0, h) for h in HV]

        def body(t0, c):
            res = []
            for h in HV:
                grad = conv_back_block(t0, h, index, taps) * k.slope[h, pl.ds(t0, R)]
                gz[h, pl.ds(t0, R)] = grad
                gx = grad * (prods[before, h, pl.ds(t0, R)] - mean[h])
                res += [c[2 * h] + accumulate(grad), c[2 * h + 1] + accumulate(gx)]
            return tuple(res)
        tot = steps_loop(R, body, tuple(jnp.zeros((8, LANES), F32) for _ in range(2 * plan.halves)))
        sums = [jnp.sum(part, axis=0, keepdims=True) for part in tot]
        exchange(back_slot + before, back_place(before), jnp.concatenate(
            [sums[2 * h] for h in HV] + [sums[2 * h + 1] * stats[before, pl.ds(2 + h, 1)] for h in HV], axis=0))

    def load_gz(t0, h):
        return gz[h, t0:t0 + R]

    def scatter_start(unit, place):
        remote(k.shares.at[place, :, :, 1 - core], k.inbox.at[unit], 6, unit, partner)

    def scatter_sum(unit, place):
        blocks_wait(chips, 7, unit)
        blocks_wait(chips, 6, unit)
        slot = lax.rem(unit, 3)
        k.sums[slot] = (k.shares[place, :, :, core].astype(F32) + k.inbox[unit].astype(F32)).astype(BF16)

    def scatter_send(unit):
        slot = lax.rem(unit, 3)
        k.gained[unit, chip] = k.sums[slot, depth, plane]
        for peer in same_core:
            remote(k.sums.at[slot, peer // 8, lax.rem(peer // 2, 4)], k.gained.at[unit, chip], 8, unit, peer)

    def scatter_finish(unit):
        blocks_wait(chips - 1, 9, unit)
        return jnp.sum(k.gained[unit].astype(F32), axis=0)

    def scatter_plane(unit):
        slot = lax.rem(unit, 3)
        k.by_plane[unit, plane] = k.sums[slot, :, plane]
        for d in (3, 2, 1):
            there = lax.rem(plane + d, 4)
            remote(k.sums.at[slot, :, there], k.by_plane.at[unit, plane], 8, unit, in_plane(d))

    def scatter_mid(unit):
        blocks_wait(12, 9, unit)
        blocks_wait(12, 8, unit)
        k.line[unit] = jnp.sum(k.by_plane[unit].astype(F32), axis=0).astype(BF16)
        k.by_depth[unit, depth] = k.line[unit, depth]

    def scatter_z(unit):
        for d in (2, 1, 3):
            there = lax.rem(depth + d, 4)
            remote(k.line.at[unit, there], k.by_depth.at[unit, depth], 10, unit, at_depth(d))

    def scatter_end(unit):
        blocks_wait(3, 11, unit)
        return jnp.sum(k.by_depth[unit].astype(F32), axis=0)

    def pair_start(pair):
        both = [k.point_grad[side].reshape(N, 8, plan.channels) for side in range(2)]
        k.shares[0] = jnp.concatenate(both, axis=1).astype(BF16).reshape(4, 4, 2, 16, plan.channels)
        scatter_start(1 + pair, 0)

    def pair_finish(pair, straight=False):
        total = scatter_finish(1 + pair) if straight else scatter_end(1 + pair)
        b = pair // (PER // 2)
        r = 2 * lax.rem(pair, PER // 2)
        k.point_out[b, r] = total[0:8]
        k.point_out[b, r + 1] = total[8:16]

    def last_start():
        k.packed[0:LANES] = jnp.zeros((LANES, LANES), F32)
        columns = []
        for h in HV:
            k.packed[0:plan.tap_rows] = k.dw_grad[0, h]
            columns.append(jnp.transpose(k.packed[0:LANES]))
        whole = jnp.concatenate(columns, axis=0)
        moved = pltpu.roll(whole, plan.tap_rows, 1).reshape(N, 8, LANES)
        k.last_mine[...] = whole.reshape(N, 8, LANES)[:, 0:4] + moved[:, 4:8]
        k.last[me] = k.last_mine[me]
        for peer in peers:
            pltpu.make_async_remote_copy(src_ref=k.last_mine.at[peer], dst_ref=k.last.at[me],
                                         send_sem=k.last_sems.at[0], recv_sem=k.last_sems.at[1],
                                         device_id=(peer,), device_id_type=MESH).start()

    def last_finish():
        wait_all(k.last, k.last_sems.at[1])
        total = jnp.sum(k.last[...], axis=0)
        both = jnp.concatenate([total, pltpu.roll(jnp.concatenate([total, total], axis=0),
                                                  LANES - plan.tap_rows, 1)[0:4]], axis=0)
        k.dw_first_out[0] = both[:, 0:plan.taps[0]]

    def values_start():
        k.packed[...] = jnp.zeros((plan.values, LANES), F32)
        blocks = []
        for b in range(2):
            columns = []
            for h in HV:
                for r in range(1 - b, SUB):
                    k.packed[plan.tap_row(r):plan.tap_row(r) + plan.tap_rows] = k.dw_grad[b * PER + r, h]
                lanes = slice(h * LANES, (h + 1) * LANES)
                k.packed[EXPAND_ROW:EXPAND_ROW + plan.hidden] = k.expand_grad[b, :, lanes]
                k.packed[SQUEEZE_ROW:SQUEEZE_ROW + plan.hidden] = k.squeeze_grad[b, :, lanes]
                columns.append(jnp.concatenate(
                    [jnp.transpose(k.packed[t * LANES:(t + 1) * LANES]) for t in range(2)], axis=1))
            blocks.append(jnp.concatenate(columns, axis=0).reshape(N, 8, plan.values))
        k.shares[1] = jnp.concatenate(blocks, axis=1).astype(BF16).reshape(4, 4, 2, 16, plan.values)
        scatter_start(0, 1)

    def values_finish():
        total = scatter_finish(0)
        for b in range(2):
            rows = total[8 * b:8 * b + 8]

            def lanes(start, size):
                tile, lane = divmod(start, LANES)
                part = rows[:, tile * LANES:(tile + 1) * LANES]
                return (pltpu.roll(part, LANES - lane, 1) if lane else part)[:, 0:size]
            dw_out = (k.dw_first_out, k.dw_second_out)[b]
            for r in range(1 - b, SUB):
                dw_out[r] = lanes(plan.tap_row(r), plan.taps[b])
            k.squeeze_out[b] = lanes(SQUEEZE_ROW, plan.hidden)
            k.expand_out[b] = lanes(EXPAND_ROW, plan.hidden)

    def own_norms():
        mine = pl.ds(pl.multiple_of(me * 8, 8), 8)
        k.packed[0:LANES] = jnp.zeros((LANES, LANES), F32)
        for h in HV:
            for b in range(2):
                for r in range(PER):
                    k.packed[16 * b + r:16 * b + r + 1] = k.gains_grad[b * PER + r, h:h + 1]
                    k.packed[16 * b + 8 + r:16 * b + 9 + r] = k.shifts_grad[b * PER + r, h:h + 1]
            k.own_norm[h * LANES:(h + 1) * LANES] = jnp.transpose(k.packed[0:LANES])
        k.packed[0:LANES] = jnp.transpose(
            jnp.concatenate([k.own_norm[mine], jnp.zeros((LANES - 8, LANES), F32)], axis=0))
        for b in range(2):
            for r in range(PER):
                k.gains_out[r, b:b + 1] = k.packed[16 * b + r:16 * b + r + 1, 0:8]
                k.shifts_out[r, b:b + 1] = k.packed[16 * b + 8 + r:16 * b + 9 + r, 0:8]

    HALF = PER // 2

    def backward_aside(b, r):
        index = b * PER + r
        if plan.fused:
            if b == 0:
                @pl.when(r == SUB - 1)
                def _():
                    scatter_sum(1 + HALF, 0)

            @pl.when(lax.rem(r, 2) == 1)
            def _():
                scatter_sum(1 + HALF * b + (r + 1) // 2, 0)
        point_back(index, gpb)

        @pl.when(r == SUB - 1)
        def _():
            res = b * PER + SUB
            norm_back(res, lambda t0, h: pre[b, h, t0:t0 + R], gqb, store_skip)
            point_back(res, gqb)
        if plan.fused:
            @pl.when(lax.rem(r, 2) == 0)
            def _():
                pair_start(HALF * b + r // 2)

    def backward_late(b, r):
        if not plan.fused:
            return
        if b == 0:
            @pl.when(r == SUB - 1)
            def _():
                pair_finish(HALF + 1)

            @pl.when(r == SUB - 2)
            def _():
                scatter_mid(1 + HALF)

            @pl.when(r == SUB - 3)
            def _():
                pair_finish(HALF)

        @pl.when(jnp.logical_or(r == 2, r == 0))
        def _():
            scatter_mid(1 + HALF * b + r // 2 + 1)

        @pl.when(r == 1)
        def _():
            pair_finish(HALF * b + 2)

    def backward_block(b):
        def go(r):
            if plan.fused:
                @pl.when(jnp.logical_or(r == 2, r == 0))
                def _():
                    scatter_plane(1 + HALF * b + r // 2 + 1)

                @pl.when(r == 1)
                def _():
                    scatter_z(1 + HALF * b + 2)
                if b == 0:
                    @pl.when(r == SUB - 1)
                    def _():
                        scatter_z(1 + HALF + 1)

                    @pl.when(r == SUB - 2)
                    def _():
                        scatter_plane(1 + HALF)

                    @pl.when(r == SUB - 3)
                    def _():
                        scatter_z(1 + HALF)

        def filtered(r):
            norm_back(b * PER + r, load_gz, gpb, store_gd, lambda: go(r))
            for h in HV:
                set_halo(gd, h)

        def step(j, c):
            r = SUB - 1 - j
            index = b * PER + r
            filtered(r)
            hidden_back(index, regular_taps(b))
            backward_aside(b, r)
            kernel_back(index, [(hid_of(b, r), regular_taps(b))])

            @pl.when(r >= 2)
            def _():
                slopes(index - 2)
            backward_late(b, r)
            return c
        lax.fori_loop(0, SUB - 1, step, 0)
        if plan.fused and b == 0:
            values_start()
        filtered(0)

    if plan.fused:
        wait_all(k.first, count_sems.at[1])
        unpack_first()
    else:
        wait_all(counts, count_sems.at[1])
        dw[...] = k.dw_in[...]
        for b in range(2):
            for r in range(SUB):
                for h in HV:
                    split_taps(b, r, h)
    count_slots()
    kept_first = forward_block(0)

    def store_middle(t0, h, values):
        hid[hid_of(1, 0), h, pl.ds(HALO + t0, RF)] = values
    tail(0, kept_first[3], store_middle)
    for h in HV:
        set_halo(hid.at[hid_of(1, 0)], h)

    def place_cot():
        load_cot.wait()
        for h in HV:
            flat[h, 0:GAP] = jnp.zeros((GAP, LANES), F32)
            flat[h, GAP + plan.slots:] = jnp.zeros((flat.shape[1] - GAP - plan.slots, LANES), F32)

        def place(i, c):
            rows = pl.ds(pl.multiple_of(i * 128, 128), 128)
            for h in HV:
                flat[h, pl.ds(pl.multiple_of(i * 128 + GAP, 16), 128)] = k.cot_v[rows, h * LANES:(h + 1) * LANES]
            return c
        lax.fori_loop(0, plan.slots // 128, place, 0)

        def pick(t0, c):
            for h in HV:
                for j in range(RF):
                    here = flat[h, pl.ds(t0 + j + GAP, 8, stride=Q)]
                    moved = flat[h, pl.ds(t0 + j, 8, stride=Q)]
                    gz[h, t0 + j] = jnp.where(first_mask[t0 + j] > 0.5, here, moved)
            return c
        steps_loop(RF, pick)
    kept_second = forward_block(1, ((0, lambda: tail_slope(0, kept_first[3])), (1, place_cot)))

    last_half = tail_half(1, kept_second[3])

    def load_last(t0, h):
        return gz[h, pl.ds(t0, RF)] * (slope_of(last_half(t0, h)) * valid[pl.ds(t0, RF)])
    found = tail_back(1, kept_second, load_last)

    def store_out(t0, h, values):
        for j in range(RF):
            flat[h, pl.ds(t0 + j, 8, stride=Q)] = values[j]

    def ungap(i, c):
        rows = pl.ds(pl.multiple_of(i * 128, 128), 128)
        slot = i * 128 + lax.broadcasted_iota(jnp.int32, (128, LANES), 0)
        for h in HV:
            moved = flat[h, pl.ds(pl.multiple_of(i * 128 + GAP, 16), 128)]
            k.cot_v[rows, h * LANES:(h + 1) * LANES] = jnp.where(slot < half0, flat[h, rows], moved)
        return c
    tail_back_aside(1, kept_second, found)
    slopes(PER + SUB - 2)
    tail(1, kept_second[3], store_out)
    lax.fori_loop(0, plan.slots // 128, ungap, 0)
    save_out.start()
    backward_block(1)

    def sum_back(t0, c):
        for h in HV:
            gz[h, pl.ds(t0, R)] = conv_back_block(t0, h, PER, regular_taps(1)) + k.skip[h, pl.ds(t0, R)]
        return c
    steps_loop(R, sum_back)
    found = tail_back(0, kept_first, lambda t0, h: gz[h, pl.ds(t0, RF)] * pre[0, h, pl.ds(t0, RF)])
    tail_back_aside(0, kept_first, found)
    slopes(SUB - 2)
    backward_aside(1, 0)
    kernel_back(PER, [(hid_of(1, 0), regular_taps(1))])
    backward_late(1, 0)
    backward_block(0)
    pieces = block_pieces(0)
    backward_aside(0, 0)
    if plan.fused:
        scatter_sum(0, 1)
        scatter_send(0)
    kernel_back(0, pieces)
    if plan.fused:
        last_start()
        scatter_sum(1, 0)
        scatter_send(1)
        backward_late(0, 0)
        scatter_z(2)
        own_norms()

    def spread(t0, c):
        v = valid[pl.ds(t0, R)]
        for h in HV:
            even = (conv_back_block(t0, h, 0, pieces[0][1]) + k.skip[h, pl.ds(t0, R)]) * v
            odd = conv_back_block(t0, h, 0, pieces[1][1]) * v
            for j in range(R):
                wide[h, pl.ds(2 * (t0 + j), 8, stride=2 * Q)] = even[j]
                wide[h, pl.ds(2 * (t0 + j) + 1, 8, stride=2 * Q)] = odd[j]
        return c
    steps_loop(R, spread)

    def ungap_wide(i, c):
        rows = pl.ds(pl.multiple_of(i * 128, 128), 128)
        slot = i * 128 + lax.broadcasted_iota(jnp.int32, (128, LANES), 0)
        for h in HV:
            moved = wide[h, pl.ds(pl.multiple_of(i * 128 + 2 * GAP, 32), 128)]
            k.frames_grad_v[lax.rem(i, 2 * per_piece), :, h * LANES:(h + 1) * LANES] = jnp.where(
                slot < len0, wide[h, rows], moved)
        return c
    pieces_out = 8
    per_piece = 2 * plan.slots // pieces_out // 128
    save_frames = []
    for piece in range(pieces_out):
        if piece >= 2:
            save_frames[piece - 2].wait()
        lax.fori_loop(piece * per_piece, (piece + 1) * per_piece, ungap_wide, 0)
        save_frames.append(pltpu.make_async_copy(
            k.frames_grad_v.at[pl.ds((piece % 2) * per_piece, per_piece)],
            k.frames_grad.at[pl.ds(piece * per_piece, per_piece)], k.io_sems.at[3 + piece]))
        save_frames[-1].start()
    if plan.fused:
        pair_finish(1)
        values_finish()
        pair_finish(0, True)
        last_finish()

    save_out.wait()
    for copy in save_frames[-2:]:
        copy.wait()
    wait_all(k.first if plan.fused else counts, count_sems.at[0])

    def drain(slot, c):
        wait_all(recv4.at[0], send_sem.at[slot])
        return c
    lax.fori_loop(0, send4.shape[0], drain, 0)
    if plan.fused:
        for unit in range(1 + PER):
            if unit != 1:
                blocks_wait(chips - 1 if unit < 2 else 3, 0, unit)
                blocks_wait(chips, 4, unit)
            if unit >= 2:
                blocks_wait(12, 2, unit)
                blocks_wait(3, 10, unit)
            else:
                blocks_wait(chips - 1, 8, unit)
        for side in range(2):
            lead_wait(chips - 1, 0, side)
            lead_wait(chips, 2, side)
        wait_all(k.last, k.last_sems.at[0])


def call_kernel(plan, inputs):
    layers, halves, Q, channels = plan.layers, plan.halves, plan.steps, plan.channels
    vals, shard, hidden, devices = plan.values, plan.shard, plan.hidden, plan.devices
    vmem = pl.BlockSpec(memory_space=pltpu.VMEM)
    anywhere = pl.BlockSpec(memory_space=pl.ANY)
    places = {"lens": pl.BlockSpec(memory_space=pltpu.SMEM), "frames": anywhere, "cot": anywhere,
              "out": anywhere, "frames_grad": anywhere}
    slots = 2 * layers

    def shape(*dims, dtype=F32):
        return jax.ShapeDtypeStruct(dims, dtype)
    outs = {
        "out": shape(plan.slots, channels),
        "frames_grad": shape(2 * plan.slots // 128, 128, channels),
    }
    params = {
        "dw": shape(layers, halves, plan.dw_rows, LANES),
        "point": shape(layers, channels, channels, dtype=BF16),
        "gains": shape(layers, halves, LANES),
        "shifts": shape(layers, halves, LANES),
        "squeeze_t": shape(2, hidden, channels),
        "expand": shape(2, hidden, channels),
    }
    grads = {
        "dw_grad": shape(layers, halves, plan.tap_rows, LANES),
        "point_grad": shape(2 if plan.fused else layers, channels, channels),
        "gains_grad": shape(layers, halves, LANES),
        "shifts_grad": shape(layers, halves, LANES),
        "squeeze_grad": shape(2, hidden, channels),
        "expand_grad": shape(2, hidden, channels),
    }
    scratch = {
        "hid": shape(2 * plan.sub + 1, halves, plan.pad, 8, LANES),
        "acts": shape(layers, plan.rows, channels, dtype=BF16),
        "prods": shape(layers, halves, Q, 8, LANES),
        "gd": shape(halves, plan.pad, 8, LANES),
        "gz": shape(halves, Q, 8, LANES),
        "gpb": shape(plan.rows, channels, dtype=BF16),
        "gqb": shape(plan.rows, channels, dtype=BF16),
        "pre": shape(2, halves, Q, 8, LANES),
        "wide": shape(halves, 2 * plan.slots + 4 * GAP, LANES),
        "frames_v": shape(2 * plan.slots, channels, dtype=BF16),
        "cot_v": shape(plan.slots, channels),
        "frames_grad_v": shape(plan.slots // 256, 128, channels),
        "first_mask": shape(Q, 8, LANES),
        "valid": shape(Q, 8, LANES),
        "slope": shape(halves, Q, 8, LANES),
        "skip": shape(halves, Q, 8, LANES),
        "psum": shape(2, 8, channels),
        "stats": shape(layers, 8, LANES),
        "send4": shape(slots, 4, LANES),
        "recv4": shape(layers, devices, 4, LANES),
        "counts": shape(devices, 4, LANES),
        "csend": shape(4, LANES),
        "norm_count": shape(4, LANES),
    }
    sems = {"send_sem": (slots,), "recv_sem": (slots,), "count_sems": (2,), "io_sems": (11,)}
    if plan.fused:
        units, chips = 1 + plan.per, devices // 2
        outs.update({
            "dw_first_out": shape(plan.sub, shard, plan.taps[0]),
            "dw_second_out": shape(plan.sub, shard, plan.taps[1]),
            "point_out": shape(2, plan.per, shard, channels),
            "gains_out": shape(plan.per, 2, shard),
            "shifts_out": shape(plan.per, 2, shard),
            "squeeze_out": shape(2, shard, hidden),
            "expand_out": shape(2, shard, hidden),
        })
        scratch.update(params)
        scratch.update(grads)
        scratch.update({
            "tile": shape(8, LANES),
            "point_t": shape(layers, channels, channels, dtype=BF16),
            "packed": shape(vals, LANES),
            "packed_t": shape(16, vals),
            "first": shape(devices, 4, LANES),
            "last_mine": shape(devices, 4, LANES),
            "last": shape(devices, 4, LANES),
            "unpacked": shape(vals, LANES),
            "gath": shape(units, 4, 4, 2, 16, channels, dtype=BF16),
            "lead": shape(2, 4, 4, 2, 16, LANES, dtype=BF16),
            "shares": shape(2, 4, 4, 2, 16, channels, dtype=BF16),
            "inbox": shape(units, 4, 4, 16, channels, dtype=BF16),
            "sums": shape(3, 4, 4, 16, channels, dtype=BF16),
            "gained": shape(2, chips, 16, channels, dtype=BF16),
            "by_plane": shape(units, 4, 4, 16, channels, dtype=BF16),
            "line": shape(units, 4, 16, channels, dtype=BF16),
            "by_depth": shape(units, 4, 16, channels, dtype=BF16),
            "own_norm": shape(channels, LANES),
        })
        sems["unit_sems"] = (12, units)
        sems["last_sems"] = (2,)
        sems["lead_sems"] = (4, 2)
        sems["param_sems"] = (len(PARAMS),)
        for name in PARAMS:
            scratch[name + "_v"] = inputs[name]
            places[name] = anywhere
    else:
        outs.update(grads)
        scratch["dw"] = params["dw"]
    names = list(inputs) + list(outs) + list(scratch) + list(sems)
    results = pl.pallas_call(
        functools.partial(kernel, plan, names),
        out_shape=list(outs.values()),
        in_specs=[places.get(name, vmem) for name in inputs],
        out_specs=[places.get(name, vmem) for name in outs],
        scratch_shapes=[pltpu.VMEM(v.shape, v.dtype) for v in scratch.values()]
        + [pltpu.SemaphoreType.DMA(v) for v in sems.values()],
        compiler_params=pltpu.CompilerParams(
            collective_id=0, has_side_effects=True, vmem_limit_bytes=63 * 1024 * 1024),
    )(*inputs.values())
    if plan.fused:
        results = hand_on(results)
    return dict(zip(outs, results, strict=True))


def hand_on(arrays):
    n = len(arrays)
    parts = []
    for i, v in enumerate(arrays):
        rows = max(1, v.shape[0] * (1 << 20) // (4 * v.size))
        parts += [(i, start, min(rows, v.shape[0] - start)) for start in range(0, v.shape[0], rows)]

    def move(*refs):
        here, there, held, sems = refs[:n], refs[n:2 * n], refs[2 * n:3 * n], refs[3 * n]
        into, out = [], []
        for p, (i, start, size) in enumerate(parts):
            rows = pl.ds(start, size)
            into.append(pltpu.make_async_copy(here[i].at[rows], held[i].at[rows], sems.at[0, p]))
            out.append(pltpu.make_async_copy(held[i].at[rows], there[i].at[rows], sems.at[1, p]))
        for copy in into:
            copy.start()
        for p in range(len(parts)):
            into[p].wait()
            out[p].start()
        for copy in out:
            copy.wait()
    anywhere = pl.BlockSpec(memory_space=pl.ANY)
    return pl.pallas_call(
        move,
        out_shape=[jax.ShapeDtypeStruct(v.shape, v.dtype) for v in arrays],
        in_specs=[anywhere] * n,
        out_specs=[anywhere] * n,
        scratch_shapes=[pltpu.VMEM(v.shape, v.dtype) for v in arrays] + [pltpu.SemaphoreType.DMA((2, len(parts)))],
    )(*arrays)


def body(frames, dw_first, dw_second, point, gains, shifts, se_down, se_up, cotangent, lengths, *, devices):
    sub, taps_first, shard = dw_first.shape
    taps_second = dw_second.shape[1]
    hidden = se_down.shape[2]
    channels = point.shape[3]
    plan = Plan(cotangent.shape[0], channels, taps_first, taps_second, sub, hidden, devices)
    if plan.fused:
        res = call_kernel(plan, {
            "lens": lengths, "frames": frames, "cot": cotangent,
            "dw_first": jnp.swapaxes(dw_first, 1, 2), "dw_second": jnp.swapaxes(dw_second, 1, 2),
            "point_in": point, "gains_in": jnp.swapaxes(gains, 0, 1), "shifts_in": jnp.swapaxes(shifts, 0, 1),
            "se_down": se_down, "se_up": jnp.swapaxes(se_up, 1, 2)})
        return (
            res["out"], res["frames_grad"].reshape(2 * plan.slots, channels), jnp.swapaxes(res["dw_first_out"], 1, 2),
            jnp.swapaxes(res["dw_second_out"], 1, 2), res["point_out"], jnp.swapaxes(res["gains_out"], 0, 1),
            jnp.swapaxes(res["shifts_out"], 0, 1), res["squeeze_out"], jnp.swapaxes(res["expand_out"], 1, 2))

    per, layers, halves = plan.per, plan.layers, plan.halves

    def gather(v, axis):
        return lax.all_gather(v, "dp", axis=axis, tiled=True)
    small = jnp.concatenate([
        dw_first.reshape(-1, shard), dw_second.reshape(-1, shard), gains.reshape(-1, shard),
        shifts.reshape(-1, shard), se_up.reshape(-1, shard),
        jnp.swapaxes(se_down, 1, 2).reshape(-1, shard)], axis=0)
    small = gather(small, 1).astype(F32)
    sizes = [sub * taps_first, sub * taps_second, layers, layers, 2 * hidden, 2 * hidden]
    part = jnp.split(small, [sum(sizes[:i]) for i in range(1, 6)], axis=0)

    def dw_layout(v, taps):
        v = v.reshape(sub, taps, halves, LANES).transpose(0, 2, 1, 3)
        return jnp.pad(v, ((0, 1), (0, 0), (0, plan.dw_rows - taps), (0, 0)))
    res = call_kernel(plan, {
        "lens": lengths, "frames": frames, "cot": cotangent,
        "dw_in": jnp.concatenate([dw_layout(part[0], taps_first), dw_layout(part[1], taps_second)], axis=0),
        "point": gather(point, 2).reshape(layers, channels, channels),
        "gains": part[2].reshape(layers, halves, LANES),
        "shifts": part[3].reshape(layers, halves, LANES),
        "squeeze_t": part[5].reshape(2, hidden, channels),
        "expand": part[4].reshape(2, hidden, channels)})

    def scatter(v, axis):
        return lax.psum_scatter(v, "dp", scatter_dimension=axis, tiled=True)

    def dw_out(v, taps):
        return v[:sub, :, :taps].transpose(0, 2, 1, 3).reshape(sub * taps, channels)
    grads = res["dw_grad"]
    packed = scatter(jnp.concatenate(
        [dw_out(grads[:per], taps_first), dw_out(grads[per:], taps_second),
         res["squeeze_grad"].reshape(-1, channels), res["expand_grad"].reshape(-1, channels)], axis=0), 1)
    g1, g2, gsq, gex = jnp.split(packed, [sizes[0], sizes[0] + sizes[1], sizes[0] + sizes[1] + sizes[5]], axis=0)

    def norm_out(v):
        return lax.dynamic_slice_in_dim(v.reshape(2, per, channels), lax.axis_index("dp") * shard, shard, 2)
    return (
        res["out"], res["frames_grad"].reshape(2 * plan.slots, channels), g1.reshape(sub, taps_first, shard), g2.reshape(sub, taps_second, shard),
        scatter(res["point_grad"].reshape(2, per, channels, channels), 2),
        norm_out(res["gains_grad"]), norm_out(res["shifts_grad"]),
        jnp.swapaxes(gsq.reshape(2, hidden, shard), 1, 2), gex.reshape(2, hidden, shard))


def solution(mesh):
    return jax.shard_map(
        functools.partial(body, devices=mesh.shape["dp"]),
        mesh=mesh,
        in_specs=(
            P("dp", None),
            P(None, None, "dp"),
            P(None, None, "dp"),
            P(None, None, "dp", None),
            P(None, None, "dp"),
            P(None, None, "dp"),
            P(None, "dp", None),
            P(None, None, "dp"),
            P("dp", None),
            P("dp"),
        ),
        out_specs=(
            P("dp", None),
            P("dp", None),
            P(None, None, "dp"),
            P(None, None, "dp"),
            P(None, None, "dp", None),
            P(None, None, "dp"),
            P(None, None, "dp"),
            P(None, "dp", None),
            P(None, None, "dp"),
        ),
        check_vma=False,
    )
```

```python
import functools

import jax
import jax.numpy as jnp
from jax import lax
from jax.experimental import pallas as pl
from jax.experimental.pallas import tpu as pltpu
from jax.sharding import PartitionSpec as P

EPSILON = 1e-05
HIGHEST = lax.Precision.HIGHEST
F32 = jnp.float32
BF16 = jnp.bfloat16
MESH = pl.DeviceIdType.MESH

GAP = 32
HALO = 13
LANES = 128


def sigmoid(v):
    return 0.5 * jnp.tanh(0.5 * v) + 0.5


class Plan:
    def __init__(self, slots, channels, taps_first, taps_second, sub_blocks, hidden, devices):
        self.slots = slots
        self.steps = (slots + GAP) // 8
        self.rows = 8 * self.steps
        self.channels = channels
        self.halves = channels // LANES
        self.taps = (taps_first, taps_second)
        self.max_taps = max(self.taps)
        self.sub = sub_blocks
        self.hidden = hidden
        self.devices = devices
        self.block = next(r for r in (44, 12, 4) if self.steps % r == 0)
        self.fine = next(r for r in (22, 12, 4) if self.steps % r == 0)
        self.pad = self.steps + 2 * HALO
        self.per = sub_blocks + 1
        self.layers = 2 * self.per
        self.tap_rows = 32
        self.tap_sets = (32, 104)
        self.dw_rows = 176
        self.values = 2 * LANES
        self.shard = channels // devices
        self.fused = self.shard == 8 and devices == 32 and sub_blocks == 5 and hidden == 32 and self.max_taps <= 32

    def tap_row(self, r):
        return r * self.tap_rows + self.tap_rows * (r // 4)


SQUEEZE_ROW, EXPAND_ROW, GAIN_ROW, SHIFT_ROW = 128, 192, 224, 232


PARAMS = ("dw_first", "dw_second", "point_in", "gains_in", "shifts_in", "se_down", "se_up")


class Refs:
    def __init__(self, names, refs):
        for name, ref in zip(names, refs, strict=True):
            setattr(self, name, ref)


def peers_of(me, n):
    if n != 32:
        return [lax.rem(me + k, n) for k in range(1, n)]
    core = lax.rem(me, 2)
    x = lax.rem(me // 2, 2)
    y = lax.rem(me // 4, 2)
    z = me // 8
    found = []
    for order, other in enumerate((3 - z, lax.rem(z + 2, 4), z + 1 - 2 * lax.rem(z, 2), z)):
        for dy in (1, 0):
            for dx in (1, 0):
                for dc in (0, 1):
                    if order == 3 and dy == 0 and dx == 0 and dc == 0:
                        continue
                    oy = lax.rem(y + dy, 2)
                    ox = lax.rem(x + dx, 2)
                    oc = lax.rem(core + dc, 2)
                    found.append((dy + dx + (3, 2, 1, 0)[order], other * 8 + oy * 4 + ox * 2 + oc))
    found.sort(key=lambda item: -item[0])
    return [item[1] for item in found]


def same_core_peers(me, n):
    if n != 32:
        return [lax.rem(me + 2 * k, n) for k in range(1, n // 2)]
    core = lax.rem(me, 2)
    x = lax.rem(me // 2, 2)
    y = lax.rem(me // 4, 2)
    z = me // 8
    found = []
    for order, other in enumerate((3 - z, lax.rem(z + 2, 4), z + 1 - 2 * lax.rem(z, 2), z)):
        for dy in (1, 0):
            for dx in (1, 0):
                if order == 3 and dy == 0 and dx == 0:
                    continue
                oy = lax.rem(y + dy, 2)
                ox = lax.rem(x + dx, 2)
                found.append((dy + dx + (3, 2, 1, 0)[order], other * 8 + oy * 4 + ox * 2 + core))
    found.sort(key=lambda item: -item[0])
    return [item[1] for item in found]


def kernel(plan, names, *refs):
    k = Refs(names, refs)
    lens, dw, point, gains, shifts = k.lens, k.dw, k.point, k.gains, k.shifts
    squeeze_t, expand = k.squeeze_t, k.expand
    hid, acts, prods, gd, gz, gpb, gqb, pre = k.hid, k.acts, k.prods, k.gd, k.gz, k.gpb, k.gqb, k.pre
    wide, first_mask, valid, stats = k.wide, k.first_mask, k.valid, k.stats
    flat = wide.at[:, pl.ds(0, plan.slots + 2 * GAP)]
    send4, recv4, counts, csend = k.send4, k.recv4, k.counts, k.csend
    send_sem, recv_sem, count_sems = k.send_sem, k.recv_sem, k.count_sems
    N = plan.devices
    Q, R, RF = plan.steps, plan.block, plan.fine
    HV = range(plan.halves)
    SUB = plan.sub
    PER = plan.per
    me = lax.axis_index("dp")
    peers = peers_of(me, N)
    chips = N // 2
    chip, core = me // 2, lax.rem(me, 2)
    partner = me + 1 - 2 * core
    depth, plane = me // 8, lax.rem(me // 2, 4)

    def at_depth(d):
        return lax.rem(depth + d, 4) * 8 + 2 * plane + core

    def in_plane(d):
        return depth * 8 + 2 * lax.rem(plane + d, 4) + core

    same_core = same_core_peers(me, N)

    barrier = pltpu.get_barrier_semaphore()
    for peer in peers:
        pl.semaphore_signal(barrier, inc=1, device_id=(peer,), device_id_type=MESH)

    load_frames = pltpu.make_async_copy(k.frames, k.frames_v, k.io_sems.at[0])
    load_params = []
    if plan.fused:
        for i, name in enumerate(PARAMS):
            load_params.append(pltpu.make_async_copy(getattr(k, name), getattr(k, name + "_v"), k.param_sems.at[i]))
            load_params[-1].start()
    load_cot = pltpu.make_async_copy(k.cot, k.cot_v, k.io_sems.at[1])
    save_out = pltpu.make_async_copy(k.cot_v, k.out, k.io_sems.at[2])
    load_frames.start()
    load_cot.start()
    len0 = lens[0]
    len1 = lens[1]
    half0 = len0 // 2
    half1 = len1 // 2
    count = (half0 + half1).astype(F32)
    inv_count = 1.0 / jnp.full((1, LANES), half0 + half1, jnp.int32).astype(F32)

    def steps_loop(width, body, init=0):
        return lax.fori_loop(0, Q // width, lambda i, c: body(i * width, c), init)

    def mask_body(t0, c):
        step = t0 + lax.broadcasted_iota(jnp.int32, (RF, 8, LANES), 0)
        slot = step + Q * lax.broadcasted_iota(jnp.int32, (RF, 8, LANES), 1)
        a = (slot < half0).astype(F32)
        b = jnp.logical_and(slot >= half0 + GAP, slot < half0 + GAP + half1).astype(F32)
        first_mask[pl.ds(t0, RF)] = a
        valid[pl.ds(t0, RF)] = a + b
        return c

    def set_halo(ref, half):
        sub = lax.broadcasted_iota(jnp.int32, (HALO, 8, LANES), 1)
        low = pltpu.roll(ref[half, pl.ds(Q, HALO)], 1, 1)
        ref[half, pl.ds(0, HALO)] = jnp.where(sub == 0, 0.0, low)
        high = pltpu.roll(ref[half, pl.ds(HALO, HALO)], 7, 1)
        ref[half, pl.ds(HALO + Q, HALO)] = jnp.where(sub == 7, 0.0, high)

    def prepare_slots():
        steps_loop(RF, mask_body)

        top = 2 * GAP + 2 * plan.slots
        for h in HV:
            wide[h, 0:2 * GAP] = jnp.zeros((2 * GAP, LANES), F32)
            wide[h, top:] = jnp.zeros((wide.shape[1] - top, LANES), F32)

        load_frames.wait()

        def widen(i, c):
            rows = pl.ds(pl.multiple_of(i * 128, 128), 128)
            for h in HV:
                values = k.frames_v[rows, h * LANES:(h + 1) * LANES].astype(F32)
                wide[h, pl.ds(pl.multiple_of(i * 128 + 2 * GAP, 32), 128)] = values
            return c

        lax.fori_loop(0, 2 * plan.slots // 128, widen, 0)

        for phase in range(2):
            def deinterleave(t0, c):
                for j in range(RF):
                    a_mask = first_mask[t0 + j]
                    b_mask = valid[t0 + j] - a_mask
                    for h in HV:
                        a = wide[h, pl.ds(2 * (t0 + j) + 2 * GAP + phase, 8, stride=2 * Q)]
                        b = wide[h, pl.ds(2 * (t0 + j) + phase, 8, stride=2 * Q)]
                        hid[phase, h, HALO + t0 + j] = a * a_mask + b * b_mask
                return c
            steps_loop(RF, deinterleave)
            for h in HV:
                set_halo(hid.at[phase], h)

    def spread_lanes(values, lane):
        k.tile[...] = jnp.zeros((8, LANES), F32)
        k.tile[:, 0:values.shape[1]] = values
        return pltpu.roll(k.tile[...], lane, 1) if lane else k.tile[...]

    def load_first():
        taps = spread_lanes(k.dw_first_v[0].astype(F32), 0)
        lane = lax.broadcasted_iota(jnp.int32, (8, LANES), 1)
        taps = jnp.where(lane == plan.tap_rows - 1, count, taps)
        k.first[me] = taps[0:4] + pltpu.roll(taps, plan.tap_rows, 1)[4:8]

    def load_shard():
        for b in range(2):
            source = (k.dw_first_v, k.dw_second_v)[b]
            tiles = [jnp.zeros((8, LANES), F32) for _ in range(2)]
            for r in range(SUB):
                tile, lane = divmod(plan.tap_row(r), LANES)
                tiles[tile] = tiles[tile] + spread_lanes(source[r].astype(F32), lane)
            tiles[1] = tiles[1] + spread_lanes(k.se_up_v[b].astype(F32), EXPAND_ROW - LANES)
            tiles[1] = tiles[1] + spread_lanes(k.se_down_v[b].astype(F32), SQUEEZE_ROW - LANES)
            k.packed[0:LANES] = jnp.zeros((LANES, LANES), F32)
            for r in range(PER):
                k.packed[GAIN_ROW - LANES + r:GAIN_ROW - LANES + r + 1, 0:8] = k.gains_in_v[r, b:b + 1].astype(F32)
                k.packed[SHIFT_ROW - LANES + r:SHIFT_ROW - LANES + r + 1, 0:8] = k.shifts_in_v[r, b:b + 1].astype(F32)
            tiles[1] = tiles[1] + jnp.transpose(k.packed[0:LANES])[0:8]
            for tile in range(2):
                k.packed_t[8 * b:8 * b + 8, tile * LANES:(tile + 1) * LANES] = tiles[tile]
        k.gath[0, depth, plane, core] = k.packed_t[...].astype(BF16)

    def load_pairs(pairs):
        for pair in pairs:
            rows = [k.point_in_v[i // PER, i % PER].astype(F32) for i in (2 * pair, 2 * pair + 1)]
            k.gath[1 + pair, depth, plane, core] = jnp.concatenate(rows, axis=0).astype(BF16)

    def remote(src, dst, sems, unit, to):
        pltpu.make_async_remote_copy(src_ref=src, dst_ref=dst, send_sem=k.unit_sems.at[sems, unit],
                                     recv_sem=k.unit_sems.at[sems + 1, unit], device_id=(to,),
                                     device_id_type=MESH).start()

    def blocks_wait(count, sem, unit):
        view = k.gained.at[0, pl.ds(0, count)]
        pltpu.make_async_copy(view, view, k.unit_sems.at[sem, unit]).wait()

    def lead_wait(count, sem, side):
        view = k.gained.at[0, pl.ds(0, count), :, pl.ds(0, LANES)]
        pltpu.make_async_copy(view, view, k.lead_sems.at[sem, side]).wait()

    def lead_copy(src, dst, sem, side, to):
        pltpu.make_async_remote_copy(src_ref=src, dst_ref=dst, send_sem=k.lead_sems.at[sem, side],
                                     recv_sem=k.lead_sems.at[sem + 1, side], device_id=(to,),
                                     device_id_type=MESH).start()

    def lead_send(side):
        rows = k.point_in_v[0, side].astype(F32)
        k.lead[side, depth, plane, core] = jnp.concatenate(
            [rows[:, h * LANES:(h + 1) * LANES] for h in HV], axis=0).astype(BF16)
        view = k.lead.at[side, depth, plane, core]
        for peer in same_core:
            lead_copy(view, view, 0, side, peer)

    def lead_core(side):
        lead_wait(chips - 1, 1, side)
        view = k.lead.at[side, :, :, core]
        lead_copy(view, view, 2, side, partner)

    def lead_unpack(side):
        lead_wait(chips, 3, side)
        got = k.lead[side].astype(F32).reshape(N, 16, LANES)
        block = jnp.concatenate([got[:, 8 * h:8 * h + 8].reshape(plan.channels, LANES) for h in HV], axis=1)
        point[side] = block.astype(BF16)
        k.point_t[side] = jnp.transpose(block).astype(BF16)

    def gather_send(unit):
        view = k.gath.at[unit, depth, plane, core]
        for peer in same_core:
            remote(view, view, 0, unit, peer)

    def gather_z(unit):
        view = k.gath.at[unit, depth, plane, core]
        for d in (2, 1, 3):
            remote(view, view, 0, unit, at_depth(d))

    def gather_plane(unit):
        blocks_wait(3, 1, unit)
        view = k.gath.at[unit, :, plane, core]
        for d in (3, 2, 1):
            remote(view, view, 2, unit, in_plane(d))

    def gather_core(unit, straight):
        blocks_wait(chips - 1 if straight else 12, 1 if straight else 3, unit)
        view = k.gath.at[unit, :, :, core]
        remote(view, view, 4, unit, partner)

    def gather_wait(unit):
        blocks_wait(chips, 5, unit)

    def split_filter(rows):
        even, odd = rows[0::2], rows[1::2]
        full = odd + [jnp.zeros((1, LANES), F32)] * (len(even) - len(odd))
        return even, odd, [o - e for e, o in zip(even, full)]

    def split_taps(b, r, h):
        taps = plan.taps[b]
        rows = [dw[b * PER + r, h, t:t + 1] for t in range(taps)]
        both = (rows, rows[::-1])
        if b == 0 and r == 0:
            start = (taps - 1) // 2 % 2
            both = (rows[start::2], rows[1 - start::2])
        for base, ordered in zip(plan.tap_sets, both):
            for i, part in enumerate(split_filter(ordered)):
                for j, piece in enumerate(split_filter(part)):
                    start = base + 24 * i + 8 * j
                    dw[b * PER + r, h, start:start + len(piece)] = jnp.concatenate(piece, axis=0)

    def unpack_first():
        got = k.first[...].reshape(4 * N, LANES)
        lane = lax.broadcasted_iota(jnp.int32, (4 * N, LANES), 1)
        low = jnp.where(lane < plan.tap_rows, got, 0.0).reshape(N, 4, LANES)
        high = jnp.where(lane < plan.tap_rows, pltpu.roll(got, LANES - plan.tap_rows, 1), 0.0).reshape(N, 4, LANES)
        counts[...] = jnp.broadcast_to(low[:, :, plan.tap_rows - 1:plan.tap_rows], counts.shape)
        block = jnp.concatenate([low, high], axis=1).reshape(plan.channels, LANES)
        for h in HV:
            k.unpacked[0:LANES] = jnp.transpose(block[h * LANES:(h + 1) * LANES])
            dw[0, h, 0:plan.tap_rows] = k.unpacked[0:plan.tap_rows]
            split_taps(0, 0, h)

    def unpack_values(b):
        got = k.gath[0].astype(F32).reshape(N, 16, plan.values)
        block = got[:, 8 * b:8 * b + 8].reshape(plan.channels, plan.values)
        for h in HV:
            for tile in range(2):
                part = block[h * LANES:(h + 1) * LANES, tile * LANES:(tile + 1) * LANES]
                k.unpacked[tile * LANES:(tile + 1) * LANES] = jnp.transpose(part)
            for r in range(1 - b, SUB):
                dw[b * PER + r, h, 0:plan.tap_rows] = k.unpacked[plan.tap_row(r):plan.tap_row(r) + plan.tap_rows]
                split_taps(b, r, h)
            for r in range(PER):
                gains[b * PER + r, h:h + 1] = k.unpacked[GAIN_ROW + r:GAIN_ROW + r + 1]
                shifts[b * PER + r, h:h + 1] = k.unpacked[SHIFT_ROW + r:SHIFT_ROW + r + 1]
            lanes = slice(h * LANES, (h + 1) * LANES)
            expand[b, :, lanes] = k.unpacked[EXPAND_ROW:EXPAND_ROW + plan.hidden]
            squeeze_t[b, :, lanes] = k.unpacked[SQUEEZE_ROW:SQUEEZE_ROW + plan.hidden]

    def unpack_pair(pair):
        got = k.gath[1 + pair].astype(F32).reshape(N, 16, plan.channels)
        for side in range(2):
            block = got[:, 8 * side:8 * side + 8].reshape(plan.channels, plan.channels)
            point[2 * pair + side] = block.astype(BF16)
            k.point_t[2 * pair + side] = jnp.transpose(block).astype(BF16)

    if plan.fused:
        for copy in load_params:
            copy.wait()
        load_first()

    if not plan.fused:
        csend[...] = jnp.full((4, LANES), count, F32)
    pl.semaphore_wait(barrier, N - 1)

    def send_to_all(src, dst, ssem, rsem):
        for peer in peers:
            pltpu.make_async_remote_copy(src_ref=src, dst_ref=dst, send_sem=ssem, recv_sem=rsem,
                                         device_id=(peer,), device_id_type=MESH).start()

    def wait_all(ref, sem):
        view = ref.at[pl.ds(0, N - 1)]
        pltpu.make_async_copy(view, view, sem).wait()

    if plan.fused:
        send_to_all(k.first.at[me], k.first.at[me], count_sems.at[0], count_sems.at[1])
        lead_send(0)
        load_shard()
        gather_send(0)
        lead_send(1)
        load_pairs(range(1, PER))
        gather_z(2)
    else:
        send_to_all(csend, counts.at[me], count_sems.at[0], count_sems.at[1])
        counts[me] = csend[...]
    prepare_slots()

    def exchange(slot, place, rows):
        send4[slot] = rows
        send_to_all(send4.at[slot], recv4.at[place, me], send_sem.at[slot], recv_sem.at[slot])
        recv4[place, me] = rows

    def received(slot, place):
        wait_all(recv4.at[place], recv_sem.at[slot])
        return recv4[place]

    def back_place(index):
        return lax.rem(index + PER, 2 * PER)

    def row(values):
        return values.reshape(1, 1, LANES)

    def accumulate(rows3):
        return jnp.sum(rows3, axis=0)

    def count_slots():
        inv_total = 1.0 / jnp.sum(counts[...], axis=0)
        k.norm_count[...] = inv_total
        counts[...] = counts[...] * inv_total

    def shares():
        return counts[...]

    def merge_stats(slot, index):
        got = received(slot, slot)
        weight = shares()
        mean = jnp.sum(weight * got, axis=0)
        mean4 = jnp.concatenate([mean[0:2], mean[0:2]], axis=0)
        diff = got - mean4
        between = jnp.sum(weight * diff * diff, axis=0)
        within = jnp.sum(got, axis=0)
        var = within[2:4] * k.norm_count[0:2] + between[0:2]
        inv = lax.rsqrt(var + EPSILON)
        scale = inv * gains[index]
        offset = shifts[index] - mean[0:2] * scale
        stats[index] = jnp.concatenate([mean[0:2], inv, scale, offset], axis=0)

    def stat_row(index, kind, h):
        return row(stats[index, pl.ds(2 * kind + h, 1)])

    def tap(index, h, t):
        return dw[index, h, pl.ds(t, 1)].reshape(1, 1, LANES)

    def direct(win, low, index, h, taps):
        acc = None
        for t, shift in taps:
            term = win[shift - low:shift - low + R] * tap(index, h, t)
            acc = term if acc is None else acc + term
        return acc

    def paired(x, count, steps, levels, run, base):
        if levels == 0:
            return run(x, count, steps, base)
        low, high = (count + 1) // 2, count // 2
        m = steps // 2
        if x.shape[0] % 2:
            x = jnp.concatenate([x, x[-1:]], axis=0)
        split = x.reshape(-1, 2, 8, LANES)
        x0, x1 = split[:, 0], split[:, 1]
        gap = 24 if levels == 2 else 8

        def part(values, n, i):
            return paired(values, n, m, levels - 1, run, base + gap * i)
        shared = part(x1[:m + low - 1], low, 2)
        first = part(x0[:m + low - 1] + x1[:m + low - 1], low, 0) + shared
        second = part(x0[1:m + high] + x1[:m + high - 1], high, 1) - shared
        return jnp.stack([first, second], axis=1).reshape(steps, 8, LANES)

    def all_taps(win, index, h, taps, side):
        def run(x, count, steps, base):
            acc = None
            for j in range(count):
                term = x[j:j + steps] * tap(index, h, base + j)
                acc = term if acc is None else acc + term
            return acc
        return paired(win, taps, R, 2, run, plan.tap_sets[side])

    def layer_conv(index, pieces, between=None):
        def body(t0, c):
            for h in HV:
                acc = None
                if len(pieces) == 1:
                    source, taps = pieces[0]
                    low = taps[0][1]
                    acc = all_taps(hid[source, h, pl.ds(t0 + HALO + low, R + len(taps) - 1)], index, h, len(taps), 0)
                else:
                    for side, (source, taps) in enumerate(pieces):
                        low, high = taps[0][1], taps[-1][1]
                        win = hid[source, h, pl.ds(t0 + HALO + low, R + high - low)]
                        part = all_taps(win, index, h, len(taps), side)
                        acc = part if acc is None else acc + part
                rows = pl.ds(pl.multiple_of(8 * t0, 16), 8 * R)
                acts[index, rows, h * LANES:(h + 1) * LANES] = acc.reshape(8 * R, LANES).astype(BF16)
            return c
        if between is None:
            steps_loop(R, body)
        else:
            cut = Q // R - 1
            lax.fori_loop(0, cut, lambda i, c: body(i * R, c), 0)
            between()
            lax.fori_loop(cut, Q // R, lambda i, c: body(i * R, c), 0)

    def half_lanes(values, h):
        return values[:, h * LANES:(h + 1) * LANES]

    def pointwise(index):
        pivot = [None] * plan.halves
        sums = [jnp.zeros((8, LANES), F32) for _ in HV]
        squares = [jnp.zeros((8, LANES), F32) for _ in HV]
        for t0 in range(0, Q, R):
            res = jnp.dot(acts[index, 8 * t0:8 * (t0 + R)], point[index], preferred_element_type=F32)
            v = valid[t0:t0 + R]
            for h in HV:
                p = half_lanes(res, h).reshape(R, 8, LANES)
                prods[index, h, t0:t0 + R] = p
                if t0 == 0:
                    pivot[h] = p[0, 0:1]
                d = p - row(pivot[h])
                dv = d * v
                sums[h] = sums[h] + accumulate(dv)
                squares[h] = squares[h] + accumulate(dv * d)
        n = jnp.full((1, LANES), count, F32)
        shift = [jnp.sum(sums[h], axis=0, keepdims=True) * inv_count for h in HV]
        spread = [jnp.sum(squares[h], axis=0, keepdims=True) - n * shift[h] * shift[h] for h in HV]
        return jnp.concatenate([pivot[h] + shift[h] for h in HV] + spread, axis=0)

    def activate(index, target):
        scales = [0.5 * stat_row(index, 2, h) for h in HV]
        offsets = [0.5 * stat_row(index, 3, h) for h in HV]

        def body(t0, c):
            v = valid[pl.ds(t0, RF)]
            for h in HV:
                u = prods[index, h, pl.ds(t0, RF)] * scales[h] + offsets[h]
                hid[target, h, pl.ds(HALO + t0, RF)] = (u + u * jnp.tanh(u)) * v
            return c
        steps_loop(RF, body)
        for h in HV:
            set_halo(hid.at[target], h)

    def hid_of(b, r):
        return b * SUB + r + 1

    def regular_taps(b):
        margin = (plan.taps[b] - 1) // 2
        return [(t, t - margin) for t in range(plan.taps[b])]

    def block_pieces(b):
        if b == 0:
            taps = regular_taps(0)
            even = [(t, s // 2) for t, s in taps if s % 2 == 0]
            odd = [(t, (s - 1) // 2) for t, s in taps if s % 2 == 1]
            return [(0, even), (1, odd)]
        return [(hid_of(1, 0), regular_taps(1))]

    def residual_forward(b):
        source = 0 if b == 0 else hid_of(1, 0)
        res = b * PER + SUB

        def body(t0, c):
            rows = pl.ds(pl.multiple_of(8 * t0, 16), 8 * R)
            for h in HV:
                values = hid[source, h, pl.ds(HALO + t0, R)].reshape(8 * R, LANES)
                acts[res, rows, h * LANES:(h + 1) * LANES] = values.astype(BF16)
            return c
        steps_loop(R, body)
        exchange(res, res, pointwise(res))

    def small(a, b, dims):
        return lax.dot_general(a, b, (dims, ((), ())), precision=HIGHEST, preferred_element_type=F32)

    def thin(a, matrix, dim):
        hi = a.astype(BF16).astype(F32)
        mid = (a - hi).astype(BF16).astype(F32)
        low = a - hi - mid
        rows = jnp.concatenate([hi, mid, low, jnp.zeros_like(a)], axis=0).astype(BF16)
        res = lax.dot_general(rows, matrix.astype(BF16), (((1,), (dim,)), ((), ())), preferred_element_type=F32)
        return res[0:2] + res[2:4] + res[4:6]

    def eight(values):
        return jnp.concatenate([values, jnp.zeros((6, values.shape[1]), F32)], axis=0)

    def whole_row(index, kind):
        return jnp.concatenate([stats[index, pl.ds(2 * kind + h, 1)] for h in HV], axis=1)

    def join(parts):
        return jnp.concatenate([jnp.sum(part, axis=0, keepdims=True) for part in parts], axis=1)

    half_count = [jnp.full((1, plan.channels), n, jnp.int32).astype(F32) for n in (half0, half1)]

    def utterance_sums(b):
        last = b * PER + SUB - 1

        def sums(t0, c):
            a = first_mask[pl.ds(t0, RF)]
            s = valid[pl.ds(t0, RF)] - a
            res = []
            for h in HV:
                p = prods[last, h, pl.ds(t0, RF)]
                res += [c[2 * h] + accumulate(p * a), c[2 * h + 1] + accumulate(p * s)]
            return tuple(res)
        tot = steps_loop(RF, sums, tuple(jnp.zeros((8, LANES), F32) for _ in range(2 * plan.halves)))
        for u in range(2):
            k.psum[b, u:u + 1] = join([tot[2 * h + u] for h in HV])

    def excite(b):
        last = b * PER + SUB - 1
        scale, offset = whole_row(last, 2), whole_row(last, 3)
        means = jnp.concatenate([scale * (k.psum[b, u:u + 1] / half_count[u]) + offset for u in range(2)], axis=0)
        inner = thin(means, squeeze_t[b], 1)
        excited = inner * sigmoid(inner)
        gate = sigmoid(thin(excited, expand[b], 0))
        return means, inner, excited, gate

    def tail_half(b, gate):
        last, res = b * PER + SUB - 1, b * PER + SUB
        consts = []
        for h in HV:
            g = [half_lanes(gate[u:u + 1], h) for u in range(2)]
            s1, o1, s2, o2 = [0.5 * stats[i, pl.ds(2 * kind + h, 1)] for i, kind in
                              ((last, 2), (last, 3), (res, 2), (res, 3))]
            consts.append([row(v) for v in (s1 * g[0], s1 * g[1], s2, o1 * g[0] + o2, o1 * g[1] + o2)])

        def get(t0, h):
            a0, a1, s2, b0, b1 = consts[h]
            a = first_mask[pl.ds(t0, RF)] > 0.5
            return (prods[last, h, pl.ds(t0, RF)] * jnp.where(a, a0, a1)
                    + prods[res, h, pl.ds(t0, RF)] * s2 + jnp.where(a, b0, b1))
        return get

    def tail(b, gate, store):
        get = tail_half(b, gate)

        def body(t0, c):
            v = valid[pl.ds(t0, RF)]
            for h in HV:
                u = get(t0, h)
                store(t0, h, (u + u * jnp.tanh(u)) * v)
            return c
        steps_loop(RF, body)

    def slope_of(u):
        t = jnp.tanh(u)
        return (0.5 * t + 0.5) * (1.0 + u - u * t)

    def tail_slope(b, gate):
        get = tail_half(b, gate)

        def body(t0, c):
            v = valid[pl.ds(t0, RF)]
            for h in HV:
                pre[b, h, pl.ds(t0, RF)] = slope_of(get(t0, h)) * v
            return c
        steps_loop(RF, body)

    def forward_aside(b, r, extras):
        if plan.fused:
            step = b * SUB + r

            @pl.when(step == 0)
            def _():
                gather_core(0, True)
                lead_core(1)
                gather_wait(0)
                lead_unpack(1)
                unpack_values(0)

            @pl.when(step == 1)
            def _():
                unpack_values(1)

            @pl.when(jnp.logical_and(step >= 1, step < PER))
            def _():
                gather_core(1 + step, False)
                gather_wait(1 + step)
                unpack_pair(step)

        @pl.when(r == SUB - 2)
        def _():
            residual_forward(b)

        @pl.when(r == SUB - 1)
        def _():
            utterance_sums(b)
        for when, extra in extras:
            pl.when(r == when)(extra)

    def forward_block(b, extras=()):
        def layer(r, pieces, before=None):
            index = b * PER + r
            first = before is not None
            layer_conv(index, pieces, (lambda: lead_core(0)) if first else None)
            if first:
                before()
            exchange(index, index, pointwise(index))
            forward_aside(b, r, extras)
            merge_stats(index, index)
            if plan.fused:
                step = b * SUB + r

                @pl.when(step < PER - 2)
                def _():
                    gather_z(3 + step)

                @pl.when(step < PER - 1)
                def _():
                    gather_plane(2 + step)

        def first_matrices():
            lead_unpack(0)
        layer(0, block_pieces(b), first_matrices if plan.fused and b == 0 else None)
        activate(b * PER, hid_of(b, 1))

        def rest(r, c):
            layer(r, [(hid_of(b, r), regular_taps(b))])

            @pl.when(r < SUB - 1)
            def _():
                activate(b * PER + r, hid_of(b, r + 1))
            return c
        lax.fori_loop(1, SUB, rest, 0)
        merge_stats(b * PER + SUB, b * PER + SUB)
        return excite(b)

    back_slot = 2 * PER

    def sum_rows(parts):
        return jnp.concatenate([jnp.sum(part, axis=0, keepdims=True) for part in parts], axis=0)

    def tail_back(b, kept, load):
        means, inner, excited, gate = kept
        last = b * PER + SUB - 1
        mean = [stat_row(last, 0, h) for h in HV]

        def first(t0, c):
            a = first_mask[pl.ds(t0, RF)]
            res = []
            for h in HV:
                gs = load(t0, h)
                pre[b, h, pl.ds(t0, RF)] = gs
                gx = gs * (prods[last, h, pl.ds(t0, RF)] - mean[h])
                res += [c[4 * h] + accumulate(gs * a), c[4 * h + 1] + accumulate(gs),
                        c[4 * h + 2] + accumulate(gx * a), c[4 * h + 3] + accumulate(gx)]
            return tuple(res)
        tot = steps_loop(RF, first, tuple(jnp.zeros((8, LANES), F32) for _ in range(4 * plan.halves)))
        s0, s_all, x0, x_all = [join([tot[4 * h + i] for h in HV]) for i in range(4)]
        gs_sum = (s0, s_all - s0)
        gx_sum = (x0, x_all - x0)
        mean_row, inv_row, scale_row = [whole_row(last, kind) for kind in range(3)]
        shift_row = jnp.concatenate([shifts[last, h:h + 1] for h in HV], axis=1)
        grad_gate = jnp.concatenate([scale_row * gx_sum[u] + shift_row * gs_sum[u] for u in range(2)], axis=0)
        grad_up = grad_gate * gate * (1.0 - gate)
        sg = sigmoid(inner)
        grad_inner = thin(grad_up, expand[b], 1) * (sg * (1.0 + inner * (1.0 - sg)))
        grad_means = thin(grad_inner, squeeze_t[b], 0)
        per_slot = [grad_means[u:u + 1] / half_count[u] for u in range(2)]
        sum1, sum2 = 0.0, 0.0
        for u in range(2):
            g = gate[u:u + 1]
            sum1 = sum1 + g * gs_sum[u] + grad_means[u:u + 1]
            sum2 = sum2 + g * gx_sum[u] + per_slot[u] * (k.psum[b, u:u + 1] - half_count[u] * mean_row)
        sum2 = sum2 * inv_row
        exchange(back_slot + last, back_place(last),
                 jnp.concatenate([half_lanes(v, h) for v in (sum1, sum2) for h in HV], axis=0))
        return grad_up, grad_inner, per_slot

    def tail_back_aside(b, kept, found):
        means, inner, excited, gate = kept
        grad_up, grad_inner, per_slot = found
        res = b * PER + SUB
        gates = [[row(half_lanes(gate[u:u + 1], h)) for h in HV] for u in range(2)]
        slots = [[row(half_lanes(per_slot[u], h)) for h in HV] for u in range(2)]
        norm = [(stat_row(res, 0, h), stats[res, pl.ds(2 + h, 1)]) for h in HV]

        def second(t0, c):
            a = first_mask[pl.ds(t0, RF)] > 0.5
            v = valid[pl.ds(t0, RF)]
            out_c = []
            for h in HV:
                gs = pre[b, h, pl.ds(t0, RF)]
                gz[h, pl.ds(t0, RF)] = (gs * jnp.where(a, gates[0][h], gates[1][h])
                                        + jnp.where(a, slots[0][h], slots[1][h]) * v)
                x = prods[res, h, pl.ds(t0, RF)] - norm[h][0]
                out_c += [c[2 * h] + accumulate(gs), c[2 * h + 1] + accumulate(gs * x)]
            return tuple(out_c)
        tot = steps_loop(RF, second, tuple(jnp.zeros((8, LANES), F32) for _ in range(2 * plan.halves)))
        sums = [jnp.sum(part, axis=0, keepdims=True) for part in tot]
        exchange(back_slot + res, back_place(res), jnp.concatenate(
            [sums[2 * h] for h in HV] + [sums[2 * h + 1] * norm[h][1] for h in HV], axis=0))
        k.expand_grad[b] = small(eight(excited), eight(grad_up), ((0,), (0,)))
        k.squeeze_grad[b] = small(eight(grad_inner), eight(means), ((0,), (0,)))

    def norm_back(index, load, target, store, then=None):
        sums = jnp.sum(received(back_slot + index, back_place(index)), axis=0)
        if then is not None:
            then()
        k.shifts_grad[index] = sums[0:2]
        k.gains_grad[index] = sums[2:4]
        inv_total = k.norm_count[0:2]
        st = stats[index]
        mean, inv, scale = st[0:2], st[2:4], st[4:6]
        k1 = scale * sums[0:2] * inv_total
        k2 = scale * sums[2:4] * inv_total * inv
        rows3 = [[row(value[h:h + 1]) for value in (mean, scale, k1, k2)] for h in HV]
        for t0 in range(0, Q, R):
            v = valid[t0:t0 + R]
            parts = []
            for h in HV:
                mean_h, scale_h, k1_h, k2_h = rows3[h]
                grad = scale_h * load(t0, h) - (k1_h + k2_h * (prods[index, h, t0:t0 + R] - mean_h)) * v
                parts.append(grad.reshape(8 * R, LANES).astype(BF16))
            both = jnp.concatenate(parts, axis=1)
            target[8 * t0:8 * (t0 + R)] = both
            if plan.fused:
                res = jnp.dot(both, k.point_t[index], preferred_element_type=F32)
            else:
                res = lax.dot_general(both, point[index], (((1,), (1,)), ((), ())), preferred_element_type=F32)
            for h in HV:
                store(t0, h, half_lanes(res, h).reshape(R, 8, LANES))

    def point_back(index, source):
        place = lax.rem(index, 2) if plan.fused else index
        k.point_grad[place] = lax.dot_general(acts[index], source[...], (((0,), (0,)), ((), ())),
                                              preferred_element_type=F32)

    def store_gd(t0, h, values):
        gd[h, HALO + t0:HALO + t0 + R] = values

    def store_skip(t0, h, values):
        k.skip[h, t0:t0 + R] = values

    def conv_back_block(t0, h, index, taps):
        low, high = -taps[-1][1], -taps[0][1]
        win = gd[h, pl.ds(t0 + HALO + low, R + high - low)]
        if len(taps) >= plan.taps[0]:
            return all_taps(win, index, h, len(taps), 1)
        return direct(win, low, index, h, [(t, -shift) for t, shift in taps])

    def kernel_back(index, pieces):
        for source, taps in pieces:
            for h in HV:
                low = min(s for _, s in taps)
                high = max(s for _, s in taps)

                def body(t0, c):
                    g = gd[h, pl.ds(HALO + t0, RF)]
                    win = hid[source, h, pl.ds(t0 + HALO + low, RF + high - low)]
                    return tuple(acc + accumulate(g * win[s - low:s - low + RF]) for acc, (_, s) in zip(c, taps))
                def paired_body(t0, c):
                    g = gd[h, pl.ds(HALO + t0, RF)].reshape(RF // 2, 2, 8, LANES)
                    win = hid[source, h, pl.ds(t0 + HALO + low, RF + high - low)]
                    if win.shape[0] % 2:
                        win = jnp.concatenate([win, win[-1:]], axis=0)
                    x = win.reshape(-1, 2, 8, LANES)
                    g0, g1, x0, x1 = g[:, 0], g[:, 1], x[:, 0], x[:, 1]
                    n, even, odd = RF // 2, (len(taps) + 1) // 2, len(taps) // 2
                    both = x0[:n + even - 1] + x1[:n + even - 1]
                    late = x0[1:n + odd] + x1[:n + odd - 1]
                    gap = g0 - g1
                    new = ([accumulate(g0 * both[i:i + n]) for i in range(even)]
                           + [accumulate(gap * x1[i:i + n]) for i in range(even)]
                           + [accumulate(g1 * late[i:i + n]) for i in range(odd)])
                    return tuple(acc + value for acc, value in zip(c, new))
                if len(taps) < plan.taps[0]:
                    even, odd = (len(taps) + 1) // 2, len(taps) // 2
                    parts = steps_loop(RF, paired_body, tuple(
                        jnp.zeros((8, LANES), F32) for _ in range(2 * even + odd)))
                    accs = [parts[2 * even + i // 2] + parts[even + i // 2] if i % 2
                            else parts[i // 2] - parts[even + i // 2] for i in range(len(taps))]
                else:
                    accs = steps_loop(RF, body, tuple(jnp.zeros((8, LANES), F32) for _ in taps))
                for acc, (tap, _) in zip(accs, taps):
                    k.dw_grad[index, h, pl.ds(tap, 1)] = jnp.sum(acc, axis=0, keepdims=True)

    def slopes(index):
        scales = [0.5 * stat_row(index, 2, h) for h in HV]
        offsets = [0.5 * stat_row(index, 3, h) for h in HV]

        def body(t0, c):
            v = valid[pl.ds(t0, RF)]
            for h in HV:
                k.slope[h, pl.ds(t0, RF)] = slope_of(prods[index, h, pl.ds(t0, RF)] * scales[h] + offsets[h]) * v
            return c
        steps_loop(RF, body)

    def hidden_back(index, taps):
        before = index - 1
        mean = [stat_row(before, 0, h) for h in HV]

        def body(t0, c):
            res = []
            for h in HV:
                grad = conv_back_block(t0, h, index, taps) * k.slope[h, pl.ds(t0, R)]
                gz[h, pl.ds(t0, R)] = grad
                gx = grad * (prods[before, h, pl.ds(t0, R)] - mean[h])
                res += [c[2 * h] + accumulate(grad), c[2 * h + 1] + accumulate(gx)]
            return tuple(res)
        tot = steps_loop(R, body, tuple(jnp.zeros((8, LANES), F32) for _ in range(2 * plan.halves)))
        sums = [jnp.sum(part, axis=0, keepdims=True) for part in tot]
        exchange(back_slot + before, back_place(before), jnp.concatenate(
            [sums[2 * h] for h in HV] + [sums[2 * h + 1] * stats[before, pl.ds(2 + h, 1)] for h in HV], axis=0))

    def load_gz(t0, h):
        return gz[h, t0:t0 + R]

    def scatter_start(unit, place):
        remote(k.shares.at[place, :, :, 1 - core], k.inbox.at[unit], 6, unit, partner)

    def scatter_sum(unit, place):
        blocks_wait(chips, 7, unit)
        blocks_wait(chips, 6, unit)
        slot = lax.rem(unit, 3)
        k.sums[slot] = (k.shares[place, :, :, core].astype(F32) + k.inbox[unit].astype(F32)).astype(BF16)

    def scatter_send(unit):
        slot = lax.rem(unit, 3)
        k.gained[unit, chip] = k.sums[slot, depth, plane]
        for peer in same_core:
            remote(k.sums.at[slot, peer // 8, lax.rem(peer // 2, 4)], k.gained.at[unit, chip], 8, unit, peer)

    def scatter_finish(unit):
        blocks_wait(chips - 1, 9, unit)
        return jnp.sum(k.gained[unit].astype(F32), axis=0)

    def scatter_plane(unit):
        slot = lax.rem(unit, 3)
        k.by_plane[unit, plane] = k.sums[slot, :, plane]
        for d in (3, 2, 1):
            there = lax.rem(plane + d, 4)
            remote(k.sums.at[slot, :, there], k.by_plane.at[unit, plane], 8, unit, in_plane(d))

    def scatter_mid(unit):
        blocks_wait(12, 9, unit)
        blocks_wait(12, 8, unit)
        k.line[unit] = jnp.sum(k.by_plane[unit].astype(F32), axis=0).astype(BF16)
        k.by_depth[unit, depth] = k.line[unit, depth]

    def scatter_z(unit):
        for d in (2, 1, 3):
            there = lax.rem(depth + d, 4)
            remote(k.line.at[unit, there], k.by_depth.at[unit, depth], 10, unit, at_depth(d))

    def scatter_end(unit):
        blocks_wait(3, 11, unit)
        return jnp.sum(k.by_depth[unit].astype(F32), axis=0)

    def pair_start(pair):
        both = [k.point_grad[side].reshape(N, 8, plan.channels) for side in range(2)]
        k.shares[0] = jnp.concatenate(both, axis=1).astype(BF16).reshape(4, 4, 2, 16, plan.channels)
        scatter_start(1 + pair, 0)

    def pair_finish(pair, straight=False):
        total = scatter_finish(1 + pair) if straight else scatter_end(1 + pair)
        b = pair // (PER // 2)
        r = 2 * lax.rem(pair, PER // 2)
        k.point_out[b, r] = total[0:8]
        k.point_out[b, r + 1] = total[8:16]

    def last_start():
        k.packed[0:LANES] = jnp.zeros((LANES, LANES), F32)
        columns = []
        for h in HV:
            k.packed[0:plan.tap_rows] = k.dw_grad[0, h]
            columns.append(jnp.transpose(k.packed[0:LANES]))
        whole = jnp.concatenate(columns, axis=0)
        moved = pltpu.roll(whole, plan.tap_rows, 1).reshape(N, 8, LANES)
        k.last_mine[...] = whole.reshape(N, 8, LANES)[:, 0:4] + moved[:, 4:8]
        k.last[me] = k.last_mine[me]
        for peer in peers:
            pltpu.make_async_remote_copy(src_ref=k.last_mine.at[peer], dst_ref=k.last.at[me],
                                         send_sem=k.last_sems.at[0], recv_sem=k.last_sems.at[1],
                                         device_id=(peer,), device_id_type=MESH).start()

    def last_finish():
        wait_all(k.last, k.last_sems.at[1])
        total = jnp.sum(k.last[...], axis=0)
        both = jnp.concatenate([total, pltpu.roll(jnp.concatenate([total, total], axis=0),
                                                  LANES - plan.tap_rows, 1)[0:4]], axis=0)
        k.dw_first_out[0] = both[:, 0:plan.taps[0]]

    def values_start():
        k.packed[...] = jnp.zeros((plan.values, LANES), F32)
        blocks = []
        for b in range(2):
            columns = []
            for h in HV:
                for r in range(1 - b, SUB):
                    k.packed[plan.tap_row(r):plan.tap_row(r) + plan.tap_rows] = k.dw_grad[b * PER + r, h]
                lanes = slice(h * LANES, (h + 1) * LANES)
                k.packed[EXPAND_ROW:EXPAND_ROW + plan.hidden] = k.expand_grad[b, :, lanes]
                k.packed[SQUEEZE_ROW:SQUEEZE_ROW + plan.hidden] = k.squeeze_grad[b, :, lanes]
                columns.append(jnp.concatenate(
                    [jnp.transpose(k.packed[t * LANES:(t + 1) * LANES]) for t in range(2)], axis=1))
            blocks.append(jnp.concatenate(columns, axis=0).reshape(N, 8, plan.values))
        k.shares[1] = jnp.concatenate(blocks, axis=1).astype(BF16).reshape(4, 4, 2, 16, plan.values)
        scatter_start(0, 1)

    def values_finish():
        total = scatter_finish(0)
        for b in range(2):
            rows = total[8 * b:8 * b + 8]

            def lanes(start, size):
                tile, lane = divmod(start, LANES)
                part = rows[:, tile * LANES:(tile + 1) * LANES]
                return (pltpu.roll(part, LANES - lane, 1) if lane else part)[:, 0:size]
            dw_out = (k.dw_first_out, k.dw_second_out)[b]
            for r in range(1 - b, SUB):
                dw_out[r] = lanes(plan.tap_row(r), plan.taps[b])
            k.squeeze_out[b] = lanes(SQUEEZE_ROW, plan.hidden)
            k.expand_out[b] = lanes(EXPAND_ROW, plan.hidden)

    def own_norms():
        mine = pl.ds(pl.multiple_of(me * 8, 8), 8)
        k.packed[0:LANES] = jnp.zeros((LANES, LANES), F32)
        for h in HV:
            for b in range(2):
                for r in range(PER):
                    k.packed[16 * b + r:16 * b + r + 1] = k.gains_grad[b * PER + r, h:h + 1]
                    k.packed[16 * b + 8 + r:16 * b + 9 + r] = k.shifts_grad[b * PER + r, h:h + 1]
            k.own_norm[h * LANES:(h + 1) * LANES] = jnp.transpose(k.packed[0:LANES])
        k.packed[0:LANES] = jnp.transpose(
            jnp.concatenate([k.own_norm[mine], jnp.zeros((LANES - 8, LANES), F32)], axis=0))
        for b in range(2):
            for r in range(PER):
                k.gains_out[r, b:b + 1] = k.packed[16 * b + r:16 * b + r + 1, 0:8]
                k.shifts_out[r, b:b + 1] = k.packed[16 * b + 8 + r:16 * b + 9 + r, 0:8]

    HALF = PER // 2

    def backward_aside(b, r):
        index = b * PER + r
        if plan.fused:
            if b == 0:
                @pl.when(r == SUB - 1)
                def _():
                    scatter_sum(1 + HALF, 0)

            @pl.when(lax.rem(r, 2) == 1)
            def _():
                scatter_sum(1 + HALF * b + (r + 1) // 2, 0)
        point_back(index, gpb)

        @pl.when(r == SUB - 1)
        def _():
            res = b * PER + SUB
            norm_back(res, lambda t0, h: pre[b, h, t0:t0 + R], gqb, store_skip)
            point_back(res, gqb)
        if plan.fused:
            @pl.when(lax.rem(r, 2) == 0)
            def _():
                pair_start(HALF * b + r // 2)

    def backward_late(b, r):
        if not plan.fused:
            return
        if b == 0:
            @pl.when(r == SUB - 1)
            def _():
                pair_finish(HALF + 1)

            @pl.when(r == SUB - 2)
            def _():
                scatter_mid(1 + HALF)

            @pl.when(r == SUB - 3)
            def _():
                pair_finish(HALF)

        @pl.when(jnp.logical_or(r == 2, r == 0))
        def _():
            scatter_mid(1 + HALF * b + r // 2 + 1)

        @pl.when(r == 1)
        def _():
            pair_finish(HALF * b + 2)

    def backward_block(b):
        def go(r):
            if plan.fused:
                @pl.when(jnp.logical_or(r == 2, r == 0))
                def _():
                    scatter_plane(1 + HALF * b + r // 2 + 1)

                @pl.when(r == 1)
                def _():
                    scatter_z(1 + HALF * b + 2)
                if b == 0:
                    @pl.when(r == 0)
                    def _():
                        scatter_send(0)

                    @pl.when(r == SUB - 1)
                    def _():
                        scatter_z(1 + HALF + 1)

                    @pl.when(r == SUB - 2)
                    def _():
                        scatter_plane(1 + HALF)

                    @pl.when(r == SUB - 3)
                    def _():
                        scatter_z(1 + HALF)

        def filtered(r):
            norm_back(b * PER + r, load_gz, gpb, store_gd, lambda: go(r))
            for h in HV:
                set_halo(gd, h)

        def step(j, c):
            r = SUB - 1 - j
            index = b * PER + r
            filtered(r)
            hidden_back(index, regular_taps(b))
            backward_aside(b, r)
            kernel_back(index, [(hid_of(b, r), regular_taps(b))])

            @pl.when(r >= 2)
            def _():
                slopes(index - 2)
            backward_late(b, r)
            return c
        lax.fori_loop(0, SUB - 1, step, 0)
        if plan.fused and b == 0:
            values_start()
            scatter_sum(0, 1)
        filtered(0)

    if plan.fused:
        wait_all(k.first, count_sems.at[1])
        unpack_first()
    else:
        wait_all(counts, count_sems.at[1])
        dw[...] = k.dw_in[...]
        for b in range(2):
            for r in range(SUB):
                for h in HV:
                    split_taps(b, r, h)
    count_slots()
    kept_first = forward_block(0)

    def store_middle(t0, h, values):
        hid[hid_of(1, 0), h, pl.ds(HALO + t0, RF)] = values
    tail(0, kept_first[3], store_middle)
    for h in HV:
        set_halo(hid.at[hid_of(1, 0)], h)

    def place_cot():
        load_cot.wait()
        for h in HV:
            flat[h, 0:GAP] = jnp.zeros((GAP, LANES), F32)
            flat[h, GAP + plan.slots:] = jnp.zeros((flat.shape[1] - GAP - plan.slots, LANES), F32)

        def place(i, c):
            rows = pl.ds(pl.multiple_of(i * 128, 128), 128)
            for h in HV:
                flat[h, pl.ds(pl.multiple_of(i * 128 + GAP, 16), 128)] = k.cot_v[rows, h * LANES:(h + 1) * LANES]
            return c
        lax.fori_loop(0, plan.slots // 128, place, 0)

        def pick(t0, c):
            for h in HV:
                for j in range(RF):
                    here = flat[h, pl.ds(t0 + j + GAP, 8, stride=Q)]
                    moved = flat[h, pl.ds(t0 + j, 8, stride=Q)]
                    gz[h, t0 + j] = jnp.where(first_mask[t0 + j] > 0.5, here, moved)
            return c
        steps_loop(RF, pick)
    kept_second = forward_block(1, ((0, lambda: tail_slope(0, kept_first[3])), (1, place_cot)))

    last_half = tail_half(1, kept_second[3])

    def load_last(t0, h):
        return gz[h, pl.ds(t0, RF)] * (slope_of(last_half(t0, h)) * valid[pl.ds(t0, RF)])
    found = tail_back(1, kept_second, load_last)

    def store_out(t0, h, values):
        for j in range(RF):
            flat[h, pl.ds(t0 + j, 8, stride=Q)] = values[j]

    def ungap(i, c):
        rows = pl.ds(pl.multiple_of(i * 128, 128), 128)
        slot = i * 128 + lax.broadcasted_iota(jnp.int32, (128, LANES), 0)
        for h in HV:
            moved = flat[h, pl.ds(pl.multiple_of(i * 128 + GAP, 16), 128)]
            k.cot_v[rows, h * LANES:(h + 1) * LANES] = jnp.where(slot < half0, flat[h, rows], moved)
        return c
    tail_back_aside(1, kept_second, found)
    slopes(PER + SUB - 2)
    tail(1, kept_second[3], store_out)
    lax.fori_loop(0, plan.slots // 128, ungap, 0)
    save_out.start()
    backward_block(1)

    def sum_back(t0, c):
        for h in HV:
            gz[h, pl.ds(t0, R)] = conv_back_block(t0, h, PER, regular_taps(1)) + k.skip[h, pl.ds(t0, R)]
        return c
    steps_loop(R, sum_back)
    found = tail_back(0, kept_first, lambda t0, h: gz[h, pl.ds(t0, RF)] * pre[0, h, pl.ds(t0, RF)])
    tail_back_aside(0, kept_first, found)
    slopes(SUB - 2)
    backward_aside(1, 0)
    kernel_back(PER, [(hid_of(1, 0), regular_taps(1))])
    backward_late(1, 0)
    backward_block(0)
    pieces = block_pieces(0)
    backward_aside(0, 0)
    kernel_back(0, pieces)
    if plan.fused:
        last_start()
        scatter_sum(1, 0)
        scatter_send(1)
        backward_late(0, 0)
        scatter_z(2)
        own_norms()

    def spread(t0, c):
        v = valid[pl.ds(t0, R)]
        for h in HV:
            even = (conv_back_block(t0, h, 0, pieces[0][1]) + k.skip[h, pl.ds(t0, R)]) * v
            odd = conv_back_block(t0, h, 0, pieces[1][1]) * v
            for j in range(R):
                wide[h, pl.ds(2 * (t0 + j), 8, stride=2 * Q)] = even[j]
                wide[h, pl.ds(2 * (t0 + j) + 1, 8, stride=2 * Q)] = odd[j]
        return c
    steps_loop(R, spread)

    def ungap_wide(i, c):
        rows = pl.ds(pl.multiple_of(i * 128, 128), 128)
        slot = i * 128 + lax.broadcasted_iota(jnp.int32, (128, LANES), 0)
        for h in HV:
            moved = wide[h, pl.ds(pl.multiple_of(i * 128 + 2 * GAP, 32), 128)]
            k.frames_grad_v[lax.rem(i, 2 * per_piece), :, h * LANES:(h + 1) * LANES] = jnp.where(
                slot < len0, wide[h, rows], moved)
        return c
    pieces_out = 8
    per_piece = 2 * plan.slots // pieces_out // 128
    save_frames = []
    for piece in range(pieces_out):
        if piece >= 2:
            save_frames[piece - 2].wait()
        lax.fori_loop(piece * per_piece, (piece + 1) * per_piece, ungap_wide, 0)
        save_frames.append(pltpu.make_async_copy(
            k.frames_grad_v.at[pl.ds((piece % 2) * per_piece, per_piece)],
            k.frames_grad.at[pl.ds(piece * per_piece, per_piece)], k.io_sems.at[3 + piece]))
        save_frames[-1].start()
    if plan.fused:
        pair_finish(1)
        values_finish()
        pair_finish(0, True)
        last_finish()

    save_out.wait()
    for copy in save_frames[-2:]:
        copy.wait()
    wait_all(k.first if plan.fused else counts, count_sems.at[0])

    def drain(slot, c):
        wait_all(recv4.at[0], send_sem.at[slot])
        return c
    lax.fori_loop(0, send4.shape[0], drain, 0)
    if plan.fused:
        for unit in range(1 + PER):
            if unit != 1:
                blocks_wait(chips - 1 if unit < 2 else 3, 0, unit)
                blocks_wait(chips, 4, unit)
            if unit >= 2:
                blocks_wait(12, 2, unit)
                blocks_wait(3, 10, unit)
            else:
                blocks_wait(chips - 1, 8, unit)
        for side in range(2):
            lead_wait(chips - 1, 0, side)
            lead_wait(chips, 2, side)
        wait_all(k.last, k.last_sems.at[0])


def call_kernel(plan, inputs):
    layers, halves, Q, channels = plan.layers, plan.halves, plan.steps, plan.channels
    vals, shard, hidden, devices = plan.values, plan.shard, plan.hidden, plan.devices
    vmem = pl.BlockSpec(memory_space=pltpu.VMEM)
    anywhere = pl.BlockSpec(memory_space=pl.ANY)
    places = {"lens": pl.BlockSpec(memory_space=pltpu.SMEM), "frames": anywhere, "cot": anywhere,
              "out": anywhere, "frames_grad": anywhere}
    slots = 2 * layers

    def shape(*dims, dtype=F32):
        return jax.ShapeDtypeStruct(dims, dtype)
    outs = {
        "out": shape(plan.slots, channels),
        "frames_grad": shape(2 * plan.slots // 128, 128, channels),
    }
    params = {
        "dw": shape(layers, halves, plan.dw_rows, LANES),
        "point": shape(layers, channels, channels, dtype=BF16),
        "gains": shape(layers, halves, LANES),
        "shifts": shape(layers, halves, LANES),
        "squeeze_t": shape(2, hidden, channels),
        "expand": shape(2, hidden, channels),
    }
    grads = {
        "dw_grad": shape(layers, halves, plan.tap_rows, LANES),
        "point_grad": shape(2 if plan.fused else layers, channels, channels),
        "gains_grad": shape(layers, halves, LANES),
        "shifts_grad": shape(layers, halves, LANES),
        "squeeze_grad": shape(2, hidden, channels),
        "expand_grad": shape(2, hidden, channels),
    }
    scratch = {
        "hid": shape(2 * plan.sub + 1, halves, plan.pad, 8, LANES),
        "acts": shape(layers, plan.rows, channels, dtype=BF16),
        "prods": shape(layers, halves, Q, 8, LANES),
        "gd": shape(halves, plan.pad, 8, LANES),
        "gz": shape(halves, Q, 8, LANES),
        "gpb": shape(plan.rows, channels, dtype=BF16),
        "gqb": shape(plan.rows, channels, dtype=BF16),
        "pre": shape(2, halves, Q, 8, LANES),
        "wide": shape(halves, 2 * plan.slots + 4 * GAP, LANES),
        "frames_v": shape(2 * plan.slots, channels, dtype=BF16),
        "cot_v": shape(plan.slots, channels),
        "frames_grad_v": shape(plan.slots // 256, 128, channels),
        "first_mask": shape(Q, 8, LANES),
        "valid": shape(Q, 8, LANES),
        "slope": shape(halves, Q, 8, LANES),
        "skip": shape(halves, Q, 8, LANES),
        "psum": shape(2, 8, channels),
        "stats": shape(layers, 8, LANES),
        "send4": shape(slots, 4, LANES),
        "recv4": shape(layers, devices, 4, LANES),
        "counts": shape(devices, 4, LANES),
        "csend": shape(4, LANES),
        "norm_count": shape(4, LANES),
    }
    sems = {"send_sem": (slots,), "recv_sem": (slots,), "count_sems": (2,), "io_sems": (11,)}
    if plan.fused:
        units, chips = 1 + plan.per, devices // 2
        outs.update({
            "dw_first_out": shape(plan.sub, shard, plan.taps[0]),
            "dw_second_out": shape(plan.sub, shard, plan.taps[1]),
            "point_out": shape(2, plan.per, shard, channels),
            "gains_out": shape(plan.per, 2, shard),
            "shifts_out": shape(plan.per, 2, shard),
            "squeeze_out": shape(2, shard, hidden),
            "expand_out": shape(2, shard, hidden),
        })
        scratch.update(params)
        scratch.update(grads)
        scratch.update({
            "tile": shape(8, LANES),
            "point_t": shape(layers, channels, channels, dtype=BF16),
            "packed": shape(vals, LANES),
            "packed_t": shape(16, vals),
            "first": shape(devices, 4, LANES),
            "last_mine": shape(devices, 4, LANES),
            "last": shape(devices, 4, LANES),
            "unpacked": shape(vals, LANES),
            "gath": shape(units, 4, 4, 2, 16, channels, dtype=BF16),
            "lead": shape(2, 4, 4, 2, 16, LANES, dtype=BF16),
            "shares": shape(2, 4, 4, 2, 16, channels, dtype=BF16),
            "inbox": shape(units, 4, 4, 16, channels, dtype=BF16),
            "sums": shape(3, 4, 4, 16, channels, dtype=BF16),
            "gained": shape(2, chips, 16, channels, dtype=BF16),
            "by_plane": shape(units, 4, 4, 16, channels, dtype=BF16),
            "line": shape(units, 4, 16, channels, dtype=BF16),
            "by_depth": shape(units, 4, 16, channels, dtype=BF16),
            "own_norm": shape(channels, LANES),
        })
        sems["unit_sems"] = (12, units)
        sems["last_sems"] = (2,)
        sems["lead_sems"] = (4, 2)
        sems["param_sems"] = (len(PARAMS),)
        for name in PARAMS:
            scratch[name + "_v"] = inputs[name]
            places[name] = anywhere
    else:
        outs.update(grads)
        scratch["dw"] = params["dw"]
    names = list(inputs) + list(outs) + list(scratch) + list(sems)
    results = pl.pallas_call(
        functools.partial(kernel, plan, names),
        out_shape=list(outs.values()),
        in_specs=[places.get(name, vmem) for name in inputs],
        out_specs=[places.get(name, vmem) for name in outs],
        scratch_shapes=[pltpu.VMEM(v.shape, v.dtype) for v in scratch.values()]
        + [pltpu.SemaphoreType.DMA(v) for v in sems.values()],
        compiler_params=pltpu.CompilerParams(
            collective_id=0, has_side_effects=True, vmem_limit_bytes=63 * 1024 * 1024),
    )(*inputs.values())
    if plan.fused:
        results = hand_on(results)
    return dict(zip(outs, results, strict=True))


def hand_on(arrays):
    n = len(arrays)
    parts = []
    for i, v in enumerate(arrays):
        rows = max(1, v.shape[0] * (1 << 20) // (4 * v.size))
        parts += [(i, start, min(rows, v.shape[0] - start)) for start in range(0, v.shape[0], rows)]

    def move(*refs):
        here, there, held, sems = refs[:n], refs[n:2 * n], refs[2 * n:3 * n], refs[3 * n]
        into, out = [], []
        for p, (i, start, size) in enumerate(parts):
            rows = pl.ds(start, size)
            into.append(pltpu.make_async_copy(here[i].at[rows], held[i].at[rows], sems.at[0, p]))
            out.append(pltpu.make_async_copy(held[i].at[rows], there[i].at[rows], sems.at[1, p]))
        for copy in into:
            copy.start()
        for p in range(len(parts)):
            into[p].wait()
            out[p].start()
        for copy in out:
            copy.wait()
    anywhere = pl.BlockSpec(memory_space=pl.ANY)
    return pl.pallas_call(
        move,
        out_shape=[jax.ShapeDtypeStruct(v.shape, v.dtype) for v in arrays],
        in_specs=[anywhere] * n,
        out_specs=[anywhere] * n,
        scratch_shapes=[pltpu.VMEM(v.shape, v.dtype) for v in arrays] + [pltpu.SemaphoreType.DMA((2, len(parts)))],
    )(*arrays)


def body(frames, dw_first, dw_second, point, gains, shifts, se_down, se_up, cotangent, lengths, *, devices):
    sub, taps_first, shard = dw_first.shape
    taps_second = dw_second.shape[1]
    hidden = se_down.shape[2]
    channels = point.shape[3]
    plan = Plan(cotangent.shape[0], channels, taps_first, taps_second, sub, hidden, devices)
    if plan.fused:
        res = call_kernel(plan, {
            "lens": lengths, "frames": frames, "cot": cotangent,
            "dw_first": jnp.swapaxes(dw_first, 1, 2), "dw_second": jnp.swapaxes(dw_second, 1, 2),
            "point_in": point, "gains_in": jnp.swapaxes(gains, 0, 1), "shifts_in": jnp.swapaxes(shifts, 0, 1),
            "se_down": se_down, "se_up": jnp.swapaxes(se_up, 1, 2)})
        return (
            res["out"], res["frames_grad"].reshape(2 * plan.slots, channels), jnp.swapaxes(res["dw_first_out"], 1, 2),
            jnp.swapaxes(res["dw_second_out"], 1, 2), res["point_out"], jnp.swapaxes(res["gains_out"], 0, 1),
            jnp.swapaxes(res["shifts_out"], 0, 1), res["squeeze_out"], jnp.swapaxes(res["expand_out"], 1, 2))

    per, layers, halves = plan.per, plan.layers, plan.halves

    def gather(v, axis):
        return lax.all_gather(v, "dp", axis=axis, tiled=True)
    small = jnp.concatenate([
        dw_first.reshape(-1, shard), dw_second.reshape(-1, shard), gains.reshape(-1, shard),
        shifts.reshape(-1, shard), se_up.reshape(-1, shard),
        jnp.swapaxes(se_down, 1, 2).reshape(-1, shard)], axis=0)
    small = gather(small, 1).astype(F32)
    sizes = [sub * taps_first, sub * taps_second, layers, layers, 2 * hidden, 2 * hidden]
    part = jnp.split(small, [sum(sizes[:i]) for i in range(1, 6)], axis=0)

    def dw_layout(v, taps):
        v = v.reshape(sub, taps, halves, LANES).transpose(0, 2, 1, 3)
        return jnp.pad(v, ((0, 1), (0, 0), (0, plan.dw_rows - taps), (0, 0)))
    res = call_kernel(plan, {
        "lens": lengths, "frames": frames, "cot": cotangent,
        "dw_in": jnp.concatenate([dw_layout(part[0], taps_first), dw_layout(part[1], taps_second)], axis=0),
        "point": gather(point, 2).reshape(layers, channels, channels),
        "gains": part[2].reshape(layers, halves, LANES),
        "shifts": part[3].reshape(layers, halves, LANES),
        "squeeze_t": part[5].reshape(2, hidden, channels),
        "expand": part[4].reshape(2, hidden, channels)})

    def scatter(v, axis):
        return lax.psum_scatter(v, "dp", scatter_dimension=axis, tiled=True)

    def dw_out(v, taps):
        return v[:sub, :, :taps].transpose(0, 2, 1, 3).reshape(sub * taps, channels)
    grads = res["dw_grad"]
    packed = scatter(jnp.concatenate(
        [dw_out(grads[:per], taps_first), dw_out(grads[per:], taps_second),
         res["squeeze_grad"].reshape(-1, channels), res["expand_grad"].reshape(-1, channels)], axis=0), 1)
    g1, g2, gsq, gex = jnp.split(packed, [sizes[0], sizes[0] + sizes[1], sizes[0] + sizes[1] + sizes[5]], axis=0)

    def norm_out(v):
        return lax.dynamic_slice_in_dim(v.reshape(2, per, channels), lax.axis_index("dp") * shard, shard, 2)
    return (
        res["out"], res["frames_grad"].reshape(2 * plan.slots, channels), g1.reshape(sub, taps_first, shard), g2.reshape(sub, taps_second, shard),
        scatter(res["point_grad"].reshape(2, per, channels, channels), 2),
        norm_out(res["gains_grad"]), norm_out(res["shifts_grad"]),
        jnp.swapaxes(gsq.reshape(2, hidden, shard), 1, 2), gex.reshape(2, hidden, shard))


def solution(mesh):
    return jax.shard_map(
        functools.partial(body, devices=mesh.shape["dp"]),
        mesh=mesh,
        in_specs=(
            P("dp", None),
            P(None, None, "dp"),
            P(None, None, "dp"),
            P(None, None, "dp", None),
            P(None, None, "dp"),
            P(None, None, "dp"),
            P(None, "dp", None),
            P(None, None, "dp"),
            P("dp", None),
            P("dp"),
        ),
        out_specs=(
            P("dp", None),
            P("dp", None),
            P(None, None, "dp"),
            P(None, None, "dp"),
            P(None, None, "dp", None),
            P(None, None, "dp"),
            P(None, None, "dp"),
            P(None, "dp", None),
            P(None, None, "dp"),
        ),
        check_vma=False,
    )
```
